32 devices in a mesh: grp: 2 (over x), fsdp: 16 (over z, y, core).
Axes of the slice: x: 2, y: 2, z: 4, core: 2. Of those that a mesh axis runs over, the one named last changes fastest.
Arguments:
- inputs: bfloat16 [2, 2048, 1536], P('grp', 'fsdp'), may hold values from -6 to 6
- cotangent: bfloat16 [2, 2048, 1536], P('grp', 'fsdp'), may hold values from -6 to 6
- weights: float32 [1536, 19968], P(('grp', 'fsdp')), may hold values from -2.44948974 to 2.44948974
- weights_first: float32 [1536, 19968], P(('grp', 'fsdp')), may hold values from -0.00030517578 to 0.00030517578
- weights_second: float32 [1536, 19968], P(('grp', 'fsdp')), may hold values from 1.6279285e-09 to 6.511714e-09
- gains: float32 [4, 1536], replicated, may hold values from 0.8 to 6.25
- gains_first: float32 [4, 1536], replicated, may hold values from -0.00030517578 to 0.00030517578
- gains_second: float32 [4, 1536], replicated, may hold values from 1.6279285e-09 to 6.511714e-09
- forget_weight: float32 [1536, 24], replicated, may hold values from -0.078125 to 0.078125
- forget_first: float32 [1536, 24], replicated, may hold values from -0.00030517578 to 0.00030517578
- forget_second: float32 [1536, 24], replicated, may hold values from 1.6279285e-09 to 6.511714e-09
- forget_bias: float32 [24], replicated
- bias_first: float32 [24], replicated, may hold values from -0.00030517578 to 0.00030517578
- bias_second: float32 [24], replicated, may hold values from 1.6279285e-09 to 6.511714e-09
Outputs:
- output: bfloat16 [2, 2048, 1536], P('grp', 'fsdp')
- input_grad: bfloat16 [2, 2048, 1536], P('grp', 'fsdp')
- grad_norm: float32 [], replicated
- new_weights: float32 [1536, 19968], P(('grp', 'fsdp'))
- new_weights_first: float32 [1536, 19968], P(('grp', 'fsdp'))
- new_weights_second: float32 [1536, 19968], P(('grp', 'fsdp'))
- new_gains: float32 [4, 1536], replicated
- new_gains_first: float32 [4, 1536], replicated
- new_gains_second: float32 [4, 1536], replicated
- new_forget_weight: float32 [1536, 24], replicated
- new_forget_first: float32 [1536, 24], replicated
- new_forget_second: float32 [1536, 24], replicated
- new_forget_bias: float32 [24], replicated
- new_bias_first: float32 [24], replicated
- new_bias_second: float32 [24], replicated
The draws below stay inside these ranges and needn't reach their ends.
All inputs are finite; a program needn't handle non-finite values.
Results may differ from the reference program's by a relative error of at most 0.038.
Values may be sent and summed in bfloat16 or wider, within the bound.
A program may use at most 640 MiB of HBM per device.

```python
import math
import jax
import jax.numpy as jnp
from jax import lax

D = 1536
H = 24
DH = 64
F = 4096
STEP = 5
SPAN = 2048
GROUPS = 2
NPARAM = 30713880


def draw_weights(key, part):
    key = jax.random.fold_in(key, 11)
    width = 5 * D + 3 * F
    columns = jnp.arange(width)
    scale = jnp.where(columns < 4 * D, D ** (-0.5), jnp.where(columns < 5 * D, 16.0 * D ** (-0.5), jnp.where(columns < 5 * D + 2 * F, D ** (-0.5), 2.0 * F ** (-0.5))))
    base = jnp.clip(jax.random.normal(key, (D, width), jnp.float32), -6.0, 6.0)
    return base * scale[None, :].astype(jnp.float32)


def draw_gains(key, part):
    key = jax.random.fold_in(key, 12)
    position = jnp.arange(D).astype(jnp.float32) / D
    rising = 1.0 + 2.0 * position
    noise = jax.random.uniform(key, (2, D), jnp.float32, 0.8, 1.25)
    heads = jax.random.uniform(jax.random.fold_in(key, 2), (2, D), jnp.float32, 0.9, 1.6)
    return jnp.concatenate([rising[None, :] * noise, heads], axis=0)


def draw_forget_bias(key, part):
    key = jax.random.fold_in(key, 13)
    upper = max(math.log(SPAN / 2.0), 3.5)
    return jax.random.uniform(key, (H,), jnp.float32, 2.5, upper)


def shard_levels(own_key, extent, cuts, least, largest):
    level, own = 1.0, jax.random.fold_in(own_key, 6)
    for axis_at, shards_of in cuts:
        heights = jnp.exp(jax.random.uniform(jax.random.fold_in(own, axis_at), (shards_of,), jnp.float32, least / len(cuts), largest / len(cuts)))
        level = level * jnp.repeat(heights, extent[axis_at] // shards_of).reshape([-1 if axis == axis_at else 1 for axis in range(len(extent))])
    return level


def scatter_about(stream_key, dims, spread, limit, shards=(), dtype=jnp.bfloat16):
    array = jax.random.normal(stream_key, dims, jnp.float32) * spread
    if len(shards) > 0:
        array = shard_levels(stream_key, dims, shards, -0.22, 0.18) * array
    return jnp.clip(array, min=-limit, max=limit).astype(dtype)


def setup_inputs(seed: int = 0) -> dict:
    splits = jax.random.split(jax.random.key(seed), 15)
    return {
        "inputs": scatter_about(splits[0], (GROUPS, SPAN, D), 1.0, 6.0, ((0, 2), (1, 16))),
        "cotangent": scatter_about(splits[1], (GROUPS, SPAN, D), 1.0, 6.0, ((0, 2), (1, 16))),
        "weights": draw_weights(jax.random.fold_in(splits[14], 71), 0),
        "weights_first": scatter_about(splits[3], (D, 5 * D + 3 * F), (0.11 / NPARAM ** 0.5), 0.00030517578, ((0, 32),), jnp.float32),
        "weights_second": jnp.clip(jnp.exp(math.log(6.511713834811417e-09) - 1.3862944 * jax.random.uniform(splits[4], (D, 5 * D + 3 * F), jnp.float32) ** shard_levels(splits[4], (D, 5 * D + 3 * F), ((0, 32),), -0.2, 0.2)), 1.6279284587028542e-09, 6.511713834811417e-09),
        "gains": draw_gains(jax.random.fold_in(splits[14], 71), 0),
        "gains_first": scatter_about(splits[6], (4, D), (0.11 / NPARAM ** 0.5), 0.00030517578, (), jnp.float32),
        "gains_second": jnp.clip(jnp.exp(jax.random.uniform(splits[7], (4, D), jnp.float32, math.log(1.6279284587028542e-09), math.log(6.511713834811417e-09))), 1.6279284587028542e-09, 6.511713834811417e-09),
        "forget_weight": scatter_about(splits[8], (D, H), (4 * D) ** -0.5, 0.078125, (), jnp.float32),
        "forget_first": scatter_about(splits[9], (D, H), (0.11 / NPARAM ** 0.5), 0.00030517578, (), jnp.float32),
        "forget_second": jnp.clip(jnp.exp(jax.random.uniform(splits[10], (D, H), jnp.float32, math.log(1.6279284587028542e-09), math.log(6.511713834811417e-09))), 1.6279284587028542e-09, 6.511713834811417e-09),
        "forget_bias": draw_forget_bias(jax.random.fold_in(splits[14], 71), 0),
        "bias_first": scatter_about(splits[12], (H,), (0.11 / NPARAM ** 0.5), 0.00030517578, (), jnp.float32),
        "bias_second": jnp.clip(jnp.exp(jax.random.uniform(splits[13], (H,), jnp.float32, math.log(1.6279284587028542e-09), math.log(6.511713834811417e-09))), 1.6279284587028542e-09, 6.511713834811417e-09),
    }


EPS = 1e-06
BETA_ONE = 0.9
BETA_TWO = 0.95
ADAM_EPS = 1e-08
RATE_MATRIX = 0.1
RATE_GAIN = 1.2
RATE_BIAS = 3.0
DECAY = 0.1
CLIP = 1.0
NEGATIVE = -1e+30
HIGH = lax.Precision.HIGHEST

@jax.custom_vjp
def low(v):
    return lax.optimization_barrier(v.astype(jnp.bfloat16)).astype(jnp.float32)

@jax.custom_vjp
def low_back(v):
    return v

def low_keep(v):
    return (low(v), None)

def low_pass(kept, grad):
    return (grad,)

def back_keep(v):
    return (v, None)

def back_low(kept, grad):
    return (low(grad),)
low.defvjp(low_keep, low_pass)
low_back.defvjp(back_keep, back_low)

def rms_rows(value, gain):
    return value * lax.rsqrt(lax.optimization_barrier(jnp.mean(value * value, axis=-1, keepdims=True)) + EPS) * gain

def head_norm(value, gain):
    count = value.shape[0]
    heads = value.reshape(count, H, DH)
    heads = heads * lax.rsqrt(lax.optimization_barrier(jnp.mean(heads * heads, axis=-1, keepdims=True)) + EPS)
    return heads.reshape(count, H * DH) * gain

def matmul(left, right):
    return jnp.dot(left, right, precision=HIGH, preferred_element_type=jnp.float32)

def attend(queries, keys, values, forget_sum):
    block = min(512, SPAN)
    count = SPAN // block
    scale = DH ** (-0.5)
    query_blocks = queries.reshape(count, block, H, DH)
    sum_blocks = forget_sum.reshape(count, block, H)
    starts = (jnp.arange(count) * block).astype(jnp.int32)
    columns = jnp.arange(SPAN).astype(jnp.int32)

    def one(pieces):
        query, query_sum, start = pieces
        inner = low_back(jnp.einsum('qhd,khd->hqk', query, keys, precision=HIGH))
        scores = inner * scale + query_sum.T[:, :, None] - forget_sum.T[:, None, :]
        positions = start + jnp.arange(block).astype(jnp.int32)
        scores = jnp.where((columns[None, :] <= positions[:, None])[None], scores, NEGATIVE)
        top = lax.optimization_barrier(jnp.max(scores, axis=-1, keepdims=True))
        lse = top + jnp.log(lax.optimization_barrier(jnp.sum(jnp.exp(scores - top), axis=-1, keepdims=True)))
        weight = low(jnp.exp(scores - lse))
        return jnp.einsum('hqk,khd->qhd', weight, values, precision=HIGH)
    result = lax.map(jax.checkpoint(one), (query_blocks, sum_blocks, starts))
    return result.reshape(SPAN, H * DH)

def span_forward(source, low_w, gains, forget_low, forget_bias):
    first = low(rms_rows(source, gains[0]))
    projected = low_back(matmul(first, low_w[:, :4 * D]))
    logit = low_back(matmul(first, forget_low) + forget_bias)
    queries = low(head_norm(projected[:, :D], gains[2]))
    keys = low(head_norm(projected[:, D:2 * D], gains[3]))
    values = low(projected[:, 2 * D:3 * D])
    forget_sum = jnp.cumsum(jax.nn.log_sigmoid(logit), axis=0)
    attended = low_back(attend(queries.reshape(SPAN, H, DH), keys.reshape(SPAN, H, DH), values.reshape(SPAN, H, DH), forget_sum))
    gated = low(attended * jax.nn.sigmoid(projected[:, 3 * D:]))
    mixed = source + low_back(matmul(gated, low_w[:, 4 * D:5 * D].T))
    second = low(rms_rows(mixed, gains[1]))
    gate_up = low_back(matmul(second, low_w[:, 5 * D:5 * D + 2 * F]))
    hidden = low(jax.nn.silu(gate_up[:, :F]) * gate_up[:, F:])
    return mixed + matmul(hidden, low_w[:, 5 * D + 2 * F:].T)

def adam(value, first, second, grad, rate, decay):
    first = BETA_ONE * first + (1.0 - BETA_ONE) * grad
    second = BETA_TWO * second + (1.0 - BETA_TWO) * grad * grad
    unbiased_first = first / (1.0 - BETA_ONE ** STEP)
    unbiased_second = second / (1.0 - BETA_TWO ** STEP)
    value = value - rate * (unbiased_first / (jnp.sqrt(unbiased_second) + ADAM_EPS) + decay * value)
    return (value, first, second)

def reference(inputs, cotangent, weights, weights_first, weights_second, gains, gains_first, gains_second, forget_weight, forget_first, forget_second, forget_bias, bias_first, bias_second):

    def layer(source, matrix, gain, forget_matrix, bias):
        low_w = low(matrix)
        forget_low = low(forget_matrix)
        return lax.map(lambda piece: span_forward(piece, low_w, gain, forget_low, bias), source)
    result, pullback = jax.vjp(layer, inputs.astype(jnp.float32), weights, gains, forget_weight, forget_bias)
    grad_x, grad_w, grad_g, grad_fw, grad_fb = pullback(cotangent.astype(jnp.float32))
    grad_norm = jnp.sqrt(jnp.sum(grad_w * grad_w) + jnp.sum(grad_g * grad_g) + jnp.sum(grad_fw * grad_fw) + jnp.sum(grad_fb * grad_fb))
    factor = CLIP / jnp.maximum(grad_norm, CLIP)
    new_w, new_wf, new_ws = adam(weights, weights_first, weights_second, grad_w * factor, RATE_MATRIX, DECAY)
    new_g, new_gf, new_gs = adam(gains, gains_first, gains_second, grad_g * factor, RATE_GAIN, 0.0)
    new_fw, new_ff, new_fs = adam(forget_weight, forget_first, forget_second, grad_fw * factor, RATE_MATRIX, DECAY)
    new_fb, new_bf, new_bs = adam(forget_bias, bias_first, bias_second, grad_fb * factor, RATE_BIAS, 0.0)
    return (result.astype(jnp.bfloat16), grad_x.astype(jnp.bfloat16), grad_norm, new_w, new_wf, new_ws, new_g, new_gf, new_gs, new_fw, new_ff, new_fs, new_fb, new_bf, new_bs)
```

```python
import functools

import jax
import jax.numpy as jnp
from jax import lax
from jax.experimental import pallas as pl
from jax.experimental.pallas import tpu as pltpu
from jax.sharding import PartitionSpec as P

D = 1536
H = 24
DH = 64
F = 4096
STEP = 5

EPS = 1e-06
BETA_ONE = 0.9
BETA_TWO = 0.95
ADAM_EPS = 1e-08
RATE_MATRIX = 0.1
RATE_GAIN = 1.2
RATE_BIAS = 3.0
DECAY = 0.1
CLIP = 1.0
NEGATIVE = -1e30

TP = 8
HEADS = H // TP
UNITS = F // TP
QKVG = HEADS * 4 * DH
WIDTH = QKVG + 3 * UNITS + 256
LANES = 128
ROWS = 256
BLOCK = 512
MESH = pl.DeviceIdType.MESH
HALF = jnp.bfloat16
FULL = jnp.float32
VMEM_BYTES = 56 * 1024 * 1024


def params(collective=None, **more):
    if collective is None:
        return pltpu.CompilerParams(vmem_limit_bytes=VMEM_BYTES, **more)
    return pltpu.CompilerParams(
        collective_id=collective, has_side_effects=True, vmem_limit_bytes=VMEM_BYTES, **more
    )


def flip(member, bits):
    for bit in (1, 2, 4):
        if bits & bit:
            member = member + bit - 2 * bit * lax.rem(lax.div(member, bit), 2)
    return member


def place():
    position = lax.axis_index("fsdp")
    return lax.axis_index("grp"), lax.div(position, TP), lax.rem(position, TP)


def greet(targets):
    barrier = pltpu.get_barrier_semaphore()
    for target in targets:
        pl.semaphore_signal(barrier, inc=1, device_id=target, device_id_type=MESH)
    pl.semaphore_wait(barrier, len(targets))


class Lines:
    def __init__(self, send, receive):
        self.send, self.receive, self.count, self.made = send, receive, 0, []

    def plan(self, source, target, device):
        copy = pltpu.make_async_remote_copy(
            src_ref=source,
            dst_ref=target,
            send_sem=self.send.at[self.count],
            recv_sem=self.receive.at[self.count],
            device_id=device,
            device_id_type=MESH,
        )
        self.count += 1
        self.made.append(copy)
        return copy


def dot(left, right, contract=(1, 0)):
    return lax.dot_general(
        left, right, (((contract[0],), (contract[1],)), ((), ())), preferred_element_type=FULL
    )


def rms_rows(value, gain):
    return value * lax.rsqrt(jnp.mean(value * value, axis=-1, keepdims=True) + EPS) * gain


def rms_back(value, gain, grad):
    inverse = lax.rsqrt(jnp.mean(value * value, axis=-1, keepdims=True) + EPS)
    normal = value * inverse
    scaled = grad * gain
    pulled = inverse * (scaled - normal * jnp.mean(scaled * normal, axis=-1, keepdims=True))
    return pulled, jnp.sum(grad * normal, axis=0, keepdims=True)


def start_counts(grps, groups):
    tokens = groups * TP - 1
    weights = (TP - 1) + (groups - 1) * TP + (grps - 1) * groups * TP
    return tokens + weights + (TP - 1)


def start_kernel(grps, groups, a_ref, c_ref, w_ref, span_ref, cot_ref, full_ref, send, receive, local):
    grp, group, member = place()

    def device(to_grp=0, to_group=0, bits=0):
        return (
            lax.rem(grp + to_grp, grps),
            lax.rem(group + to_group, groups) * TP + flip(member, bits),
        )

    greet(
        [device(bits=bits) for bits in range(1, TP)]
        + [device(to_group=step) for step in range(1, groups)]
        + [device(to_grp=step) for step in range(1, grps)]
    )
    lines = Lines(send, receive)
    tokens, cots, first, across, over = {}, {}, {}, {}, {}
    for back in range(groups):
        origin = lax.rem(group + back, groups)
        if back:
            tokens[back, 0] = lines.plan(a_ref, span_ref.at[group, member], device(to_group=groups - back))
        for bits in (1, 2, 4, 6):
            slot = span_ref.at[origin, member]
            source = a_ref if back == 0 else slot
            tokens[back, bits] = lines.plan(source, slot, device(bits=bits))
        for bits in (2, 4, 6):
            slot = span_ref.at[origin, flip(member, bits)]
            tokens[back, bits + 1] = lines.plan(slot, slot, device(bits=1))
    for bits in (1, 2, 4, 6):
        cots[bits] = lines.plan(c_ref, cot_ref.at[member], device(bits=bits))
    for bits in (2, 4, 6):
        slot = cot_ref.at[flip(member, bits)]
        cots[bits + 1] = lines.plan(slot, slot, device(bits=1))
    for bits in range(1, TP):
        first[bits] = lines.plan(w_ref.at[flip(member, bits)], full_ref.at[grp, group, member], device(bits=bits))
    for bits in range(TP):
        slot = full_ref.at[grp, group, flip(member, bits)]
        source = w_ref.at[member] if bits == 0 else slot
        for back in range(1, groups):
            across[back, bits] = lines.plan(source, slot, device(to_group=groups - back))
        for step in range(1, grps):
            over[step, 0, bits] = lines.plan(source, slot, device(to_grp=step))
        for back in range(1, groups):
            passed = full_ref.at[grp, lax.rem(group + back, groups), flip(member, bits)]
            for step in range(1, grps):
                over[step, back, bits] = lines.plan(passed, passed, device(to_grp=step))

    own = [
        pltpu.make_async_copy(a_ref, span_ref.at[group, member], local.at[0]),
        pltpu.make_async_copy(c_ref, cot_ref.at[member], local.at[1]),
        pltpu.make_async_copy(w_ref.at[member], full_ref.at[grp, group, member], local.at[2]),
    ]
    for back in range(1, groups):
        tokens[back, 0].start()
        across[back, 0].start()
    for bits in (2, 4, 6, 1):
        tokens[0, bits].start()
    for step in range(1, grps):
        over[step, 0, 0].start()
    for bits in range(1, TP):
        first[bits].start()
    for bits in (2, 4, 6, 1):
        cots[bits].start()
    for copy in own:
        copy.start()
    for bits in (2, 4, 6):
        tokens[0, bits].wait_recv()
        tokens[0, bits + 1].start()
    for bits in range(1, TP):
        first[bits].wait_recv()
        for back in range(1, groups):
            across[back, bits].start()
        for step in range(1, grps):
            over[step, 0, bits].start()
    for back in range(1, groups):
        tokens[back, 0].wait_recv()
        for bits in (2, 4, 6, 1):
            tokens[back, bits].start()
    for bits in (2, 4, 6):
        cots[bits].wait_recv()
        cots[bits + 1].start()
    for back in range(1, groups):
        for bits in (2, 4, 6):
            tokens[back, bits].wait_recv()
            tokens[back, bits + 1].start()
    for back in range(1, groups):
        for bits in range(TP):
            across[back, bits].wait_recv()
            for step in range(1, grps):
                over[step, back, bits].start()
    for back in range(groups):
        for bits in (1, 3, 5, 7):
            tokens[back, bits].wait_recv()
    for bits in (1, 3, 5, 7):
        cots[bits].wait_recv()
    for copy in over.values():
        copy.wait_recv()
    for copy in lines.made:
        copy.wait_send()
    for copy in own:
        copy.wait()


def start(low, cotangent, pack, grps, groups):
    rows, own = low.shape[0], pack.shape[1]
    count = start_counts(grps, groups)
    spec = pl.BlockSpec(memory_space=pl.ANY)
    return pl.pallas_call(
        functools.partial(start_kernel, grps, groups),
        out_shape=(
            jax.ShapeDtypeStruct((groups, TP, rows, D), HALF),
            jax.ShapeDtypeStruct((TP, rows, D), HALF),
            jax.ShapeDtypeStruct((grps, groups, TP, own, WIDTH), HALF),
        ),
        in_specs=[spec] * 3,
        out_specs=(spec,) * 3,
        scratch_shapes=[
            pltpu.SemaphoreType.DMA((count,)),
            pltpu.SemaphoreType.DMA((count,)),
            pltpu.SemaphoreType.DMA((3,)),
        ],
        compiler_params=params(1),
        name="start",
    )(low, cotangent, pack)


def column(value, lane):
    lanes = lax.broadcasted_iota(jnp.int32, value.shape, 1)
    return jnp.sum(jnp.where(lanes == lane, value, 0.0), axis=1, keepdims=True)


def three(value):
    high = value.astype(HALF).astype(FULL)
    rest = value - high
    middle = rest.astype(HALF).astype(FULL)
    return high, middle, (rest - middle).astype(HALF).astype(FULL)


def at_lanes(lanes, pairs, other):
    for lane, value in pairs:
        other = jnp.where(lanes == lane, value, other)
    return other


def halves_mean(value, lanes):
    lower = jnp.sum(jnp.where(lanes < DH, value, 0.0), axis=1, keepdims=True)
    upper = jnp.sum(jnp.where(lanes < DH, 0.0, value), axis=1, keepdims=True)
    return jnp.where(lanes < DH, lower, upper) * (1.0 / DH)


def project_kernel(a_ref, w_ref, f_ref, b_ref, g_ref, q_ref, k_ref, v_ref, p_ref, z_ref, s_ref, carry):
    @pl.when(pl.program_id(0) == 0)
    def clear():
        carry[...] = jnp.zeros_like(carry)

    low = a_ref[...]
    made = dot(low, w_ref[...])
    p_ref[...] = made
    logit = dot(low, f_ref[...]) + b_ref[...]
    z_ref[...] = logit
    log_gate = jnp.minimum(logit, 0.0) - jnp.log1p(jnp.exp(-jnp.abs(logit)))
    count = low.shape[0]
    row = lax.broadcasted_iota(jnp.int32, (count, count), 0)
    col = lax.broadcasted_iota(jnp.int32, (count, count), 1)
    sums = (
        lax.dot_general(
            jnp.where(col <= row, 1.0, 0.0),
            log_gate,
            (((1,), (0,)), ((), ())),
            precision=lax.Precision.HIGHEST,
            preferred_element_type=FULL,
        )
        + carry[0:1]
    )
    carry[0:1] = sums[count - 1 : count]
    s_ref[...] = sums
    lanes = lax.broadcasted_iota(jnp.int32, (count, LANES), 1)
    for head in range(HEADS):
        pair = made[:, 256 * head : 256 * head + LANES]
        value = made[:, 256 * head + LANES : 256 * head + 2 * LANES]
        normal = pair * lax.rsqrt(halves_mean(pair * pair, lanes) + EPS) * g_ref[head : head + 1]
        normal = normal.astype(HALF).astype(FULL)
        high, middle, least = three(column(sums, head))
        ones = jnp.where(lanes < DH + 6, 1.0, 0.0)
        q_ref[head] = jnp.where(
            lanes < DH,
            normal * (DH**-0.5),
            at_lanes(lanes, ((DH, high), (DH + 1, middle), (DH + 2, least)), ones),
        ).astype(HALF)
        ones = jnp.where(lanes < DH + 3, 1.0, 0.0)
        k_ref[head] = jnp.where(
            lanes < DH,
            pltpu.roll(normal, DH, 1),
            at_lanes(lanes, ((DH + 3, -high), (DH + 4, -middle), (DH + 5, -least)), ones),
        ).astype(HALF)
        v_ref[head] = jnp.where(lanes < DH, value, ones).astype(HALF)


def project(span, full, forget, bias, gains):
    tokens = span.shape[0]
    tile = pl.BlockSpec((HEADS, ROWS, LANES), lambda i: (0, i, 0))
    return pl.pallas_call(
        project_kernel,
        grid=(tokens // ROWS,),
        out_shape=(
            jax.ShapeDtypeStruct((HEADS, tokens, LANES), HALF),
            jax.ShapeDtypeStruct((HEADS, tokens, LANES), HALF),
            jax.ShapeDtypeStruct((HEADS, tokens, LANES), HALF),
            jax.ShapeDtypeStruct((tokens, QKVG), FULL),
            jax.ShapeDtypeStruct((tokens, LANES), FULL),
            jax.ShapeDtypeStruct((tokens, LANES), FULL),
        ),
        in_specs=[
            pl.BlockSpec((ROWS, D), lambda i: (i, 0)),
            pl.BlockSpec((D, QKVG), lambda i: (0, 0)),
            pl.BlockSpec((D, LANES), lambda i: (0, 0)),
            pl.BlockSpec((1, LANES), lambda i: (0, 0)),
            pl.BlockSpec((8, LANES), lambda i: (0, 0)),
        ],
        out_specs=(
            tile,
            tile,
            tile,
            pl.BlockSpec((ROWS, QKVG), lambda i: (i, 0)),
            pl.BlockSpec((ROWS, LANES), lambda i: (i, 0)),
            pl.BlockSpec((ROWS, LANES), lambda i: (i, 0)),
        ),
        scratch_shapes=[pltpu.VMEM((8, LANES), FULL)],
        compiler_params=params(),
        name="project",
    )(span, full, forget, bias, gains)


def sigmoid(value):
    return 1.0 / (1.0 + jnp.exp(-value))


def gates_of(made, lanes):
    second = [made[:, 256 * head + LANES : 256 * head + 2 * LANES] for head in range(HEADS)]
    left = jnp.where(lanes < DH, pltpu.roll(second[0], DH, 1), second[1])
    right = jnp.where(lanes < DH, pltpu.roll(second[2], DH, 1), 0.0)
    return left, right


def attend_kernel(where_ref, q_ref, k_ref, v_ref, p_ref, u_ref, o_ref, l_ref):
    count = q_ref.shape[1]
    before = where_ref[0] * (1024 // count) + pl.program_id(0)
    queries = [q_ref[head] for head in range(HEADS)]

    def visit(state, at, masked):
        new = []
        for head in range(HEADS):
            top, total, accum = state[head]
            scores = dot(queries[head], k_ref[head, pl.ds(at * count, count)], (1, 1))
            if masked:
                row = lax.broadcasted_iota(jnp.int32, scores.shape, 0)
                col = lax.broadcasted_iota(jnp.int32, scores.shape, 1)
                scores = jnp.where(col <= row, scores, NEGATIVE)
            high = jnp.maximum(top, jnp.max(scores, axis=1, keepdims=True))
            shrink = jnp.exp(top - high)
            weight = jnp.exp(scores - high)
            total = total * shrink + jnp.sum(weight, axis=1, keepdims=True)
            accum = accum * shrink + dot(weight.astype(HALF), v_ref[head, pl.ds(at * count, count)])
            new.append((high, total, accum))
        return tuple(new)

    state = tuple(
        (
            jnp.full((count, 1), NEGATIVE, FULL),
            jnp.zeros((count, 1), FULL),
            jnp.zeros((count, LANES), FULL),
        )
        for head in range(HEADS)
    )
    state = lax.fori_loop(0, before, lambda at, inner: visit(inner, at, False), state)
    state = visit(state, before, True)
    lanes = lax.broadcasted_iota(jnp.int32, (count, LANES), 1)
    out = [jnp.where(lanes < DH, accum / total, 0.0) for top, total, accum in state]
    left, right = gates_of(p_ref[...], lanes)
    pair = out[0] + pltpu.roll(out[1], DH, 1)
    o_ref[:, :LANES] = pair
    o_ref[:, LANES:] = out[2]
    u_ref[:, :LANES] = (pair * sigmoid(left)).astype(HALF)
    u_ref[:, LANES:] = (out[2] * sigmoid(right)).astype(HALF)
    logs = [top + jnp.log(total) for top, total, accum in state]
    l_ref[...] = at_lanes(lanes, tuple(enumerate(logs)), 0.0)


def attend(where, queries, keys, values, made, own):
    tokens = queries.shape[1]
    count = min(BLOCK, own)
    steps = own // count
    whole = pl.BlockSpec((HEADS, tokens, LANES), lambda i, w: (0, 0, 0))
    return pl.pallas_call(
        attend_kernel,
        grid_spec=pltpu.PrefetchScalarGridSpec(
            num_scalar_prefetch=1,
            grid=(steps,),
            in_specs=[
                pl.BlockSpec((HEADS, count, LANES), lambda i, w: (0, w[0] * steps + i, 0)),
                whole,
                whole,
                pl.BlockSpec((count, QKVG), lambda i, w: (w[0] * steps + i, 0)),
            ],
            out_specs=(
                pl.BlockSpec((count, 256), lambda i, w: (i, 0)),
                pl.BlockSpec((count, 256), lambda i, w: (i, 0)),
                pl.BlockSpec((count, LANES), lambda i, w: (i, 0)),
            ),
        ),
        out_shape=(
            jax.ShapeDtypeStruct((own, 256), HALF),
            jax.ShapeDtypeStruct((own, 256), FULL),
            jax.ShapeDtypeStruct((own, LANES), FULL),
        ),
        compiler_params=params(),
        name="attend",
    )(where, queries, keys, values, made)


def group_device(bits):
    grp, group, member = place()
    return (grp, group * TP + flip(member, bits))


def blocks_of(ref, core):
    value = ref[:, pl.ds(core, 1)]
    return value.reshape(ref.shape[0] * ref.shape[2], ref.shape[3])


def sum_plan(lines, stage):
    give, take, out, came = stage
    sibling = [lines.plan(give.at[at], take.at[at], group_device(1)) for at in range(4)]
    others = [lines.plan(out.at[at], came.at[at], group_device(bits)) for at, bits in enumerate((2, 4, 6))]
    return sibling, others


def sum_send(pairs, stage, plan, mine):
    give, take, out, came = stage
    sibling, others = plan
    grp, group, member = place()
    core, chip = lax.rem(member, 2), lax.div(member, 2)
    count = give.shape[1]
    theirs = sum(dot(blocks_of(left, 1 - core), right[...], (1, 1)) for left, right in pairs)
    mine[...] = theirs.reshape(4, count, D)
    order = [lax.div(flip(member, bits), 2) for bits in (2, 4, 6, 0)]
    for at in range(4):
        give[at] = mine[order[at]].astype(HALF)
        sibling[at].start()
    own = sum(dot(blocks_of(left, core), right[...], (1, 1)) for left, right in pairs)
    mine[...] = own.reshape(4, count, D)
    for at in range(3):
        sibling[at].wait_recv()
        out[at] = (mine[order[at]] + take[at].astype(FULL)).astype(HALF)
        others[at].start()
    sibling[3].wait_recv()
    return mine[chip] + take[3].astype(FULL)


def sum_take(total, stage, plan):
    give, take, out, came = stage
    for at in range(3):
        plan[1][at].wait_recv()
        total = total + came[at].astype(FULL)
    return total


def sum_scratch(rows):
    return [
        pltpu.VMEM((4, rows, D), HALF),
        pltpu.VMEM((4, rows, D), HALF),
        pltpu.VMEM((3, rows, D), HALF),
        pltpu.VMEM((3, rows, D), HALF),
    ]


def gather_plan(lines, block, all_ref):
    grp, group, member = place()
    plan = {bits: lines.plan(block, all_ref.at[member], group_device(bits)) for bits in (2, 4, 6, 1)}
    for bits in (2, 4, 6):
        slot = all_ref.at[flip(member, bits)]
        plan[bits + 1] = lines.plan(slot, slot, group_device(1))
    return plan


def gather_run(plan, own):
    own.start()
    for bits in (2, 4, 6, 1):
        plan[bits].start()
    for bits in (2, 4, 6):
        plan[bits].wait_recv()
        plan[bits + 1].start()
    for bits in (1, 3, 5, 7):
        plan[bits].wait_recv()
    own.wait()


def mix_kernel(u_ref, w_ref, x_ref, g_ref, y_ref, all_ref, mine, block, give, take, out, came, send, receive, local):
    greet([group_device(bits) for bits in (1, 2, 4, 6)])
    member = place()[2]
    lines = Lines(send, receive)
    stage = (give, take, out, came)
    sums = sum_plan(lines, stage)
    gathered = gather_plan(lines, block, all_ref)
    total = sum_take(sum_send([(u_ref, w_ref)], stage, sums, mine), stage, sums)
    mixed = x_ref[...].astype(FULL) + total
    y_ref[...] = mixed
    block[...] = rms_rows(mixed, g_ref[...]).astype(HALF)
    gather_run(gathered, pltpu.make_async_copy(block, all_ref.at[member], local.at[0]))
    for copy in lines.made:
        copy.wait_send()


def whole_spec(shape):
    zeros = (0,) * len(shape)
    return pl.BlockSpec(shape, lambda i: zeros)


def weight_spec(columns, at):
    return pl.BlockSpec((D, columns), lambda i: (0, at))


def mix(gated, full, source, gain):
    rows = source.shape[0]
    return pl.pallas_call(
        mix_kernel,
        grid=(1,),
        out_shape=(
            jax.ShapeDtypeStruct((rows, D), FULL),
            jax.ShapeDtypeStruct((TP, rows, D), HALF),
        ),
        in_specs=[
            whole_spec((4, 2, rows, 256)),
            weight_spec(256, (QKVG + 3 * UNITS) // 256),
            whole_spec((rows, D)),
            whole_spec((1, D)),
        ],
        out_specs=(whole_spec((rows, D)), pl.BlockSpec(memory_space=pl.ANY)),
        scratch_shapes=[pltpu.VMEM((4, rows, D), FULL), pltpu.VMEM((rows, D), HALF)]
        + sum_scratch(rows)
        + [
            pltpu.SemaphoreType.DMA((14,)),
            pltpu.SemaphoreType.DMA((14,)),
            pltpu.SemaphoreType.DMA((1,)),
        ],
        compiler_params=params(2),
        name="mix",
    )(gated.reshape(4, 2, rows, 256), full, source, gain)


def unmix_kernel(
    d_ref, wgu_ref, m_ref, wd_ref, x_ref, g_ref, c_ref,
    y_ref, dx_ref, dg_ref, all_ref,
    mine, block, give, take, out, came, give2, take2, out2, came2, send, receive, local,
):
    greet([group_device(bits) for bits in (1, 2, 4, 6)])
    member = place()[2]
    lines = Lines(send, receive)
    stage = (give, take, out, came)
    stage2 = (give2, take2, out2, came2)
    sums = sum_plan(lines, stage)
    sums2 = sum_plan(lines, stage2)
    gathered = gather_plan(lines, block, all_ref)
    total = sum_send([(d_ref, wgu_ref)], stage, sums, mine)
    forward = sum_send([(m_ref, wd_ref)], stage2, sums2, mine)
    total = sum_take(total, stage, sums)
    mixed = x_ref[...]
    pulled, dgain = rms_back(mixed, g_ref[...], total)
    grad = c_ref[...].astype(FULL) + pulled
    dx_ref[...] = grad
    dg_ref[...] = dgain
    block[...] = grad.astype(HALF)
    gather_run(gathered, pltpu.make_async_copy(block, all_ref.at[member], local.at[0]))
    y_ref[...] = (mixed + sum_take(forward, stage2, sums2)).astype(HALF)
    for copy in lines.made:
        copy.wait_send()


def unmix(grads, hidden, full, mixed, gain, returned):
    rows = mixed.shape[0]
    return pl.pallas_call(
        unmix_kernel,
        grid=(1,),
        out_shape=(
            jax.ShapeDtypeStruct((rows, D), HALF),
            jax.ShapeDtypeStruct((rows, D), FULL),
            jax.ShapeDtypeStruct((1, D), FULL),
            jax.ShapeDtypeStruct((TP, rows, D), HALF),
        ),
        in_specs=[
            whole_spec((4, 2, rows, 2 * UNITS)),
            pl.BlockSpec((D, 2 * UNITS), lambda i: (0, 0)),
            whole_spec((4, 2, rows, UNITS)),
            pl.BlockSpec((D, UNITS), lambda i: (0, 0)),
            whole_spec((rows, D)),
            whole_spec((1, D)),
            whole_spec((rows, D)),
        ],
        out_specs=(
            whole_spec((rows, D)),
            whole_spec((rows, D)),
            whole_spec((1, D)),
            pl.BlockSpec(memory_space=pl.ANY),
        ),
        scratch_shapes=[pltpu.VMEM((4, rows, D), FULL), pltpu.VMEM((rows, D), HALF)]
        + sum_scratch(rows) * 2
        + [
            pltpu.SemaphoreType.DMA((21,)),
            pltpu.SemaphoreType.DMA((21,)),
            pltpu.SemaphoreType.DMA((1,)),
        ],
        compiler_params=params(3),
        name="unmix",
    )(
        grads.reshape(4, 2, rows, 2 * UNITS),
        full[:, QKVG : QKVG + 2 * UNITS],
        hidden.reshape(4, 2, rows, UNITS),
        full[:, QKVG + 2 * UNITS : QKVG + 3 * UNITS],
        mixed,
        gain,
        returned,
    )


def finish_kernel(
    p_ref, w_ref, z_ref, f_ref, x_ref, g_ref, d_ref, y_ref, dg_ref, mine, give, take, out, came, send, receive
):
    greet([group_device(bits) for bits in (1, 2, 4, 6)])
    lines = Lines(send, receive)
    stage = (give, take, out, came)
    sums = sum_plan(lines, stage)
    total = sum_send([(p_ref, w_ref), (z_ref, f_ref)], stage, sums, mine)
    total = sum_take(total, stage, sums)
    pulled, dgain = rms_back(x_ref[...].astype(FULL), g_ref[...], total)
    y_ref[...] = (d_ref[...] + pulled).astype(HALF)
    dg_ref[...] = dgain
    for copy in lines.made:
        copy.wait_send()


def finish(projected, full, logits, forget, source, gain, grad):
    rows = source.shape[0]
    return pl.pallas_call(
        finish_kernel,
        grid=(1,),
        out_shape=(
            jax.ShapeDtypeStruct((rows, D), HALF),
            jax.ShapeDtypeStruct((1, D), FULL),
        ),
        in_specs=[
            whole_spec((4, 2, rows, QKVG)),
            weight_spec(QKVG, 0),
            whole_spec((4, 2, rows, LANES)),
            whole_spec((D, LANES)),
            whole_spec((rows, D)),
            whole_spec((1, D)),
            whole_spec((rows, D)),
        ],
        out_specs=(whole_spec((rows, D)), whole_spec((1, D))),
        scratch_shapes=[pltpu.VMEM((4, rows, D), FULL)]
        + sum_scratch(rows)
        + [pltpu.SemaphoreType.DMA((7,)), pltpu.SemaphoreType.DMA((7,))],
        compiler_params=params(4),
        name="finish",
    )(
        projected.reshape(4, 2, rows, QKVG),
        full,
        logits.reshape(4, 2, rows, LANES),
        forget,
        source,
        gain,
        grad,
    )


def feed_kernel(a_ref, c_ref, wgu_ref, wd_ref, m_ref, d_ref):
    made = dot(a_ref[...], wgu_ref[...])
    gate, up = made[:, :UNITS], made[:, UNITS:]
    sig = sigmoid(gate)
    swish = gate * sig
    m_ref[...] = (swish * up).astype(HALF)
    grad = dot(c_ref[...], wd_ref[...])
    d_ref[:, :UNITS] = (grad * up * sig * (1.0 + gate * (1.0 - sig))).astype(HALF)
    d_ref[:, UNITS:] = (grad * swish).astype(HALF)


def feed(second, returned, full):
    tokens = second.shape[0]
    return pl.pallas_call(
        feed_kernel,
        grid=(tokens // ROWS,),
        out_shape=(
            jax.ShapeDtypeStruct((tokens, UNITS), HALF),
            jax.ShapeDtypeStruct((tokens, 2 * UNITS), HALF),
        ),
        in_specs=[
            pl.BlockSpec((ROWS, D), lambda i: (i, 0)),
            pl.BlockSpec((ROWS, D), lambda i: (i, 0)),
            pl.BlockSpec((D, 2 * UNITS), lambda i: (0, 0)),
            pl.BlockSpec((D, UNITS), lambda i: (0, 0)),
        ],
        out_specs=(
            pl.BlockSpec((ROWS, UNITS), lambda i: (i, 0)),
            pl.BlockSpec((ROWS, 2 * UNITS), lambda i: (i, 0)),
        ),
        compiler_params=params(),
        name="feed",
    )(second, returned, full[:, QKVG : QKVG + 2 * UNITS], full[:, QKVG + 2 * UNITS : QKVG + 3 * UNITS])


def ungate_kernel(where_ref, d_ref, w_ref, o_ref, p_ref, l_ref, s_ref, q_ref, do_ref, qb_ref, dg_ref, pack_ref):
    grad = dot(d_ref[...], w_ref[...])
    count = grad.shape[0]
    lanes = lax.broadcasted_iota(jnp.int32, (count, LANES), 1)
    gates = gates_of(p_ref[...], lanes)
    heads = []
    sent = []
    for at in range(2):
        part = grad[:, LANES * at : LANES * (at + 1)]
        attended = o_ref[:, LANES * at : LANES * (at + 1)]
        sig = sigmoid(gates[at])
        low = (part * sig).astype(HALF).astype(FULL)
        sent.append(low)
        dg_ref[:, LANES * at : LANES * (at + 1)] = part * attended * sig * (1.0 - sig)
        product = low * attended
        heads.append((low, jnp.sum(jnp.where(lanes < DH, product, 0.0), axis=1, keepdims=True)))
        if at == 0:
            heads.append(
                (
                    pltpu.roll(low, DH, 1),
                    jnp.sum(jnp.where(lanes < DH, 0.0, product), axis=1, keepdims=True),
                )
            )
    extra = jnp.zeros_like(lanes, FULL)
    for head, (low, delta) in enumerate(heads):
        minus = three(-delta)
        decay = three(column(s_ref[...], head) - column(l_ref[...], head))
        do_ref[head] = jnp.where(
            lanes < DH, low, at_lanes(lanes, [(DH + i, minus[i]) for i in range(3)], 0.0)
        ).astype(HALF)
        qb_ref[head] = at_lanes(
            lanes, [(DH + i, decay[i]) for i in range(3)], q_ref[head].astype(FULL)
        ).astype(HALF)
        extra = at_lanes(
            lanes,
            [(DH + 6 * head + i, minus[i]) for i in range(3)] + [(DH + 6 * head + 3 + i, decay[i]) for i in range(3)],
            extra,
        )
    pack_ref[:, :LANES] = sent[0].astype(HALF)
    pack_ref[:, LANES:] = jnp.where(lanes < DH, sent[1], extra).astype(HALF)


def ungate(where, grads, full, attended, made, logs, sums, queries):
    own = grads.shape[0]
    steps = own // ROWS
    head_tile = pl.BlockSpec((HEADS, ROWS, LANES), lambda i, w: (0, i, 0))
    return pl.pallas_call(
        ungate_kernel,
        grid_spec=pltpu.PrefetchScalarGridSpec(
            num_scalar_prefetch=1,
            grid=(steps,),
            in_specs=[
                pl.BlockSpec((ROWS, D), lambda i, w: (i, 0)),
                pl.BlockSpec((D, 256), lambda i, w: (0, (QKVG + 3 * UNITS) // 256)),
                pl.BlockSpec((ROWS, 256), lambda i, w: (i, 0)),
                pl.BlockSpec((ROWS, QKVG), lambda i, w: (w[0] * steps + i, 0)),
                pl.BlockSpec((ROWS, LANES), lambda i, w: (i, 0)),
                pl.BlockSpec((ROWS, LANES), lambda i, w: (w[0] * steps + i, 0)),
                pl.BlockSpec((HEADS, ROWS, LANES), lambda i, w: (0, w[0] * steps + i, 0)),
            ],
            out_specs=(
                head_tile,
                head_tile,
                pl.BlockSpec((ROWS, 256), lambda i, w: (i, 0)),
                pl.BlockSpec((ROWS, 256), lambda i, w: (i, 0)),
            ),
        ),
        out_shape=(
            jax.ShapeDtypeStruct((HEADS, own, LANES), HALF),
            jax.ShapeDtypeStruct((HEADS, own, LANES), HALF),
            jax.ShapeDtypeStruct((own, 256), FULL),
            jax.ShapeDtypeStruct((own, 256), HALF),
        ),
        compiler_params=params(),
        name="ungate",
    )(where, grads, full, attended, made, logs, sums, queries)


def pieces(scores, product, masked, transposed):
    prob = jnp.exp(scores)
    if masked:
        row = lax.broadcasted_iota(jnp.int32, scores.shape, 0)
        col = lax.broadcasted_iota(jnp.int32, scores.shape, 1)
        keep = row <= col if transposed else col <= row
        prob = jnp.where(keep, prob, 0.0)
    return prob.astype(HALF), (prob * product).astype(HALF)


def own_kernel(where_ref, q_ref, do_ref, k_ref, v_ref, dq_ref, dk_ref, dv_ref):
    count = min(BLOCK, q_ref.shape[1])
    steps = q_ref.shape[1] // count
    before = where_ref[0] * steps
    dk_ref[0] = jnp.zeros_like(dk_ref[0])
    dv_ref[0] = jnp.zeros_like(dv_ref[0])
    for at in range(steps):
        here = pl.ds(at * count, count)
        query, grad = q_ref[0, here], do_ref[0, here]

        def earlier(step, total):
            there = pl.ds(step * count, count)
            key = k_ref[0, there]
            prob, dscore = pieces(
                dot(query, key, (1, 1)), dot(grad, v_ref[0, there], (1, 1)), False, False
            )
            return total + dot(dscore, key)

        total = lax.fori_loop(0, before, earlier, jnp.zeros((count, LANES), FULL))
        for step in range(at + 1):
            there = pl.ds((before + step) * count, count)
            key = k_ref[0, there]
            prob, dscore = pieces(
                dot(key, query, (1, 1)), dot(v_ref[0, there], grad, (1, 1)), step == at, True
            )
            local = pl.ds(step * count, count)
            dk_ref[0, local] += dot(dscore, query)
            dv_ref[0, local] += dot(prob, grad)
            total = total + dot(dscore, key, (0, 0))
        dq_ref[0, here] = total


def own_back(where, queries, grads, keys, values):
    own, tokens = queries.shape[1], keys.shape[1]
    mine = pl.BlockSpec((1, own, LANES), lambda h, w: (h, 0, 0))
    whole = pl.BlockSpec((1, tokens, LANES), lambda h, w: (h, 0, 0))
    return pl.pallas_call(
        own_kernel,
        grid_spec=pltpu.PrefetchScalarGridSpec(
            num_scalar_prefetch=1,
            grid=(HEADS,),
            in_specs=[mine, mine, whole, whole],
            out_specs=(mine, mine, mine),
        ),
        out_shape=(jax.ShapeDtypeStruct((HEADS, own, LANES), FULL),) * 3,
        compiler_params=params(),
        name="own_back",
    )(where, queries, grads, keys, values)


def later_kernel(where_ref, q_ref, pack_ref, k_ref, v_ref, dk_in, dv_in, dk_ref, dv_ref, late_ref):
    own = k_ref.shape[1]
    head = pl.program_id(0)
    count = min(BLOCK, own)
    steps = own // count
    group, groups = where_ref[0], where_ref[1]
    dk_ref[0] = jnp.zeros_like(dk_ref[0])
    dv_ref[0] = dv_in[0]
    lanes = lax.broadcasted_iota(jnp.int32, (count, LANES), 1)

    def visit(at, carry):
        sent = pack_ref[pl.ds(at * count, count)].astype(FULL)
        left, right = sent[:, :LANES], sent[:, LANES:]
        grad = jnp.where(head == 0, left, jnp.where(head == 1, pltpu.roll(left, DH, 1), right))
        minus = [column(right, DH + 6 * head + i) for i in range(3)]
        decay = [column(right, DH + 6 * head + 3 + i) for i in range(3)]
        grad = jnp.where(
            lanes < DH, grad, at_lanes(lanes, [(DH + i, minus[i]) for i in range(3)], 0.0)
        ).astype(HALF)
        query = q_ref[0, pl.ds((group + 1) * own + at * count, count)].astype(FULL)
        query = at_lanes(lanes, [(DH + i, decay[i]) for i in range(3)], query).astype(HALF)
        for step in range(steps):
            here = pl.ds(step * count, count)
            prob, dscore = pieces(
                dot(k_ref[0, here], query, (1, 1)), dot(v_ref[0, here], grad, (1, 1)), False, True
            )
            dk_ref[0, here] += dot(dscore, query)
            dv_ref[0, here] += dot(prob, grad)
        return carry

    lax.fori_loop(0, (groups - 1 - group) * steps, visit, 0)
    late_ref[0] = jnp.broadcast_to(jnp.sum(dk_ref[0], axis=0, keepdims=True), (8, LANES))
    dk_ref[0] += dk_in[0]


def later_back(where, queries, pack, keys, values, dkeys, dvalues):
    own, tokens = dkeys.shape[1], keys.shape[1]
    mine = pl.BlockSpec((1, own, LANES), lambda h, w: (h, 0, 0))
    here = pl.BlockSpec((1, own, LANES), lambda h, w: (h, w[0], 0))
    return pl.pallas_call(
        later_kernel,
        grid_spec=pltpu.PrefetchScalarGridSpec(
            num_scalar_prefetch=1,
            grid=(HEADS,),
            in_specs=[
                pl.BlockSpec((1, tokens, LANES), lambda h, w: (h, 0, 0)),
                pl.BlockSpec(pack.shape, lambda h, w: (0, 0)),
                here,
                here,
                mine,
                mine,
            ],
            out_specs=(mine, mine, pl.BlockSpec((1, 8, LANES), lambda h, w: (h, 0, 0))),
        ),
        out_shape=(
            jax.ShapeDtypeStruct((HEADS, own, LANES), FULL),
            jax.ShapeDtypeStruct((HEADS, own, LANES), FULL),
            jax.ShapeDtypeStruct((HEADS, 8, LANES), FULL),
        ),
        compiler_params=params(),
        name="later_back",
    )(where, queries, pack, keys, values, dkeys, dvalues)


def unproject_kernel(
    where_ref, dq_ref, dk_ref, dv_ref, dg_ref, p_ref, z_ref, g_ref, late_ref, dp_ref, dz_ref, gain_ref, bias_ref, carry
):
    @pl.when(pl.program_id(0) == 0)
    def clear():
        carry[0:1] = late_ref[...]
        gain_ref[...] = jnp.zeros_like(gain_ref)
        bias_ref[...] = jnp.zeros_like(bias_ref)

    count = p_ref.shape[0]
    lanes = lax.broadcasted_iota(jnp.int32, (count, LANES), 1)
    sums = jnp.zeros((count, LANES), FULL)
    gates = [
        pltpu.roll(dg_ref[:, :LANES], DH, 1),
        dg_ref[:, :LANES],
        pltpu.roll(dg_ref[:, LANES:], DH, 1),
    ]
    for head in range(HEADS):
        dquery, dkey = dq_ref[head], dk_ref[head]
        sums = jnp.where(lanes == head, column(dquery, DH) - column(dkey, DH + 3), sums)
        grad = jnp.where(lanes < DH, dquery * (DH**-0.5), pltpu.roll(dkey, DH, 1))
        pair = p_ref[:, 256 * head : 256 * head + LANES]
        inverse = lax.rsqrt(halves_mean(pair * pair, lanes) + EPS)
        normal = pair * inverse
        scaled = grad * g_ref[head : head + 1]
        gain_ref[head : head + 1] += jnp.sum(grad * normal, axis=0, keepdims=True)
        pulled = inverse * (scaled - normal * halves_mean(scaled * normal, lanes))
        dp_ref[:, 256 * head : 256 * head + LANES] = pulled.astype(HALF)
        dp_ref[:, 256 * head + LANES : 256 * head + 2 * LANES] = jnp.where(
            lanes < DH, dv_ref[head], gates[head]
        ).astype(HALF)
    row = lax.broadcasted_iota(jnp.int32, (count, count), 0)
    col = lax.broadcasted_iota(jnp.int32, (count, count), 1)
    later = (
        lax.dot_general(
            jnp.where(col >= row, 1.0, 0.0),
            sums,
            (((1,), (0,)), ((), ())),
            precision=lax.Precision.HIGHEST,
            preferred_element_type=FULL,
        )
        + carry[0:1]
    )
    carry[0:1] = later[0:1]
    low = jnp.where(lanes < HEADS, later * sigmoid(-z_ref[...]), 0.0).astype(HALF)
    dz_ref[...] = low
    bias_ref[0:1] += jnp.sum(low.astype(FULL), axis=0, keepdims=True)


def unproject(where, dqueries, dkeys, dvalues, dgates, made, logits, gains, late):
    own = dqueries.shape[1]
    steps = own // ROWS
    head_tile = pl.BlockSpec((HEADS, ROWS, LANES), lambda i, w: (0, steps - 1 - i, 0))
    small = pl.BlockSpec((8, LANES), lambda i, w: (0, 0))
    return pl.pallas_call(
        unproject_kernel,
        grid_spec=pltpu.PrefetchScalarGridSpec(
            num_scalar_prefetch=1,
            grid=(steps,),
            in_specs=[
                head_tile,
                head_tile,
                head_tile,
                pl.BlockSpec((ROWS, 256), lambda i, w: (steps - 1 - i, 0)),
                pl.BlockSpec((ROWS, QKVG), lambda i, w: (w[0] * steps + steps - 1 - i, 0)),
                pl.BlockSpec((ROWS, LANES), lambda i, w: (w[0] * steps + steps - 1 - i, 0)),
                small,
                pl.BlockSpec((1, LANES), lambda i, w: (0, 0)),
            ],
            out_specs=(
                pl.BlockSpec((ROWS, QKVG), lambda i, w: (steps - 1 - i, 0)),
                pl.BlockSpec((ROWS, LANES), lambda i, w: (steps - 1 - i, 0)),
                small,
                small,
            ),
            scratch_shapes=[pltpu.VMEM((8, LANES), FULL)],
        ),
        out_shape=(
            jax.ShapeDtypeStruct((own, QKVG), HALF),
            jax.ShapeDtypeStruct((own, LANES), HALF),
            jax.ShapeDtypeStruct((8, LANES), FULL),
            jax.ShapeDtypeStruct((8, LANES), FULL),
        ),
        compiler_params=params(),
        name="unproject",
    )(where, dqueries, dkeys, dvalues, dgates, made, logits, gains, late)


def return_counts(grps, groups):
    return (grps - 1) * groups * TP + (groups - 1) * TP + TP - 1


def return_kernel(grps, groups, g_ref, o_ref, mine, over_got, across_out, across_got, last, send, receive, local):
    grp, group, member = place()

    def device(to_grp=0, to_group=0, bits=0):
        return (
            lax.rem(grp + to_grp, grps),
            lax.rem(group + to_group, groups) * TP + flip(member, bits),
        )

    greet(
        [device(bits=bits) for bits in range(1, TP)]
        + [device(to_group=step) for step in range(1, groups)]
        + [device(to_grp=step) for step in range(1, grps)]
    )
    lines = Lines(send, receive)
    over, across, home = {}, {}, {}
    for ahead in list(range(1, groups)) + [0]:
        there = lax.rem(group + ahead, groups)
        for bits in range(TP):
            for step in range(1, grps):
                over[step, ahead, bits] = lines.plan(
                    g_ref.at[lax.rem(grp + step, grps), there, flip(member, bits)],
                    over_got.at[step - 1, ahead, bits],
                    device(to_grp=step),
                )
            if ahead:
                across[ahead, bits] = lines.plan(
                    across_out.at[ahead - 1, bits], across_got.at[ahead - 1, bits], device(to_group=ahead)
                )
            elif bits:
                home[bits] = lines.plan(last.at[bits], o_ref.at[member], device(bits=bits))
    own = pltpu.make_async_copy(g_ref.at[grp], mine, local.at[0])
    own.start()
    for copy in over.values():
        copy.start()
    own.wait()
    for ahead in range(1, groups):
        there = lax.rem(group + ahead, groups)
        for bits in range(TP):
            total = mine[there, flip(member, bits)].astype(FULL)
            for step in range(1, grps):
                over[step, ahead, bits].wait_recv()
                total = total + over_got[step - 1, ahead, bits].astype(FULL)
            across_out[ahead - 1, bits] = total.astype(HALF)
            across[ahead, bits].start()
    for bits in list(range(1, TP)) + [0]:
        total = mine[group, flip(member, bits)].astype(FULL)
        for step in range(1, grps):
            over[step, 0, bits].wait_recv()
            total = total + over_got[step - 1, 0, bits].astype(FULL)
        for ahead in range(1, groups):
            across[ahead, bits].wait_recv()
            total = total + across_got[ahead - 1, bits].astype(FULL)
        last[bits] = total.astype(HALF)
        if bits:
            home[bits].start()
    keep = pltpu.make_async_copy(last.at[0], o_ref.at[member], local.at[0])
    keep.start()
    for copy in home.values():
        copy.wait_recv()
    keep.wait()
    for copy in lines.made:
        copy.wait_send()


def give_back(grads, grps, groups):
    own, width = grads.shape[3], grads.shape[4]
    count = return_counts(grps, groups)
    spec = pl.BlockSpec(memory_space=pl.ANY)
    return pl.pallas_call(
        functools.partial(return_kernel, grps, groups),
        out_shape=jax.ShapeDtypeStruct((TP, own, width), HALF),
        in_specs=[spec],
        out_specs=spec,
        scratch_shapes=[
            pltpu.VMEM((groups, TP, own, width), HALF),
            pltpu.VMEM((grps - 1, groups, TP, own, width), HALF),
            pltpu.VMEM((groups - 1, TP, own, width), HALF),
            pltpu.VMEM((groups - 1, TP, own, width), HALF),
            pltpu.VMEM((TP, own, width), HALF),
            pltpu.SemaphoreType.DMA((count,)),
            pltpu.SemaphoreType.DMA((count,)),
            pltpu.SemaphoreType.DMA((1,)),
        ],
        compiler_params=params(5),
        name="give_back",
    )(grads)


def total_kernel(bits, value_ref, out_ref, total, got, send, receive):
    grp, position = lax.axis_index("grp"), lax.axis_index("fsdp")

    def partner(bit):
        if bit == 0:
            return (1 - grp, position)
        return (grp, position + bit - 2 * bit * lax.rem(lax.div(position, bit), 2))

    greet([partner(bit) for bit in bits])
    lines = Lines(send, receive)
    out_ref[...] = value_ref[...]
    for at, bit in enumerate(bits):
        total[at] = out_ref[...]
        copy = lines.plan(total.at[at], got.at[at], partner(bit))
        copy.start()
        copy.wait_recv()
        out_ref[...] += got[at]
    for copy in lines.made:
        copy.wait_send()


def total_of(value, collective):
    bits, bit = [], 1
    while bit < lax.axis_size("fsdp"):
        bits.append(bit)
        bit *= 2
    if lax.axis_size("grp") == 2:
        bits.append(0)
    spec = pl.BlockSpec(memory_space=pltpu.VMEM)
    return pl.pallas_call(
        functools.partial(total_kernel, tuple(bits)),
        out_shape=jax.ShapeDtypeStruct(value.shape, FULL),
        in_specs=[spec],
        out_specs=spec,
        scratch_shapes=[
            pltpu.VMEM((len(bits),) + value.shape, FULL),
            pltpu.VMEM((len(bits),) + value.shape, FULL),
            pltpu.SemaphoreType.DMA((len(bits),)),
            pltpu.SemaphoreType.DMA((len(bits),)),
        ],
        compiler_params=params(collective),
        name="total_of",
    )(value)


def adam(value, first, second, grad, rate, decay):
    first = BETA_ONE * first + (1.0 - BETA_ONE) * grad
    second = BETA_TWO * second + (1.0 - BETA_TWO) * grad * grad
    unbiased_first = first / (1.0 - BETA_ONE**STEP)
    unbiased_second = second / (1.0 - BETA_TWO**STEP)
    value = value - rate * (unbiased_first / (jnp.sqrt(unbiased_second) + ADAM_EPS) + decay * value)
    return (value, first, second)


def pack_columns(weights):
    rows = weights.shape[0]
    low = weights.astype(HALF)
    edge = 5 * D + 2 * F
    heads = low[:, : 4 * D].reshape(rows, 4, TP, HEADS, DH).transpose(2, 0, 3, 1, 4).reshape(TP, rows, QKVG)
    out = low[:, 4 * D : 5 * D].reshape(rows, TP, HEADS * DH).transpose(1, 0, 2)
    both = low[:, 5 * D : edge].reshape(rows, 2, TP, UNITS).transpose(2, 0, 1, 3).reshape(TP, rows, 2 * UNITS)
    down = low[:, edge:].reshape(rows, TP, UNITS).transpose(1, 0, 2)
    return jnp.concatenate([heads, both, down, out, jnp.zeros((TP, rows, 256 - HEADS * DH), HALF)], axis=2)


def unpack_columns(grads):
    rows = grads.shape[1]
    wide = grads.astype(FULL)
    at = QKVG + 2 * UNITS
    heads = wide[:, :, :QKVG].reshape(TP, rows, HEADS, 4, DH).transpose(1, 3, 0, 2, 4).reshape(rows, 4 * D)
    out = wide[:, :, at + UNITS : at + UNITS + HEADS * DH].transpose(1, 0, 2).reshape(rows, D)
    both = wide[:, :, QKVG:at].reshape(TP, rows, 2, UNITS).transpose(1, 2, 0, 3).reshape(rows, 2 * F)
    down = wide[:, :, at : at + UNITS].transpose(1, 0, 2).reshape(rows, F)
    return jnp.concatenate([heads, out, both, down], axis=1)


def pad_lanes(value, width=LANES):
    return jnp.pad(value, ((0, 0), (0, width - value.shape[1])))


def grad_of(left, right):
    return jnp.einsum("tr,tc->rc", left, right, preferred_element_type=FULL).astype(HALF)


def shards(
    inputs,
    cotangent,
    weights,
    weights_first,
    weights_second,
    gains,
    gains_first,
    gains_second,
    forget_weight,
    forget_first,
    forget_second,
    forget_bias,
    bias_first,
    bias_second,
):
    grps, groups = lax.axis_size("grp"), lax.axis_size("fsdp") // TP
    grp, group, member = place()
    rows, own_rows = inputs.shape[1], weights.shape[0]
    group_tokens = TP * rows
    span = groups * group_tokens
    source, returned = inputs[0], cotangent[0]
    where = jnp.stack([group, jnp.int32(groups)]).astype(jnp.int32)

    low = rms_rows(source.astype(FULL), gains[0]).astype(HALF)
    tokens, returned_all, full = start(low, returned, pack_columns(weights), grps, groups)
    tokens = tokens.reshape(span, D)
    returned_all = returned_all.reshape(group_tokens, D)
    full = full.reshape(D, WIDTH)

    forget_low = pad_lanes(lax.dynamic_slice_in_dim(forget_weight, member * HEADS, HEADS, 1).astype(HALF))
    bias = pad_lanes(lax.dynamic_slice_in_dim(forget_bias[None], member * HEADS, HEADS, 1))
    head_gains = lax.dynamic_slice_in_dim(gains[2:4], member * HEADS * DH, HEADS * DH, 1)
    head_gains = head_gains.reshape(2, HEADS, DH).transpose(1, 0, 2).reshape(HEADS, 2 * DH)
    head_gains = jnp.pad(head_gains, ((0, 8 - HEADS), (0, 0)))
    queries, keys, values, made, logits, sums = project(tokens, full, forget_low, bias, head_gains)
    gated, attended, logs = attend(where, queries, keys, values, made, group_tokens)
    mixed, second = mix(gated, full, source, gains[1:2])
    second = second.reshape(group_tokens, D)
    hidden, grad_both = feed(second, returned_all, full)
    output, grad_mixed, grad_gain_mid, branch = unmix(grad_both, hidden, full, mixed, gains[1:2], returned)
    branch = branch.reshape(group_tokens, D)

    grads_low, queries_back, grad_gates, pack = ungate(where, branch, full, attended, made, logs, sums, queries)
    size = lax.axis_size("fsdp")
    others = [
        lax.ppermute(pack, "fsdp", [((at + step * TP) % size, at) for at in range(size)])
        for step in range(1, groups)
    ]
    others = jnp.concatenate(others, axis=0)
    dqueries, dkeys, dvalues = own_back(where, queries_back, grads_low, keys, values)
    dkeys, dvalues, late = later_back(where, queries, others, keys, values, dkeys, dvalues)
    later = pad_lanes(late[:, 0, DH + 3][None])
    if groups > 2:
        everyone = lax.all_gather(dkeys[:, :, DH + 3].sum(axis=1) - dqueries[:, :, DH].sum(axis=1), "fsdp")
        ahead = (jnp.arange(size) // TP > group) & (jnp.arange(size) % TP == member)
        later = pad_lanes(-jnp.sum(jnp.where(ahead[:, None], everyone, 0.0), axis=0)[None])
    grad_projected, grad_logits, grad_heads, grad_bias = unproject(
        where, dqueries, dkeys, dvalues, grad_gates, made, logits, head_gains, later
    )
    input_grad, grad_gain_in = finish(
        grad_projected, full, grad_logits, forget_low, source, gains[0:1], grad_mixed
    )

    first = lax.dynamic_slice_in_dim(tokens, group * group_tokens, group_tokens, 0)
    partial = jnp.concatenate(
        [
            grad_of(first, grad_projected),
            grad_of(second, grad_both),
            grad_of(returned_all, hidden),
            grad_of(branch, gated),
        ],
        axis=1,
    )
    mine = give_back(partial.reshape(grps, groups, TP, own_rows, WIDTH), grps, groups)

    grad_forget = jnp.einsum("th,td->hd", grad_logits[:, :HEADS], first, preferred_element_type=FULL)
    grad_heads = grad_heads[:HEADS].reshape(HEADS, 2, DH).transpose(1, 0, 2).reshape(2, HEADS * DH)
    small = jnp.zeros((32, D), FULL)
    small = lax.dynamic_update_slice(small, grad_forget, (member * HEADS, 0))
    small = lax.dynamic_update_slice(small, grad_gain_in, (H, 0))
    small = lax.dynamic_update_slice(small, grad_gain_mid, (H + 1, 0))
    small = lax.dynamic_update_slice(small, grad_heads, (H + 2, member * HEADS * DH))
    small = lax.dynamic_update_slice(small, grad_bias[0:1, :HEADS], (H + 4, member * HEADS))
    small = total_of(small, 6)
    grad_forget = small[:H].T
    grad_gains = small[H : H + 4]
    grad_bias = small[H + 4, :H]

    wide = mine.astype(FULL)
    squares = total_of(jnp.full((8, LANES), jnp.sum(wide * wide), FULL), 7)[0, 0]
    grad_norm = jnp.sqrt(squares + jnp.sum(small * small))
    factor = CLIP / jnp.maximum(grad_norm, CLIP)
    new_w, new_wf, new_ws = adam(
        weights, weights_first, weights_second, unpack_columns(mine) * factor, RATE_MATRIX, DECAY
    )
    new_g, new_gf, new_gs = adam(gains, gains_first, gains_second, grad_gains * factor, RATE_GAIN, 0.0)
    new_fw, new_ff, new_fs = adam(
        forget_weight, forget_first, forget_second, grad_forget * factor, RATE_MATRIX, DECAY
    )
    new_fb, new_bf, new_bs = adam(
        forget_bias, bias_first, bias_second, grad_bias * factor, RATE_BIAS, 0.0
    )
    return (
        output[None],
        input_grad[None],
        grad_norm,
        new_w,
        new_wf,
        new_ws,
        new_g,
        new_gf,
        new_gs,
        new_fw,
        new_ff,
        new_fs,
        new_fb,
        new_bf,
        new_bs,
    )


def solution(mesh):
    tokens = P("grp", "fsdp", None)
    matrix = P(("grp", "fsdp"), None)
    return jax.shard_map(
        shards,
        mesh=mesh,
        in_specs=(tokens,) * 2 + (matrix,) * 3 + (P(),) * 9,
        out_specs=(tokens,) * 2 + (P(),) + (matrix,) * 3 + (P(),) * 9,
        check_vma=False,
    )
```

```python
import functools

import jax
import jax.numpy as jnp
from jax import lax
from jax.experimental import pallas as pl
from jax.experimental.pallas import tpu as pltpu
from jax.sharding import PartitionSpec as P

D = 1536
H = 24
DH = 64
F = 4096
STEP = 5

EPS = 1e-06
BETA_ONE = 0.9
BETA_TWO = 0.95
ADAM_EPS = 1e-08
RATE_MATRIX = 0.1
RATE_GAIN = 1.2
RATE_BIAS = 3.0
DECAY = 0.1
CLIP = 1.0
NEGATIVE = -1e30

TP = 8
HEADS = H // TP
UNITS = F // TP
QKVG = HEADS * 4 * DH
OUT = 256
NEAR = QKVG + OUT
LANES = 128
ROWS = 256
BLOCK = 512
MESH = pl.DeviceIdType.MESH
HALF = jnp.bfloat16
FULL = jnp.float32
VMEM_BYTES = 56 * 1024 * 1024


def params(collective=None, **more):
    if collective is None:
        return pltpu.CompilerParams(vmem_limit_bytes=VMEM_BYTES, **more)
    return pltpu.CompilerParams(
        collective_id=collective, has_side_effects=True, vmem_limit_bytes=VMEM_BYTES, **more
    )


def flip(member, bits):
    for bit in (1, 2, 4):
        if bits & bit:
            member = member + bit - 2 * bit * lax.rem(lax.div(member, bit), 2)
    return member


def place():
    position = lax.axis_index("fsdp")
    return lax.axis_index("grp"), lax.div(position, TP), lax.rem(position, TP)


def cost(micros):
    return pl.CostEstimate(flops=0, bytes_accessed=3_000_000 * micros, transcendentals=0)


def call_out(targets):
    barrier = pltpu.get_barrier_semaphore()
    for target in targets:
        pl.semaphore_signal(barrier, inc=1, device_id=target, device_id_type=MESH)


def hear(targets):
    pl.semaphore_wait(pltpu.get_barrier_semaphore(), len(targets))


def greet(targets):
    call_out(targets)
    hear(targets)


def neighbours(grps, groups):
    grp, group, member = place()

    def device(to_grp=0, to_group=0, bits=0):
        return (
            lax.rem(grp + to_grp, grps),
            lax.rem(group + to_group, groups) * TP + flip(member, bits),
        )

    return device, (
        [device(bits=bits) for bits in range(1, TP)]
        + [device(to_group=step) for step in range(1, groups)]
        + [device(to_grp=step) for step in range(1, grps)]
    )


class Lines:
    def __init__(self, send, receive):
        self.send, self.receive, self.count, self.made = send, receive, 0, []

    def plan(self, source, target, device):
        copy = pltpu.make_async_remote_copy(
            src_ref=source,
            dst_ref=target,
            send_sem=self.send.at[self.count],
            recv_sem=self.receive.at[self.count],
            device_id=device,
            device_id_type=MESH,
        )
        self.count += 1
        self.made.append(copy)
        return copy


def dot(left, right, contract=(1, 0)):
    return lax.dot_general(
        left, right, (((contract[0],), (contract[1],)), ((), ())), preferred_element_type=FULL
    )


def rms_rows(value, gain):
    return value * lax.rsqrt(jnp.mean(value * value, axis=-1, keepdims=True) + EPS) * gain


def rms_back(value, gain, grad):
    inverse = lax.rsqrt(jnp.mean(value * value, axis=-1, keepdims=True) + EPS)
    normal = value * inverse
    scaled = grad * gain
    pulled = inverse * (scaled - normal * jnp.mean(scaled * normal, axis=-1, keepdims=True))
    return pulled, jnp.sum(grad * normal, axis=0, keepdims=True)


def half_lanes(value, column, upper):
    base = column // LANES * LANES
    part = value[:, base : base + LANES]
    if (column % LANES != 0) != upper:
        part = pltpu.roll(part, DH, 1)
    return part


def two_halves(value, lower, upper, lanes):
    low = half_lanes(value, lower, False)
    if upper is None:
        return jnp.where(lanes < DH, low, 0.0)
    return jnp.where(lanes < DH, low, half_lanes(value, upper, True))


def pack_near(w_ref, near):
    lanes = lax.broadcasted_iota(jnp.int32, (w_ref.shape[0], LANES), 1)
    for member in range(TP):
        for head in range(HEADS):
            at = (member * HEADS + head) * DH
            near[member, :, 256 * head : 256 * head + LANES] = two_halves(w_ref, at, D + at, lanes).astype(HALF)
            near[member, :, 256 * head + LANES : 256 * head + 256] = two_halves(
                w_ref, 2 * D + at, 3 * D + at, lanes
            ).astype(HALF)
        at = 4 * D + member * HEADS * DH
        near[member, :, QKVG : QKVG + LANES] = two_halves(w_ref, at, at + DH, lanes).astype(HALF)
        near[member, :, QKVG + LANES :] = two_halves(w_ref, at + 2 * DH, None, lanes).astype(HALF)


def pack_far(w_ref, both, down):
    edge = 5 * D
    for member in range(TP):
        at = edge + member * UNITS
        both[member, :, :UNITS] = w_ref[:, at : at + UNITS].astype(HALF)
        both[member, :, UNITS:] = w_ref[:, at + F : at + F + UNITS].astype(HALF)
        down[member] = w_ref[:, at + 2 * F : at + 2 * F + UNITS].astype(HALF)


def start_counts(grps, groups):
    tokens = groups * TP - 1
    weights = (TP - 1) + (groups - 1) * TP + (grps - 1) * groups * TP
    return tokens + weights + 2 * (TP - 1)


def start_kernel(
    grps, groups, x_ref, g_ref, w_ref, span_ref, full_ref, both_ref, down_ref,
    block, near, both, down, send, receive, local,
):
    grp, group, member = place()
    device, everyone = neighbours(grps, groups)
    call_out(everyone)
    block[...] = rms_rows(x_ref[...].astype(FULL), g_ref[...]).astype(HALF)
    lines = Lines(send, receive)
    tokens, first, across, over, far = {}, {}, {}, {}, []
    for back in range(groups):
        origin = lax.rem(group + back, groups)
        if back:
            tokens[back, 0] = lines.plan(block, span_ref.at[group, member], device(to_group=groups - back))
        for bits in (1, 2, 4):
            slot = span_ref.at[origin, member]
            source = block if back == 0 else slot
            tokens[back, bits] = lines.plan(source, slot, device(bits=bits))
        slot = span_ref.at[origin, flip(member, 4)]
        tokens[back, 6] = lines.plan(slot, slot, device(bits=2))
        for bits in (2, 4, 6):
            slot = span_ref.at[origin, flip(member, bits)]
            tokens[back, bits + 1] = lines.plan(slot, slot, device(bits=1))
    for bits in range(1, TP):
        first[bits] = lines.plan(near.at[flip(member, bits)], full_ref.at[grp, group, member], device(bits=bits))
    for bits in range(TP):
        slot = full_ref.at[grp, group, flip(member, bits)]
        source = near.at[member] if bits == 0 else slot
        for back in range(1, groups):
            across[back, bits] = lines.plan(source, slot, device(to_group=groups - back))
        for step in range(1, grps):
            over[step, 0, bits] = lines.plan(source, slot, device(to_grp=step))
        for back in range(1, groups):
            passed = full_ref.at[grp, lax.rem(group + back, groups), flip(member, bits)]
            for step in range(1, grps):
                over[step, back, bits] = lines.plan(passed, passed, device(to_grp=step))
    for bits in range(1, TP):
        there = flip(member, bits)
        far.append(lines.plan(both.at[there], both_ref.at[member], device(bits=bits)))
        far.append(lines.plan(down.at[there], down_ref.at[member], device(bits=bits)))

    own = [
        pltpu.make_async_copy(block, span_ref.at[group, member], local.at[0]),
        pltpu.make_async_copy(near.at[member], full_ref.at[grp, group, member], local.at[1]),
        pltpu.make_async_copy(both.at[member], both_ref.at[member], local.at[2]),
        pltpu.make_async_copy(down.at[member], down_ref.at[member], local.at[3]),
    ]
    hear(everyone)
    for back in range(1, groups):
        tokens[back, 0].start()
    for bits in (4, 2, 1):
        tokens[0, bits].start()
    own[0].start()
    pack_near(w_ref, near)
    for bits in range(1, TP):
        first[bits].start()
    for back in range(1, groups):
        across[back, 0].start()
    for step in range(1, grps):
        over[step, 0, 0].start()
    own[1].start()
    pack_far(w_ref, both, down)
    tokens[0, 4].wait_recv()
    tokens[0, 6].start()
    tokens[0, 5].start()
    tokens[0, 2].wait_recv()
    tokens[0, 3].start()
    for bits in range(1, TP):
        first[bits].wait_recv()
        for back in range(1, groups):
            across[back, bits].start()
        for step in range(1, grps):
            over[step, 0, bits].start()
    for copy in far:
        copy.start()
    own[2].start()
    own[3].start()
    tokens[0, 6].wait_recv()
    tokens[0, 7].start()
    for back in range(1, groups):
        tokens[back, 0].wait_recv()
        for bits in (4, 2, 1):
            tokens[back, bits].start()
    for back in range(1, groups):
        for bits in range(TP):
            across[back, bits].wait_recv()
            for step in range(1, grps):
                over[step, back, bits].start()
            if bits == 2:
                tokens[back, 4].wait_recv()
                tokens[back, 6].start()
                tokens[back, 5].start()
            if bits in (4, 6):
                tokens[back, bits - 2 if bits == 4 else 6].wait_recv()
                tokens[back, bits - 1 if bits == 4 else 7].start()
    for back in range(groups):
        for bits in (1, 3, 5, 7):
            tokens[back, bits].wait_recv()
    for copy in far:
        copy.wait_recv()
    for copy in over.values():
        copy.wait_recv()
    for copy in lines.made:
        copy.wait_send()
    for copy in own:
        copy.wait()


def start(source, gain, weights, grps, groups):
    rows, own = source.shape[0], weights.shape[0]
    count = start_counts(grps, groups)
    vmem, anywhere = pl.BlockSpec(memory_space=pltpu.VMEM), pl.BlockSpec(memory_space=pl.ANY)
    return pl.pallas_call(
        functools.partial(start_kernel, grps, groups),
        out_shape=(
            jax.ShapeDtypeStruct((groups, TP, rows, D), HALF),
            jax.ShapeDtypeStruct((grps, groups, TP, own, NEAR), HALF),
            jax.ShapeDtypeStruct((TP, own, 2 * UNITS), HALF),
            jax.ShapeDtypeStruct((TP, own, UNITS), HALF),
        ),
        in_specs=[vmem] * 3,
        out_specs=(anywhere,) * 4,
        scratch_shapes=[
            pltpu.VMEM((rows, D), HALF),
            pltpu.VMEM((TP, own, NEAR), HALF),
            pltpu.VMEM((TP, own, 2 * UNITS), HALF),
            pltpu.VMEM((TP, own, UNITS), HALF),
            pltpu.SemaphoreType.DMA((count,)),
            pltpu.SemaphoreType.DMA((count,)),
            pltpu.SemaphoreType.DMA((4,)),
        ],
        compiler_params=params(1),
        name="start",
        cost_estimate=cost(60),
    )(source, gain, weights)


def column(value, lane):
    lanes = lax.broadcasted_iota(jnp.int32, value.shape, 1)
    return jnp.sum(jnp.where(lanes == lane, value, 0.0), axis=1, keepdims=True)


def three(value):
    high = value.astype(HALF).astype(FULL)
    rest = value - high
    middle = rest.astype(HALF).astype(FULL)
    return high, middle, (rest - middle).astype(HALF).astype(FULL)


def at_lanes(lanes, pairs, other):
    for lane, value in pairs:
        other = jnp.where(lanes == lane, value, other)
    return other


def halves_mean(value, lanes):
    lower = jnp.sum(jnp.where(lanes < DH, value, 0.0), axis=1, keepdims=True)
    upper = jnp.sum(jnp.where(lanes < DH, 0.0, value), axis=1, keepdims=True)
    return jnp.where(lanes < DH, lower, upper) * (1.0 / DH)


def project_kernel(
    steps, a_ref, w_ref, f_ref, b_ref, g_ref, c_ref,
    q_ref, k_ref, v_ref, p_ref, z_ref, s_ref, all_ref, carry, send, receive, local,
):
    member = place()[2]
    own = pltpu.make_async_copy(c_ref, all_ref.at[member], local.at[0])
    near = [group_device(bits) for bits in (1, 2, 4, 6)]

    @pl.when(pl.program_id(0) == 0)
    def begin():
        carry[...] = jnp.zeros_like(carry)
        greet(near)
        gather_start(gather_plan(Lines(send, receive), c_ref, all_ref), own)

    @pl.when(pl.program_id(0) == steps // 2)
    def turn():
        gather_turn(gather_plan(Lines(send, receive), c_ref, all_ref))

    @pl.when(pl.program_id(0) == steps - 2)
    def pass_on():
        gather_pass(gather_plan(Lines(send, receive), c_ref, all_ref))

    @pl.when(pl.program_id(0) == steps - 1)
    def end():
        lines = Lines(send, receive)
        gather_end(gather_plan(lines, c_ref, all_ref), own)
        for copy in lines.made:
            copy.wait_send()

    low = a_ref[...]
    made = dot(low, w_ref[...])
    p_ref[...] = made
    logit = dot(low, f_ref[...]) + b_ref[...]
    z_ref[...] = logit
    log_gate = jnp.minimum(logit, 0.0) - jnp.log1p(jnp.exp(-jnp.abs(logit)))
    count = low.shape[0]
    row = lax.broadcasted_iota(jnp.int32, (count, count), 0)
    col = lax.broadcasted_iota(jnp.int32, (count, count), 1)
    sums = (
        lax.dot_general(
            jnp.where(col <= row, 1.0, 0.0),
            log_gate,
            (((1,), (0,)), ((), ())),
            precision=lax.Precision.HIGHEST,
            preferred_element_type=FULL,
        )
        + carry[0:1]
    )
    carry[0:1] = sums[count - 1 : count]
    s_ref[...] = sums
    lanes = lax.broadcasted_iota(jnp.int32, (count, LANES), 1)
    for head in range(HEADS):
        pair = made[:, 256 * head : 256 * head + LANES]
        value = made[:, 256 * head + LANES : 256 * head + 2 * LANES]
        normal = pair * lax.rsqrt(halves_mean(pair * pair, lanes) + EPS) * g_ref[head : head + 1]
        normal = normal.astype(HALF).astype(FULL)
        high, middle, least = three(column(sums, head))
        ones = jnp.where(lanes < DH + 6, 1.0, 0.0)
        q_ref[head] = jnp.where(
            lanes < DH,
            normal * (DH**-0.5),
            at_lanes(lanes, ((DH, high), (DH + 1, middle), (DH + 2, least)), ones),
        ).astype(HALF)
        ones = jnp.where(lanes < DH + 3, 1.0, 0.0)
        k_ref[head] = jnp.where(
            lanes < DH,
            pltpu.roll(normal, DH, 1),
            at_lanes(lanes, ((DH + 3, -high), (DH + 4, -middle), (DH + 5, -least)), ones),
        ).astype(HALF)
        v_ref[head] = jnp.where(lanes < DH, value, ones).astype(HALF)


def project(span, full, forget, bias, gains, returned):
    tokens, rows = span.shape[0], returned.shape[0]
    steps = tokens // ROWS
    tile = pl.BlockSpec((HEADS, ROWS, LANES), lambda i: (0, i, 0))
    return pl.pallas_call(
        functools.partial(project_kernel, steps),
        grid=(steps,),
        out_shape=(
            jax.ShapeDtypeStruct((HEADS, tokens, LANES), HALF),
            jax.ShapeDtypeStruct((HEADS, tokens, LANES), HALF),
            jax.ShapeDtypeStruct((HEADS, tokens, LANES), HALF),
            jax.ShapeDtypeStruct((tokens, QKVG), FULL),
            jax.ShapeDtypeStruct((tokens, LANES), FULL),
            jax.ShapeDtypeStruct((tokens, LANES), FULL),
            jax.ShapeDtypeStruct((TP, rows, D), HALF),
        ),
        in_specs=[
            pl.BlockSpec((ROWS, D), lambda i: (i, 0)),
            pl.BlockSpec((D, QKVG), lambda i: (0, 0)),
            pl.BlockSpec((D, LANES), lambda i: (0, 0)),
            pl.BlockSpec((1, LANES), lambda i: (0, 0)),
            pl.BlockSpec((8, LANES), lambda i: (0, 0)),
            pl.BlockSpec(memory_space=pl.ANY),
        ],
        out_specs=(
            tile,
            tile,
            tile,
            pl.BlockSpec((ROWS, QKVG), lambda i: (i, 0)),
            pl.BlockSpec((ROWS, LANES), lambda i: (i, 0)),
            pl.BlockSpec((ROWS, LANES), lambda i: (i, 0)),
            pl.BlockSpec(memory_space=pl.ANY),
        ),
        scratch_shapes=[
            pltpu.VMEM((8, LANES), FULL),
            pltpu.SemaphoreType.DMA((7,)),
            pltpu.SemaphoreType.DMA((7,)),
            pltpu.SemaphoreType.DMA((1,)),
        ],
        compiler_params=params(8),
        name="project",
        cost_estimate=cost(20),
    )(span, full, forget, bias, gains, returned)


def sigmoid(value):
    return 1.0 / (1.0 + jnp.exp(-value))


def gates_of(made, lanes):
    second = [made[:, 256 * head + LANES : 256 * head + 2 * LANES] for head in range(HEADS)]
    left = jnp.where(lanes < DH, pltpu.roll(second[0], DH, 1), second[1])
    right = jnp.where(lanes < DH, pltpu.roll(second[2], DH, 1), 0.0)
    return left, right


def attend_kernel(where_ref, q_ref, k_ref, v_ref, p_ref, u_ref, o_ref, l_ref):
    count = q_ref.shape[1]
    before = where_ref[0] * (1024 // count) + pl.program_id(0)
    queries = [q_ref[head] for head in range(HEADS)]

    def visit(state, at, masked):
        new = []
        for head in range(HEADS):
            top, total, accum = state[head]
            scores = dot(queries[head], k_ref[head, pl.ds(at * count, count)], (1, 1))
            if masked:
                row = lax.broadcasted_iota(jnp.int32, scores.shape, 0)
                col = lax.broadcasted_iota(jnp.int32, scores.shape, 1)
                scores = jnp.where(col <= row, scores, NEGATIVE)
            high = jnp.maximum(top, jnp.max(scores, axis=1, keepdims=True))
            shrink = jnp.exp(top - high)
            weight = jnp.exp(scores - high)
            total = total * shrink + jnp.sum(weight, axis=1, keepdims=True)
            accum = accum * shrink + dot(weight.astype(HALF), v_ref[head, pl.ds(at * count, count)])
            new.append((high, total, accum))
        return tuple(new)

    state = tuple(
        (
            jnp.full((count, 1), NEGATIVE, FULL),
            jnp.zeros((count, 1), FULL),
            jnp.zeros((count, LANES), FULL),
        )
        for head in range(HEADS)
    )
    state = lax.fori_loop(0, before, lambda at, inner: visit(inner, at, False), state)
    state = visit(state, before, True)
    lanes = lax.broadcasted_iota(jnp.int32, (count, LANES), 1)
    out = [jnp.where(lanes < DH, accum / total, 0.0) for top, total, accum in state]
    left, right = gates_of(p_ref[...], lanes)
    pair = out[0] + pltpu.roll(out[1], DH, 1)
    o_ref[:, :LANES] = pair
    o_ref[:, LANES:] = out[2]
    u_ref[:, :LANES] = (pair * sigmoid(left)).astype(HALF)
    u_ref[:, LANES:] = (out[2] * sigmoid(right)).astype(HALF)
    logs = [top + jnp.log(total) for top, total, accum in state]
    l_ref[...] = at_lanes(lanes, tuple(enumerate(logs)), 0.0)


def attend(where, queries, keys, values, made, own):
    tokens = queries.shape[1]
    count = min(BLOCK, own)
    steps = own // count
    whole = pl.BlockSpec((HEADS, tokens, LANES), lambda i, w: (0, 0, 0))
    return pl.pallas_call(
        attend_kernel,
        grid_spec=pltpu.PrefetchScalarGridSpec(
            num_scalar_prefetch=1,
            grid=(steps,),
            in_specs=[
                pl.BlockSpec((HEADS, count, LANES), lambda i, w: (0, w[0] * steps + i, 0)),
                whole,
                whole,
                pl.BlockSpec((count, QKVG), lambda i, w: (w[0] * steps + i, 0)),
            ],
            out_specs=(
                pl.BlockSpec((count, 256), lambda i, w: (i, 0)),
                pl.BlockSpec((count, 256), lambda i, w: (i, 0)),
                pl.BlockSpec((count, LANES), lambda i, w: (i, 0)),
            ),
        ),
        out_shape=(
            jax.ShapeDtypeStruct((own, 256), HALF),
            jax.ShapeDtypeStruct((own, 256), FULL),
            jax.ShapeDtypeStruct((own, LANES), FULL),
        ),
        compiler_params=params(),
        name="attend",
        cost_estimate=cost(16),
    )(where, queries, keys, values, made)


def group_device(bits):
    grp, group, member = place()
    return (grp, group * TP + flip(member, bits))


def blocks_of(ref, core):
    value = ref[:, pl.ds(core, 1)]
    return value.reshape(ref.shape[0] * ref.shape[2], ref.shape[3])


def sum_plan(lines, stage):
    give, take, out, came = stage
    sibling = [lines.plan(give.at[at], take.at[at], group_device(1)) for at in range(4)]
    others = [lines.plan(out.at[at], came.at[at], group_device(bits)) for at, bits in enumerate((2, 4, 6))]
    return sibling, others


def sum_give(pairs, stage, plan, mine):
    give = stage[0]
    grp, group, member = place()
    core = lax.rem(member, 2)
    count = give.shape[1]
    theirs = sum(dot(blocks_of(left, 1 - core), right[...], (1, 1)) for left, right in pairs)
    mine[...] = theirs.reshape(4, count, D)
    for at, bits in enumerate((2, 4, 6, 0)):
        give[at] = mine[lax.div(flip(member, bits), 2)].astype(HALF)
        plan[0][at].start()
    own = sum(dot(blocks_of(left, core), right[...], (1, 1)) for left, right in pairs)
    mine[...] = own.reshape(4, count, D)


def sum_pass(stage, plan, mine):
    give, take, out, came = stage
    member = place()[2]
    for at, bits in enumerate((2, 4, 6)):
        plan[0][at].wait_recv()
        out[at] = (mine[lax.div(flip(member, bits), 2)] + take[at].astype(FULL)).astype(HALF)
        plan[1][at].start()
    plan[0][3].wait_recv()
    return mine[lax.div(member, 2)] + take[3].astype(FULL)


def sum_send(pairs, stage, plan, mine):
    sum_give(pairs, stage, plan, mine)
    return sum_pass(stage, plan, mine)


def sum_take(total, stage, plan):
    give, take, out, came = stage
    for at in range(3):
        plan[1][at].wait_recv()
        total = total + came[at].astype(FULL)
    return total


def sum_scratch(rows):
    return [
        pltpu.VMEM((4, rows, D), HALF),
        pltpu.VMEM((4, rows, D), HALF),
        pltpu.VMEM((3, rows, D), HALF),
        pltpu.VMEM((3, rows, D), HALF),
    ]


def gather_plan(lines, block, all_ref):
    grp, group, member = place()
    plan = {bits: lines.plan(block, all_ref.at[member], group_device(bits)) for bits in (4, 2, 1)}
    slot = all_ref.at[flip(member, 4)]
    plan[6] = lines.plan(slot, slot, group_device(2))
    for bits in (2, 4, 6):
        slot = all_ref.at[flip(member, bits)]
        plan[bits + 1] = lines.plan(slot, slot, group_device(1))
    return plan


def gather_start(plan, own):
    own.start()
    for bits in (4, 2, 1):
        plan[bits].start()


def gather_turn(plan):
    plan[4].wait_recv()
    plan[6].start()
    plan[5].start()


def gather_pass(plan):
    for bits in (2, 6):
        plan[bits].wait_recv()
        plan[bits + 1].start()


def gather_end(plan, own):
    for bits in (1, 3, 5, 7):
        plan[bits].wait_recv()
    own.wait()


def gather_run(plan, own):
    gather_start(plan, own)
    gather_turn(plan)
    gather_pass(plan)
    gather_end(plan, own)


def mix_kernel(u_ref, w_ref, x_ref, g_ref, y_ref, all_ref, mine, block, give, take, out, came, send, receive, local):
    greet([group_device(bits) for bits in (1, 2, 4, 6)])
    member = place()[2]
    lines = Lines(send, receive)
    stage = (give, take, out, came)
    sums = sum_plan(lines, stage)
    gathered = gather_plan(lines, block, all_ref)
    total = sum_take(sum_send([(u_ref, w_ref)], stage, sums, mine), stage, sums)
    mixed = x_ref[...].astype(FULL) + total
    y_ref[...] = mixed
    block[...] = rms_rows(mixed, g_ref[...]).astype(HALF)
    gather_run(gathered, pltpu.make_async_copy(block, all_ref.at[member], local.at[0]))
    for copy in lines.made:
        copy.wait_send()


def whole_spec(shape):
    zeros = (0,) * len(shape)
    return pl.BlockSpec(shape, lambda i: zeros)


def weight_spec(columns, at):
    return pl.BlockSpec((D, columns), lambda i: (0, at))


def mix(gated, full, source, gain):
    rows = source.shape[0]
    return pl.pallas_call(
        mix_kernel,
        grid=(1,),
        out_shape=(
            jax.ShapeDtypeStruct((rows, D), FULL),
            jax.ShapeDtypeStruct((TP, rows, D), HALF),
        ),
        in_specs=[
            whole_spec((4, 2, rows, 256)),
            weight_spec(OUT, QKVG // OUT),
            whole_spec((rows, D)),
            whole_spec((1, D)),
        ],
        out_specs=(whole_spec((rows, D)), pl.BlockSpec(memory_space=pl.ANY)),
        scratch_shapes=[pltpu.VMEM((4, rows, D), FULL), pltpu.VMEM((rows, D), HALF)]
        + sum_scratch(rows)
        + [
            pltpu.SemaphoreType.DMA((14,)),
            pltpu.SemaphoreType.DMA((14,)),
            pltpu.SemaphoreType.DMA((1,)),
        ],
        compiler_params=params(2),
        name="mix",
        cost_estimate=cost(40),
    )(gated.reshape(4, 2, rows, 256), full, source, gain)


def unmix_kernel(
    d_ref, w_ref, x_ref, g_ref, c_ref, dx_ref, dg_ref, all_ref,
    mine, block, give, take, out, came, send, receive, local,
):
    greet([group_device(bits) for bits in (1, 2, 4, 6)])
    member = place()[2]
    lines = Lines(send, receive)
    stage = (give, take, out, came)
    sums = sum_plan(lines, stage)
    gathered = gather_plan(lines, block, all_ref)
    total = sum_take(sum_send([(d_ref, w_ref)], stage, sums, mine), stage, sums)
    pulled, dgain = rms_back(x_ref[...], g_ref[...], total)
    grad = c_ref[...].astype(FULL) + pulled
    dx_ref[...] = grad
    dg_ref[...] = dgain
    block[...] = grad.astype(HALF)
    gather_run(gathered, pltpu.make_async_copy(block, all_ref.at[member], local.at[0]))
    for copy in lines.made:
        copy.wait_send()


def unmix(grads, both, mixed, gain, returned):
    rows = mixed.shape[0]
    return pl.pallas_call(
        unmix_kernel,
        grid=(1,),
        out_shape=(
            jax.ShapeDtypeStruct((rows, D), FULL),
            jax.ShapeDtypeStruct((1, D), FULL),
            jax.ShapeDtypeStruct((TP, rows, D), HALF),
        ),
        in_specs=[
            whole_spec((4, 2, rows, 2 * UNITS)),
            whole_spec((D, 2 * UNITS)),
            whole_spec((rows, D)),
            whole_spec((1, D)),
            whole_spec((rows, D)),
        ],
        out_specs=(
            whole_spec((rows, D)),
            whole_spec((1, D)),
            pl.BlockSpec(memory_space=pl.ANY),
        ),
        scratch_shapes=[pltpu.VMEM((4, rows, D), FULL), pltpu.VMEM((rows, D), HALF)]
        + sum_scratch(rows)
        + [
            pltpu.SemaphoreType.DMA((14,)),
            pltpu.SemaphoreType.DMA((14,)),
            pltpu.SemaphoreType.DMA((1,)),
        ],
        compiler_params=params(3),
        name="unmix",
        cost_estimate=cost(40),
    )(grads.reshape(4, 2, rows, 2 * UNITS), both, mixed, gain, returned)


def feed_kernel(a_ref, c_ref, wgu_ref, wd_ref, m_ref, d_ref):
    made = dot(a_ref[...], wgu_ref[...])
    gate, up = made[:, :UNITS], made[:, UNITS:]
    sig = sigmoid(gate)
    swish = gate * sig
    m_ref[...] = (swish * up).astype(HALF)
    grad = dot(c_ref[...], wd_ref[...])
    d_ref[:, :UNITS] = (grad * up * sig * (1.0 + gate * (1.0 - sig))).astype(HALF)
    d_ref[:, UNITS:] = (grad * swish).astype(HALF)


def feed(second, returned, both, down):
    tokens = second.shape[0]
    return pl.pallas_call(
        feed_kernel,
        grid=(tokens // ROWS,),
        out_shape=(
            jax.ShapeDtypeStruct((tokens, UNITS), HALF),
            jax.ShapeDtypeStruct((tokens, 2 * UNITS), HALF),
        ),
        in_specs=[
            pl.BlockSpec((ROWS, D), lambda i: (i, 0)),
            pl.BlockSpec((ROWS, D), lambda i: (i, 0)),
            pl.BlockSpec((D, 2 * UNITS), lambda i: (0, 0)),
            pl.BlockSpec((D, UNITS), lambda i: (0, 0)),
        ],
        out_specs=(
            pl.BlockSpec((ROWS, UNITS), lambda i: (i, 0)),
            pl.BlockSpec((ROWS, 2 * UNITS), lambda i: (i, 0)),
        ),
        compiler_params=params(),
        name="feed",
        cost_estimate=cost(10),
    )(second, returned, both, down)


def ungate_kernel(where_ref, d_ref, w_ref, o_ref, p_ref, l_ref, s_ref, q_ref, do_ref, qb_ref, dg_ref, pack_ref):
    grad = dot(d_ref[...], w_ref[...])
    count = grad.shape[0]
    lanes = lax.broadcasted_iota(jnp.int32, (count, LANES), 1)
    gates = gates_of(p_ref[...], lanes)
    heads = []
    sent = []
    for at in range(2):
        part = grad[:, LANES * at : LANES * (at + 1)]
        attended = o_ref[:, LANES * at : LANES * (at + 1)]
        sig = sigmoid(gates[at])
        low = (part * sig).astype(HALF).astype(FULL)
        sent.append(low)
        dg_ref[:, LANES * at : LANES * (at + 1)] = part * attended * sig * (1.0 - sig)
        product = low * attended
        heads.append((low, jnp.sum(jnp.where(lanes < DH, product, 0.0), axis=1, keepdims=True)))
        if at == 0:
            heads.append(
                (
                    pltpu.roll(low, DH, 1),
                    jnp.sum(jnp.where(lanes < DH, 0.0, product), axis=1, keepdims=True),
                )
            )
    extra = jnp.zeros_like(lanes, FULL)
    for head, (low, delta) in enumerate(heads):
        minus = three(-delta)
        decay = three(column(s_ref[...], head) - column(l_ref[...], head))
        do_ref[head] = jnp.where(
            lanes < DH, low, at_lanes(lanes, [(DH + i, minus[i]) for i in range(3)], 0.0)
        ).astype(HALF)
        qb_ref[head] = at_lanes(
            lanes, [(DH + i, decay[i]) for i in range(3)], q_ref[head].astype(FULL)
        ).astype(HALF)
        extra = at_lanes(
            lanes,
            [(DH + 6 * head + i, minus[i]) for i in range(3)] + [(DH + 6 * head + 3 + i, decay[i]) for i in range(3)],
            extra,
        )
    pack_ref[:, :LANES] = sent[0].astype(HALF)
    pack_ref[:, LANES:] = jnp.where(lanes < DH, sent[1], extra).astype(HALF)


def ungate(where, grads, full, attended, made, logs, sums, queries):
    own = grads.shape[0]
    steps = own // ROWS
    head_tile = pl.BlockSpec((HEADS, ROWS, LANES), lambda i, w: (0, i, 0))
    return pl.pallas_call(
        ungate_kernel,
        grid_spec=pltpu.PrefetchScalarGridSpec(
            num_scalar_prefetch=1,
            grid=(steps,),
            in_specs=[
                pl.BlockSpec((ROWS, D), lambda i, w: (i, 0)),
                pl.BlockSpec((D, OUT), lambda i, w: (0, QKVG // OUT)),
                pl.BlockSpec((ROWS, 256), lambda i, w: (i, 0)),
                pl.BlockSpec((ROWS, QKVG), lambda i, w: (w[0] * steps + i, 0)),
                pl.BlockSpec((ROWS, LANES), lambda i, w: (i, 0)),
                pl.BlockSpec((ROWS, LANES), lambda i, w: (w[0] * steps + i, 0)),
                pl.BlockSpec((HEADS, ROWS, LANES), lambda i, w: (0, w[0] * steps + i, 0)),
            ],
            out_specs=(
                head_tile,
                head_tile,
                pl.BlockSpec((ROWS, 256), lambda i, w: (i, 0)),
                pl.BlockSpec((ROWS, 256), lambda i, w: (i, 0)),
            ),
        ),
        out_shape=(
            jax.ShapeDtypeStruct((HEADS, own, LANES), HALF),
            jax.ShapeDtypeStruct((HEADS, own, LANES), HALF),
            jax.ShapeDtypeStruct((own, 256), FULL),
            jax.ShapeDtypeStruct((own, 256), HALF),
        ),
        compiler_params=params(),
        name="ungate",
        cost_estimate=cost(8),
    )(where, grads, full, attended, made, logs, sums, queries)


def pieces(scores, product, masked, transposed):
    prob = jnp.exp(scores)
    if masked:
        row = lax.broadcasted_iota(jnp.int32, scores.shape, 0)
        col = lax.broadcasted_iota(jnp.int32, scores.shape, 1)
        keep = row <= col if transposed else col <= row
        prob = jnp.where(keep, prob, 0.0)
    return prob.astype(HALF), (prob * product).astype(HALF)


def own_kernel(
    q_ref, do_ref, k_ref, v_ref, m_ref, w_ref, x_ref, dq_ref, dk_ref, dv_ref, y_ref,
    mine, total, give, take, out, came, send, receive,
):
    stage = (give, take, out, came)

    @pl.when(pl.program_id(0) == 0)
    def begin():
        greet([group_device(bits) for bits in (1, 2, 4, 6)])
        sum_give([(m_ref, w_ref)], stage, sum_plan(Lines(send, receive), stage), mine)

    @pl.when(pl.program_id(0) == 1)
    def pass_on():
        total[...] = sum_pass(stage, sum_plan(Lines(send, receive), stage), mine)

    count = min(BLOCK, q_ref.shape[1])
    steps = q_ref.shape[1] // count
    before = place()[1] * steps
    dk_ref[0] = jnp.zeros_like(dk_ref[0])
    dv_ref[0] = jnp.zeros_like(dv_ref[0])
    for at in range(steps):
        here = pl.ds(at * count, count)
        query, grad = q_ref[0, here], do_ref[0, here]

        def earlier(step, inner):
            there = pl.ds(step * count, count)
            key = k_ref[0, there]
            prob, dscore = pieces(
                dot(query, key, (1, 1)), dot(grad, v_ref[0, there], (1, 1)), False, False
            )
            return inner + dot(dscore, key)

        dquery = lax.fori_loop(0, before, earlier, jnp.zeros((count, LANES), FULL))
        for step in range(at + 1):
            there = pl.ds((before + step) * count, count)
            key = k_ref[0, there]
            prob, dscore = pieces(
                dot(key, query, (1, 1)), dot(v_ref[0, there], grad, (1, 1)), step == at, True
            )
            local = pl.ds(step * count, count)
            dk_ref[0, local] += dot(dscore, query)
            dv_ref[0, local] += dot(prob, grad)
            dquery = dquery + dot(dscore, key, (0, 0))
        dq_ref[0, here] = dquery

    @pl.when(pl.program_id(0) == HEADS - 1)
    def end():
        lines = Lines(send, receive)
        y_ref[...] = (x_ref[...] + sum_take(total[...], stage, sum_plan(lines, stage))).astype(HALF)
        for copy in lines.made:
            copy.wait_send()


def own_back(queries, grads, keys, values, hidden, down, mixed):
    own, tokens, rows = queries.shape[1], keys.shape[1], mixed.shape[0]
    mine = pl.BlockSpec((1, own, LANES), lambda h: (h, 0, 0))
    whole = pl.BlockSpec((1, tokens, LANES), lambda h: (h, 0, 0))
    return pl.pallas_call(
        own_kernel,
        grid=(HEADS,),
        in_specs=[
            mine,
            mine,
            whole,
            whole,
            whole_spec((4, 2, rows, UNITS)),
            whole_spec((D, UNITS)),
            whole_spec((rows, D)),
        ],
        out_specs=(mine, mine, mine, whole_spec((rows, D))),
        out_shape=(jax.ShapeDtypeStruct((HEADS, own, LANES), FULL),) * 3
        + (jax.ShapeDtypeStruct((rows, D), HALF),),
        scratch_shapes=[pltpu.VMEM((4, rows, D), FULL), pltpu.VMEM((rows, D), FULL)]
        + sum_scratch(rows)
        + [pltpu.SemaphoreType.DMA((7,)), pltpu.SemaphoreType.DMA((7,))],
        compiler_params=params(5),
        name="own_back",
        cost_estimate=cost(18),
    )(queries, grads, keys, values, hidden.reshape(4, 2, rows, UNITS), down, mixed)


def later_kernel(where_ref, q_ref, pack_ref, k_ref, v_ref, dk_in, dv_in, dk_ref, dv_ref, late_ref):
    own = k_ref.shape[1]
    head = pl.program_id(0)
    count = min(BLOCK, own)
    steps = own // count
    group, groups = where_ref[0], where_ref[1]
    dk_ref[0] = jnp.zeros_like(dk_ref[0])
    dv_ref[0] = dv_in[0]
    lanes = lax.broadcasted_iota(jnp.int32, (count, LANES), 1)

    def visit(at, carry):
        sent = pack_ref[pl.ds(at * count, count)].astype(FULL)
        left, right = sent[:, :LANES], sent[:, LANES:]
        grad = jnp.where(head == 0, left, jnp.where(head == 1, pltpu.roll(left, DH, 1), right))
        minus = [column(right, DH + 6 * head + i) for i in range(3)]
        decay = [column(right, DH + 6 * head + 3 + i) for i in range(3)]
        grad = jnp.where(
            lanes < DH, grad, at_lanes(lanes, [(DH + i, minus[i]) for i in range(3)], 0.0)
        ).astype(HALF)
        query = q_ref[0, pl.ds((group + 1) * own + at * count, count)].astype(FULL)
        query = at_lanes(lanes, [(DH + i, decay[i]) for i in range(3)], query).astype(HALF)
        for step in range(steps):
            here = pl.ds(step * count, count)
            prob, dscore = pieces(
                dot(k_ref[0, here], query, (1, 1)), dot(v_ref[0, here], grad, (1, 1)), False, True
            )
            dk_ref[0, here] += dot(dscore, query)
            dv_ref[0, here] += dot(prob, grad)
        return carry

    lax.fori_loop(0, (groups - 1 - group) * steps, visit, 0)
    late_ref[0] = jnp.broadcast_to(jnp.sum(dk_ref[0], axis=0, keepdims=True), (8, LANES))
    dk_ref[0] += dk_in[0]


def later_back(where, queries, pack, keys, values, dkeys, dvalues):
    own, tokens = dkeys.shape[1], keys.shape[1]
    mine = pl.BlockSpec((1, own, LANES), lambda h, w: (h, 0, 0))
    here = pl.BlockSpec((1, own, LANES), lambda h, w: (h, w[0], 0))
    return pl.pallas_call(
        later_kernel,
        grid_spec=pltpu.PrefetchScalarGridSpec(
            num_scalar_prefetch=1,
            grid=(HEADS,),
            in_specs=[
                pl.BlockSpec((1, tokens, LANES), lambda h, w: (h, 0, 0)),
                pl.BlockSpec(pack.shape, lambda h, w: (0, 0)),
                here,
                here,
                mine,
                mine,
            ],
            out_specs=(mine, mine, pl.BlockSpec((1, 8, LANES), lambda h, w: (h, 0, 0))),
        ),
        out_shape=(
            jax.ShapeDtypeStruct((HEADS, own, LANES), FULL),
            jax.ShapeDtypeStruct((HEADS, own, LANES), FULL),
            jax.ShapeDtypeStruct((HEADS, 8, LANES), FULL),
        ),
        compiler_params=params(),
        name="later_back",
        cost_estimate=cost(14),
    )(where, queries, pack, keys, values, dkeys, dvalues)


def unproject_kernel(
    where_ref, dq_ref, dk_ref, dv_ref, dg_ref, p_ref, z_ref, g_ref, late_ref, dp_ref, dz_ref, gain_ref, bias_ref, carry
):
    @pl.when(pl.program_id(0) == 0)
    def clear():
        carry[0:1] = late_ref[...]
        gain_ref[...] = jnp.zeros_like(gain_ref)
        bias_ref[...] = jnp.zeros_like(bias_ref)

    count = p_ref.shape[0]
    lanes = lax.broadcasted_iota(jnp.int32, (count, LANES), 1)
    sums = jnp.zeros((count, LANES), FULL)
    gates = [
        pltpu.roll(dg_ref[:, :LANES], DH, 1),
        dg_ref[:, :LANES],
        pltpu.roll(dg_ref[:, LANES:], DH, 1),
    ]
    for head in range(HEADS):
        dquery, dkey = dq_ref[head], dk_ref[head]
        sums = jnp.where(lanes == head, column(dquery, DH) - column(dkey, DH + 3), sums)
        grad = jnp.where(lanes < DH, dquery * (DH**-0.5), pltpu.roll(dkey, DH, 1))
        pair = p_ref[:, 256 * head : 256 * head + LANES]
        inverse = lax.rsqrt(halves_mean(pair * pair, lanes) + EPS)
        normal = pair * inverse
        scaled = grad * g_ref[head : head + 1]
        gain_ref[head : head + 1] += jnp.sum(grad * normal, axis=0, keepdims=True)
        pulled = inverse * (scaled - normal * halves_mean(scaled * normal, lanes))
        dp_ref[:, 256 * head : 256 * head + LANES] = pulled.astype(HALF)
        dp_ref[:, 256 * head + LANES : 256 * head + 2 * LANES] = jnp.where(
            lanes < DH, dv_ref[head], gates[head]
        ).astype(HALF)
    row = lax.broadcasted_iota(jnp.int32, (count, count), 0)
    col = lax.broadcasted_iota(jnp.int32, (count, count), 1)
    later = (
        lax.dot_general(
            jnp.where(col >= row, 1.0, 0.0),
            sums,
            (((1,), (0,)), ((), ())),
            precision=lax.Precision.HIGHEST,
            preferred_element_type=FULL,
        )
        + carry[0:1]
    )
    carry[0:1] = later[0:1]
    low = jnp.where(lanes < HEADS, later * sigmoid(-z_ref[...]), 0.0).astype(HALF)
    dz_ref[...] = low
    bias_ref[0:1] += jnp.sum(low.astype(FULL), axis=0, keepdims=True)


def unproject(where, dqueries, dkeys, dvalues, dgates, made, logits, gains, late):
    own = dqueries.shape[1]
    steps = own // ROWS
    head_tile = pl.BlockSpec((HEADS, ROWS, LANES), lambda i, w: (0, steps - 1 - i, 0))
    small = pl.BlockSpec((8, LANES), lambda i, w: (0, 0))
    return pl.pallas_call(
        unproject_kernel,
        grid_spec=pltpu.PrefetchScalarGridSpec(
            num_scalar_prefetch=1,
            grid=(steps,),
            in_specs=[
                head_tile,
                head_tile,
                head_tile,
                pl.BlockSpec((ROWS, 256), lambda i, w: (steps - 1 - i, 0)),
                pl.BlockSpec((ROWS, QKVG), lambda i, w: (w[0] * steps + steps - 1 - i, 0)),
                pl.BlockSpec((ROWS, LANES), lambda i, w: (w[0] * steps + steps - 1 - i, 0)),
                small,
                pl.BlockSpec((1, LANES), lambda i, w: (0, 0)),
            ],
            out_specs=(
                pl.BlockSpec((ROWS, QKVG), lambda i, w: (steps - 1 - i, 0)),
                pl.BlockSpec((ROWS, LANES), lambda i, w: (steps - 1 - i, 0)),
                small,
                small,
            ),
            scratch_shapes=[pltpu.VMEM((8, LANES), FULL)],
        ),
        out_shape=(
            jax.ShapeDtypeStruct((own, QKVG), HALF),
            jax.ShapeDtypeStruct((own, LANES), HALF),
            jax.ShapeDtypeStruct((8, LANES), FULL),
            jax.ShapeDtypeStruct((8, LANES), FULL),
        ),
        compiler_params=params(),
        name="unproject",
        cost_estimate=cost(9),
    )(where, dqueries, dkeys, dvalues, dgates, made, logits, gains, late)


def across_groups(part, groups):
    size = groups * TP
    return [part] + [
        lax.ppermute(part, "fsdp", [((at + step * TP) % size, at) for at in range(size)])
        for step in range(1, groups)
    ]


def over_grps(parts, grps):
    return [
        [part] + [lax.ppermute(part, "grp", [((at + turn) % grps, at) for at in range(grps)]) for turn in range(1, grps)]
        for part in parts
    ]


def assemble(parts, grps, groups):
    grp, group, member = place()
    shape = parts[0][0].shape
    whole = jnp.zeros((grps, groups) + shape, HALF)
    for step, turns in enumerate(parts):
        for turn, piece in enumerate(turns):
            whole = lax.dynamic_update_slice(
                whole, piece[None, None], (lax.rem(grp + turn, grps), lax.rem(group + step, groups), 0, 0, 0)
            )
    return whole.reshape(grps * groups * shape[0] * shape[1], shape[2])


def collect_grps(partial, grps, groups, own):
    grp = place()[0]
    parts = partial.reshape(grps, groups, TP, own, partial.shape[1])
    got = [lax.dynamic_index_in_dim(parts, grp, 0, False)]
    for turn in range(1, grps):
        give = lax.dynamic_index_in_dim(parts, lax.rem(grp + turn, grps), 0, False)
        got.append(lax.ppermute(give, "grp", [(at, (at + turn) % grps) for at in range(grps)]))
    return got


def collect_groups(got, groups):
    group, size = place()[1], groups * TP
    total = sum(part.astype(FULL) for part in got).astype(HALF)
    kept = [lax.dynamic_index_in_dim(total, group, 0, False)]
    for step in range(1, groups):
        give = lax.dynamic_index_in_dim(total, lax.rem(group + step, groups), 0, False)
        kept.append(lax.ppermute(give, "fsdp", [(at, (at + step * TP) % size) for at in range(size)]))
    return kept


def collected(kept):
    return sum(part.astype(FULL) for part in kept).astype(HALF)


def unpack(grad_ref, near, both, down, out):
    lanes = lax.broadcasted_iota(jnp.int32, (near.shape[1], LANES), 1)

    def half(ref, part, upper):
        member, at, side = part
        value = ref[member, :, at : at + LANES].astype(FULL)
        return pltpu.roll(value, DH, 1) if side != upper else value

    def store(at, ref, lower, upper):
        value = jnp.where(lanes < DH, half(ref, lower, False), half(ref, upper, True))
        grad_ref[:, at : at + LANES] = value.astype(HALF)

    for at in range(0, H, 2):
        for kind in range(4):
            pair = [
                (head // HEADS, 256 * (head % HEADS) + LANES * (kind // 2), kind % 2 == 1) for head in (at, at + 1)
            ]
            store(kind * D + at * DH, near, *pair)
        pair = [
            (head // HEADS, LANES * (head % HEADS // 2), head % HEADS % 2 == 1) for head in (at, at + 1)
        ]
        store(4 * D + at * DH, out, *pair)
    for member in range(TP):
        at = 5 * D + member * UNITS
        grad_ref[:, at : at + UNITS] = both[member, :, :UNITS]
        grad_ref[:, at + F : at + F + UNITS] = both[member, :, UNITS:]
        grad_ref[:, at + 2 * F : at + 2 * F + UNITS] = down[member]


def end_counts(grps, groups):
    replicas = grps * groups - 1
    return 7 + (grps - 1) * groups * TP + (groups - 1) * TP + 4 * (TP - 1) + 2 * (replicas + TP - 1)


def end_kernel(
    grps, groups,
    p_ref, w_ref, z_ref, f_ref, x_ref, g_ref, d_ref, near_ref, both_ref, down_ref, out_ref, s_ref,
    y_ref, grad_ref, small_ref, norm_ref, hnear_ref, hboth_ref, hdown_ref, hout_ref,
    mine, give, take, out, came, kept, over_got, across_out, across_got, last,
    packet, packets, scalar, scalars, members, send, receive, local,
):
    grp, group, member = place()
    device, everyone = neighbours(grps, groups)
    replicas = [
        (turn, step) for turn in range(grps) for step in range(groups) if turn or step
    ]
    everyone = everyone + [device(turn, step) for turn, step in replicas if turn and step]
    call_out(everyone)
    lines = Lines(send, receive)
    stage = (give, take, out, came)
    sums = sum_plan(lines, stage)
    over, across, home, far = {}, {}, {}, []
    for ahead in list(range(1, groups)) + [0]:
        there = lax.rem(group + ahead, groups)
        for bits in range(TP):
            for step in range(1, grps):
                over[step, ahead, bits] = lines.plan(
                    near_ref.at[lax.rem(grp + step, grps), there, flip(member, bits)],
                    over_got.at[step - 1, ahead, bits],
                    device(to_grp=step),
                )
            if ahead:
                across[ahead, bits] = lines.plan(
                    across_out.at[ahead - 1, bits], across_got.at[ahead - 1, bits], device(to_group=ahead)
                )
            elif bits:
                home[bits] = lines.plan(last.at[bits], hnear_ref.at[member], device(bits=bits))
    for source, target in ((both_ref, hboth_ref), (down_ref, hdown_ref), (out_ref, hout_ref)):
        for bits in range(1, TP):
            far.append(lines.plan(source.at[flip(member, bits)], target.at[member], device(bits=bits)))
    shared = [
        lines.plan(packet, packets.at[at], device(turn, step)) for at, (turn, step) in enumerate(replicas)
    ]
    told = [
        lines.plan(small_ref.at[member], small_ref.at[member], device(bits=bits)) for bits in range(1, TP)
    ]
    added = [
        lines.plan(scalar.at[0], scalars.at[at], device(turn, step)) for at, (turn, step) in enumerate(replicas)
    ]
    closed = [lines.plan(scalar.at[1], members.at[bits - 1], device(bits=bits)) for bits in range(1, TP)]
    own = pltpu.make_async_copy(near_ref.at[grp], kept, local.at[0])
    own.start()
    hear(everyone)
    for copy in over.values():
        copy.start()
    for copy in far:
        copy.start()
    sum_give([(p_ref, w_ref), (z_ref, f_ref)], stage, sums, mine)
    own.wait()
    for ahead in range(1, groups):
        there = lax.rem(group + ahead, groups)
        for bits in range(TP):
            total = kept[there, flip(member, bits)].astype(FULL)
            for step in range(1, grps):
                over[step, ahead, bits].wait_recv()
                total = total + over_got[step - 1, ahead, bits].astype(FULL)
            across_out[ahead - 1, bits] = total.astype(HALF)
            across[ahead, bits].start()
    summed = sum_take(sum_pass(stage, sums, mine), stage, sums)
    pulled, dgain = rms_back(x_ref[...].astype(FULL), g_ref[...], summed)
    y_ref[...] = (d_ref[...] + pulled).astype(HALF)
    packet[...] = s_ref[...]
    packet[HEADS : HEADS + 1] = dgain
    for copy in shared:
        copy.start()
    for source, target in ((both_ref, hboth_ref), (down_ref, hdown_ref), (out_ref, hout_ref)):
        target[member] = source[member]
    for bits in list(range(1, TP)) + [0]:
        total = kept[group, flip(member, bits)].astype(FULL)
        for step in range(1, grps):
            over[step, 0, bits].wait_recv()
            total = total + over_got[step - 1, 0, bits].astype(FULL)
        for ahead in range(1, groups):
            across[ahead, bits].wait_recv()
            total = total + across_got[ahead - 1, bits].astype(FULL)
        if bits:
            last[bits] = total.astype(HALF)
            home[bits].start()
        else:
            hnear_ref[member] = total.astype(HALF)
    total = packet[...]
    for at, copy in enumerate(shared):
        copy.wait_recv()
        total = total + packets[at]
    small_ref[member] = total
    for copy in told:
        copy.start()
    for copy in far:
        copy.wait_recv()
    squares = jnp.zeros((8, LANES), FULL)

    def square(ref):
        value = ref[...].astype(FULL)
        return jnp.sum(value * value)

    squares = square(hboth_ref) + square(hdown_ref) + square(hout_ref)
    for copy in home.values():
        copy.wait_recv()
    squares = squares + square(hnear_ref)
    scalar[0] = jnp.full((8, LANES), squares, FULL)
    for copy in added:
        copy.start()
    unpack(grad_ref, hnear_ref, hboth_ref, hdown_ref, hout_ref)
    for copy in told:
        copy.wait_recv()
    every = small_ref[...]
    heads = jnp.sum(every[:, :HEADS] * every[:, :HEADS])
    heads = heads + jnp.sum(every[:, HEADS + 2] * every[:, HEADS + 2])
    shared_gains = jnp.sum(every[:, HEADS : HEADS + 2], axis=0)
    heads = heads + jnp.sum(shared_gains * shared_gains)
    total = scalar[0]
    for at, copy in enumerate(added):
        copy.wait_recv()
        total = total + scalars[at]
    scalar[1] = total
    for copy in closed:
        copy.start()
    total = total + heads
    for at, copy in enumerate(closed):
        copy.wait_recv()
        total = total + members[at]
    norm_ref[...] = jnp.sqrt(total)
    for copy in lines.made:
        copy.wait_send()


def end(projected, weights, logits, forget, source, gain, grad, near, both, down, out, small, grps, groups):
    rows, own = source.shape[0], both.shape[1]
    count = end_counts(grps, groups)
    replicas = grps * groups - 1
    vmem = pl.BlockSpec(memory_space=pltpu.VMEM)
    return pl.pallas_call(
        functools.partial(end_kernel, grps, groups),
        out_shape=(
            jax.ShapeDtypeStruct((rows, D), HALF),
            jax.ShapeDtypeStruct((own, 5 * D + 3 * F), HALF),
            jax.ShapeDtypeStruct((TP, 8, D), FULL),
            jax.ShapeDtypeStruct((8, LANES), FULL),
        ),
        in_specs=[vmem] * 7 + [pl.BlockSpec(memory_space=pl.ANY)] + [vmem] * 4,
        out_specs=(vmem,) * 4,
        scratch_shapes=[
            pltpu.VMEM((TP, own, QKVG), HALF),
            pltpu.VMEM((TP, own, 2 * UNITS), HALF),
            pltpu.VMEM((TP, own, UNITS), HALF),
            pltpu.VMEM((TP, own, OUT), HALF),
            pltpu.VMEM((4, rows, D), FULL),
        ]
        + sum_scratch(rows)
        + [
            pltpu.VMEM((groups, TP, own, QKVG), HALF),
            pltpu.VMEM((grps - 1, groups, TP, own, QKVG), HALF),
            pltpu.VMEM((groups - 1, TP, own, QKVG), HALF),
            pltpu.VMEM((groups - 1, TP, own, QKVG), HALF),
            pltpu.VMEM((TP, own, QKVG), HALF),
            pltpu.VMEM((8, D), FULL),
            pltpu.VMEM((replicas, 8, D), FULL),
            pltpu.VMEM((2, 8, LANES), FULL),
            pltpu.VMEM((replicas, 8, LANES), FULL),
            pltpu.VMEM((TP - 1, 8, LANES), FULL),
            pltpu.SemaphoreType.DMA((count,)),
            pltpu.SemaphoreType.DMA((count,)),
            pltpu.SemaphoreType.DMA((1,)),
        ],
        compiler_params=params(4),
        name="end",
        cost_estimate=cost(60),
    )(
        projected.reshape(4, 2, rows, QKVG),
        weights,
        logits.reshape(4, 2, rows, LANES),
        forget,
        source,
        gain,
        grad,
        near,
        both,
        down,
        out,
        small,
    )


def adam(value, first, second, grad, rate, decay):
    first = BETA_ONE * first + (1.0 - BETA_ONE) * grad
    second = BETA_TWO * second + (1.0 - BETA_TWO) * grad * grad
    unbiased_first = first / (1.0 - BETA_ONE**STEP)
    unbiased_second = second / (1.0 - BETA_TWO**STEP)
    value = value - rate * (unbiased_first / (jnp.sqrt(unbiased_second) + ADAM_EPS) + decay * value)
    return (value, first, second)


def update_kernel(norm_ref, w_ref, m_ref, v_ref, g_ref, nw_ref, nm_ref, nv_ref):
    factor = CLIP / jnp.maximum(norm_ref[0:1, 0:1], CLIP)
    new = adam(w_ref[...], m_ref[...], v_ref[...], g_ref[...].astype(FULL) * factor, RATE_MATRIX, DECAY)
    nw_ref[...], nm_ref[...], nv_ref[...] = new


def update(norm, weights, first, second, grads):
    own, width = weights.shape
    tile = pl.BlockSpec((own, D), lambda i: (0, i))
    return pl.pallas_call(
        update_kernel,
        grid=(width // D,),
        out_shape=(jax.ShapeDtypeStruct((own, width), FULL),) * 3,
        in_specs=[whole_spec((8, LANES)), tile, tile, tile, tile],
        out_specs=(tile,) * 3,
        compiler_params=params(),
        name="update",
        cost_estimate=cost(9),
    )(norm, weights, first, second, grads)


def pad_lanes(value, width=LANES):
    return jnp.pad(value, ((0, 0), (0, width - value.shape[1])))


def grad_of(left, right):
    return jnp.einsum("tr,tc->rc", left, right, preferred_element_type=FULL).astype(HALF)


def shards(
    inputs,
    cotangent,
    weights,
    weights_first,
    weights_second,
    gains,
    gains_first,
    gains_second,
    forget_weight,
    forget_first,
    forget_second,
    forget_bias,
    bias_first,
    bias_second,
):
    grps, groups = lax.axis_size("grp"), lax.axis_size("fsdp") // TP
    grp, group, member = place()
    rows, own_rows = inputs.shape[1], weights.shape[0]
    group_tokens = TP * rows
    span = groups * group_tokens
    source, returned = inputs[0], cotangent[0]
    where = jnp.stack([group, jnp.int32(groups)]).astype(jnp.int32)

    tokens, near, both, down = start(source, gains[0:1], weights, grps, groups)
    tokens = tokens.reshape(span, D)
    near = near.reshape(D, NEAR)
    both_parts, down_parts = across_groups(both, groups), across_groups(down, groups)

    forget_low = pad_lanes(lax.dynamic_slice_in_dim(forget_weight, member * HEADS, HEADS, 1).astype(HALF))
    bias = pad_lanes(lax.dynamic_slice_in_dim(forget_bias[None], member * HEADS, HEADS, 1))
    head_gains = lax.dynamic_slice_in_dim(gains[2:4], member * HEADS * DH, HEADS * DH, 1)
    head_gains = head_gains.reshape(2, HEADS, DH).transpose(1, 0, 2).reshape(HEADS, 2 * DH)
    head_gains = jnp.pad(head_gains, ((0, 8 - HEADS), (0, 0)))
    queries, keys, values, made, logits, sums, returned_all = project(
        tokens, near, forget_low, bias, head_gains, returned
    )
    returned_all = returned_all.reshape(group_tokens, D)
    gated, attended, logs = attend(where, queries, keys, values, made, group_tokens)
    gated, both_parts, down_parts = lax.optimization_barrier((gated, both_parts, down_parts))
    both_parts, down_parts = over_grps(both_parts, grps), over_grps(down_parts, grps)
    mixed, second = mix(gated, near, source, gains[1:2])
    both, down = assemble(both_parts, grps, groups), assemble(down_parts, grps, groups)
    second = second.reshape(group_tokens, D)
    hidden, grad_both = feed(second, returned_all, both, down)
    far = [
        collect_grps(grad_of(second, grad_both), grps, groups, own_rows),
        collect_grps(grad_of(returned_all, hidden), grps, groups, own_rows),
    ]
    grad_mixed, grad_gain_mid, branch = unmix(grad_both, both, mixed, gains[1:2], returned)
    branch = branch.reshape(group_tokens, D)
    branch, far = lax.optimization_barrier((branch, far))
    far = [collect_groups(got, groups) for got in far]
    far_out = collect_grps(grad_of(branch, gated), grps, groups, own_rows)

    grads_low, queries_back, grad_gates, pack = ungate(where, branch, near, attended, made, logs, sums, queries)
    size = lax.axis_size("fsdp")
    others = [
        lax.ppermute(pack, "fsdp", [((at + step * TP) % size, at) for at in range(size)])
        for step in range(1, groups)
    ]
    others = jnp.concatenate(others, axis=0)
    queries_back, far_out = lax.optimization_barrier((queries_back, far_out))
    far_out = collect_groups(far_out, groups)
    dqueries, dkeys, dvalues, output = own_back(queries_back, grads_low, keys, values, hidden, down, mixed)
    dkeys, dvalues, late = later_back(where, queries, others, keys, values, dkeys, dvalues)
    later = pad_lanes(late[:, 0, DH + 3][None])
    if groups > 2:
        everyone = lax.all_gather(dkeys[:, :, DH + 3].sum(axis=1) - dqueries[:, :, DH].sum(axis=1), "fsdp")
        ahead = (jnp.arange(size) // TP > group) & (jnp.arange(size) % TP == member)
        later = pad_lanes(-jnp.sum(jnp.where(ahead[:, None], everyone, 0.0), axis=0)[None])
    grad_projected, grad_logits, grad_heads, grad_bias = unproject(
        where, dqueries, dkeys, dvalues, grad_gates, made, logits, head_gains, later
    )

    first = lax.dynamic_slice_in_dim(tokens, group * group_tokens, group_tokens, 0)
    grad_near = grad_of(first, grad_projected).reshape(grps, groups, TP, own_rows, QKVG)
    grad_forget = jnp.einsum("th,td->hd", grad_logits[:, :HEADS], first, preferred_element_type=FULL)
    grad_heads = grad_heads[:HEADS].reshape(HEADS, 2, DH).transpose(1, 0, 2).reshape(1, 2 * HEADS * DH)
    rest = jnp.concatenate([grad_heads, grad_bias[0:1, :HEADS]], axis=1)
    small = jnp.concatenate(
        [grad_forget, jnp.zeros((1, D), FULL), grad_gain_mid, pad_lanes(rest, D), jnp.zeros((2, D), FULL)], axis=0
    )
    input_grad, grads, small, norm = end(
        grad_projected,
        near[:, :QKVG],
        grad_logits,
        forget_low,
        source,
        gains[0:1],
        grad_mixed,
        grad_near,
        collected(far[0]),
        collected(far[1]),
        collected(far_out),
        small,
        grps,
        groups,
    )
    grad_norm = norm[0, 0]
    grad_forget = small[:, :HEADS].reshape(H, D).T
    edge = HEADS * DH
    grad_gains = jnp.concatenate(
        [
            jnp.sum(small[:, HEADS : HEADS + 2], axis=0),
            small[:, HEADS + 2, :edge].reshape(1, D),
            small[:, HEADS + 2, edge : 2 * edge].reshape(1, D),
        ],
        axis=0,
    )
    grad_bias = small[:, HEADS + 2, 2 * edge : 2 * edge + HEADS].reshape(H)
    factor = CLIP / jnp.maximum(grad_norm, CLIP)
    new_w, new_wf, new_ws = update(norm, weights, weights_first, weights_second, grads)
    new_g, new_gf, new_gs = adam(gains, gains_first, gains_second, grad_gains * factor, RATE_GAIN, 0.0)
    new_fw, new_ff, new_fs = adam(
        forget_weight, forget_first, forget_second, grad_forget * factor, RATE_MATRIX, DECAY
    )
    new_fb, new_bf, new_bs = adam(
        forget_bias, bias_first, bias_second, grad_bias * factor, RATE_BIAS, 0.0
    )
    return (
        output[None],
        input_grad[None],
        grad_norm,
        new_w,
        new_wf,
        new_ws,
        new_g,
        new_gf,
        new_gs,
        new_fw,
        new_ff,
        new_fs,
        new_fb,
        new_bf,
        new_bs,
    )


def solution(mesh):
    tokens = P("grp", "fsdp", None)
    matrix = P(("grp", "fsdp"), None)
    return jax.shard_map(
        shards,
        mesh=mesh,
        in_specs=(tokens,) * 2 + (matrix,) * 3 + (P(),) * 9,
        out_specs=(tokens,) * 2 + (P(),) + (matrix,) * 3 + (P(),) * 9,
        check_vma=False,
    )
```

```python
import functools

import jax
import jax.numpy as jnp
from jax import lax
from jax.experimental import pallas as pl
from jax.experimental.pallas import tpu as pltpu
from jax.sharding import PartitionSpec as P

D = 1536
H = 24
DH = 64
F = 4096
STEP = 5

EPS = 1e-06
BETA_ONE = 0.9
BETA_TWO = 0.95
ADAM_EPS = 1e-08
RATE_MATRIX = 0.1
RATE_GAIN = 1.2
RATE_BIAS = 3.0
DECAY = 0.1
CLIP = 1.0
NEGATIVE = -1e30

TP = 8
HEADS = H // TP
UNITS = F // TP
QKVG = HEADS * 4 * DH
OUT = 256
NEAR = QKVG + OUT
LANES = 128
ROWS = 256
TALL = 512
BLOCK = 512
MESH = pl.DeviceIdType.MESH
HALF = jnp.bfloat16
FULL = jnp.float32
VMEM_BYTES = 56 * 1024 * 1024


def params(collective=None, **more):
    if collective is None:
        return pltpu.CompilerParams(vmem_limit_bytes=VMEM_BYTES, **more)
    return pltpu.CompilerParams(
        collective_id=collective, has_side_effects=True, vmem_limit_bytes=VMEM_BYTES, **more
    )


def flip(member, bits):
    for bit in (1, 2, 4):
        if bits & bit:
            member = member + bit - 2 * bit * lax.rem(lax.div(member, bit), 2)
    return member


def place():
    position = lax.axis_index("fsdp")
    return lax.axis_index("grp"), lax.div(position, TP), lax.rem(position, TP)


def cost(micros):
    return pl.CostEstimate(flops=0, bytes_accessed=3_000_000 * micros, transcendentals=0)


def call_out(targets):
    barrier = pltpu.get_barrier_semaphore()
    for target in targets:
        pl.semaphore_signal(barrier, inc=1, device_id=target, device_id_type=MESH)


def hear(targets):
    pl.semaphore_wait(pltpu.get_barrier_semaphore(), len(targets))


def greet(targets):
    call_out(targets)
    hear(targets)


def neighbours(grps, groups):
    grp, group, member = place()

    def device(to_grp=0, to_group=0, bits=0):
        return (
            lax.rem(grp + to_grp, grps),
            lax.rem(group + to_group, groups) * TP + flip(member, bits),
        )

    return device, (
        [device(bits=bits) for bits in range(1, TP)]
        + [device(to_group=step) for step in range(1, groups)]
        + [device(to_grp=step) for step in range(1, grps)]
    )


class Lines:
    def __init__(self, send, receive):
        self.send, self.receive, self.count, self.made = send, receive, 0, []

    def plan(self, source, target, device):
        copy = pltpu.make_async_remote_copy(
            src_ref=source,
            dst_ref=target,
            send_sem=self.send.at[self.count],
            recv_sem=self.receive.at[self.count],
            device_id=device,
            device_id_type=MESH,
        )
        self.count += 1
        self.made.append(copy)
        return copy


def dot(left, right, contract=(1, 0)):
    return lax.dot_general(
        left, right, (((contract[0],), (contract[1],)), ((), ())), preferred_element_type=FULL
    )


def rms_rows(value, gain):
    return value * lax.rsqrt(jnp.mean(value * value, axis=-1, keepdims=True) + EPS) * gain


def rms_back(value, gain, grad):
    inverse = lax.rsqrt(jnp.mean(value * value, axis=-1, keepdims=True) + EPS)
    normal = value * inverse
    scaled = grad * gain
    pulled = inverse * (scaled - normal * jnp.mean(scaled * normal, axis=-1, keepdims=True))
    return pulled, jnp.sum(grad * normal, axis=0, keepdims=True)


def half_lanes(value, column, upper):
    base = column // LANES * LANES
    part = value[:, base : base + LANES]
    if (column % LANES != 0) != upper:
        part = pltpu.roll(part, DH, 1)
    return part


def two_halves(value, lower, upper, lanes):
    low = half_lanes(value, lower, False)
    if upper is None:
        return jnp.where(lanes < DH, low, 0.0)
    return jnp.where(lanes < DH, low, half_lanes(value, upper, True))


def pack_near(w_ref, near):
    lanes = lax.broadcasted_iota(jnp.int32, (w_ref.shape[0], LANES), 1)
    for member in range(TP):
        for head in range(HEADS):
            at = (member * HEADS + head) * DH
            near[member, :, 256 * head : 256 * head + LANES] = two_halves(w_ref, at, D + at, lanes).astype(HALF)
            near[member, :, 256 * head + LANES : 256 * head + 256] = two_halves(
                w_ref, 2 * D + at, 3 * D + at, lanes
            ).astype(HALF)
        at = 4 * D + member * HEADS * DH
        near[member, :, QKVG : QKVG + LANES] = two_halves(w_ref, at, at + DH, lanes).astype(HALF)
        near[member, :, QKVG + LANES :] = two_halves(w_ref, at + 2 * DH, None, lanes).astype(HALF)


def pack_far(w_ref, both, down):
    edge = 5 * D
    for member in range(TP):
        at = edge + member * UNITS
        both[member, :, :UNITS] = w_ref[:, at : at + UNITS].astype(HALF)
        both[member, :, UNITS:] = w_ref[:, at + F : at + F + UNITS].astype(HALF)
        down[member] = w_ref[:, at + 2 * F : at + 2 * F + UNITS].astype(HALF)


def halves(ref):
    count = ref.shape[0] // 2
    return [ref.at[pl.ds(at * count, count)] for at in range(2)]


def start_counts(grps, groups):
    tokens = 2 * (groups * TP - 1)
    weights = (TP - 1) + (groups - 1) * TP + (grps - 1) * groups * TP
    return tokens + weights + 2 * (TP - 1) + 1


def start_kernel(
    grps, groups, x_ref, g_ref, w_ref, c_ref, span_ref, full_ref, both_ref, down_ref, cot_ref,
    block, near, both, down, send, receive, local,
):
    grp, group, member = place()
    device, everyone = neighbours(grps, groups)
    call_out(everyone)
    block[...] = rms_rows(x_ref[...].astype(FULL), g_ref[...]).astype(HALF)
    lines = Lines(send, receive)
    tokens, first, across, over, far = {}, {}, {}, {}, []
    for back in range(groups):
        origin = lax.rem(group + back, groups)
        for half in range(2):

            def slot(bits, at=origin):
                return halves(span_ref.at[at, flip(member, bits)])[half]

            if back:
                tokens[back, 0, half] = lines.plan(
                    halves(block)[half], slot(0, group), device(to_group=groups - back)
                )
            for bits in (1, 2, 4):
                source = halves(block)[half] if back == 0 else slot(0)
                tokens[back, bits, half] = lines.plan(source, slot(0), device(bits=bits))
            tokens[back, 6, half] = lines.plan(slot(4), slot(4), device(bits=2))
            for bits in (2, 4, 6):
                tokens[back, bits + 1, half] = lines.plan(slot(bits), slot(bits), device(bits=1))
    for bits in range(1, TP):
        first[bits] = lines.plan(near.at[flip(member, bits)], full_ref.at[grp, group, member], device(bits=bits))
    for bits in range(TP):
        slot = full_ref.at[grp, group, flip(member, bits)]
        source = near.at[member] if bits == 0 else slot
        for back in range(1, groups):
            across[back, bits] = lines.plan(source, slot, device(to_group=groups - back))
        for step in range(1, grps):
            over[step, 0, bits] = lines.plan(source, slot, device(to_grp=step))
        for back in range(1, groups):
            passed = full_ref.at[grp, lax.rem(group + back, groups), flip(member, bits)]
            for step in range(1, grps):
                over[step, back, bits] = lines.plan(passed, passed, device(to_grp=step))
    for bits in range(1, TP):
        there = flip(member, bits)
        far.append(lines.plan(both.at[there], both_ref.at[member], device(bits=bits)))
        far.append(lines.plan(down.at[there], down_ref.at[member], device(bits=bits)))
    returned = lines.plan(c_ref, cot_ref.at[member], device(bits=4))

    own = [
        pltpu.make_async_copy(block, span_ref.at[group, member], local.at[0]),
        pltpu.make_async_copy(near.at[member], full_ref.at[grp, group, member], local.at[1]),
        pltpu.make_async_copy(both.at[member], both_ref.at[member], local.at[2]),
        pltpu.make_async_copy(down.at[member], down_ref.at[member], local.at[3]),
        pltpu.make_async_copy(c_ref, cot_ref.at[member], local.at[4]),
    ]

    def begin(back):
        for half in range(2):
            for bits in (4, 2, 1):
                tokens[back, bits, half].start()

    def turn(back):
        for half in range(2):
            tokens[back, 4, half].wait_recv()
            tokens[back, 6, half].start()
            tokens[back, 5, half].start()

    def pass_on(back, bits):
        for half in range(2):
            tokens[back, bits, half].wait_recv()
            tokens[back, bits + 1, half].start()

    hear(everyone)
    for back in range(1, groups):
        for half in range(2):
            tokens[back, 0, half].start()
    begin(0)
    own[0].start()
    pack_near(w_ref, near)
    for bits in (4, 2, 6, 1, 5, 3, 7):
        first[bits].start()
    for back in range(1, groups):
        across[back, 0].start()
    for step in range(1, grps):
        over[step, 0, 0].start()
    own[1].start()
    pack_far(w_ref, both, down)
    turn(0)
    for bits in (1, 5, 3, 7, 2, 4, 6):
        first[bits].wait_recv()
        for back in range(1, groups):
            across[back, bits].start()
        for step in range(1, grps):
            over[step, 0, bits].start()
    pass_on(0, 2)
    for copy in far:
        copy.start()
    for copy in own[2:]:
        copy.start()
    returned.start()
    for back in range(1, groups):
        for half in range(2):
            tokens[back, 0, half].wait_recv()
            for bits in (4, 2, 1):
                tokens[back, bits, half].start()
    pass_on(0, 6)
    for back in range(1, groups):
        for at, bits in enumerate((0, 1, 5, 3, 7, 2, 4, 6)):
            across[back, bits].wait_recv()
            for step in range(1, grps):
                over[step, back, bits].start()
            if at == 1:
                turn(back)
            if at == 3:
                pass_on(back, 2)
            if at == 5:
                pass_on(back, 6)
    for back in range(groups):
        for bits in (1, 3, 5, 7):
            for half in range(2):
                tokens[back, bits, half].wait_recv()
    for copy in far:
        copy.wait_recv()
    returned.wait_recv()
    for copy in over.values():
        copy.wait_recv()
    for copy in lines.made:
        copy.wait_send()
    for copy in own:
        copy.wait()


def start(source, gain, weights, returned, grps, groups):
    rows, own = source.shape[0], weights.shape[0]
    count = start_counts(grps, groups)
    vmem, anywhere = pl.BlockSpec(memory_space=pltpu.VMEM), pl.BlockSpec(memory_space=pl.ANY)
    return pl.pallas_call(
        functools.partial(start_kernel, grps, groups),
        out_shape=(
            jax.ShapeDtypeStruct((groups, TP, rows, D), HALF),
            jax.ShapeDtypeStruct((grps, groups, TP, own, NEAR), HALF),
            jax.ShapeDtypeStruct((TP, own, 2 * UNITS), HALF),
            jax.ShapeDtypeStruct((TP, own, UNITS), HALF),
            jax.ShapeDtypeStruct((TP, rows, D), HALF),
        ),
        in_specs=[vmem] * 4,
        out_specs=(anywhere,) * 5,
        scratch_shapes=[
            pltpu.VMEM((rows, D), HALF),
            pltpu.VMEM((TP, own, NEAR), HALF),
            pltpu.VMEM((TP, own, 2 * UNITS), HALF),
            pltpu.VMEM((TP, own, UNITS), HALF),
            pltpu.SemaphoreType.DMA((count,)),
            pltpu.SemaphoreType.DMA((count,)),
            pltpu.SemaphoreType.DMA((5,)),
        ],
        compiler_params=params(1),
        name="start",
        cost_estimate=cost(60),
    )(source, gain, weights, returned)


def three(value):
    high = value.astype(HALF).astype(FULL)
    rest = value - high
    middle = rest.astype(HALF).astype(FULL)
    return high, middle, (rest - middle).astype(HALF).astype(FULL)


def two(value):
    high = value.astype(HALF)
    return high, (value - high.astype(FULL)).astype(HALF)


def at_lanes(lanes, pairs, other):
    for lane, value in pairs:
        other = jnp.where(lanes == lane, value, other)
    return other


def side_by_side(values, lanes):
    packed = jnp.zeros_like(values[0])
    for at, value in enumerate(values):
        if at:
            value = pltpu.roll(value, HEADS * at, 1)
        packed = jnp.where((lanes >= HEADS * at) & (lanes < HEADS * (at + 1)), value, packed)
    return packed.astype(HALF)


def picker(targets):
    def build(width, find, sign=1.0):
        row = lax.broadcasted_iota(jnp.int32, (LANES, width), 0)
        col = lax.broadcasted_iota(jnp.int32, (LANES, width), 1)
        return jnp.where(row == find(col), sign, 0.0).astype(HALF)

    return build(*targets)


def spread_lanes(first, at):
    def find(col):
        head, lane = lax.div(col, LANES), lax.rem(col, LANES) - at
        return jnp.where((lane >= 0) & (lane < 3), HEADS * (first + lane) + head, -1)

    return find


def halves_matrix(scale):
    row = lax.broadcasted_iota(jnp.int32, (LANES, LANES), 0)
    col = lax.broadcasted_iota(jnp.int32, (LANES, LANES), 1)
    return jnp.where((row < DH) == (col < DH), scale, 0.0).astype(HALF)


def halves_mean(value, matrix):
    high, least = two(value)
    return dot(high, matrix) + dot(least, matrix)


def project_kernel(
    steps, a_ref, w_ref, f_ref, b_ref, g_ref, c_ref,
    q_ref, k_ref, v_ref, p_ref, t_ref, z_ref, s_ref, all_ref, carry, send, receive,
):
    @pl.when(pl.program_id(0) == 0)
    def begin():
        carry[...] = jnp.zeros_like(carry)
        greet([group_device(bits) for bits in (2, 1)])
        plan = second_leg(Lines(send, receive), all_ref)
        for bits in (2, 6, 1, 5):
            plan[bits].start()

    @pl.when(pl.program_id(0) == steps - 1)
    def pass_on():
        plan = second_leg(Lines(send, receive), all_ref)
        for bits in (2, 6):
            plan[bits].wait_recv()
            plan[bits + 1].start()

    low = a_ref[...]
    logit = dot(low, f_ref[...]) + b_ref[...]
    z_ref[...] = logit
    log_gate = jnp.minimum(logit, 0.0) - jnp.log1p(jnp.exp(-jnp.abs(logit)))
    count = low.shape[0]
    row = lax.broadcasted_iota(jnp.int32, (ROWS, ROWS), 0)
    col = lax.broadcasted_iota(jnp.int32, (ROWS, ROWS), 1)
    lower = jnp.where(col <= row, 1.0, 0.0)
    parts = []
    before = carry[0:1]
    for at in range(count // ROWS):
        part = before + lax.dot_general(
            lower,
            log_gate[at * ROWS : (at + 1) * ROWS],
            (((1,), (0,)), ((), ())),
            precision=lax.Precision.HIGHEST,
            preferred_element_type=FULL,
        )
        before = part[ROWS - 1 : ROWS]
        parts.append(part)
    carry[0:1] = before
    sums = jnp.concatenate(parts, axis=0)
    s_ref[...] = sums
    made = dot(low, w_ref[...])
    lanes = lax.broadcasted_iota(jnp.int32, (count, LANES), 1)
    means = halves_matrix(1.0 / DH)
    packed = side_by_side(three(jnp.where(lanes < HEADS, sums, 0.0)), lanes)
    plus = dot(packed, picker((HEADS * LANES, spread_lanes(0, DH))))
    minus = dot(packed, picker((HEADS * LANES, spread_lanes(0, DH + 3), -1.0)))
    ones_after = jnp.where((lanes >= DH + 3) & (lanes < DH + 6), 1.0, 0.0)
    ones_before = jnp.where((lanes >= DH) & (lanes < DH + 3), 1.0, 0.0)
    for head in range(HEADS):
        here = slice(LANES * head, LANES * (head + 1))
        pair = made[:, 256 * head : 256 * head + LANES]
        value = made[:, 256 * head + LANES : 256 * head + 2 * LANES]
        p_ref[:, LANES * head : LANES * (head + 1)] = pair
        normal = pair * lax.rsqrt(halves_mean(pair * pair, means) + EPS) * g_ref[head : head + 1]
        normal = normal.astype(HALF).astype(FULL)
        q_ref[head] = jnp.where(lanes < DH, normal * (DH**-0.5), plus[:, here] + ones_after).astype(HALF)
        k_ref[head] = jnp.where(lanes < DH, pltpu.roll(normal, DH, 1), minus[:, here] + ones_before).astype(HALF)
        v_ref[head] = jnp.where(lanes < DH, value, ones_before).astype(HALF)
    left, right = gates_of(made, lanes)
    t_ref[:, :LANES] = left
    t_ref[:, LANES:] = right

    @pl.when(pl.program_id(0) == steps - 1)
    def end():
        plan = second_leg(Lines(send, receive), all_ref)
        for bits in (1, 5, 3, 7):
            plan[bits].wait_recv()
        for copy in plan.values():
            copy.wait_send()


def second_leg(lines, all_ref):
    member = place()[2]

    def copy(block, bits):
        slot = all_ref.at[flip(member, block)]
        return lines.plan(slot, slot, group_device(bits))

    return {2: copy(0, 2), 6: copy(4, 2), 1: copy(0, 1), 5: copy(4, 1), 3: copy(2, 1), 7: copy(6, 1)}


def project(span, full, forget, bias, gains, gathered):
    tokens = span.shape[0]
    count = TALL
    steps = tokens // count
    tile = pl.BlockSpec((HEADS, count, LANES), lambda i: (0, i, 0))
    return pl.pallas_call(
        functools.partial(project_kernel, steps),
        grid=(steps,),
        out_shape=(
            jax.ShapeDtypeStruct((HEADS, tokens, LANES), HALF),
            jax.ShapeDtypeStruct((HEADS, tokens, LANES), HALF),
            jax.ShapeDtypeStruct((HEADS, tokens, LANES), HALF),
            jax.ShapeDtypeStruct((tokens, HEADS * LANES), FULL),
            jax.ShapeDtypeStruct((tokens, OUT), FULL),
            jax.ShapeDtypeStruct((tokens, LANES), FULL),
            jax.ShapeDtypeStruct((tokens, LANES), FULL),
            jax.ShapeDtypeStruct(gathered.shape, HALF),
        ),
        in_specs=[
            pl.BlockSpec((count, D), lambda i: (i, 0)),
            pl.BlockSpec((D, QKVG), lambda i: (0, 0)),
            pl.BlockSpec((D, LANES), lambda i: (0, 0)),
            pl.BlockSpec((1, LANES), lambda i: (0, 0)),
            pl.BlockSpec((8, LANES), lambda i: (0, 0)),
            pl.BlockSpec(memory_space=pl.ANY),
        ],
        out_specs=(
            tile,
            tile,
            tile,
            pl.BlockSpec((count, HEADS * LANES), lambda i: (i, 0)),
            pl.BlockSpec((count, OUT), lambda i: (i, 0)),
            pl.BlockSpec((count, LANES), lambda i: (i, 0)),
            pl.BlockSpec((count, LANES), lambda i: (i, 0)),
            pl.BlockSpec(memory_space=pl.ANY),
        ),
        scratch_shapes=[
            pltpu.VMEM((8, LANES), FULL),
            pltpu.SemaphoreType.DMA((6,)),
            pltpu.SemaphoreType.DMA((6,)),
        ],
        input_output_aliases={5: 7},
        compiler_params=params(8),
        name="project",
        cost_estimate=cost(20),
    )(span, full, forget, bias, gains, gathered)


def sigmoid(value):
    return 1.0 / (1.0 + jnp.exp(-value))


def gates_of(made, lanes):
    second = [made[:, 256 * head + LANES : 256 * head + 2 * LANES] for head in range(HEADS)]
    left = jnp.where(lanes < DH, pltpu.roll(second[0], DH, 1), second[1])
    right = jnp.where(lanes < DH, pltpu.roll(second[2], DH, 1), 0.0)
    return left, right


def attend_kernel(steps, q_ref, k_ref, v_ref, t_ref, u_ref, o_ref, l_ref, gates, local):
    count = u_ref.shape[0]
    before = place()[1] * steps + pl.program_id(0)
    rows = pl.ds(before * count, count)
    own = pltpu.make_async_copy(t_ref.at[rows], gates, local.at[0])
    own.start()

    queries = [q_ref[head, rows] for head in range(HEADS)]

    def visit(state, at, masked):
        new = []
        for head in range(HEADS):
            top, accum = state[head]
            scores = dot(queries[head], k_ref[head, pl.ds(at * count, count)], (1, 1))
            if masked:
                row = lax.broadcasted_iota(jnp.int32, scores.shape, 0)
                col = lax.broadcasted_iota(jnp.int32, scores.shape, 1)
                scores = jnp.where(col <= row, scores, NEGATIVE)
            high = jnp.maximum(top, jnp.max(scores, axis=1, keepdims=True))
            weight = jnp.exp(scores - high)
            accum = accum * jnp.exp(top - high) + dot(weight.astype(HALF), v_ref[head, pl.ds(at * count, count)])
            new.append((high, accum))
        return tuple(new)

    state = tuple(
        (jnp.full((count, 1), NEGATIVE, FULL), jnp.zeros((count, LANES), FULL)) for head in range(HEADS)
    )
    state = lax.fori_loop(0, before, lambda at, inner: visit(inner, at, False), state)
    state = visit(state, before, True)
    lanes = lax.broadcasted_iota(jnp.int32, (count, LANES), 1)
    out, logs = [], []
    for top, accum in state:
        total = jnp.sum(jnp.where(lanes == DH, accum, 0.0), axis=1, keepdims=True)
        out.append(jnp.where(lanes < DH, accum / total, 0.0))
        logs.append(top + jnp.log(total))
    own.wait()
    left, right = gates[:, :LANES], gates[:, LANES:]
    pair = out[0] + pltpu.roll(out[1], DH, 1)
    o_ref[:, :LANES] = pair
    o_ref[:, LANES:] = out[2]
    u_ref[:, :LANES] = (pair * sigmoid(left)).astype(HALF)
    u_ref[:, LANES:] = (out[2] * sigmoid(right)).astype(HALF)
    l_ref[...] = at_lanes(lanes, tuple(enumerate(logs)), 0.0)


def attend(queries, keys, values, gates, own):
    tokens = queries.shape[1]
    count = min(BLOCK, own)
    steps = own // count
    whole = pl.BlockSpec((HEADS, tokens, LANES), lambda i: (0, 0, 0), pipeline_mode=pl.Buffered(1))
    anywhere = pl.BlockSpec(memory_space=pl.ANY)
    return pl.pallas_call(
        functools.partial(attend_kernel, steps),
        grid=(steps,),
        in_specs=[whole, whole, whole, anywhere],
        out_specs=(
            pl.BlockSpec((count, OUT), lambda i: (i, 0)),
            pl.BlockSpec((count, OUT), lambda i: (i, 0)),
            pl.BlockSpec((count, LANES), lambda i: (i, 0)),
        ),
        out_shape=(
            jax.ShapeDtypeStruct((own, OUT), HALF),
            jax.ShapeDtypeStruct((own, OUT), FULL),
            jax.ShapeDtypeStruct((own, LANES), FULL),
        ),
        scratch_shapes=[
            pltpu.VMEM((count, OUT), FULL),
            pltpu.SemaphoreType.DMA((1,)),
        ],
        compiler_params=params(),
        name="attend",
        cost_estimate=cost(16),
    )(queries, keys, values, gates)


def group_device(bits):
    grp, group, member = place()
    return (grp, group * TP + flip(member, bits))


def blocks_of(ref, core):
    value = ref[:, pl.ds(core, 1)]
    return value.reshape(ref.shape[0] * ref.shape[2], ref.shape[3])


def sum_plan(lines, stage):
    give, take, out, came = stage
    sibling = [lines.plan(give.at[at], take.at[at], group_device(1)) for at in range(4)]
    others = [lines.plan(out.at[at], came.at[at], group_device(bits)) for at, bits in enumerate((2, 4, 6))]
    return sibling, others


def sum_give(pairs, stage, plan, mine):
    give = stage[0]
    grp, group, member = place()
    core = lax.rem(member, 2)
    count = give.shape[1]
    theirs = sum(dot(blocks_of(left, 1 - core), right[...], (1, 1)) for left, right in pairs)
    mine[...] = theirs.reshape(4, count, D)
    for at, bits in enumerate((2, 4, 6, 0)):
        give[at] = mine[lax.div(flip(member, bits), 2)].astype(HALF)
        plan[0][at].start()
    own = sum(dot(blocks_of(left, core), right[...], (1, 1)) for left, right in pairs)
    mine[...] = own.reshape(4, count, D)


def sum_pass(stage, plan, mine):
    give, take, out, came = stage
    member = place()[2]
    for at, bits in enumerate((2, 4, 6)):
        plan[0][at].wait_recv()
        out[at] = (mine[lax.div(flip(member, bits), 2)] + take[at].astype(FULL)).astype(HALF)
        plan[1][at].start()
    plan[0][3].wait_recv()
    return mine[lax.div(member, 2)] + take[3].astype(FULL)


def sum_send(pairs, stage, plan, mine):
    sum_give(pairs, stage, plan, mine)
    return sum_pass(stage, plan, mine)


def sum_take(total, stage, plan):
    give, take, out, came = stage
    for at in range(3):
        plan[1][at].wait_recv()
        total = total + came[at].astype(FULL)
    return total


def sum_scratch(rows):
    return [
        pltpu.VMEM((4, rows, D), HALF),
        pltpu.VMEM((4, rows, D), HALF),
        pltpu.VMEM((3, rows, D), HALF),
        pltpu.VMEM((3, rows, D), HALF),
    ]


def gather_plan(lines, block, all_ref):
    member = place()[2]

    def slot(bits):
        return halves(all_ref.at[flip(member, bits)])

    plan = {(bits, half): lines.plan(halves(block)[half], slot(0)[half], group_device(bits)) for bits in (4, 2) for half in range(2)}
    plan[1] = lines.plan(block, all_ref.at[member], group_device(1))
    plan[6, 0] = lines.plan(slot(4)[0], slot(4)[0], group_device(2))
    plan[6, 1] = lines.plan(slot(2)[1], slot(2)[1], group_device(4))
    for bits in (4, 2, 6):
        for half in range(2):
            plan[bits + 1, half] = lines.plan(slot(bits)[half], slot(bits)[half], group_device(1))
    return plan


GATHER = 13


def gather_start(plan, own):
    own.start()
    for key in ((4, 0), (2, 1), (4, 1), (2, 0), 1):
        plan[key].start()


def gather_turn(plan):
    for bits, half in ((4, 0), (2, 1)):
        plan[bits, half].wait_recv()
        plan[6, half].start()
        plan[bits + 1, half].start()


def gather_pass(plan):
    for bits, half in ((4, 1), (2, 0), (6, 0), (6, 1)):
        plan[bits, half].wait_recv()
        plan[bits + 1, half].start()


def gather_end(plan, own):
    plan[1].wait_recv()
    for bits in (5, 3, 7):
        for half in range(2):
            plan[bits, half].wait_recv()
    own.wait()


def mix_kernel(
    grps, groups, u_ref, w_ref, x_ref, g_ref, far_ref, y_ref, all_ref, *rest
):
    far_refs, rest = rest[: grps * groups - 1], rest[grps * groups - 1 :]
    mine, block, give, take, out, came, send, receive, local = rest
    across_refs, over_refs = far_refs[: groups - 1], far_refs[groups - 1 :]
    device, everyone = neighbours(grps, groups)
    everyone = [group_device(bits) for bits in (1, 2, 4, 6)] + everyone[TP - 1 :]
    greet(everyone)
    member = place()[2]
    lines = Lines(send, receive)
    stage = (give, take, out, came)
    sums = sum_plan(lines, stage)
    gathered = gather_plan(lines, block, all_ref)
    across = [
        lines.plan(far_ref, across_refs[step - 1], device(to_group=groups - step)) for step in range(1, groups)
    ]
    over = [
        [
            lines.plan(far_ref if step == 0 else across_refs[step - 1], over_refs[(turn - 1) * groups + step], device(turn))
            for turn in range(1, grps)
        ]
        for step in range(groups)
    ]
    sum_give([(u_ref, w_ref)], stage, sums, mine)
    total = sum_pass(stage, sums, mine)
    for copy in across + over[0]:
        copy.start()
    total = sum_take(total, stage, sums)
    mixed = x_ref[...].astype(FULL) + total
    y_ref[...] = mixed
    block[...] = rms_rows(mixed, g_ref[...]).astype(HALF)
    own = pltpu.make_async_copy(block, all_ref.at[member], local.at[0])
    gather_start(gathered, own)
    gather_turn(gathered)
    for step in range(1, groups):
        across[step - 1].wait_recv()
        for copy in over[step]:
            copy.start()
    gather_pass(gathered)
    gather_end(gathered, own)
    for turns in over:
        for copy in turns:
            copy.wait_recv()
    for copy in lines.made:
        copy.wait_send()


def whole_spec(shape):
    zeros = (0,) * len(shape)
    return pl.BlockSpec(shape, lambda i: zeros)


def weight_spec(columns, at):
    return pl.BlockSpec((D, columns), lambda i: (0, at))


def mix(gated, full, source, gain, far, grps, groups):
    rows = source.shape[0]
    count = 7 + GATHER + groups - 1 + (grps - 1) * groups
    anywhere = pl.BlockSpec(memory_space=pl.ANY)
    return pl.pallas_call(
        functools.partial(mix_kernel, grps, groups),
        grid=(1,),
        out_shape=(
            jax.ShapeDtypeStruct((rows, D), FULL),
            jax.ShapeDtypeStruct((TP, rows, D), HALF),
        )
        + (jax.ShapeDtypeStruct(far.shape, HALF),) * (grps * groups - 1),
        in_specs=[
            whole_spec((4, 2, rows, 256)),
            weight_spec(OUT, QKVG // OUT),
            whole_spec((rows, D)),
            whole_spec((1, D)),
            anywhere,
        ],
        out_specs=(whole_spec((rows, D)),) + (anywhere,) * (grps * groups),
        scratch_shapes=[pltpu.VMEM((4, rows, D), FULL), pltpu.VMEM((rows, D), HALF)]
        + sum_scratch(rows)
        + [
            pltpu.SemaphoreType.DMA((count,)),
            pltpu.SemaphoreType.DMA((count,)),
            pltpu.SemaphoreType.DMA((1,)),
        ],
        compiler_params=params(2),
        name="mix",
        cost_estimate=cost(40),
    )(gated.reshape(4, 2, rows, 256), full, source, gain, far)


def slabs(grps, groups):
    grp, group, member = place()
    return [
        (turn, step, lax.rem(grp + turn, grps) * groups + lax.rem(group + step, groups))
        for turn in range(grps)
        for step in range(groups)
    ]


def load_rows(refs, whole, semaphores, grps, groups):
    rows = whole.shape[0] // (grps * groups)
    copies = []
    for at, (turn, step, index) in enumerate(slabs(grps, groups)):
        copies.append(pltpu.make_async_copy(refs[at], whole.at[pl.ds(index * rows, rows)], semaphores.at[at]))
    return copies


def unmix_kernel(
    grps, groups, d_ref, x_ref, g_ref, c_ref, m_ref, a_ref, r_ref, *rest
):
    total_slabs = grps * groups
    both_refs, down_refs = rest[:total_slabs], rest[total_slabs : 2 * total_slabs]
    dx_ref, dg_ref, all_ref, out_ref, gate_ref, up_ref, down_ref, *rest = rest[2 * total_slabs :]
    wgu, wdn, mine, block, give, take, out, came, give2, take2, *rest = rest
    grad_gate, grad_down, over_gate, over_down, across_out, across_got, send, receive, local = rest
    device, everyone = neighbours(grps, groups)
    everyone = [group_device(bits) for bits in (1, 2, 4, 6)] + everyone[TP - 1 :]
    call_out(everyone)
    grp, group, member = place()
    core = lax.rem(member, 2)
    load_both = load_rows(both_refs, wgu, local.at[pl.ds(0, total_slabs)], grps, groups)
    load_down = load_rows(down_refs, wdn, local.at[pl.ds(total_slabs, total_slabs)], grps, groups)
    for copy in load_both + load_down:
        copy.start()
    lines = Lines(send, receive)
    stage = (give, take, out, came)
    sums = sum_plan(lines, stage)
    gathered = gather_plan(lines, block, all_ref)
    output = lines.plan(give2, take2, group_device(1))
    rows = grad_down.shape[0] // total_slabs
    places = slabs(grps, groups)
    over_d, over_b = {}, {}
    for turn, step, index in places:
        if turn:
            here = pl.ds(index * rows, rows)
            over_d[turn, step] = lines.plan(grad_down.at[here], over_down.at[turn - 1, step], device(turn))
            over_b[turn, step] = lines.plan(grad_gate.at[here], over_gate.at[turn - 1, step], device(turn))
    across = [
        lines.plan(across_out.at[step - 1], across_got.at[step - 1], device(to_group=step)) for step in range(1, groups)
    ]
    for copy in load_both:
        copy.wait()
    hear(everyone)
    sum_give([(d_ref, wgu)], stage, sums, mine)
    hidden = m_ref[...].reshape(r_ref.shape[0], UNITS)
    cut = D // 4
    for at in range(4):
        grad_down[at * cut : (at + 1) * cut] = dot(r_ref[:, at * cut : (at + 1) * cut], hidden, (0, 0)).astype(HALF)
    for step in list(range(1, groups)) + [0]:
        for turn in range(1, grps):
            over_d[turn, step].start()
    total = sum_pass(stage, sums, mine)
    both = d_ref[...].reshape(a_ref.shape[0], 2 * UNITS)
    for at in range(4):
        here = slice(at * cut, (at + 1) * cut)
        grad_gate[here] = dot(a_ref[:, here], both[:, :UNITS], (0, 0)).astype(HALF)
    for copy in over_b.values():
        copy.start()
    for copy in load_down:
        copy.wait()
    count = x_ref.shape[0]
    give2[...] = dot(blocks_of(m_ref, 1 - core), wdn[...], (1, 1)).astype(HALF).reshape(4, count, D)
    output.start()
    kept = []
    for step in list(range(1, groups)) + [0]:
        here = pl.ds(places[step][2] * rows, rows)
        value = grad_down[here].astype(FULL)
        for turn in range(1, grps):
            over_d[turn, step].wait_recv()
            value = value + over_down[turn - 1, step].astype(FULL)
        if step:
            across_out[step - 1] = value.astype(HALF)
            across[step - 1].start()
        else:
            down_ref[...] = value
    total = sum_take(total, stage, sums)
    pulled, dgain = rms_back(x_ref[...], g_ref[...], total)
    grad = c_ref[...].astype(FULL) + pulled
    dx_ref[...] = grad
    dg_ref[...] = dgain
    block[...] = grad.astype(HALF)
    own = pltpu.make_async_copy(block, all_ref.at[member], local.at[2 * total_slabs])
    gather_start(gathered, own)
    mine[...] = dot(blocks_of(m_ref, core), wdn[...], (1, 1)).reshape(4, count, D)
    gather_turn(gathered)
    for at in range(4):
        here = slice(at * cut, (at + 1) * cut)
        up_ref[here] = dot(a_ref[:, here], both[:, UNITS:], (0, 0)).astype(HALF)
    output.wait_recv()
    for at, bits in enumerate((2, 4, 6, 0)):
        chip = lax.div(flip(member, bits), 2)
        out_ref[at] = (mine[chip] + take2[chip].astype(FULL)).astype(HALF)
    gather_pass(gathered)
    gather_end(gathered, own)
    for step in range(groups):
        here = pl.ds(places[step][2] * rows, rows)
        value = grad_gate[here].astype(FULL)
        for turn in range(1, grps):
            over_b[turn, step].wait_recv()
            value = value + over_gate[turn - 1, step].astype(FULL)
        gate_ref[step] = value.astype(HALF)
    for step in range(1, groups):
        across[step - 1].wait_recv()
        down_ref[...] += across_got[step - 1].astype(FULL)
    for copy in lines.made:
        copy.wait_send()


def unmix(grads, both, down, mixed, gain, returned, hidden, second, returned_all, grps, groups):
    rows, tokens = mixed.shape[0], second.shape[0]
    slab = both[0].shape[0]
    total_slabs = grps * groups
    count = 8 + GATHER + 2 * (grps - 1) * groups + groups - 1
    return pl.pallas_call(
        functools.partial(unmix_kernel, grps, groups),
        grid=(1,),
        out_shape=(
            jax.ShapeDtypeStruct((rows, D), FULL),
            jax.ShapeDtypeStruct((1, D), FULL),
            jax.ShapeDtypeStruct((TP, rows, D), HALF),
            jax.ShapeDtypeStruct((4, rows, D), HALF),
            jax.ShapeDtypeStruct((groups, slab, UNITS), HALF),
            jax.ShapeDtypeStruct((D, UNITS), HALF),
            jax.ShapeDtypeStruct((slab, UNITS), FULL),
        ),
        in_specs=[
            whole_spec((4, 2, rows, 2 * UNITS)),
            whole_spec((rows, D)),
            whole_spec((1, D)),
            whole_spec((rows, D)),
            whole_spec((4, 2, rows, UNITS)),
            whole_spec((tokens, D)),
            whole_spec((tokens, D)),
        ]
        + [pl.BlockSpec(memory_space=pl.ANY)] * (2 * total_slabs),
        out_specs=(
            whole_spec((rows, D)),
            whole_spec((1, D)),
            pl.BlockSpec(memory_space=pl.ANY),
            whole_spec((4, rows, D)),
            whole_spec((groups, slab, UNITS)),
            whole_spec((D, UNITS)),
            whole_spec((slab, UNITS)),
        ),
        scratch_shapes=[
            pltpu.VMEM((D, 2 * UNITS), HALF),
            pltpu.VMEM((D, UNITS), HALF),
            pltpu.VMEM((4, rows, D), FULL),
            pltpu.VMEM((rows, D), HALF),
        ]
        + sum_scratch(rows)
        + [
            pltpu.VMEM((4, rows, D), HALF),
            pltpu.VMEM((4, rows, D), HALF),
            pltpu.VMEM((D, UNITS), HALF),
            pltpu.VMEM((D, UNITS), HALF),
            pltpu.VMEM((grps - 1, groups, slab, UNITS), HALF),
            pltpu.VMEM((grps - 1, groups, slab, UNITS), HALF),
            pltpu.VMEM((groups - 1, slab, UNITS), HALF),
            pltpu.VMEM((groups - 1, slab, UNITS), HALF),
            pltpu.SemaphoreType.DMA((count,)),
            pltpu.SemaphoreType.DMA((count,)),
            pltpu.SemaphoreType.DMA((2 * total_slabs + 1,)),
        ],
        compiler_params=params(3),
        name="unmix",
        cost_estimate=cost(45),
    )(
        grads.reshape(4, 2, rows, 2 * UNITS),
        mixed,
        gain,
        returned,
        hidden.reshape(4, 2, rows, UNITS),
        second,
        returned_all,
        *both,
        *down,
    )


def feed_kernel(grps, groups, a_ref, c_ref, *rest):
    total_slabs = grps * groups
    both_refs, down_refs = rest[:total_slabs], rest[total_slabs : 2 * total_slabs]
    m_ref, d_ref, wgu, wdn, local = rest[2 * total_slabs :]

    @pl.when(pl.program_id(0) == 0)
    def load():
        copies = load_rows(both_refs, wgu, local.at[pl.ds(0, total_slabs)], grps, groups)
        copies = copies + load_rows(down_refs, wdn, local.at[pl.ds(total_slabs, total_slabs)], grps, groups)
        for copy in copies:
            copy.start()
        for copy in copies:
            copy.wait()

    made = dot(a_ref[...], wgu[...])
    gate, up = made[:, :UNITS], made[:, UNITS:]
    sig = sigmoid(gate)
    swish = gate * sig
    m_ref[...] = (swish * up).astype(HALF)
    grad = dot(c_ref[...], wdn[...])
    d_ref[:, :UNITS] = (grad * up * sig * (1.0 + gate * (1.0 - sig))).astype(HALF)
    d_ref[:, UNITS:] = (grad * swish).astype(HALF)


def feed(second, returned, both, down, grps, groups):
    tokens = second.shape[0]
    count = TALL
    return pl.pallas_call(
        functools.partial(feed_kernel, grps, groups),
        grid=(tokens // count,),
        out_shape=(
            jax.ShapeDtypeStruct((tokens, UNITS), HALF),
            jax.ShapeDtypeStruct((tokens, 2 * UNITS), HALF),
        ),
        in_specs=[
            pl.BlockSpec((count, D), lambda i: (i, 0)),
            pl.BlockSpec((count, D), lambda i: (i, 0)),
        ]
        + [pl.BlockSpec(memory_space=pl.ANY)] * (2 * grps * groups),
        out_specs=(
            pl.BlockSpec((count, UNITS), lambda i: (i, 0)),
            pl.BlockSpec((count, 2 * UNITS), lambda i: (i, 0)),
        ),
        scratch_shapes=[
            pltpu.VMEM((D, 2 * UNITS), HALF),
            pltpu.VMEM((D, UNITS), HALF),
            pltpu.SemaphoreType.DMA((2 * grps * groups,)),
        ],
        compiler_params=params(),
        name="feed",
        cost_estimate=cost(10),
    )(second, returned, *both, *down)


def ungate_kernel(where_ref, d_ref, w_ref, o_ref, t_ref, l_ref, s_ref, q_ref, do_ref, qb_ref, dg_ref, pack_ref):
    grad = dot(d_ref[...], w_ref[...])
    count = grad.shape[0]
    lanes = lax.broadcasted_iota(jnp.int32, (count, LANES), 1)
    gates = (t_ref[:, :LANES], t_ref[:, LANES:])
    sums, sent = [], []
    for at in range(2):
        part = grad[:, LANES * at : LANES * (at + 1)]
        attended = o_ref[:, LANES * at : LANES * (at + 1)]
        sig = sigmoid(gates[at])
        low = (part * sig).astype(HALF).astype(FULL)
        sent.append(low)
        dg_ref[:, LANES * at : LANES * (at + 1)] = part * attended * sig * (1.0 - sig)
        sums.append(two(low * attended))
    row = lax.broadcasted_iota(jnp.int32, (LANES, LANES), 0)
    col = lax.broadcasted_iota(jnp.int32, (LANES, LANES), 1)
    of_left = jnp.where(((row < DH) & (col == 0)) | ((row >= DH) & (col == 1)), -1.0, 0.0).astype(HALF)
    of_right = jnp.where((row < DH) & (col == 2), -1.0, 0.0).astype(HALF)
    minus = dot(sums[0][0], of_left) + dot(sums[0][1], of_left) + dot(sums[1][0], of_right) + dot(sums[1][1], of_right)
    decay = jnp.where(lanes < HEADS, s_ref[...] - l_ref[...], 0.0)
    packed = side_by_side(three(minus) + three(decay), lanes)
    grads = dot(packed, picker((HEADS * LANES, spread_lanes(0, DH))))
    sinks = dot(packed, picker((HEADS * LANES, spread_lanes(3, DH))))

    def sent_lanes(col):
        head, part = lax.div(col - DH, 6), lax.rem(col - DH, 6)
        return jnp.where((col >= DH) & (col < DH + 6 * HEADS), HEADS * part + head, -1)

    extra = dot(packed, picker((LANES, sent_lanes)))
    heads = [sent[0], pltpu.roll(sent[0], DH, 1), sent[1]]
    for head in range(HEADS):
        here = slice(LANES * head, LANES * (head + 1))
        do_ref[head] = jnp.where(lanes < DH, heads[head], grads[:, here]).astype(HALF)
        kept = jnp.where((lanes >= DH) & (lanes < DH + 3), 0.0, q_ref[head].astype(FULL))
        qb_ref[head] = (kept + sinks[:, here]).astype(HALF)
    pack_ref[:, :LANES] = sent[0].astype(HALF)
    pack_ref[:, LANES:] = jnp.where(lanes < DH, sent[1], extra).astype(HALF)


def ungate(where, grads, full, attended, gates, logs, sums, queries):
    own = grads.shape[0]
    steps = own // ROWS
    head_tile = pl.BlockSpec((HEADS, ROWS, LANES), lambda i, w: (0, i, 0))
    return pl.pallas_call(
        ungate_kernel,
        grid_spec=pltpu.PrefetchScalarGridSpec(
            num_scalar_prefetch=1,
            grid=(steps,),
            in_specs=[
                pl.BlockSpec((ROWS, D), lambda i, w: (i, 0)),
                pl.BlockSpec((D, OUT), lambda i, w: (0, QKVG // OUT)),
                pl.BlockSpec((ROWS, 256), lambda i, w: (i, 0)),
                pl.BlockSpec((ROWS, OUT), lambda i, w: (w[0] * steps + i, 0)),
                pl.BlockSpec((ROWS, LANES), lambda i, w: (i, 0)),
                pl.BlockSpec((ROWS, LANES), lambda i, w: (w[0] * steps + i, 0)),
                pl.BlockSpec((HEADS, ROWS, LANES), lambda i, w: (0, w[0] * steps + i, 0)),
            ],
            out_specs=(
                head_tile,
                head_tile,
                pl.BlockSpec((ROWS, 256), lambda i, w: (i, 0)),
                pl.BlockSpec((ROWS, 256), lambda i, w: (i, 0)),
            ),
        ),
        out_shape=(
            jax.ShapeDtypeStruct((HEADS, own, LANES), HALF),
            jax.ShapeDtypeStruct((HEADS, own, LANES), HALF),
            jax.ShapeDtypeStruct((own, 256), FULL),
            jax.ShapeDtypeStruct((own, 256), HALF),
        ),
        compiler_params=params(),
        name="ungate",
        cost_estimate=cost(8),
    )(where, grads, full, attended, gates, logs, sums, queries)


def pieces(scores, product, masked, transposed):
    prob = jnp.exp(scores)
    if masked:
        row = lax.broadcasted_iota(jnp.int32, scores.shape, 0)
        col = lax.broadcasted_iota(jnp.int32, scores.shape, 1)
        keep = row <= col if transposed else col <= row
        prob = jnp.where(keep, prob, 0.0)
    return prob.astype(HALF), (prob * product).astype(HALF)


def pack_lines(groups, pack_ref, others_ref, send, receive):
    device = neighbours(lax.axis_size("grp"), groups)[0]
    lines = Lines(send, receive)
    for step in range(1, groups):
        lines.plan(pack_ref, others_ref.at[step - 1], device(to_group=groups - step))
    return lines.made


def own_kernel(groups, q_ref, do_ref, k_ref, v_ref, pack_ref, dq_ref, dk_ref, dv_ref, others_ref, send, receive):
    @pl.when(pl.program_id(0) == 0)
    def begin():
        greet(neighbours(lax.axis_size("grp"), groups)[1][TP - 1 : TP - 2 + groups])
        for copy in pack_lines(groups, pack_ref, others_ref, send, receive):
            copy.start()

    count = min(BLOCK, q_ref.shape[1])
    steps = q_ref.shape[1] // count
    before = place()[1] * steps
    dk_ref[0] = jnp.zeros_like(dk_ref[0])
    dv_ref[0] = jnp.zeros_like(dv_ref[0])
    for at in range(steps):
        here = pl.ds(at * count, count)
        query, grad = q_ref[0, here], do_ref[0, here]

        def earlier(step, inner):
            there = pl.ds(step * count, count)
            key = k_ref[0, there]
            prob, dscore = pieces(
                dot(query, key, (1, 1)), dot(grad, v_ref[0, there], (1, 1)), False, False
            )
            return inner + dot(dscore, key)

        dquery = lax.fori_loop(0, before, earlier, jnp.zeros((count, LANES), FULL))
        for step in range(at + 1):
            there = pl.ds((before + step) * count, count)
            key = k_ref[0, there]
            prob, dscore = pieces(
                dot(key, query, (1, 1)), dot(v_ref[0, there], grad, (1, 1)), step == at, True
            )
            local = pl.ds(step * count, count)
            dk_ref[0, local] += dot(dscore, query)
            dv_ref[0, local] += dot(prob, grad)
            dquery = dquery + dot(dscore, key, (0, 0))
        dq_ref[0, here] = dquery

    @pl.when(pl.program_id(0) == HEADS - 1)
    def end():
        for copy in pack_lines(groups, pack_ref, others_ref, send, receive):
            copy.wait()


def own_back(queries, grads, keys, values, pack, groups):
    own, tokens = queries.shape[1], keys.shape[1]
    mine = pl.BlockSpec((1, own, LANES), lambda h: (h, 0, 0))
    whole = pl.BlockSpec((1, tokens, LANES), lambda h: (h, 0, 0))
    anywhere = pl.BlockSpec(memory_space=pl.ANY)
    return pl.pallas_call(
        functools.partial(own_kernel, groups),
        grid=(HEADS,),
        in_specs=[mine, mine, whole, whole, anywhere],
        out_specs=(mine, mine, mine, anywhere),
        out_shape=(jax.ShapeDtypeStruct((HEADS, own, LANES), FULL),) * 3
        + (jax.ShapeDtypeStruct((groups - 1,) + pack.shape, HALF),),
        scratch_shapes=[pltpu.SemaphoreType.DMA((groups - 1,)), pltpu.SemaphoreType.DMA((groups - 1,))],
        compiler_params=params(5),
        name="own_back",
        cost_estimate=cost(18),
    )(queries, grads, keys, values, pack)


def later_kernel(where_ref, q_ref, pack_ref, k_ref, v_ref, dk_in, dv_in, dk_ref, dv_ref, late_ref):
    own = k_ref.shape[1]
    head = pl.program_id(0)
    count = min(BLOCK, own)
    steps = own // count
    group, groups = where_ref[0], where_ref[1]
    dk_ref[0] = jnp.zeros_like(dk_ref[0])
    dv_ref[0] = dv_in[0]
    lanes = lax.broadcasted_iota(jnp.int32, (count, LANES), 1)

    def lanes_from(first):
        def find(col):
            part = col - DH
            return jnp.where((part >= 0) & (part < 3), DH + 6 * head + first + part, -1)

        return picker((LANES, find))

    minus, decay = lanes_from(0), lanes_from(3)

    def visit(at, carry):
        rows = pl.ds(at * count, count)
        sent = pack_ref[rows].astype(FULL)
        left, right = sent[:, :LANES], sent[:, LANES:]
        grad = jnp.where(head == 0, left, jnp.where(head == 1, pltpu.roll(left, DH, 1), right))
        grad = jnp.where(lanes < DH, grad, dot(pack_ref[rows, LANES:], minus)).astype(HALF)
        query = q_ref[0, pl.ds((group + 1) * own + at * count, count)].astype(FULL)
        query = jnp.where((lanes >= DH) & (lanes < DH + 3), 0.0, query)
        query = (query + dot(pack_ref[rows, LANES:], decay)).astype(HALF)
        for step in range(steps):
            here = pl.ds(step * count, count)
            prob, dscore = pieces(
                dot(k_ref[0, here], query, (1, 1)), dot(v_ref[0, here], grad, (1, 1)), False, True
            )
            dk_ref[0, here] += dot(dscore, query)
            dv_ref[0, here] += dot(prob, grad)
        return carry

    lax.fori_loop(0, (groups - 1 - group) * steps, visit, 0)
    late_ref[0] = jnp.broadcast_to(jnp.sum(dk_ref[0], axis=0, keepdims=True), (8, LANES))
    dk_ref[0] += dk_in[0]


def later_back(where, queries, pack, keys, values, dkeys, dvalues):
    own, tokens = dkeys.shape[1], keys.shape[1]
    mine = pl.BlockSpec((1, own, LANES), lambda h, w: (h, 0, 0))
    here = pl.BlockSpec((1, own, LANES), lambda h, w: (h, w[0], 0))
    return pl.pallas_call(
        later_kernel,
        grid_spec=pltpu.PrefetchScalarGridSpec(
            num_scalar_prefetch=1,
            grid=(HEADS,),
            in_specs=[
                pl.BlockSpec((1, tokens, LANES), lambda h, w: (h, 0, 0)),
                pl.BlockSpec(pack.shape, lambda h, w: (0, 0)),
                here,
                here,
                mine,
                mine,
            ],
            out_specs=(mine, mine, pl.BlockSpec((1, 8, LANES), lambda h, w: (h, 0, 0))),
        ),
        out_shape=(
            jax.ShapeDtypeStruct((HEADS, own, LANES), FULL),
            jax.ShapeDtypeStruct((HEADS, own, LANES), FULL),
            jax.ShapeDtypeStruct((HEADS, 8, LANES), FULL),
        ),
        compiler_params=params(),
        name="later_back",
        cost_estimate=cost(14),
    )(where, queries, pack, keys, values, dkeys, dvalues)


def unproject_kernel(
    where_ref, dq_ref, dk_ref, dv_ref, dg_ref, p_ref, z_ref, g_ref, late_ref, dp_ref, dz_ref, gain_ref, bias_ref, carry
):
    @pl.when(pl.program_id(0) == 0)
    def clear():
        carry[0:1] = late_ref[...]
        gain_ref[...] = jnp.zeros_like(gain_ref)
        bias_ref[...] = jnp.zeros_like(bias_ref)

    count = p_ref.shape[0]
    lanes = lax.broadcasted_iota(jnp.int32, (count, LANES), 1)
    sums = jnp.zeros((count, LANES), FULL)
    means = halves_matrix(1.0 / DH)
    gates = [
        pltpu.roll(dg_ref[:, :LANES], DH, 1),
        dg_ref[:, :LANES],
        pltpu.roll(dg_ref[:, LANES:], DH, 1),
    ]
    for head in range(HEADS):
        dquery, dkey = dq_ref[head], dk_ref[head]
        found = pltpu.roll(dquery, DH + head, 1) - pltpu.roll(dkey, DH - 3 + head, 1)
        sums = jnp.where(lanes == head, found, sums)
        grad = jnp.where(lanes < DH, dquery * (DH**-0.5), pltpu.roll(dkey, DH, 1))
        pair = p_ref[:, LANES * head : LANES * (head + 1)]
        inverse = lax.rsqrt(halves_mean(pair * pair, means) + EPS)
        normal = pair * inverse
        scaled = grad * g_ref[head : head + 1]
        gain_ref[head : head + 1] += jnp.sum(grad * normal, axis=0, keepdims=True)
        pulled = inverse * (scaled - normal * halves_mean(scaled * normal, means))
        dp_ref[:, 256 * head : 256 * head + LANES] = pulled.astype(HALF)
        dp_ref[:, 256 * head + LANES : 256 * head + 2 * LANES] = jnp.where(
            lanes < DH, dv_ref[head], gates[head]
        ).astype(HALF)
    row = lax.broadcasted_iota(jnp.int32, (count, count), 0)
    col = lax.broadcasted_iota(jnp.int32, (count, count), 1)
    later = (
        lax.dot_general(
            jnp.where(col >= row, 1.0, 0.0),
            sums,
            (((1,), (0,)), ((), ())),
            precision=lax.Precision.HIGHEST,
            preferred_element_type=FULL,
        )
        + carry[0:1]
    )
    carry[0:1] = later[0:1]
    low = jnp.where(lanes < HEADS, later * sigmoid(-z_ref[...]), 0.0).astype(HALF)
    dz_ref[...] = low
    bias_ref[0:1] += jnp.sum(low.astype(FULL), axis=0, keepdims=True)


def unproject(where, dqueries, dkeys, dvalues, dgates, pairs, logits, gains, late):
    own = dqueries.shape[1]
    steps = own // ROWS
    head_tile = pl.BlockSpec((HEADS, ROWS, LANES), lambda i, w: (0, steps - 1 - i, 0))
    small = pl.BlockSpec((8, LANES), lambda i, w: (0, 0))
    return pl.pallas_call(
        unproject_kernel,
        grid_spec=pltpu.PrefetchScalarGridSpec(
            num_scalar_prefetch=1,
            grid=(steps,),
            in_specs=[
                head_tile,
                head_tile,
                head_tile,
                pl.BlockSpec((ROWS, 256), lambda i, w: (steps - 1 - i, 0)),
                pl.BlockSpec((ROWS, HEADS * LANES), lambda i, w: (w[0] * steps + steps - 1 - i, 0)),
                pl.BlockSpec((ROWS, LANES), lambda i, w: (w[0] * steps + steps - 1 - i, 0)),
                small,
                pl.BlockSpec((1, LANES), lambda i, w: (0, 0)),
            ],
            out_specs=(
                pl.BlockSpec((ROWS, QKVG), lambda i, w: (steps - 1 - i, 0)),
                pl.BlockSpec((ROWS, LANES), lambda i, w: (steps - 1 - i, 0)),
                small,
                small,
            ),
            scratch_shapes=[pltpu.VMEM((8, LANES), FULL)],
        ),
        out_shape=(
            jax.ShapeDtypeStruct((own, QKVG), HALF),
            jax.ShapeDtypeStruct((own, LANES), HALF),
            jax.ShapeDtypeStruct((8, LANES), FULL),
            jax.ShapeDtypeStruct((8, LANES), FULL),
        ),
        compiler_params=params(),
        name="unproject",
        cost_estimate=cost(9),
    )(where, dqueries, dkeys, dvalues, dgates, pairs, logits, gains, late)


def across_groups(part, groups):
    size = groups * TP
    return [part] + [
        lax.ppermute(part, "fsdp", [((at + step * TP) % size, at) for at in range(size)])
        for step in range(1, groups)
    ]


def over_grps(parts, grps):
    return [
        [part] + [lax.ppermute(part, "grp", [((at + turn) % grps, at) for at in range(grps)]) for turn in range(1, grps)]
        for part in parts
    ]


def in_order(parts):
    return [turns[turn] for turn in range(len(parts[0])) for turns in parts]


def collect_grps(partial, grps, groups, own):
    grp = place()[0]
    parts = partial.reshape(grps, groups, TP, own, partial.shape[1])
    got = [lax.dynamic_index_in_dim(parts, grp, 0, False)]
    for turn in range(1, grps):
        give = lax.dynamic_index_in_dim(parts, lax.rem(grp + turn, grps), 0, False)
        got.append(lax.ppermute(give, "grp", [(at, (at + turn) % grps) for at in range(grps)]))
    return got


def collect_groups(got, groups):
    group, size = place()[1], groups * TP
    total = sum(part.astype(FULL) for part in got).astype(HALF)
    kept = [lax.dynamic_index_in_dim(total, group, 0, False)]
    for step in range(1, groups):
        give = lax.dynamic_index_in_dim(total, lax.rem(group + step, groups), 0, False)
        kept.append(lax.ppermute(give, "fsdp", [(at, (at + step * TP) % size) for at in range(size)]))
    return kept


def collected(kept):
    return sum(part.astype(FULL) for part in kept).astype(HALF)


def unpack(grad_ref, near, gate, up, down, out):
    lanes = lax.broadcasted_iota(jnp.int32, (near.shape[1], LANES), 1)

    def half(ref, part, upper):
        member, at, side = part
        value = ref[member, :, at : at + LANES].astype(FULL)
        return pltpu.roll(value, DH, 1) if side != upper else value

    def store(at, ref, lower, upper):
        value = jnp.where(lanes < DH, half(ref, lower, False), half(ref, upper, True))
        grad_ref[:, at : at + LANES] = value.astype(HALF)

    for at in range(0, H, 2):
        for kind in range(4):
            pair = [
                (head // HEADS, 256 * (head % HEADS) + LANES * (kind // 2), kind % 2 == 1) for head in (at, at + 1)
            ]
            store(kind * D + at * DH, near, *pair)
        pair = [
            (head // HEADS, LANES * (head % HEADS // 2), head % HEADS % 2 == 1) for head in (at, at + 1)
        ]
        store(4 * D + at * DH, out, *pair)
    for member in range(TP):
        at = 5 * D + member * UNITS
        grad_ref[:, at : at + UNITS] = gate[member]
        grad_ref[:, at + F : at + F + UNITS] = up[member]
        grad_ref[:, at + 2 * F : at + 2 * F + UNITS] = down[member]


PARTS = 2


def end_counts(grps, groups):
    replicas = grps * groups - 1
    return 7 + PARTS * ((grps - 1) * groups + groups - 1) + 5 * (TP - 1) + 2 * (replicas + TP - 1)


def end_kernel(
    grps, groups,
    p_ref, z_ref, f_ref, x_ref, g_ref, d_ref, s_ref, gate_ref, up_ref, down_ref, out_ref, w_ref, t_ref,
    y_ref, grad_ref, small_ref, norm_ref, hnear_ref, hgate_ref, hup_ref, hdown_ref, hout_ref,
    weights, tokens, near, mine, give, take, out, came, over_got, across_out, across_got, last,
    packet, packets, scalar, scalars, members, send, receive, local,
):
    grp, group, member = place()
    device, everyone = neighbours(grps, groups)
    replicas = [(turn, step) for turn in range(grps) for step in range(groups) if turn or step]
    everyone = everyone + [device(turn, step) for turn, step in replicas if turn and step]
    call_out(everyone)
    count = tokens.shape[0]
    load_tokens = pltpu.make_async_copy(t_ref.at[pl.ds(group * count, count)], tokens, local.at[0])
    load_weights = pltpu.make_async_copy(w_ref.at[:, pl.ds(0, QKVG)], weights, local.at[1])
    load_tokens.start()
    load_weights.start()
    lines = Lines(send, receive)
    stage = (give, take, out, came)
    sums = sum_plan(lines, stage)
    slab = near.shape[0] // (grps * groups)
    part_rows = slab // PARTS
    own = last.shape[2]
    over, across, home, far = {}, {}, {}, []

    def rows_of(turn, step, part):
        side = lax.div(member, 4)
        side = side + part - 2 * part * side
        index = lax.rem(grp + turn, grps) * groups + lax.rem(group + step, groups)
        return pl.ds(index * slab + side * part_rows, part_rows)

    order = [(ahead, part) for ahead in list(range(1, groups)) + [0] for part in (1, 0)]
    for ahead, part in order:
        for turn in range(1, grps):
            over[turn, ahead, part] = lines.plan(
                near.at[rows_of(turn, ahead, part)], over_got.at[turn - 1, ahead, part], device(turn)
            )
        if ahead:
            across[ahead, part] = lines.plan(
                across_out.at[ahead - 1, part], across_got.at[ahead - 1, part], device(to_group=ahead)
            )
    for bits in range(1, TP):
        source = last.at[bits // 4, lax.rem(flip(member, bits), 4)]
        home[bits] = lines.plan(source, hnear_ref.at[member], device(bits=bits))
    pairs = ((gate_ref, hgate_ref), (up_ref, hup_ref), (down_ref, hdown_ref), (out_ref, hout_ref))
    for source, target in pairs:
        for bits in range(1, TP):
            far.append(lines.plan(source.at[flip(member, bits)], target.at[member], device(bits=bits)))
    shared = [lines.plan(packet, packets.at[at], device(turn, step)) for at, (turn, step) in enumerate(replicas)]
    told = [lines.plan(small_ref.at[member], small_ref.at[member], device(bits=bits)) for bits in range(1, TP)]
    added = [lines.plan(scalar.at[0], scalars.at[at], device(turn, step)) for at, (turn, step) in enumerate(replicas)]
    closed = [lines.plan(scalar.at[1], members.at[bits - 1], device(bits=bits)) for bits in range(1, TP)]

    projected = p_ref[...].reshape(count, QKVG)
    cut = D // 4
    load_tokens.wait()
    for at in range(4):
        here = slice(at * cut, (at + 1) * cut)
        near[here] = dot(tokens[:, here], projected, (0, 0)).astype(HALF)
    hear(everyone)
    for ahead, part in order:
        if ahead:
            for turn in range(1, grps):
                over[turn, ahead, part].start()
    load_weights.wait()
    sum_give([(p_ref, weights), (z_ref, f_ref)], stage, sums, mine)
    for turn in range(1, grps):
        for part in (1, 0):
            over[turn, 0, part].start()
    summed = sum_pass(stage, sums, mine)
    for ahead, part in order:
        if ahead:
            total = near[rows_of(0, ahead, part)].astype(FULL)
            for turn in range(1, grps):
                over[turn, ahead, part].wait_recv()
                total = total + over_got[turn - 1, ahead, part].astype(FULL)
            across_out[ahead - 1, part] = total.astype(HALF)
            across[ahead, part].start()
    for copy in far:
        copy.start()
    for source, target in pairs:
        target[member] = source[member]
    packet[...] = s_ref[...]
    forget = dot(z_ref[...].reshape(count, LANES), tokens[...], (0, 0))
    packet[0:HEADS] = forget[0:HEADS]
    summed = sum_take(summed, stage, sums)
    pulled, dgain = rms_back(x_ref[...].astype(FULL), g_ref[...], summed)
    y_ref[...] = (d_ref[...] + pulled).astype(HALF)
    packet[HEADS : HEADS + 1] = dgain
    for copy in shared:
        copy.start()
    for part in (1, 0):
        total = near[rows_of(0, 0, part)].astype(FULL)
        for turn in range(1, grps):
            over[turn, 0, part].wait_recv()
            total = total + over_got[turn - 1, 0, part].astype(FULL)
        for ahead in range(1, groups):
            across[ahead, part].wait_recv()
            total = total + across_got[ahead - 1, part].astype(FULL)
        for at in range(4):
            last[part, at] = total[at * own : (at + 1) * own].astype(HALF)
        for bits in range(max(4 * part, 1), 4 * part + 4):
            home[bits].start()
    hnear_ref[member] = last[0, lax.rem(member, 4)]
    total = packet[...]
    for at, copy in enumerate(shared):
        copy.wait_recv()
        total = total + packets[at]
    small_ref[member] = total
    for copy in told:
        copy.start()
    for copy in far:
        copy.wait_recv()

    def square(ref):
        value = ref[...].astype(FULL)
        return jnp.sum(value * value)

    squares = square(hgate_ref) + square(hup_ref) + square(hdown_ref) + square(hout_ref)
    for copy in home.values():
        copy.wait_recv()
    squares = squares + square(hnear_ref)
    scalar[0] = jnp.full((8, LANES), squares, FULL)
    for copy in added:
        copy.start()
    unpack(grad_ref, hnear_ref, hgate_ref, hup_ref, hdown_ref, hout_ref)
    for copy in told:
        copy.wait_recv()
    every = small_ref[...]
    heads = jnp.sum(every[:, :HEADS] * every[:, :HEADS])
    heads = heads + jnp.sum(every[:, HEADS + 2] * every[:, HEADS + 2])
    shared_gains = jnp.sum(every[:, HEADS : HEADS + 2], axis=0)
    heads = heads + jnp.sum(shared_gains * shared_gains)
    total = scalar[0]
    for at, copy in enumerate(added):
        copy.wait_recv()
        total = total + scalars[at]
    scalar[1] = total
    for copy in closed:
        copy.start()
    total = total + heads
    for at, copy in enumerate(closed):
        copy.wait_recv()
        total = total + members[at]
    norm_ref[...] = jnp.sqrt(total)
    for copy in lines.made:
        copy.wait_send()


def end(projected, logits, forget, source, gain, grad, small, gate, up, down, out, near, tokens, grps, groups):
    rows, own = source.shape[0], gate.shape[1]
    count = end_counts(grps, groups)
    replicas = grps * groups - 1
    slab = TP * own
    part = (slab // PARTS, QKVG)
    vmem, anywhere = pl.BlockSpec(memory_space=pltpu.VMEM), pl.BlockSpec(memory_space=pl.ANY)
    return pl.pallas_call(
        functools.partial(end_kernel, grps, groups),
        out_shape=(
            jax.ShapeDtypeStruct((rows, D), HALF),
            jax.ShapeDtypeStruct((own, 5 * D + 3 * F), HALF),
            jax.ShapeDtypeStruct((TP, 8, D), FULL),
            jax.ShapeDtypeStruct((8, LANES), FULL),
        ),
        in_specs=[vmem] * 11 + [anywhere] * 2,
        out_specs=(vmem,) * 4,
        scratch_shapes=[
            pltpu.VMEM((TP, own, QKVG), HALF),
            pltpu.VMEM((TP, own, UNITS), HALF),
            pltpu.VMEM((TP, own, UNITS), HALF),
            pltpu.VMEM((TP, own, UNITS), HALF),
            pltpu.VMEM((TP, own, OUT), HALF),
            pltpu.VMEM((D, QKVG), HALF),
            pltpu.VMEM((TP * rows, D), HALF),
            pltpu.VMEM((D, QKVG), HALF),
            pltpu.VMEM((4, rows, D), FULL),
        ]
        + sum_scratch(rows)
        + [
            pltpu.VMEM((grps - 1, groups, PARTS) + part, HALF),
            pltpu.VMEM((groups - 1, PARTS) + part, HALF),
            pltpu.VMEM((groups - 1, PARTS) + part, HALF),
            pltpu.VMEM((PARTS, 4, own, QKVG), HALF),
            pltpu.VMEM((8, D), FULL),
            pltpu.VMEM((replicas, 8, D), FULL),
            pltpu.VMEM((2, 8, LANES), FULL),
            pltpu.VMEM((replicas, 8, LANES), FULL),
            pltpu.VMEM((TP - 1, 8, LANES), FULL),
            pltpu.SemaphoreType.DMA((count,)),
            pltpu.SemaphoreType.DMA((count,)),
            pltpu.SemaphoreType.DMA((2,)),
        ],
        compiler_params=params(4),
        name="end",
        cost_estimate=cost(60),
    )(
        projected.reshape(4, 2, rows, QKVG),
        logits.reshape(4, 2, rows, LANES),
        forget,
        source,
        gain,
        grad,
        small,
        gate,
        up,
        down,
        out,
        near,
        tokens,
    )


def adam(value, first, second, grad, rate, decay):
    first = BETA_ONE * first + (1.0 - BETA_ONE) * grad
    second = BETA_TWO * second + (1.0 - BETA_TWO) * grad * grad
    unbiased_first = first / (1.0 - BETA_ONE**STEP)
    unbiased_second = second / (1.0 - BETA_TWO**STEP)
    value = value - rate * (unbiased_first / (jnp.sqrt(unbiased_second) + ADAM_EPS) + decay * value)
    return (value, first, second)


def update_kernel(norm_ref, w_ref, m_ref, v_ref, g_ref, nw_ref, nm_ref, nv_ref):
    factor = CLIP / jnp.maximum(norm_ref[0:1, 0:1], CLIP)
    new = adam(w_ref[...], m_ref[...], v_ref[...], g_ref[...].astype(FULL) * factor, RATE_MATRIX, DECAY)
    nw_ref[...], nm_ref[...], nv_ref[...] = new


def update(norm, weights, first, second, grads):
    own, width = weights.shape
    wide = 3 * D + 3 * LANES
    tile = pl.BlockSpec((own, wide), lambda i: (0, i))
    return pl.pallas_call(
        update_kernel,
        grid=(width // wide,),
        out_shape=(jax.ShapeDtypeStruct((own, width), FULL),) * 3,
        in_specs=[whole_spec((8, LANES)), tile, tile, tile, tile],
        out_specs=(tile,) * 3,
        compiler_params=params(),
        name="update",
        cost_estimate=cost(9),
    )(norm, weights, first, second, grads)


def pad_lanes(value, width=LANES):
    return jnp.pad(value, ((0, 0), (0, width - value.shape[1])))


def grad_of(left, right):
    return jnp.einsum("tr,tc->rc", left, right, preferred_element_type=FULL).astype(HALF)


def shards(
    inputs,
    cotangent,
    weights,
    weights_first,
    weights_second,
    gains,
    gains_first,
    gains_second,
    forget_weight,
    forget_first,
    forget_second,
    forget_bias,
    bias_first,
    bias_second,
):
    grps, groups = lax.axis_size("grp"), lax.axis_size("fsdp") // TP
    grp, group, member = place()
    rows, own_rows = inputs.shape[1], weights.shape[0]
    group_tokens = TP * rows
    span = groups * group_tokens
    source, returned = inputs[0], cotangent[0]
    where = jnp.stack([group, jnp.int32(groups)]).astype(jnp.int32)

    tokens, near, both, down, gathered = start(source, gains[0:1], weights, returned, grps, groups)
    slab = TP * own_rows
    both, down = both.reshape(slab, 2 * UNITS), down.reshape(slab, UNITS)
    tokens = tokens.reshape(span, D)
    near = near.reshape(D, NEAR)
    both_parts = across_groups(both, groups)
    both_own = over_grps(both_parts[:1], grps)

    forget_low = pad_lanes(lax.dynamic_slice_in_dim(forget_weight, member * HEADS, HEADS, 1).astype(HALF))
    bias = pad_lanes(lax.dynamic_slice_in_dim(forget_bias[None], member * HEADS, HEADS, 1))
    head_gains = lax.dynamic_slice_in_dim(gains[2:4], member * HEADS * DH, HEADS * DH, 1)
    head_gains = head_gains.reshape(2, HEADS, DH).transpose(1, 0, 2).reshape(HEADS, 2 * DH)
    head_gains = jnp.pad(head_gains, ((0, 8 - HEADS), (0, 0)))
    queries, keys, values, pairs, gates, logits, sums, gathered = project(
        tokens, near, forget_low, bias, head_gains, gathered
    )
    gated, attended, logs = attend(queries, keys, values, gates, group_tokens)
    returned_all = gathered.reshape(group_tokens, D)
    gated, both_parts = lax.optimization_barrier((gated, both_parts[1:]))
    both_parts = both_own + over_grps(both_parts, grps)
    mixed, second, *down_pieces = mix(gated, near, source, gains[1:2], down, grps, groups)
    both_pieces, down_pieces = in_order(both_parts), [down, *down_pieces]
    second = second.reshape(group_tokens, D)
    hidden, grad_both = feed(second, returned_all, both_pieces, down_pieces, grps, groups)
    grad_mixed, grad_gain_mid, branch, out_sums, far_gate, far_up, far_down = unmix(
        grad_both, both_pieces, down_pieces, mixed, gains[1:2], returned, hidden, second, returned_all, grps, groups
    )
    branch = branch.reshape(group_tokens, D)
    far_up = collect_grps(far_up, grps, groups, own_rows)
    far_out = collect_grps(grad_of(branch, gated), grps, groups, own_rows)
    size = lax.axis_size("fsdp")
    far_gate = [far_gate[0]] + [
        lax.ppermute(far_gate[step], "fsdp", [(at, (at + step * TP) % size) for at in range(size)])
        for step in range(1, groups)
    ]

    grads_low, queries_back, grad_gates, pack = ungate(where, branch, near, attended, gates, logs, sums, queries)
    dqueries, dkeys, dvalues, others = own_back(queries_back, grads_low, keys, values, pack, groups)
    others = others.reshape((groups - 1) * group_tokens, OUT)
    dkeys, far_out, far_up = lax.optimization_barrier((dkeys, far_out, far_up))
    far_out, far_up = collect_groups(far_out, groups), collect_groups(far_up, groups)
    dkeys, dvalues, late = later_back(where, queries, others, keys, values, dkeys, dvalues)
    later = pad_lanes(late[:, 0, DH + 3][None])
    if groups > 2:
        everyone = lax.all_gather(dkeys[:, :, DH + 3].sum(axis=1) - dqueries[:, :, DH].sum(axis=1), "fsdp")
        ahead = (jnp.arange(size) // TP > group) & (jnp.arange(size) % TP == member)
        later = pad_lanes(-jnp.sum(jnp.where(ahead[:, None], everyone, 0.0), axis=0)[None])
    grad_projected, grad_logits, grad_heads, grad_bias = unproject(
        where, dqueries, dkeys, dvalues, grad_gates, pairs, logits, head_gains, later
    )

    grad_heads = grad_heads[:HEADS].reshape(HEADS, 2, DH).transpose(1, 0, 2).reshape(1, 2 * HEADS * DH)
    rest = jnp.concatenate([grad_heads, grad_bias[0:1, :HEADS]], axis=1)
    small = jnp.concatenate(
        [jnp.zeros((HEADS + 1, D), FULL), grad_gain_mid, pad_lanes(rest, D), jnp.zeros((2, D), FULL)], axis=0
    )
    input_grad, grads, small, norm = end(
        grad_projected,
        grad_logits,
        forget_low,
        source,
        gains[0:1],
        grad_mixed,
        small,
        collected(far_gate).reshape(TP, own_rows, UNITS),
        collected(far_up),
        far_down.astype(HALF).reshape(TP, own_rows, UNITS),
        collected(far_out),
        near,
        tokens,
        grps,
        groups,
    )
    norm, out_sums = lax.optimization_barrier((norm, out_sums))
    result = mixed + out_sums[3].astype(FULL)
    for at, bits in enumerate((2, 4, 6)):
        result = result + lax.ppermute(out_sums[at], "fsdp", [(to, to ^ bits) for to in range(size)]).astype(FULL)
    output = result.astype(HALF)
    grad_norm = norm[0, 0]
    grad_forget = small[:, :HEADS].reshape(H, D).T
    edge = HEADS * DH
    grad_gains = jnp.concatenate(
        [
            jnp.sum(small[:, HEADS : HEADS + 2], axis=0),
            small[:, HEADS + 2, :edge].reshape(1, D),
            small[:, HEADS + 2, edge : 2 * edge].reshape(1, D),
        ],
        axis=0,
    )
    grad_bias = small[:, HEADS + 2, 2 * edge : 2 * edge + HEADS].reshape(H)
    factor = CLIP / jnp.maximum(grad_norm, CLIP)
    new_w, new_wf, new_ws = update(norm, weights, weights_first, weights_second, grads)
    new_g, new_gf, new_gs = adam(gains, gains_first, gains_second, grad_gains * factor, RATE_GAIN, 0.0)
    new_fw, new_ff, new_fs = adam(
        forget_weight, forget_first, forget_second, grad_forget * factor, RATE_MATRIX, DECAY
    )
    new_fb, new_bf, new_bs = adam(
        forget_bias, bias_first, bias_second, grad_bias * factor, RATE_BIAS, 0.0
    )
    return (
        output[None],
        input_grad[None],
        grad_norm,
        new_w,
        new_wf,
        new_ws,
        new_g,
        new_gf,
        new_gs,
        new_fw,
        new_ff,
        new_fs,
        new_fb,
        new_bf,
        new_bs,
    )


def solution(mesh):
    tokens = P("grp", "fsdp", None)
    matrix = P(("grp", "fsdp"), None)
    return jax.shard_map(
        shards,
        mesh=mesh,
        in_specs=(tokens,) * 2 + (matrix,) * 3 + (P(),) * 9,
        out_specs=(tokens,) * 2 + (P(),) + (matrix,) * 3 + (P(),) * 9,
        check_vma=False,
    )
```

```python
import functools

import jax
import jax.numpy as jnp
from jax import lax
from jax.experimental import pallas as pl
from jax.experimental.pallas import tpu as pltpu
from jax.sharding import PartitionSpec as P

D = 1536
H = 24
DH = 64
F = 4096
STEP = 5

EPS = 1e-06
BETA_ONE = 0.9
BETA_TWO = 0.95
ADAM_EPS = 1e-08
RATE_MATRIX = 0.1
RATE_GAIN = 1.2
RATE_BIAS = 3.0
DECAY = 0.1
CLIP = 1.0
NEGATIVE = -1e30

TP = 8
HEADS = H // TP
UNITS = F // TP
QKVG = HEADS * 4 * DH
OUT = 256
NEAR = QKVG + OUT
LANES = 128
ROWS = 256
TALL = 512
BLOCK = 512
MESH = pl.DeviceIdType.MESH
HALF = jnp.bfloat16
FULL = jnp.float32
VMEM_BYTES = 56 * 1024 * 1024


def params(collective=None, **more):
    if collective is None:
        return pltpu.CompilerParams(vmem_limit_bytes=VMEM_BYTES, **more)
    return pltpu.CompilerParams(
        collective_id=collective, has_side_effects=True, vmem_limit_bytes=VMEM_BYTES, **more
    )


def flip(member, bits):
    for bit in (1, 2, 4):
        if bits & bit:
            member = member + bit - 2 * bit * lax.rem(lax.div(member, bit), 2)
    return member


def place():
    position = lax.axis_index("fsdp")
    return lax.axis_index("grp"), lax.div(position, TP), lax.rem(position, TP)


def cost(micros):
    return pl.CostEstimate(flops=0, bytes_accessed=3_000_000 * micros, transcendentals=0)


def call_out(targets):
    barrier = pltpu.get_barrier_semaphore()
    for target in targets:
        pl.semaphore_signal(barrier, inc=1, device_id=target, device_id_type=MESH)


def hear(targets):
    pl.semaphore_wait(pltpu.get_barrier_semaphore(), len(targets))


def greet(targets):
    call_out(targets)
    hear(targets)


def neighbours(grps, groups):
    grp, group, member = place()

    def device(to_grp=0, to_group=0, bits=0):
        return (
            lax.rem(grp + to_grp, grps),
            lax.rem(group + to_group, groups) * TP + flip(member, bits),
        )

    return device, (
        [device(bits=bits) for bits in range(1, TP)]
        + [device(to_group=step) for step in range(1, groups)]
        + [device(to_grp=step) for step in range(1, grps)]
    )


class Lines:
    def __init__(self, send, receive):
        self.send, self.receive, self.count, self.made = send, receive, 0, []

    def plan(self, source, target, device):
        copy = pltpu.make_async_remote_copy(
            src_ref=source,
            dst_ref=target,
            send_sem=self.send.at[self.count],
            recv_sem=self.receive.at[self.count],
            device_id=device,
            device_id_type=MESH,
        )
        self.count += 1
        self.made.append(copy)
        return copy


def dot(left, right, contract=(1, 0)):
    return lax.dot_general(
        left, right, (((contract[0],), (contract[1],)), ((), ())), preferred_element_type=FULL
    )


def rms_rows(value, gain):
    return value * lax.rsqrt(jnp.mean(value * value, axis=-1, keepdims=True) + EPS) * gain


def rms_back(value, gain, grad):
    inverse = lax.rsqrt(jnp.mean(value * value, axis=-1, keepdims=True) + EPS)
    normal = value * inverse
    scaled = grad * gain
    pulled = inverse * (scaled - normal * jnp.mean(scaled * normal, axis=-1, keepdims=True))
    return pulled, jnp.sum(grad * normal, axis=0, keepdims=True)


def half_lanes(value, column, upper):
    base = column // LANES * LANES
    part = value[:, base : base + LANES]
    if (column % LANES != 0) != upper:
        part = pltpu.roll(part, DH, 1)
    return part


def two_halves(value, lower, upper, lanes):
    low = half_lanes(value, lower, False)
    if upper is None:
        return jnp.where(lanes < DH, low, 0.0)
    return jnp.where(lanes < DH, low, half_lanes(value, upper, True))


def pack_near(w_ref, near):
    lanes = lax.broadcasted_iota(jnp.int32, (w_ref.shape[0], LANES), 1)
    for member in range(TP):
        for head in range(HEADS):
            at = (member * HEADS + head) * DH
            near[member, :, 256 * head : 256 * head + LANES] = two_halves(w_ref, at, D + at, lanes).astype(HALF)
            near[member, :, 256 * head + LANES : 256 * head + 256] = two_halves(
                w_ref, 2 * D + at, 3 * D + at, lanes
            ).astype(HALF)
        at = 4 * D + member * HEADS * DH
        near[member, :, QKVG : QKVG + LANES] = two_halves(w_ref, at, at + DH, lanes).astype(HALF)
        near[member, :, QKVG + LANES :] = two_halves(w_ref, at + 2 * DH, None, lanes).astype(HALF)


def pack_far(w_ref, both, down):
    edge = 5 * D
    for member in range(TP):
        at = edge + member * UNITS
        both[member, :, :UNITS] = w_ref[:, at : at + UNITS].astype(HALF)
        both[member, :, UNITS:] = w_ref[:, at + F : at + F + UNITS].astype(HALF)
        down[member] = w_ref[:, at + 2 * F : at + 2 * F + UNITS].astype(HALF)


def halves(ref):
    count = ref.shape[0] // 2
    return [ref.at[pl.ds(at * count, count)] for at in range(2)]


def halves(ref):
    count = ref.shape[0] // 2
    return [ref.at[pl.ds(at * count, count)] for at in range(2)]


def start_counts(grps, groups):
    weights = (TP - 1) + (groups - 1) * TP + (grps - 1) * groups * TP
    return GATHER + 2 * (groups - 1) + weights + 2 * (TP - 1)


def start_kernel(
    grps, groups, x_ref, g_ref, w_ref, all_ref, next_ref, full_ref, both_ref, down_ref,
    block, near, both, down, send, receive, local,
):
    grp, group, member = place()
    device, everyone = neighbours(grps, groups)
    call_out(everyone)
    block[...] = rms_rows(x_ref[...].astype(FULL), g_ref[...]).astype(HALF)
    lines = Lines(send, receive)
    first, across, over, far = {}, {}, {}, []
    tokens = gather_plan(lines, block, all_ref, True)
    ahead, aside = [], []
    for back in range(1, groups):
        ahead.append(lines.plan(block, next_ref.at[back - 1, 0], device(to_group=groups - back)))
        aside.append(lines.plan(next_ref.at[back - 1, 0], next_ref.at[back - 1, 1], device(bits=4)))
    for bits in range(1, TP):
        first[bits] = lines.plan(near.at[flip(member, bits)], full_ref.at[grp, group, member], device(bits=bits))
    for bits in range(TP):
        slot = full_ref.at[grp, group, flip(member, bits)]
        source = near.at[member] if bits == 0 else slot
        for back in range(1, groups):
            across[back, bits] = lines.plan(source, slot, device(to_group=groups - back))
        for step in range(1, grps):
            over[step, 0, bits] = lines.plan(source, slot, device(to_grp=step))
        for back in range(1, groups):
            passed = full_ref.at[grp, lax.rem(group + back, groups), flip(member, bits)]
            for step in range(1, grps):
                over[step, back, bits] = lines.plan(passed, passed, device(to_grp=step))
    for bits in range(1, TP):
        there = flip(member, bits)
        far.append(lines.plan(both.at[there], both_ref.at[member], device(bits=bits)))
        far.append(lines.plan(down.at[there], down_ref.at[member], device(bits=bits)))

    own_tokens = pltpu.make_async_copy(block, all_ref.at[member], local.at[0])
    own = [
        pltpu.make_async_copy(near.at[member], full_ref.at[grp, group, member], local.at[1]),
        pltpu.make_async_copy(both.at[member], both_ref.at[member], local.at[2]),
        pltpu.make_async_copy(down.at[member], down_ref.at[member], local.at[3]),
    ]
    hear(everyone)
    for copy in ahead:
        copy.start()
    pack_near(w_ref, near)
    for bits in (4, 2, 6, 1, 5, 3, 7):
        first[bits].start()
    for back in range(1, groups):
        across[back, 0].start()
    for step in range(1, grps):
        over[step, 0, 0].start()
    gather_start(tokens, own_tokens)
    own[0].start()
    pack_far(w_ref, both, down)
    for bits in (1, 5, 3, 7, 2, 4, 6):
        first[bits].wait_recv()
        for back in range(1, groups):
            across[back, bits].start()
        for step in range(1, grps):
            over[step, 0, bits].start()
    gather_turn(tokens, True)
    for copy in far:
        copy.start()
    for copy in own[1:]:
        copy.start()
    for come, gone in zip(ahead, aside):
        come.wait_recv()
        gone.start()
    gather_pass(tokens, True)
    for back in range(1, groups):
        for bits in (0, 1, 5, 3, 7, 2, 4, 6):
            across[back, bits].wait_recv()
            for step in range(1, grps):
                over[step, back, bits].start()
    gather_end(tokens, own_tokens)
    for copy in aside + far + list(over.values()):
        copy.wait_recv()
    for copy in lines.made:
        copy.wait_send()
    for copy in own:
        copy.wait()


def start(source, gain, weights, grps, groups):
    rows, own = source.shape[0], weights.shape[0]
    count = start_counts(grps, groups)
    vmem, anywhere = pl.BlockSpec(memory_space=pltpu.VMEM), pl.BlockSpec(memory_space=pl.ANY)
    return pl.pallas_call(
        functools.partial(start_kernel, grps, groups),
        out_shape=(
            jax.ShapeDtypeStruct((TP, rows, D), HALF),
            jax.ShapeDtypeStruct((groups - 1, 2, rows, D), HALF),
            jax.ShapeDtypeStruct((grps, groups, TP, own, NEAR), HALF),
            jax.ShapeDtypeStruct((TP, own, 2 * UNITS), HALF),
            jax.ShapeDtypeStruct((TP, own, UNITS), HALF),
        ),
        in_specs=[vmem] * 3,
        out_specs=(anywhere,) * 5,
        scratch_shapes=[
            pltpu.VMEM((rows, D), HALF),
            pltpu.VMEM((TP, own, NEAR), HALF),
            pltpu.VMEM((TP, own, 2 * UNITS), HALF),
            pltpu.VMEM((TP, own, UNITS), HALF),
            pltpu.SemaphoreType.DMA((count,)),
            pltpu.SemaphoreType.DMA((count,)),
            pltpu.SemaphoreType.DMA((4,)),
        ],
        compiler_params=params(1),
        name="start",
        cost_estimate=cost(60),
    )(source, gain, weights)


def three(value):
    high = value.astype(HALF).astype(FULL)
    rest = value - high
    middle = rest.astype(HALF).astype(FULL)
    return high, middle, (rest - middle).astype(HALF).astype(FULL)


def two(value):
    high = value.astype(HALF)
    return high, (value - high.astype(FULL)).astype(HALF)


def at_lanes(lanes, pairs, other):
    for lane, value in pairs:
        other = jnp.where(lanes == lane, value, other)
    return other


def side_by_side(values, lanes):
    packed = jnp.zeros_like(values[0])
    for at, value in enumerate(values):
        if at:
            value = pltpu.roll(value, HEADS * at, 1)
        packed = jnp.where((lanes >= HEADS * at) & (lanes < HEADS * (at + 1)), value, packed)
    return packed.astype(HALF)


def picker(targets):
    def build(width, find, sign=1.0):
        row = lax.broadcasted_iota(jnp.int32, (LANES, width), 0)
        col = lax.broadcasted_iota(jnp.int32, (LANES, width), 1)
        return jnp.where(row == find(col), sign, 0.0).astype(HALF)

    return build(*targets)


def spread_lanes(first, at):
    def find(col):
        head, lane = lax.div(col, LANES), lax.rem(col, LANES) - at
        return jnp.where((lane >= 0) & (lane < 3), HEADS * (first + lane) + head, -1)

    return find


def halves_matrix(scale):
    row = lax.broadcasted_iota(jnp.int32, (LANES, LANES), 0)
    col = lax.broadcasted_iota(jnp.int32, (LANES, LANES), 1)
    return jnp.where((row < DH) == (col < DH), scale, 0.0).astype(HALF)


def halves_mean(value, matrix):
    high, least = two(value)
    return dot(high, matrix) + dot(least, matrix)


def side_plan(lines, pair_ref, all_ref):
    member = place()[2]
    plan = {}
    for at, bits in ((0, 0), (1, 4)):
        there = flip(member, bits)
        plan[bits + 2] = lines.plan(pair_ref.at[at], all_ref.at[there], group_device(2))
        plan[bits + 1] = lines.plan(pair_ref.at[at], all_ref.at[there], group_device(1))
    for bits in (2, 6):
        slot = all_ref.at[flip(member, bits)]
        plan[bits + 1] = lines.plan(slot, slot, group_device(1))
    return plan


def first_leg(lines, block, all_ref):
    member = place()[2]
    return {bits: lines.plan(block, all_ref.at[member], group_device(bits)) for bits in (2, 4)}


def third_leg(lines, all_ref):
    member = place()[2]

    def copy(block, bits):
        slot = all_ref.at[flip(member, block)]
        return lines.plan(slot, slot, group_device(bits))

    return {6: copy(4, 2), 1: copy(0, 1), 3: copy(2, 1), 5: copy(4, 1), 7: copy(6, 1)}


def project_kernel(
    groups, a_ref, n_ref, w_ref, f_ref, b_ref, g_ref, c_ref,
    q_ref, k_ref, v_ref, p_ref, t_ref, z_ref, all_ref, others, decays, totals, send, receive, local,
):
    turn = pl.program_id(0)
    grp, group, member = place()
    own = a_ref.shape[0]
    rows = own // TP
    lanes = lax.broadcasted_iota(jnp.int32, (TALL, LANES), 1)

    def plans():
        lines = Lines(send, receive)
        sides = [side_plan(lines, n_ref.at[at], others.at[at]) for at in range(groups - 1)]
        copies = [
            pltpu.make_async_copy(n_ref.at[at, half], others.at[at, flip(member, 4 * half)], local.at[2 * at + half])
            for at in range(groups - 1)
            for half in range(2)
        ]
        copies.append(pltpu.make_async_copy(c_ref, all_ref.at[member], local.at[2 * groups - 2]))
        return lines, sides, copies, first_leg(lines, c_ref, all_ref)

    def low_rows(index, start, count):
        if index == 0:
            return a_ref[start : start + count]
        return others[index - 1, start // rows : (start + count) // rows].reshape(count, D)

    def scan(index):
        row = lax.broadcasted_iota(jnp.int32, (ROWS, ROWS), 0)
        col = lax.broadcasted_iota(jnp.int32, (ROWS, ROWS), 1)
        lower = jnp.where(col <= row, 1.0, 0.0)
        carry = jnp.zeros((1, LANES), FULL)
        for start in range(0, own, ROWS):
            logit = dot(low_rows(index, start, ROWS), f_ref[...]) + b_ref[...]
            if index == 0:
                z_ref[start : start + ROWS] = logit
            log_gate = jnp.minimum(logit, 0.0) - jnp.log1p(jnp.exp(-jnp.abs(logit)))
            part = carry + lax.dot_general(
                lower,
                log_gate,
                (((1,), (0,)), ((), ())),
                precision=lax.Precision.HIGHEST,
                preferred_element_type=FULL,
            )
            decays[index, start : start + ROWS] = part
            carry = part[ROWS - 1 : ROWS]
        totals[index : index + 1] = carry

    def rows_done(low, sums, start, first):
        here = slice(start, start + TALL)
        made = dot(low, w_ref[...])
        means = halves_matrix(1.0 / DH)
        packed = side_by_side(three(jnp.where(lanes < HEADS, sums, 0.0)), lanes)
        plus = dot(packed, picker((HEADS * LANES, spread_lanes(0, DH))))
        minus = dot(packed, picker((HEADS * LANES, spread_lanes(0, DH + 3), -1.0)))
        ones_of_query = jnp.where((lanes >= DH + 3) & (lanes < DH + 6), 1.0, 0.0)
        ones_of_value = jnp.where((lanes >= DH) & (lanes < DH + 3), 1.0, 0.0)
        ones_of_key = jnp.where((lanes >= DH + 6) & (lanes < DH + 9), 1.0, ones_of_value)
        for head in range(HEADS):
            register = slice(LANES * head, LANES * (head + 1))
            pair = made[:, 256 * head : 256 * head + LANES]
            value = made[:, 256 * head + LANES : 256 * head + 2 * LANES]
            normal = pair * lax.rsqrt(halves_mean(pair * pair, means) + EPS) * g_ref[head : head + 1]
            normal = normal.astype(HALF).astype(FULL)
            q_ref[head, here] = jnp.where(
                lanes < DH, normal * (DH**-0.5), plus[:, register] + ones_of_query
            ).astype(HALF)
            k_ref[head, here] = jnp.where(
                lanes < DH, pltpu.roll(normal, DH, 1), minus[:, register] + ones_of_key
            ).astype(HALF)
            v_ref[head, here] = jnp.where(lanes < DH, value, ones_of_value).astype(HALF)
            if first:
                p_ref[here, register] = pair
        if first:
            left, right = gates_of(made, lanes)
            t_ref[here, :LANES] = left
            t_ref[here, LANES:] = right

    @pl.when(turn == 0)
    def begin():
        greet([group_device(bits) for bits in (4, 2, 1)])
        lines, sides, copies, leg = plans()
        for copy in copies:
            copy.start()
        for side in sides:
            for bits in (2, 6, 1, 5):
                side[bits].start()
        leg[4].start()
        scan(0)
        for start in range(0, own, TALL):
            rows_done(low_rows(0, start, TALL), decays[0, start : start + TALL], start, True)
        leg[2].start()
        for side in sides:
            for bits in (2, 6):
                side[bits].wait_recv()
                side[bits + 1].start()

    @pl.when(turn == 1)
    def arrived():
        lines, sides, copies, leg = plans()
        for copy in copies[:-1]:
            copy.wait()
        for side in sides:
            for bits in (1, 3, 5, 7):
                side[bits].wait_recv()
        for index in range(1, groups):
            scan(index)

    @pl.when(turn > 0)
    def next_group():
        ahead = turn < groups - group
        base = jnp.zeros((1, LANES), FULL)
        for index in range(groups):
            weight = jnp.where(ahead, jnp.where(index < turn, 1.0, 0.0), jnp.where(index >= turn, -1.0, 0.0))
            base = base + weight * totals[index : index + 1]
        for start in range(0, own, TALL):
            low = others[turn - 1, start // rows : (start + TALL) // rows].reshape(TALL, D)
            rows_done(low, decays[turn, start : start + TALL] + base, start, False)

    @pl.when(turn == groups - 1)
    def end():
        lines, sides, copies, leg = plans()
        copies[-1].wait()
        for copy in leg.values():
            copy.wait_recv()
        for copy in lines.made:
            copy.wait_send()


def project(tokens, following, full, forget, bias, gains, returned):
    own, groups = tokens.shape[0], following.shape[0] + 1
    rows = returned.shape[0]
    count = 6 * (groups - 1) + 2
    tile = pl.BlockSpec((HEADS, own, LANES), lambda i: (0, i, 0))
    anywhere = pl.BlockSpec(memory_space=pl.ANY)
    return pl.pallas_call(
        functools.partial(project_kernel, groups),
        grid=(groups,),
        out_shape=(
            jax.ShapeDtypeStruct((HEADS, groups * own, LANES), HALF),
            jax.ShapeDtypeStruct((HEADS, groups * own, LANES), HALF),
            jax.ShapeDtypeStruct((HEADS, groups * own, LANES), HALF),
            jax.ShapeDtypeStruct((own, HEADS * LANES), FULL),
            jax.ShapeDtypeStruct((own, OUT), FULL),
            jax.ShapeDtypeStruct((own, LANES), FULL),
            jax.ShapeDtypeStruct((TP, rows, D), HALF),
        ),
        in_specs=[
            whole_spec((own, D)),
            anywhere,
            weight_spec(QKVG, 0),
            whole_spec((D, LANES)),
            whole_spec((1, LANES)),
            whole_spec((8, LANES)),
            whole_spec((rows, D)),
        ],
        out_specs=(
            tile,
            tile,
            tile,
            whole_spec((own, HEADS * LANES)),
            whole_spec((own, OUT)),
            whole_spec((own, LANES)),
            anywhere,
        ),
        scratch_shapes=[
            pltpu.VMEM((groups - 1, TP, rows, D), HALF),
            pltpu.VMEM((groups, own, LANES), FULL),
            pltpu.VMEM((max(groups, 8), LANES), FULL),
            pltpu.SemaphoreType.DMA((count,)),
            pltpu.SemaphoreType.DMA((count,)),
            pltpu.SemaphoreType.DMA((2 * groups - 1,)),
        ],
        compiler_params=params(8),
        name="project",
        cost_estimate=cost(25),
    )(tokens, following, full, forget, bias, gains, returned)


def sigmoid(value):
    return 1.0 / (1.0 + jnp.exp(-value))


def gates_of(made, lanes):
    second = [made[:, 256 * head + LANES : 256 * head + 2 * LANES] for head in range(HEADS)]
    left = jnp.where(lanes < DH, pltpu.roll(second[0], DH, 1), second[1])
    right = jnp.where(lanes < DH, pltpu.roll(second[2], DH, 1), 0.0)
    return left, right


def attend_kernel(
    groups, steps, q_ref, k_ref, v_ref, t_ref, c_ref, u_ref, o_ref, l_ref, all_ref, send, receive
):
    count = u_ref.shape[0]
    at_step = pl.program_id(0)

    @pl.when(at_step == 0)
    def begin():
        greet([group_device(bits) for bits in (2, 1)])
        plan = third_leg(Lines(send, receive), all_ref)
        for bits in (6, 1, 3, 5):
            plan[bits].start()

    @pl.when(at_step == steps - 1)
    def pass_on():
        plan = third_leg(Lines(send, receive), all_ref)
        plan[6].wait_recv()
        plan[7].start()

    queries = [q_ref[head] for head in range(HEADS)]

    def visit(state, at, masked):
        new = []
        for head in range(HEADS):
            top, accum = state[head]
            scores = dot(queries[head], k_ref[head, pl.ds(at * count, count)], (1, 1))
            if masked:
                row = lax.broadcasted_iota(jnp.int32, scores.shape, 0)
                col = lax.broadcasted_iota(jnp.int32, scores.shape, 1)
                scores = jnp.where(col <= row, scores, NEGATIVE)
            high = jnp.maximum(top, jnp.max(scores, axis=1, keepdims=True))
            weight = jnp.exp(scores - high)
            accum = accum * jnp.exp(top - high) + dot(weight.astype(HALF), v_ref[head, pl.ds(at * count, count)])
            new.append((high, accum))
        return tuple(new)

    state = tuple(
        (jnp.full((count, 1), NEGATIVE, FULL), jnp.zeros((count, LANES), FULL)) for head in range(HEADS)
    )
    earlier = (groups - place()[1]) * steps
    state = lax.fori_loop(earlier, groups * steps, lambda at, inner: visit(inner, at, False), state)
    state = lax.fori_loop(0, at_step, lambda at, inner: visit(inner, at, False), state)
    state = visit(state, at_step, True)
    lanes = lax.broadcasted_iota(jnp.int32, (count, LANES), 1)
    out, logs = [], []
    for top, accum in state:
        total = jnp.sum(jnp.where(lanes == DH, accum, 0.0), axis=1, keepdims=True)
        out.append(jnp.where(lanes < DH, accum / total, 0.0))
        logs.append(top + jnp.log(total))
    left, right = t_ref[:, :LANES], t_ref[:, LANES:]
    pair = out[0] + pltpu.roll(out[1], DH, 1)
    o_ref[:, :LANES] = pair
    o_ref[:, LANES:] = out[2]
    u_ref[:, :LANES] = (pair * sigmoid(left)).astype(HALF)
    u_ref[:, LANES:] = (out[2] * sigmoid(right)).astype(HALF)
    l_ref[...] = at_lanes(lanes, tuple(enumerate(logs)), 0.0)

    @pl.when(at_step == steps - 1)
    def end():
        plan = third_leg(Lines(send, receive), all_ref)
        for bits in (1, 3, 5, 7):
            plan[bits].wait_recv()
        for copy in plan.values():
            copy.wait_send()


def attend(queries, keys, values, gates, gathered, groups):
    tokens = keys.shape[1]
    own = tokens // groups
    count = min(BLOCK, own)
    steps = own // count
    whole = pl.BlockSpec((HEADS, tokens, LANES), lambda i: (0, 0, 0), pipeline_mode=pl.Buffered(1))
    anywhere = pl.BlockSpec(memory_space=pl.ANY)
    return pl.pallas_call(
        functools.partial(attend_kernel, groups, steps),
        grid=(steps,),
        in_specs=[
            pl.BlockSpec((HEADS, count, LANES), lambda i: (0, i, 0)),
            whole,
            whole,
            pl.BlockSpec((count, OUT), lambda i: (i, 0)),
            anywhere,
        ],
        out_specs=(
            pl.BlockSpec((count, OUT), lambda i: (i, 0)),
            pl.BlockSpec((count, OUT), lambda i: (i, 0)),
            pl.BlockSpec((count, LANES), lambda i: (i, 0)),
            anywhere,
        ),
        out_shape=(
            jax.ShapeDtypeStruct((own, OUT), HALF),
            jax.ShapeDtypeStruct((own, OUT), FULL),
            jax.ShapeDtypeStruct((own, LANES), FULL),
            jax.ShapeDtypeStruct(gathered.shape, HALF),
        ),
        scratch_shapes=[pltpu.SemaphoreType.DMA((5,)), pltpu.SemaphoreType.DMA((5,))],
        input_output_aliases={4: 3},
        compiler_params=params(9),
        name="attend",
        cost_estimate=cost(16),
    )(queries, keys, values, gates, gathered)


def group_device(bits):
    grp, group, member = place()
    return (grp, group * TP + flip(member, bits))


def blocks_of(ref, core):
    value = ref[:, pl.ds(core, 1)]
    return value.reshape(ref.shape[0] * ref.shape[2], ref.shape[3])


def sum_plan(lines, stage):
    give, take, out, came = stage
    sibling = [lines.plan(give.at[at], take.at[at], group_device(1)) for at in range(4)]
    others = [lines.plan(out.at[at], came.at[at], group_device(bits)) for at, bits in enumerate((2, 4, 6))]
    return sibling, others


def sum_give(pairs, stage, plan, mine):
    give = stage[0]
    grp, group, member = place()
    core = lax.rem(member, 2)
    count = give.shape[1]
    theirs = sum(dot(blocks_of(left, 1 - core), right[...], (1, 1)) for left, right in pairs)
    mine[...] = theirs.reshape(4, count, D)
    for at, bits in enumerate((2, 4, 6, 0)):
        give[at] = mine[lax.div(flip(member, bits), 2)].astype(HALF)
        plan[0][at].start()
    own = sum(dot(blocks_of(left, core), right[...], (1, 1)) for left, right in pairs)
    mine[...] = own.reshape(4, count, D)


def sum_pass(stage, plan, mine):
    give, take, out, came = stage
    member = place()[2]
    for at, bits in enumerate((2, 4, 6)):
        plan[0][at].wait_recv()
        out[at] = (mine[lax.div(flip(member, bits), 2)] + take[at].astype(FULL)).astype(HALF)
        plan[1][at].start()
    plan[0][3].wait_recv()
    return mine[lax.div(member, 2)] + take[3].astype(FULL)


def sum_send(pairs, stage, plan, mine):
    sum_give(pairs, stage, plan, mine)
    return sum_pass(stage, plan, mine)


def sum_take(total, stage, plan):
    give, take, out, came = stage
    for at in range(3):
        plan[1][at].wait_recv()
        total = total + came[at].astype(FULL)
    return total


def sum_scratch(rows):
    return [
        pltpu.VMEM((4, rows, D), HALF),
        pltpu.VMEM((4, rows, D), HALF),
        pltpu.VMEM((3, rows, D), HALF),
        pltpu.VMEM((3, rows, D), HALF),
    ]


def gather_plan(lines, block, all_ref, light=False):
    member = place()[2]

    def slot(bits):
        return halves(all_ref.at[flip(member, bits)])

    plan = {(bits, half): lines.plan(halves(block)[half], slot(0)[half], group_device(bits)) for bits in (4, 2) for half in range(2)}
    plan[1] = lines.plan(block, all_ref.at[member], group_device(1))
    plan[6, 0] = lines.plan(slot(4)[0], slot(4)[0], group_device(2))
    if light:
        plan[6, 1] = lines.plan(slot(4)[1], slot(4)[1], group_device(2))
    else:
        plan[6, 1] = lines.plan(slot(2)[1], slot(2)[1], group_device(4))
    for bits in (4, 2, 6):
        for half in range(2):
            plan[bits + 1, half] = lines.plan(slot(bits)[half], slot(bits)[half], group_device(1))
    return plan


GATHER = 13


def gather_start(plan, own):
    own.start()
    for key in ((4, 0), (2, 1), (4, 1), (2, 0), 1):
        plan[key].start()


def gather_turn(plan, light=False):
    for bits, half in ((4, 0), (4, 1) if light else (2, 1)):
        plan[bits, half].wait_recv()
        plan[6, half].start()
        plan[bits + 1, half].start()


def gather_pass(plan, light=False):
    for bits, half in ((2, 1) if light else (4, 1), (2, 0), (6, 0), (6, 1)):
        plan[bits, half].wait_recv()
        plan[bits + 1, half].start()


def gather_end(plan, own):
    plan[1].wait_recv()
    for bits in (5, 3, 7):
        for half in range(2):
            plan[bits, half].wait_recv()
    own.wait()


def gather_run(plan, own):
    gather_start(plan, own)
    gather_turn(plan)
    gather_pass(plan)
    gather_end(plan, own)


def mix_kernel(u_ref, w_ref, x_ref, g_ref, y_ref, all_ref, mine, block, give, take, out, came, send, receive, local):
    greet([group_device(bits) for bits in (1, 2, 4, 6)])
    member = place()[2]
    lines = Lines(send, receive)
    stage = (give, take, out, came)
    sums = sum_plan(lines, stage)
    gathered = gather_plan(lines, block, all_ref)
    total = sum_take(sum_send([(u_ref, w_ref)], stage, sums, mine), stage, sums)
    mixed = x_ref[...].astype(FULL) + total
    y_ref[...] = mixed
    block[...] = rms_rows(mixed, g_ref[...]).astype(HALF)
    gather_run(gathered, pltpu.make_async_copy(block, all_ref.at[member], local.at[0]))
    for copy in lines.made:
        copy.wait_send()


def whole_spec(shape):
    zeros = (0,) * len(shape)
    return pl.BlockSpec(shape, lambda i: zeros)


def weight_spec(columns, at):
    return pl.BlockSpec((D, columns), lambda i: (0, at))


def mix(gated, full, source, gain):
    rows = source.shape[0]
    count = 7 + GATHER
    return pl.pallas_call(
        mix_kernel,
        grid=(1,),
        out_shape=(
            jax.ShapeDtypeStruct((rows, D), FULL),
            jax.ShapeDtypeStruct((TP, rows, D), HALF),
        ),
        in_specs=[
            whole_spec((4, 2, rows, OUT)),
            weight_spec(OUT, QKVG // OUT),
            whole_spec((rows, D)),
            whole_spec((1, D)),
        ],
        out_specs=(whole_spec((rows, D)), pl.BlockSpec(memory_space=pl.ANY)),
        scratch_shapes=[pltpu.VMEM((4, rows, D), FULL), pltpu.VMEM((rows, D), HALF)]
        + sum_scratch(rows)
        + [
            pltpu.SemaphoreType.DMA((count,)),
            pltpu.SemaphoreType.DMA((count,)),
            pltpu.SemaphoreType.DMA((1,)),
        ],
        compiler_params=params(2),
        name="mix",
        cost_estimate=cost(40),
    )(gated.reshape(4, 2, rows, OUT), full, source, gain)


def slabs(grps, groups):
    grp, group, member = place()
    return [
        (turn, step, lax.rem(grp + turn, grps) * groups + lax.rem(group + step, groups))
        for turn in range(grps)
        for step in range(groups)
    ]


def load_rows(refs, whole, semaphores, grps, groups):
    rows = whole.shape[0] // (grps * groups)
    copies = []
    for at, (turn, step, index) in enumerate(slabs(grps, groups)):
        copies.append(pltpu.make_async_copy(refs[at], whole.at[pl.ds(index * rows, rows)], semaphores.at[at]))
    return copies


def unmix_kernel(grps, groups, d_ref, x_ref, g_ref, c_ref, m_ref, a_ref, r_ref, *rest):
    total_slabs = grps * groups
    both_refs, down_refs = rest[:total_slabs], rest[total_slabs : 2 * total_slabs]
    dx_ref, dg_ref, all_ref, out_ref, gate_ref, down_ref, *rest = rest[2 * total_slabs :]
    up_refs, rest = rest[:groups], rest[groups:]
    wgu, wdn, mine, block, give, take, out, came, give2, take2, *rest = rest
    grads, over_got, across_out, across_got, kept, send, receive, local = rest
    device, everyone = neighbours(grps, groups)
    everyone = [group_device(bits) for bits in (1, 2, 4, 6)] + everyone[TP - 1 :]
    call_out(everyone)
    grp, group, member = place()
    core = lax.rem(member, 2)
    load_both = load_rows(both_refs, wgu, local.at[pl.ds(0, total_slabs)], grps, groups)
    load_down = load_rows(down_refs, wdn, local.at[pl.ds(total_slabs, total_slabs)], grps, groups)
    for copy in load_both + load_down:
        copy.start()
    lines = Lines(send, receive)
    stage = (give, take, out, came)
    sums = sum_plan(lines, stage)
    gathered = gather_plan(lines, block, all_ref)
    output = lines.plan(give2, take2, group_device(1))
    rows = D // total_slabs
    places = slabs(grps, groups)
    down, gate, up = range(3)
    over = [
        {
            (turn, step): lines.plan(
                grads.at[kind, pl.ds(index * rows, rows)], over_got.at[kind, turn - 1, step], device(turn)
            )
            for turn, step, index in places
            if turn
        }
        for kind in range(3)
    ]
    across = [
        [
            lines.plan(across_out.at[kind, step - 1], across_got.at[kind, step - 1], device(to_group=step))
            for step in range(1, groups)
        ]
        for kind in (down, gate)
    ]
    cut = D // 4

    def grad_of(kind, left, right):
        for at in range(4):
            here = slice(at * cut, (at + 1) * cut)
            grads[kind, here] = dot(left[:, here], right, (0, 0)).astype(HALF)

    def over_sum(kind, step):
        value = grads[kind, pl.ds(places[step][2] * rows, rows)].astype(FULL)
        for turn in range(1, grps):
            over[kind][turn, step].wait_recv()
            value = value + over_got[kind, turn - 1, step].astype(FULL)
        return value

    def cross(kind):
        for step in range(1, groups):
            across_out[kind, step - 1] = over_sum(kind, step).astype(HALF)
            across[kind][step - 1].start()
        kept[kind] = over_sum(kind, 0)

    def crossed(kind):
        value = kept[kind]
        for step in range(1, groups):
            across[kind][step - 1].wait_recv()
            value = value + across_got[kind, step - 1].astype(FULL)
        return value.astype(HALF)

    for copy in load_both:
        copy.wait()
    hear(everyone)
    sum_give([(d_ref, wgu)], stage, sums, mine)
    tokens, count = r_ref.shape[0], x_ref.shape[0]
    hidden, both = m_ref[...].reshape(tokens, UNITS), d_ref[...].reshape(tokens, 2 * UNITS)
    grad_of(down, r_ref, hidden)
    for copy in over[down].values():
        copy.start()
    total = sum_pass(stage, sums, mine)
    grad_of(gate, a_ref, both[:, :UNITS])
    for copy in load_down:
        copy.wait()
    give2[...] = dot(blocks_of(m_ref, 1 - core), wdn[...], (1, 1)).astype(HALF).reshape(4, count, D)
    output.start()
    grad_of(up, a_ref, both[:, UNITS:])
    mine[...] = dot(blocks_of(m_ref, core), wdn[...], (1, 1)).reshape(4, count, D)
    cross(down)
    for copy in over[gate].values():
        copy.start()
    total = sum_take(total, stage, sums)
    pulled, dgain = rms_back(x_ref[...], g_ref[...], total)
    grad = c_ref[...].astype(FULL) + pulled
    block[...] = grad.astype(HALF)
    own = pltpu.make_async_copy(block, all_ref.at[member], local.at[2 * total_slabs])
    gather_start(gathered, own)
    dx_ref[...] = grad
    dg_ref[...] = dgain
    output.wait_recv()
    for at, bits in enumerate((2, 4, 6, 0)):
        chip = lax.div(flip(member, bits), 2)
        out_ref[at] = (mine[chip] + take2[chip].astype(FULL)).astype(HALF)
    gather_turn(gathered)
    gather_pass(gathered)
    cross(gate)
    for copy in over[up].values():
        copy.start()
    gather_end(gathered, own)
    down_ref[...] = crossed(down)
    for step in range(groups):
        up_refs[step][...] = over_sum(up, step).astype(HALF)
    gate_ref[...] = crossed(gate)
    for copy in lines.made:
        copy.wait_send()


def unmix(grads, both, down, mixed, gain, returned, hidden, second, returned_all, grps, groups):
    rows, tokens = mixed.shape[0], second.shape[0]
    slab = both[0].shape[0]
    total_slabs = grps * groups
    count = 8 + GATHER + 3 * (grps - 1) * groups + 2 * (groups - 1)
    piece = jax.ShapeDtypeStruct((slab, UNITS), HALF)
    return pl.pallas_call(
        functools.partial(unmix_kernel, grps, groups),
        grid=(1,),
        out_shape=(
            jax.ShapeDtypeStruct((rows, D), FULL),
            jax.ShapeDtypeStruct((1, D), FULL),
            jax.ShapeDtypeStruct((TP, rows, D), HALF),
            jax.ShapeDtypeStruct((4, rows, D), HALF),
        )
        + (piece,) * (2 + groups),
        in_specs=[
            whole_spec((4, 2, rows, 2 * UNITS)),
            whole_spec((rows, D)),
            whole_spec((1, D)),
            whole_spec((rows, D)),
            whole_spec((4, 2, rows, UNITS)),
            whole_spec((tokens, D)),
            whole_spec((tokens, D)),
        ]
        + [pl.BlockSpec(memory_space=pl.ANY)] * (2 * total_slabs),
        out_specs=(
            whole_spec((rows, D)),
            whole_spec((1, D)),
            pl.BlockSpec(memory_space=pl.ANY),
            whole_spec((4, rows, D)),
        )
        + (whole_spec((slab, UNITS)),) * (2 + groups),
        scratch_shapes=[
            pltpu.VMEM((D, 2 * UNITS), HALF),
            pltpu.VMEM((D, UNITS), HALF),
            pltpu.VMEM((4, rows, D), FULL),
            pltpu.VMEM((rows, D), HALF),
        ]
        + sum_scratch(rows)
        + [
            pltpu.VMEM((4, rows, D), HALF),
            pltpu.VMEM((4, rows, D), HALF),
            pltpu.VMEM((3, D, UNITS), HALF),
            pltpu.VMEM((3, grps - 1, groups, slab, UNITS), HALF),
            pltpu.VMEM((2, groups - 1, slab, UNITS), HALF),
            pltpu.VMEM((2, groups - 1, slab, UNITS), HALF),
            pltpu.VMEM((2, slab, UNITS), FULL),
            pltpu.SemaphoreType.DMA((count,)),
            pltpu.SemaphoreType.DMA((count,)),
            pltpu.SemaphoreType.DMA((2 * total_slabs + 1,)),
        ],
        compiler_params=params(3),
        name="unmix",
        cost_estimate=cost(55),
    )(
        grads.reshape(4, 2, rows, 2 * UNITS),
        mixed,
        gain,
        returned,
        hidden.reshape(4, 2, rows, UNITS),
        second,
        returned_all,
        *both,
        *down,
    )


def feed_kernel(grps, groups, a_ref, c_ref, *rest):
    total_slabs = grps * groups
    both_refs, down_refs = rest[:total_slabs], rest[total_slabs : 2 * total_slabs]
    m_ref, d_ref, wgu, wdn, local = rest[2 * total_slabs :]

    @pl.when(pl.program_id(0) == 0)
    def load():
        copies = load_rows(both_refs, wgu, local.at[pl.ds(0, total_slabs)], grps, groups)
        copies = copies + load_rows(down_refs, wdn, local.at[pl.ds(total_slabs, total_slabs)], grps, groups)
        for copy in copies:
            copy.start()
        for copy in copies:
            copy.wait()

    made = dot(a_ref[...], wgu[...])
    gate, up = made[:, :UNITS], made[:, UNITS:]
    sig = sigmoid(gate)
    swish = gate * sig
    m_ref[...] = (swish * up).astype(HALF)
    grad = dot(c_ref[...], wdn[...])
    d_ref[:, :UNITS] = (grad * up * sig * (1.0 + gate * (1.0 - sig))).astype(HALF)
    d_ref[:, UNITS:] = (grad * swish).astype(HALF)


def feed(second, returned, both, down, grps, groups):
    tokens = second.shape[0]
    count = TALL
    return pl.pallas_call(
        functools.partial(feed_kernel, grps, groups),
        grid=(tokens // count,),
        out_shape=(
            jax.ShapeDtypeStruct((tokens, UNITS), HALF),
            jax.ShapeDtypeStruct((tokens, 2 * UNITS), HALF),
        ),
        in_specs=[
            pl.BlockSpec((count, D), lambda i: (i, 0)),
            pl.BlockSpec((count, D), lambda i: (i, 0)),
        ]
        + [pl.BlockSpec(memory_space=pl.ANY)] * (2 * grps * groups),
        out_specs=(
            pl.BlockSpec((count, UNITS), lambda i: (i, 0)),
            pl.BlockSpec((count, 2 * UNITS), lambda i: (i, 0)),
        ),
        scratch_shapes=[
            pltpu.VMEM((D, 2 * UNITS), HALF),
            pltpu.VMEM((D, UNITS), HALF),
            pltpu.SemaphoreType.DMA((2 * grps * groups,)),
        ],
        compiler_params=params(),
        name="feed",
        cost_estimate=cost(10),
    )(second, returned, *both, *down)


def ungate_kernel(
    grps, groups, steps, d_ref, w_ref, o_ref, t_ref, l_ref, q_ref, u_ref,
    do_ref, qb_ref, dg_ref, pack_ref, keep_ref, give_ref, whole,
):
    cut = D // 4
    for at in range(4):
        here = slice(at * cut, (at + 1) * cut)
        part = dot(d_ref[:, here], u_ref[...], (0, 0))
        whole[here] = jnp.where(pl.program_id(0) == 0, part, whole[here] + part)

    @pl.when(pl.program_id(0) == steps - 1)
    def sort():
        rows = D // (grps * groups)
        for turn, step, index in slabs(grps, groups):
            target = give_ref.at[turn - 1, step] if turn else keep_ref.at[step]
            target[...] = whole[pl.ds(index * rows, rows)].astype(HALF)

    grad = dot(d_ref[...], w_ref[...])
    count = grad.shape[0]
    lanes = lax.broadcasted_iota(jnp.int32, (count, LANES), 1)
    gates = (t_ref[:, :LANES], t_ref[:, LANES:])
    sums, sent = [], []
    for at in range(2):
        part = grad[:, LANES * at : LANES * (at + 1)]
        attended = o_ref[:, LANES * at : LANES * (at + 1)]
        sig = sigmoid(gates[at])
        low = (part * sig).astype(HALF).astype(FULL)
        sent.append(low)
        dg_ref[:, LANES * at : LANES * (at + 1)] = part * attended * sig * (1.0 - sig)
        sums.append(two(low * attended))
    row = lax.broadcasted_iota(jnp.int32, (LANES, LANES), 0)
    col = lax.broadcasted_iota(jnp.int32, (LANES, LANES), 1)
    of_left = jnp.where(((row < DH) & (col == 0)) | ((row >= DH) & (col == 1)), -1.0, 0.0).astype(HALF)
    of_right = jnp.where((row < DH) & (col == 2), -1.0, 0.0).astype(HALF)
    minus = dot(sums[0][0], of_left) + dot(sums[0][1], of_left) + dot(sums[1][0], of_right) + dot(sums[1][1], of_right)
    logs = jnp.where(lanes < HEADS, -l_ref[...], 0.0)
    packed = side_by_side(three(minus) + three(logs), lanes)
    grads = dot(packed, picker((HEADS * LANES, spread_lanes(0, DH))))
    sinks = dot(packed, picker((HEADS * LANES, spread_lanes(3, DH + 6))))

    def sent_lanes(col):
        head, part = lax.div(col - DH, 6), lax.rem(col - DH, 6)
        return jnp.where((col >= DH) & (col < DH + 6 * HEADS), HEADS * part + head, -1)

    extra = dot(packed, picker((LANES, sent_lanes)))
    heads = [sent[0], pltpu.roll(sent[0], DH, 1), sent[1]]
    for head in range(HEADS):
        here = slice(LANES * head, LANES * (head + 1))
        do_ref[head] = jnp.where(lanes < DH, heads[head], grads[:, here]).astype(HALF)
        qb_ref[head] = (q_ref[head].astype(FULL) + sinks[:, here]).astype(HALF)
    pack_ref[:, :LANES] = sent[0].astype(HALF)
    pack_ref[:, LANES:] = jnp.where(lanes < DH, sent[1], extra).astype(HALF)


def ungate(grads, full, attended, gates, logs, queries, gated, grps, groups):
    own = grads.shape[0]
    steps = own // TALL
    slab = D // (grps * groups)
    head_tile = pl.BlockSpec((HEADS, TALL, LANES), lambda i: (0, i, 0))
    wide_tile = pl.BlockSpec((TALL, OUT), lambda i: (i, 0))
    return pl.pallas_call(
        functools.partial(ungate_kernel, grps, groups, steps),
        grid=(steps,),
        in_specs=[
            pl.BlockSpec((TALL, D), lambda i: (i, 0)),
            weight_spec(OUT, QKVG // OUT),
            wide_tile,
            wide_tile,
            pl.BlockSpec((TALL, LANES), lambda i: (i, 0)),
            head_tile,
            wide_tile,
        ],
        out_specs=(
            head_tile,
            head_tile,
            wide_tile,
            wide_tile,
            whole_spec((groups, slab, OUT)),
            whole_spec((grps - 1, groups, slab, OUT)),
        ),
        out_shape=(
            jax.ShapeDtypeStruct((HEADS, own, LANES), HALF),
            jax.ShapeDtypeStruct((HEADS, own, LANES), HALF),
            jax.ShapeDtypeStruct((own, OUT), FULL),
            jax.ShapeDtypeStruct((own, OUT), HALF),
            jax.ShapeDtypeStruct((groups, slab, OUT), HALF),
            jax.ShapeDtypeStruct((grps - 1, groups, slab, OUT), HALF),
        ),
        scratch_shapes=[pltpu.VMEM((D, OUT), FULL)],
        compiler_params=params(),
        name="ungate",
        cost_estimate=cost(9),
    )(grads, full, attended, gates, logs, queries, gated)


def pieces(scores, product, masked, transposed):
    prob = jnp.exp(scores)
    if masked:
        row = lax.broadcasted_iota(jnp.int32, scores.shape, 0)
        col = lax.broadcasted_iota(jnp.int32, scores.shape, 1)
        keep = row <= col if transposed else col <= row
        prob = jnp.where(keep, prob, 0.0)
    return prob.astype(HALF), (prob * product).astype(HALF)


def home_plan(lines, pairs):
    member = place()[2]
    return [
        lines.plan(source.at[flip(member, bits)], target.at[member], group_device(bits))
        for source, target in pairs
        for bits in range(1, TP)
    ]


def back_kernel(
    grps, groups, q_ref, do_ref, k_ref, v_ref, a_ref, pack_ref, out_ref, out_give, gate_ref, down_ref,
    dq_ref, dk_ref, dv_ref, late_ref, done_ref, hgate_ref, hdown_ref,
    others, out_got, across_out, across_got, send, receive, local,
):
    device, everyone = neighbours(grps, groups)
    call_out(everyone)
    group, member = place()[1:]
    own = q_ref.shape[1]
    count = min(BLOCK, own)
    steps = own // count
    lines = Lines(send, receive)
    halves_of = [pl.ds(at * count, count) for at in range(steps)]
    packs = [
        [lines.plan(pack_ref.at[half], others.at[step - 1, half], device(to_group=groups - step)) for step in range(1, groups)]
        for half in halves_of
    ]
    over = [lines.plan(out_give.at[turn - 1], out_got.at[turn - 1], device(to_grp=turn)) for turn in range(1, grps)]
    across = [
        lines.plan(across_out.at[step - 1], across_got.at[step - 1], device(to_group=step)) for step in range(1, groups)
    ]
    pairs = ((gate_ref, hgate_ref), (down_ref, hdown_ref))
    home = home_plan(lines, pairs)
    kept = [
        pltpu.make_async_copy(source.at[member], target.at[member], local.at[at])
        for at, (source, target) in enumerate(pairs)
    ]
    hear(everyone)
    for copy in packs[0] + over + home + kept:
        copy.start()
    dk_ref[...] = jnp.zeros_like(dk_ref)
    dv_ref[...] = jnp.zeros_like(dv_ref)
    earliest = (groups - group) * steps
    for head in range(HEADS):
        for at in range(steps):
            here = halves_of[at]
            query, grad = q_ref[head, here], do_ref[head, here]

            def earlier(step, inner):
                there = pl.ds(step * count, count)
                key = k_ref[head, there]
                prob, dscore = pieces(
                    dot(query, key, (1, 1)), dot(grad, v_ref[head, there], (1, 1)), False, False
                )
                return inner + dot(dscore, key)

            dquery = lax.fori_loop(earliest, groups * steps, earlier, jnp.zeros((count, LANES), FULL))
            for step in range(at + 1):
                there = halves_of[step]
                key = k_ref[head, there]
                prob, dscore = pieces(
                    dot(key, query, (1, 1)), dot(v_ref[head, there], grad, (1, 1)), step == at, True
                )
                dk_ref[head, there] += dot(dscore, query)
                dv_ref[head, there] += dot(prob, grad)
                dquery = dquery + dot(dscore, key, (0, 0))
            dq_ref[head, here] = dquery
        if head == 0:
            for copies in packs[1:]:
                for copy in copies:
                    copy.start()
        if head == 1:
            for copy in over:
                copy.wait_recv()
            for step in range(1, groups):
                value = out_ref[step].astype(FULL)
                for turn in range(1, grps):
                    value = value + out_got[turn - 1, step].astype(FULL)
                across_out[step - 1] = value.astype(HALF)
                across[step - 1].start()

    lanes = lax.broadcasted_iota(jnp.int32, (count, LANES), 1)
    late_ref[...] = jnp.zeros_like(late_ref)

    def visit(head, carry, step, at):
        def lanes_from(first, start):
            def find(col):
                part = col - start
                return jnp.where((part >= 0) & (part < 3), DH + 6 * head + first + part, -1)

            return picker((LANES, find))

        minus, logs = lanes_from(0, DH), lanes_from(3, DH + 6)
        sent = others[step - 1, halves_of[at]].astype(FULL)
        left, right = sent[:, :LANES], sent[:, LANES:]
        grad = jnp.where(head == 0, left, jnp.where(head == 1, pltpu.roll(left, DH, 1), right))
        packed = others[step - 1, halves_of[at], LANES:]
        grad = jnp.where(lanes < DH, grad, dot(packed, minus)).astype(HALF)
        query = a_ref[head, pl.ds(step * own + at * count, count)].astype(FULL)
        query = (query + dot(packed, logs)).astype(HALF)
        for there in halves_of:
            prob, dscore = pieces(
                dot(k_ref[head, there], query, (1, 1)), dot(v_ref[head, there], grad, (1, 1)), False, True
            )
            part = dot(dscore, query)
            dk_ref[head, there] += part
            dv_ref[head, there] += dot(prob, grad)
            late_ref[head] += jnp.broadcast_to(jnp.sum(part, axis=0, keepdims=True), (8, LANES))
        return carry

    for at in range(steps):
        for step in range(1, groups):
            packs[at][step - 1].wait_recv()

            @pl.when(step < groups - group)
            def later():
                lax.fori_loop(0, HEADS, functools.partial(visit, step=step, at=at), 0)

    value = out_ref[0].astype(FULL)
    for turn in range(1, grps):
        value = value + out_got[turn - 1, 0].astype(FULL)
    for step in range(1, groups):
        across[step - 1].wait_recv()
        value = value + across_got[step - 1].astype(FULL)
    done_ref[...] = value.astype(HALF)
    for copy in home:
        copy.wait_recv()
    for copy in kept:
        copy.wait()
    for copy in lines.made:
        copy.wait_send()


def attend_back(queries, grads, keys, values, span_queries, pack, out, out_give, gate, down):
    own, tokens = queries.shape[1], keys.shape[1]
    grps, groups, slab = out_give.shape[0] + 1, out.shape[0], out.shape[1]
    steps = own // min(BLOCK, own)
    count = steps * (groups - 1) + grps - 1 + groups - 1 + 2 * (TP - 1)
    vmem, anywhere = pl.BlockSpec(memory_space=pltpu.VMEM), pl.BlockSpec(memory_space=pl.ANY)
    return pl.pallas_call(
        functools.partial(back_kernel, grps, groups),
        in_specs=[vmem] * 5 + [anywhere, vmem] + [anywhere] * 3,
        out_specs=(vmem,) * 5 + (anywhere,) * 2,
        out_shape=(jax.ShapeDtypeStruct((HEADS, own, LANES), FULL),) * 3
        + (
            jax.ShapeDtypeStruct((HEADS, 8, LANES), FULL),
            jax.ShapeDtypeStruct((slab, OUT), HALF),
            jax.ShapeDtypeStruct(gate.shape, HALF),
            jax.ShapeDtypeStruct(down.shape, HALF),
        ),
        scratch_shapes=[
            pltpu.VMEM((groups - 1, own, OUT), HALF),
            pltpu.VMEM(out_give.shape, HALF),
            pltpu.VMEM((groups - 1, slab, OUT), HALF),
            pltpu.VMEM((groups - 1, slab, OUT), HALF),
            pltpu.SemaphoreType.DMA((count,)),
            pltpu.SemaphoreType.DMA((count,)),
            pltpu.SemaphoreType.DMA((2,)),
        ],
        compiler_params=params(5),
        name="attend_back",
        cost_estimate=cost(35),
    )(queries, grads, keys, values, span_queries, pack, out, out_give, gate, down)


def unproject_kernel(
    dq_ref, dk_ref, dv_ref, dg_ref, p_ref, z_ref, g_ref, late_ref, dp_ref, dz_ref, gain_ref, bias_ref, carry
):
    @pl.when(pl.program_id(0) == 0)
    def clear():
        carry[0:1] = late_ref[...]
        gain_ref[...] = jnp.zeros_like(gain_ref)
        bias_ref[...] = jnp.zeros_like(bias_ref)

    count = p_ref.shape[0]
    lanes = lax.broadcasted_iota(jnp.int32, (count, LANES), 1)
    sums = jnp.zeros((count, LANES), FULL)
    means = halves_matrix(1.0 / DH)
    gates = [
        pltpu.roll(dg_ref[:, :LANES], DH, 1),
        dg_ref[:, :LANES],
        pltpu.roll(dg_ref[:, LANES:], DH, 1),
    ]
    for head in range(HEADS):
        dquery, dkey = dq_ref[head], dk_ref[head]
        found = pltpu.roll(dquery, DH + head, 1) - pltpu.roll(dkey, DH - 3 + head, 1)
        sums = jnp.where(lanes == head, found, sums)
        grad = jnp.where(lanes < DH, dquery * (DH**-0.5), pltpu.roll(dkey, DH, 1))
        pair = p_ref[:, LANES * head : LANES * (head + 1)]
        inverse = lax.rsqrt(halves_mean(pair * pair, means) + EPS)
        normal = pair * inverse
        scaled = grad * g_ref[head : head + 1]
        gain_ref[head : head + 1] += jnp.sum(grad * normal, axis=0, keepdims=True)
        pulled = inverse * (scaled - normal * halves_mean(scaled * normal, means))
        dp_ref[:, 256 * head : 256 * head + LANES] = pulled.astype(HALF)
        dp_ref[:, 256 * head + LANES : 256 * head + 2 * LANES] = jnp.where(
            lanes < DH, dv_ref[head], gates[head]
        ).astype(HALF)
    row = lax.broadcasted_iota(jnp.int32, (count, count), 0)
    col = lax.broadcasted_iota(jnp.int32, (count, count), 1)
    later = (
        lax.dot_general(
            jnp.where(col >= row, 1.0, 0.0),
            sums,
            (((1,), (0,)), ((), ())),
            precision=lax.Precision.HIGHEST,
            preferred_element_type=FULL,
        )
        + carry[0:1]
    )
    carry[0:1] = later[0:1]
    low = jnp.where(lanes < HEADS, later * sigmoid(-z_ref[...]), 0.0).astype(HALF)
    dz_ref[...] = low
    bias_ref[0:1] += jnp.sum(low.astype(FULL), axis=0, keepdims=True)


def unproject(dqueries, dkeys, dvalues, dgates, pairs, logits, gains, late):
    own = dqueries.shape[1]
    steps = own // TALL

    def back(width):
        return pl.BlockSpec((TALL, width), lambda i: (steps - 1 - i, 0))

    head_tile = pl.BlockSpec((HEADS, TALL, LANES), lambda i: (0, steps - 1 - i, 0))
    small = whole_spec((8, LANES))
    return pl.pallas_call(
        unproject_kernel,
        grid=(steps,),
        in_specs=[
            head_tile,
            head_tile,
            head_tile,
            back(OUT),
            back(HEADS * LANES),
            back(LANES),
            small,
            whole_spec((1, LANES)),
        ],
        out_specs=(back(QKVG), back(LANES), small, small),
        scratch_shapes=[pltpu.VMEM((8, LANES), FULL)],
        out_shape=(
            jax.ShapeDtypeStruct((own, QKVG), HALF),
            jax.ShapeDtypeStruct((own, LANES), HALF),
            jax.ShapeDtypeStruct((8, LANES), FULL),
            jax.ShapeDtypeStruct((8, LANES), FULL),
        ),
        compiler_params=params(),
        name="unproject",
        cost_estimate=cost(9),
    )(dqueries, dkeys, dvalues, dgates, pairs, logits, gains, late)


def across_groups(part, groups):
    size = groups * TP
    return [part] + [
        lax.ppermute(part, "fsdp", [((at + step * TP) % size, at) for at in range(size)])
        for step in range(1, groups)
    ]


def over_grps(parts, grps):
    return [
        [part] + [lax.ppermute(part, "grp", [((at + turn) % grps, at) for at in range(grps)]) for turn in range(1, grps)]
        for part in parts
    ]


def in_order(parts):
    return [turns[turn] for turn in range(len(parts[0])) for turns in parts]


def collected(kept):
    return sum(part.astype(FULL) for part in kept).astype(HALF)


def unpack(grad_ref, near, gate, up, down, out):
    lanes = lax.broadcasted_iota(jnp.int32, (near.shape[1], LANES), 1)

    def half(ref, part, upper):
        member, at, side = part
        value = ref[member, :, at : at + LANES].astype(FULL)
        return pltpu.roll(value, DH, 1) if side != upper else value

    def store(at, ref, lower, upper):
        value = jnp.where(lanes < DH, half(ref, lower, False), half(ref, upper, True))
        grad_ref[:, at : at + LANES] = value.astype(HALF)

    for at in range(0, H, 2):
        for kind in range(4):
            pair = [
                (head // HEADS, 256 * (head % HEADS) + LANES * (kind // 2), kind % 2 == 1) for head in (at, at + 1)
            ]
            store(kind * D + at * DH, near, *pair)
        pair = [
            (head // HEADS, LANES * (head % HEADS // 2), head % HEADS % 2 == 1) for head in (at, at + 1)
        ]
        store(4 * D + at * DH, out, *pair)
    for member in range(TP):
        at = 5 * D + member * UNITS
        grad_ref[:, at : at + UNITS] = gate[member]
        grad_ref[:, at + F : at + F + UNITS] = up[member]
        grad_ref[:, at + 2 * F : at + 2 * F + UNITS] = down[member]


PARTS = 2


def light_plan(lines, stage):
    give, take, out, came = stage
    sibling = [lines.plan(give.at[at], take.at[at], group_device(1)) for at in range(4)]
    others = [lines.plan(out.at[at], came.at[at], group_device(bits)) for at, bits in enumerate((2, 2, 4))]
    return sibling, others


def light_across(stage, plan, mine):
    give, take, out, came = stage
    plan[0][2].wait_recv()
    out[1] = (mine[lax.div(flip(place()[2], 6), 2)] + take[2].astype(FULL)).astype(HALF)
    plan[1][1].start()


def light_beside(stage, plan, mine):
    give, take, out, came = stage
    plan[0][0].wait_recv()
    out[0] = (mine[lax.div(flip(place()[2], 2), 2)] + take[0].astype(FULL)).astype(HALF)
    plan[1][0].start()
    plan[0][3].wait_recv()
    return mine[lax.div(place()[2], 2)] + take[3].astype(FULL)


def light_turn(stage, plan, mine):
    give, take, out, came = stage
    plan[0][1].wait_recv()
    plan[1][1].wait_recv()
    value = mine[lax.div(flip(place()[2], 4), 2)] + take[1].astype(FULL)
    out[2] = (value + came[1].astype(FULL)).astype(HALF)
    plan[1][2].start()


def light_take(total, stage, plan):
    came = stage[3]
    for at in (0, 2):
        plan[1][at].wait_recv()
        total = total + came[at].astype(FULL)
    return total


def end_counts(grps, groups):
    replicas = grps * groups - 1
    return 7 + PARTS * ((grps - 1) * groups + groups - 1) + 3 * (TP - 1) + 2 * (replicas + TP - 1)


def sort_small(every, gains_ref, forget_ref, bias_ref):
    lanes = lax.broadcasted_iota(jnp.int32, (1, LANES), 1)
    rest = HEADS + 2
    gains_ref[0:2] = jnp.sum(every[:, HEADS : HEADS + 2], axis=0)

    def part(head, kind, upper):
        row = every[head // HEADS, rest : rest + 1]
        return half_lanes(row, (kind * HEADS + head % HEADS) * DH, upper)

    for kind in range(2):
        for head in range(0, H, 2):
            gains_ref[2 + kind : 3 + kind, head * DH : (head + 2) * DH] = jnp.where(
                lanes < DH, part(head, kind, False), part(head + 1, kind, True)
            )
    bias = jnp.zeros((1, LANES), FULL)
    edge = 2 * HEADS * DH
    for member in range(TP):
        forget_ref[member * HEADS : (member + 1) * HEADS] = every[member, :HEADS]
        moved = every[member, rest : rest + 1, edge : edge + LANES]
        if member:
            moved = pltpu.roll(moved, member * HEADS, 1)
        bias = jnp.where((lanes >= member * HEADS) & (lanes < (member + 1) * HEADS), moved, bias)
    bias_ref[...] = jnp.broadcast_to(bias, bias_ref.shape)


def end_kernel(
    grps, groups,
    p_ref, z_ref, f_ref, x_ref, g_ref, d_ref, s_ref, up_ref, out_ref, hgate_ref, hdown_ref, w_ref, t_ref,
    y_ref, grad_ref, gains_ref, forget_ref, bias_ref, norm_ref, small_ref, hnear_ref, hup_ref, hout_ref,
    weights, tokens, near, mine, give, take, out, came, over_got, across_out, across_got, last,
    packet, packets, scalar, scalars, members, send, receive, local,
):
    grp, group, member = place()
    device, everyone = neighbours(grps, groups)
    replicas = [(turn, step) for turn in range(grps) for step in range(groups) if turn or step]
    everyone = everyone + [device(turn, step) for turn, step in replicas if turn and step]
    call_out(everyone)
    count = tokens.shape[0]
    load_tokens = pltpu.make_async_copy(t_ref, tokens, local.at[0])
    load_weights = pltpu.make_async_copy(w_ref.at[:, pl.ds(0, QKVG)], weights, local.at[1])
    load_tokens.start()
    load_weights.start()
    lines = Lines(send, receive)
    stage = (give, take, out, came)
    sums = light_plan(lines, stage)
    slab = near.shape[0] // (grps * groups)
    part_rows = slab // PARTS
    own = last.shape[2]
    over, across, home, far = {}, {}, {}, []

    def rows_of(turn, step, part):
        side = lax.div(member, 4)
        side = side + part - 2 * part * side
        index = lax.rem(grp + turn, grps) * groups + lax.rem(group + step, groups)
        return pl.ds(index * slab + side * part_rows, part_rows)

    order = [(ahead, part) for ahead in list(range(1, groups)) + [0] for part in (1, 0)]
    for ahead, part in order:
        for turn in range(1, grps):
            over[turn, ahead, part] = lines.plan(
                near.at[rows_of(turn, ahead, part)], over_got.at[turn - 1, ahead, part], device(turn)
            )
        if ahead:
            across[ahead, part] = lines.plan(
                across_out.at[ahead - 1, part], across_got.at[ahead - 1, part], device(to_group=ahead)
            )
    for bits in range(1, TP):
        source = last.at[bits // 4, lax.rem(flip(member, bits), 4)]
        home[bits] = lines.plan(source, hnear_ref.at[member], device(bits=bits))
    pairs = ((up_ref, hup_ref), (out_ref, hout_ref))
    for source, target in pairs:
        for bits in range(1, TP):
            far.append(lines.plan(source.at[flip(member, bits)], target.at[member], device(bits=bits)))
    shared = [lines.plan(packet, packets.at[at], device(turn, step)) for at, (turn, step) in enumerate(replicas)]
    told = [lines.plan(small_ref.at[member], small_ref.at[member], device(bits=bits)) for bits in range(1, TP)]
    added = [lines.plan(scalar.at[0], scalars.at[at], device(turn, step)) for at, (turn, step) in enumerate(replicas)]
    closed = [lines.plan(scalar.at[1], members.at[bits - 1], device(bits=bits)) for bits in range(1, TP)]

    projected = p_ref[...].reshape(count, QKVG)
    cut = D // 4
    load_tokens.wait()
    for at in range(4):
        here = slice(at * cut, (at + 1) * cut)
        near[here] = dot(tokens[:, here], projected, (0, 0)).astype(HALF)
    hear(everyone)
    for turn in range(1, grps):
        for ahead in range(1, groups):
            over[turn, ahead, 1].start()
    load_weights.wait()
    sum_give([(p_ref, weights), (z_ref, f_ref)], stage, sums, mine)
    light_across(stage, sums, mine)
    for part in (1, 0):
        for ahead in range(1, groups):
            if part == 1:
                for turn in range(1, grps):
                    over[turn, ahead, 1].wait_recv()
                    over[turn, ahead, 0].start()
            elif ahead == 1:
                for turn in range(1, grps):
                    for last_part in (1, 0):
                        over[turn, 0, last_part].start()
            total = near[rows_of(0, ahead, part)].astype(FULL)
            for turn in range(1, grps):
                if part == 0:
                    over[turn, ahead, part].wait_recv()
                total = total + over_got[turn - 1, ahead, part].astype(FULL)
            across_out[ahead - 1, part] = total.astype(HALF)
            across[ahead, part].start()
    summed = light_beside(stage, sums, mine)
    for copy in far:
        copy.start()
    for source, target in pairs:
        target[member] = source[member]
    packet[...] = s_ref[...]
    forget = dot(z_ref[...].reshape(count, LANES), tokens[...], (0, 0))
    packet[0:HEADS] = forget[0:HEADS]
    light_turn(stage, sums, mine)
    summed = light_take(summed, stage, sums)
    pulled, dgain = rms_back(x_ref[...].astype(FULL), g_ref[...], summed)
    y_ref[...] = (d_ref[...] + pulled).astype(HALF)
    packet[HEADS : HEADS + 1] = dgain
    for copy in shared:
        copy.start()
    for part in (1, 0):
        total = near[rows_of(0, 0, part)].astype(FULL)
        for turn in range(1, grps):
            over[turn, 0, part].wait_recv()
            total = total + over_got[turn - 1, 0, part].astype(FULL)
        for ahead in range(1, groups):
            across[ahead, part].wait_recv()
            total = total + across_got[ahead - 1, part].astype(FULL)
        for at in range(4):
            last[part, at] = total[at * own : (at + 1) * own].astype(HALF)
        for bits in range(max(4 * part, 1), 4 * part + 4):
            home[bits].start()
    hnear_ref[member] = last[0, lax.rem(member, 4)]
    total = packet[...]
    for at, copy in enumerate(shared):
        copy.wait_recv()
        total = total + packets[at]
    small_ref[member] = total
    for copy in told:
        copy.start()
    for copy in far:
        copy.wait_recv()

    def square(ref):
        value = ref[...].astype(FULL)
        return jnp.sum(value * value)

    squares = square(hgate_ref) + square(hup_ref) + square(hdown_ref) + square(hout_ref)
    for copy in home.values():
        copy.wait_recv()
    squares = squares + square(hnear_ref)
    scalar[0] = jnp.full((8, LANES), squares, FULL)
    for copy in added:
        copy.start()
    unpack(grad_ref, hnear_ref, hgate_ref, hup_ref, hdown_ref, hout_ref)
    for copy in told:
        copy.wait_recv()
    every = small_ref[...]
    sort_small(every, gains_ref, forget_ref, bias_ref)
    heads = jnp.sum(every[:, :HEADS] * every[:, :HEADS])
    heads = heads + jnp.sum(every[:, HEADS + 2] * every[:, HEADS + 2])
    shared_gains = jnp.sum(every[:, HEADS : HEADS + 2], axis=0)
    heads = heads + jnp.sum(shared_gains * shared_gains)
    total = scalar[0]
    for at, copy in enumerate(added):
        copy.wait_recv()
        total = total + scalars[at]
    scalar[1] = total
    for copy in closed:
        copy.start()
    total = total + heads
    for at, copy in enumerate(closed):
        copy.wait_recv()
        total = total + members[at]
    norm_ref[...] = jnp.sqrt(total)
    for copy in lines.made:
        copy.wait_send()


def end(projected, logits, forget, source, gain, grad, small, up, out, gate, down, near, tokens, grps, groups):
    rows, own = source.shape[0], gate.shape[1]
    count = end_counts(grps, groups)
    replicas = grps * groups - 1
    slab = TP * own
    part = (slab // PARTS, QKVG)
    vmem, anywhere = pl.BlockSpec(memory_space=pltpu.VMEM), pl.BlockSpec(memory_space=pl.ANY)
    return pl.pallas_call(
        functools.partial(end_kernel, grps, groups),
        out_shape=(
            jax.ShapeDtypeStruct((rows, D), HALF),
            jax.ShapeDtypeStruct((own, 5 * D + 3 * F), HALF),
            jax.ShapeDtypeStruct((4, D), FULL),
            jax.ShapeDtypeStruct((H, D), FULL),
            jax.ShapeDtypeStruct((8, LANES), FULL),
            jax.ShapeDtypeStruct((8, LANES), FULL),
        ),
        in_specs=[vmem] * 11 + [anywhere] * 2,
        out_specs=(vmem,) * 6,
        scratch_shapes=[
            pltpu.VMEM((TP, 8, D), FULL),
            pltpu.VMEM((TP, own, QKVG), HALF),
            pltpu.VMEM((TP, own, UNITS), HALF),
            pltpu.VMEM((TP, own, OUT), HALF),
            pltpu.VMEM((D, QKVG), HALF),
            pltpu.VMEM((TP * rows, D), HALF),
            pltpu.VMEM((D, QKVG), HALF),
            pltpu.VMEM((4, rows, D), FULL),
        ]
        + sum_scratch(rows)
        + [
            pltpu.VMEM((grps - 1, groups, PARTS) + part, HALF),
            pltpu.VMEM((groups - 1, PARTS) + part, HALF),
            pltpu.VMEM((groups - 1, PARTS) + part, HALF),
            pltpu.VMEM((PARTS, 4, own, QKVG), HALF),
            pltpu.VMEM((8, D), FULL),
            pltpu.VMEM((replicas, 8, D), FULL),
            pltpu.VMEM((2, 8, LANES), FULL),
            pltpu.VMEM((replicas, 8, LANES), FULL),
            pltpu.VMEM((TP - 1, 8, LANES), FULL),
            pltpu.SemaphoreType.DMA((count,)),
            pltpu.SemaphoreType.DMA((count,)),
            pltpu.SemaphoreType.DMA((2,)),
        ],
        compiler_params=params(4),
        name="end",
        cost_estimate=cost(60),
    )(
        projected.reshape(4, 2, rows, QKVG),
        logits.reshape(4, 2, rows, LANES),
        forget,
        source,
        gain,
        grad,
        small,
        up,
        out,
        gate,
        down,
        near,
        tokens,
    )


def adam(value, first, second, grad, rate, decay):
    first = BETA_ONE * first + (1.0 - BETA_ONE) * grad
    second = BETA_TWO * second + (1.0 - BETA_TWO) * grad * grad
    unbiased_first = first / (1.0 - BETA_ONE**STEP)
    unbiased_second = second / (1.0 - BETA_TWO**STEP)
    value = value - rate * (unbiased_first / (jnp.sqrt(unbiased_second) + ADAM_EPS) + decay * value)
    return (value, first, second)


def update_kernel(norm_ref, w_ref, m_ref, v_ref, g_ref, nw_ref, nm_ref, nv_ref):
    factor = CLIP / jnp.maximum(norm_ref[0:1, 0:1], CLIP)
    new = adam(w_ref[...], m_ref[...], v_ref[...], g_ref[...].astype(FULL) * factor, RATE_MATRIX, DECAY)
    nw_ref[...], nm_ref[...], nv_ref[...] = new


def update(norm, weights, first, second, grads):
    own, width = weights.shape
    rows = 8 if own % 8 == 0 else own
    tile = pl.BlockSpec((rows, width), lambda i: (i, 0))
    return pl.pallas_call(
        update_kernel,
        grid=(own // rows,),
        out_shape=(jax.ShapeDtypeStruct((own, width), FULL),) * 3,
        in_specs=[whole_spec((8, LANES)), tile, tile, tile, tile],
        out_specs=(tile,) * 3,
        compiler_params=params(),
        name="update",
        cost_estimate=cost(9),
    )(norm, weights, first, second, grads)


def pad_lanes(value, width=LANES):
    return jnp.pad(value, ((0, 0), (0, width - value.shape[1])))


def shards(
    inputs,
    cotangent,
    weights,
    weights_first,
    weights_second,
    gains,
    gains_first,
    gains_second,
    forget_weight,
    forget_first,
    forget_second,
    forget_bias,
    bias_first,
    bias_second,
):
    grps, groups = lax.axis_size("grp"), lax.axis_size("fsdp") // TP
    grp, group, member = place()
    rows, own_rows = inputs.shape[1], weights.shape[0]
    group_tokens = TP * rows
    source, returned = inputs[0], cotangent[0]

    tokens, following, near, both, down = start(source, gains[0:1], weights, grps, groups)
    slab = TP * own_rows
    both, down = both.reshape(slab, 2 * UNITS), down.reshape(slab, UNITS)
    tokens = tokens.reshape(group_tokens, D)
    near = near.reshape(D, NEAR)
    both_parts = across_groups(both, groups)
    both_own, down_own = over_grps(both_parts[:1], grps), over_grps([down], grps)

    forget_low = pad_lanes(lax.dynamic_slice_in_dim(forget_weight, member * HEADS, HEADS, 1).astype(HALF))
    bias = pad_lanes(lax.dynamic_slice_in_dim(forget_bias[None], member * HEADS, HEADS, 1))
    head_gains = lax.dynamic_slice_in_dim(gains[2:4], member * HEADS * DH, HEADS * DH, 1)
    head_gains = head_gains.reshape(2, HEADS, DH).transpose(1, 0, 2).reshape(HEADS, 2 * DH)
    head_gains = jnp.pad(head_gains, ((0, 8 - HEADS), (0, 0)))
    queries, keys, values, pairs, gates, logits, gathered = project(
        tokens, following, near, forget_low, bias, head_gains, returned
    )
    queries, down = lax.optimization_barrier((queries, down))
    down_parts = across_groups(down, groups)
    gated, attended, logs, gathered = attend(queries, keys, values, gates, gathered, groups)
    returned_all = gathered.reshape(group_tokens, D)
    gated, both_parts, down_parts = lax.optimization_barrier((gated, both_parts[1:], down_parts[1:]))
    both_pieces = in_order(both_own + over_grps(both_parts, grps))
    down_pieces = in_order(down_own + over_grps(down_parts, grps))
    mixed, second = mix(gated, near, source, gains[1:2])
    second = second.reshape(group_tokens, D)
    hidden, grad_both = feed(second, returned_all, both_pieces, down_pieces, grps, groups)
    grad_mixed, grad_gain_mid, branch, out_sums, far_gate, far_down, *far_up = unmix(
        grad_both, both_pieces, down_pieces, mixed, gains[1:2], returned, hidden, second, returned_all, grps, groups
    )
    branch = branch.reshape(group_tokens, D)
    size = lax.axis_size("fsdp")
    far_up = [far_up[0]] + [
        lax.ppermute(far_up[step], "fsdp", [(at, (at + step * TP) % size) for at in range(size)])
        for step in range(1, groups)
    ]

    grads_low, queries_back, grad_gates, pack, out_keep, out_give = ungate(
        branch, near, attended, gates, logs, queries, gated, grps, groups
    )
    dqueries, dkeys, dvalues, late, far_out, home_gate, home_down = attend_back(
        queries_back,
        grads_low,
        keys,
        values,
        queries,
        pack,
        out_keep,
        out_give,
        far_gate.reshape(TP, own_rows, UNITS),
        far_down.reshape(TP, own_rows, UNITS),
    )
    later = pad_lanes(late[:, 0, DH + 3][None])
    if groups > 2:
        everyone = lax.all_gather(dkeys[:, :, DH + 3].sum(axis=1) - dqueries[:, :, DH].sum(axis=1), "fsdp")
        ahead = (jnp.arange(size) // TP > group) & (jnp.arange(size) % TP == member)
        later = pad_lanes(-jnp.sum(jnp.where(ahead[:, None], everyone, 0.0), axis=0)[None])
    grad_projected, grad_logits, grad_heads, grad_bias = unproject(
        dqueries, dkeys, dvalues, grad_gates, pairs, logits, head_gains, later
    )

    grad_heads = grad_heads[:HEADS].reshape(HEADS, 2, DH).transpose(1, 0, 2).reshape(1, 2 * HEADS * DH)
    rest = jnp.concatenate([grad_heads, grad_bias[0:1, :HEADS]], axis=1)
    small = jnp.concatenate(
        [jnp.zeros((HEADS + 1, D), FULL), grad_gain_mid, pad_lanes(rest, D), jnp.zeros((2, D), FULL)], axis=0
    )
    input_grad, grads, grad_gains, grad_forget, grad_bias, norm = end(
        grad_projected,
        grad_logits,
        forget_low,
        source,
        gains[0:1],
        grad_mixed,
        small,
        collected(far_up).reshape(TP, own_rows, UNITS),
        far_out.reshape(TP, own_rows, OUT),
        home_gate,
        home_down,
        near,
        tokens,
        grps,
        groups,
    )
    norm, out_sums = lax.optimization_barrier((norm, out_sums))
    result = mixed + out_sums[3].astype(FULL)
    for at, bits in enumerate((2, 4, 6)):
        result = result + lax.ppermute(out_sums[at], "fsdp", [(to, to ^ bits) for to in range(size)]).astype(FULL)
    output = result.astype(HALF)
    grad_norm = norm[0, 0]
    grad_forget, grad_bias = grad_forget.T, grad_bias[0, :H]
    factor = CLIP / jnp.maximum(grad_norm, CLIP)
    new_w, new_wf, new_ws = update(norm, weights, weights_first, weights_second, grads)
    new_g, new_gf, new_gs = adam(gains, gains_first, gains_second, grad_gains * factor, RATE_GAIN, 0.0)
    new_fw, new_ff, new_fs = adam(
        forget_weight, forget_first, forget_second, grad_forget * factor, RATE_MATRIX, DECAY
    )
    new_fb, new_bf, new_bs = adam(
        forget_bias, bias_first, bias_second, grad_bias * factor, RATE_BIAS, 0.0
    )
    return (
        output[None],
        input_grad[None],
        grad_norm,
        new_w,
        new_wf,
        new_ws,
        new_g,
        new_gf,
        new_gs,
        new_fw,
        new_ff,
        new_fs,
        new_fb,
        new_bf,
        new_bs,
    )


def solution(mesh):
    tokens = P("grp", "fsdp", None)
    matrix = P(("grp", "fsdp"), None)
    return jax.shard_map(
        shards,
        mesh=mesh,
        in_specs=(tokens,) * 2 + (matrix,) * 3 + (P(),) * 9,
        out_specs=(tokens,) * 2 + (P(),) + (matrix,) * 3 + (P(),) * 9,
        check_vma=False,
    )
```

```python
import functools

import jax
import jax.numpy as jnp
from jax import lax
from jax.experimental import pallas as pl
from jax.experimental.pallas import tpu as pltpu
from jax.sharding import PartitionSpec as P

D = 1536
H = 24
DH = 64
F = 4096
STEP = 5

EPS = 1e-06
BETA_ONE = 0.9
BETA_TWO = 0.95
ADAM_EPS = 1e-08
RATE_MATRIX = 0.1
RATE_GAIN = 1.2
RATE_BIAS = 3.0
DECAY = 0.1
CLIP = 1.0
NEGATIVE = -1e30

TP = 8
HEADS = H // TP
UNITS = F // TP
QKVG = HEADS * 4 * DH
OUT = 256
NEAR = QKVG + OUT
LANES = 128
ROWS = 256
TALL = 512
BLOCK = 512
MESH = pl.DeviceIdType.MESH
HALF = jnp.bfloat16
FULL = jnp.float32
VMEM_BYTES = 56 * 1024 * 1024


def params(collective=None, **more):
    if collective is None:
        return pltpu.CompilerParams(vmem_limit_bytes=VMEM_BYTES, **more)
    return pltpu.CompilerParams(
        collective_id=collective, has_side_effects=True, vmem_limit_bytes=VMEM_BYTES, **more
    )


def flip(member, bits):
    for bit in (1, 2, 4):
        if bits & bit:
            member = member + bit - 2 * bit * lax.rem(lax.div(member, bit), 2)
    return member


def place():
    position = lax.axis_index("fsdp")
    return lax.axis_index("grp"), lax.div(position, TP), lax.rem(position, TP)


def cost(micros):
    return pl.CostEstimate(flops=0, bytes_accessed=3_000_000 * micros, transcendentals=0)


def call_out(targets):
    barrier = pltpu.get_barrier_semaphore()
    for target in targets:
        pl.semaphore_signal(barrier, inc=1, device_id=target, device_id_type=MESH)


def hear(targets):
    pl.semaphore_wait(pltpu.get_barrier_semaphore(), len(targets))


def greet(targets):
    call_out(targets)
    hear(targets)


def neighbours(grps, groups):
    grp, group, member = place()

    def device(to_grp=0, to_group=0, bits=0):
        return (
            lax.rem(grp + to_grp, grps),
            lax.rem(group + to_group, groups) * TP + flip(member, bits),
        )

    return device, (
        [device(bits=bits) for bits in range(1, TP)]
        + [device(to_group=step) for step in range(1, groups)]
        + [device(to_grp=step) for step in range(1, grps)]
    )


class Lines:
    def __init__(self, send, receive):
        self.send, self.receive, self.count, self.made = send, receive, 0, []

    def plan(self, source, target, device):
        copy = pltpu.make_async_remote_copy(
            src_ref=source,
            dst_ref=target,
            send_sem=self.send.at[self.count],
            recv_sem=self.receive.at[self.count],
            device_id=device,
            device_id_type=MESH,
        )
        self.count += 1
        self.made.append(copy)
        return copy


def dot(left, right, contract=(1, 0)):
    return lax.dot_general(
        left, right, (((contract[0],), (contract[1],)), ((), ())), preferred_element_type=FULL
    )


def rms_rows(value, gain):
    return value * lax.rsqrt(jnp.mean(value * value, axis=-1, keepdims=True) + EPS) * gain


def rms_back(value, gain, grad):
    inverse = lax.rsqrt(jnp.mean(value * value, axis=-1, keepdims=True) + EPS)
    normal = value * inverse
    scaled = grad * gain
    pulled = inverse * (scaled - normal * jnp.mean(scaled * normal, axis=-1, keepdims=True))
    return pulled, jnp.sum(grad * normal, axis=0, keepdims=True)


def half_lanes(value, column, upper):
    base = column // LANES * LANES
    part = value[:, base : base + LANES]
    if (column % LANES != 0) != upper:
        part = pltpu.roll(part, DH, 1)
    return part


def two_halves(value, lower, upper, lanes):
    low = half_lanes(value, lower, False)
    if upper is None:
        return jnp.where(lanes < DH, low, 0.0)
    return jnp.where(lanes < DH, low, half_lanes(value, upper, True))


def pack_near(w_ref, near):
    lanes = lax.broadcasted_iota(jnp.int32, (w_ref.shape[0], LANES), 1)
    for member in range(TP):
        for head in range(HEADS):
            at = (member * HEADS + head) * DH
            near[member, :, 256 * head : 256 * head + LANES] = two_halves(w_ref, at, D + at, lanes).astype(HALF)
            near[member, :, 256 * head + LANES : 256 * head + 256] = two_halves(
                w_ref, 2 * D + at, 3 * D + at, lanes
            ).astype(HALF)
        at = 4 * D + member * HEADS * DH
        near[member, :, QKVG : QKVG + LANES] = two_halves(w_ref, at, at + DH, lanes).astype(HALF)
        near[member, :, QKVG + LANES :] = two_halves(w_ref, at + 2 * DH, None, lanes).astype(HALF)


def pack_far(w_ref, both, down):
    edge = 5 * D
    for member in range(TP):
        at = edge + member * UNITS
        both[member, :, :UNITS] = w_ref[:, at : at + UNITS].astype(HALF)
        both[member, :, UNITS:] = w_ref[:, at + F : at + F + UNITS].astype(HALF)
        down[member] = w_ref[:, at + 2 * F : at + 2 * F + UNITS].astype(HALF)


def halves(ref):
    count = ref.shape[0] // 2
    return [ref.at[pl.ds(at * count, count)] for at in range(2)]


def halves(ref):
    count = ref.shape[0] // 2
    return [ref.at[pl.ds(at * count, count)] for at in range(2)]


def start_counts(grps, groups):
    weights = (TP - 1) + (groups - 1) * TP + (grps - 1) * groups * TP
    return GATHER + 2 * (groups - 1) + weights + 2 * (TP - 1)


def start_kernel(
    grps, groups, x_ref, g_ref, w_ref, all_ref, next_ref, full_ref, both_ref, down_ref,
    block, near, both, down, send, receive, local,
):
    grp, group, member = place()
    device, everyone = neighbours(grps, groups)
    call_out(everyone)
    block[...] = rms_rows(x_ref[...].astype(FULL), g_ref[...]).astype(HALF)
    lines = Lines(send, receive)
    first, across, over, far = {}, {}, {}, []
    tokens = gather_plan(lines, block, all_ref, True)
    ahead, aside = [], []
    for back in range(1, groups):
        ahead.append(lines.plan(block, next_ref.at[back - 1, 0], device(to_group=groups - back)))
        aside.append(lines.plan(next_ref.at[back - 1, 0], next_ref.at[back - 1, 1], device(bits=4)))
    for bits in range(1, TP):
        first[bits] = lines.plan(near.at[flip(member, bits)], full_ref.at[grp, group, member], device(bits=bits))
    for bits in range(TP):
        slot = full_ref.at[grp, group, flip(member, bits)]
        source = near.at[member] if bits == 0 else slot
        for back in range(1, groups):
            across[back, bits] = lines.plan(source, slot, device(to_group=groups - back))
        for step in range(1, grps):
            over[step, 0, bits] = lines.plan(source, slot, device(to_grp=step))
        for back in range(1, groups):
            passed = full_ref.at[grp, lax.rem(group + back, groups), flip(member, bits)]
            for step in range(1, grps):
                over[step, back, bits] = lines.plan(passed, passed, device(to_grp=step))
    for bits in range(1, TP):
        there = flip(member, bits)
        far.append(lines.plan(both.at[there], both_ref.at[member], device(bits=bits)))
        far.append(lines.plan(down.at[there], down_ref.at[member], device(bits=bits)))

    own_tokens = pltpu.make_async_copy(block, all_ref.at[member], local.at[0])
    own = [
        pltpu.make_async_copy(near.at[member], full_ref.at[grp, group, member], local.at[1]),
        pltpu.make_async_copy(both.at[member], both_ref.at[member], local.at[2]),
        pltpu.make_async_copy(down.at[member], down_ref.at[member], local.at[3]),
    ]
    hear(everyone)
    for copy in ahead:
        copy.start()
    pack_near(w_ref, near)
    for bits in (4, 2, 6, 1, 5, 3, 7):
        first[bits].start()
    for back in range(1, groups):
        across[back, 0].start()
    for step in range(1, grps):
        over[step, 0, 0].start()
    gather_start(tokens, own_tokens)
    own[0].start()
    pack_far(w_ref, both, down)
    for bits in (1, 5, 3, 7, 2, 4, 6):
        first[bits].wait_recv()
        for back in range(1, groups):
            across[back, bits].start()
        for step in range(1, grps):
            over[step, 0, bits].start()
    gather_turn(tokens, True)
    for copy in far:
        copy.start()
    for copy in own[1:]:
        copy.start()
    for come, gone in zip(ahead, aside):
        come.wait_recv()
        gone.start()
    gather_pass(tokens, True)
    for back in range(1, groups):
        for bits in (0, 1, 5, 3, 7, 2, 4, 6):
            across[back, bits].wait_recv()
            for step in range(1, grps):
                over[step, back, bits].start()
    gather_end(tokens, own_tokens)
    for copy in aside + far + list(over.values()):
        copy.wait_recv()
    for copy in lines.made:
        copy.wait_send()
    for copy in own:
        copy.wait()


def start(source, gain, weights, grps, groups):
    rows, own = source.shape[0], weights.shape[0]
    count = start_counts(grps, groups)
    vmem, anywhere = pl.BlockSpec(memory_space=pltpu.VMEM), pl.BlockSpec(memory_space=pl.ANY)
    return pl.pallas_call(
        functools.partial(start_kernel, grps, groups),
        out_shape=(
            jax.ShapeDtypeStruct((TP, rows, D), HALF),
            jax.ShapeDtypeStruct((groups - 1, 2, rows, D), HALF),
            jax.ShapeDtypeStruct((grps, groups, TP, own, NEAR), HALF),
            jax.ShapeDtypeStruct((TP, own, 2 * UNITS), HALF),
            jax.ShapeDtypeStruct((TP, own, UNITS), HALF),
        ),
        in_specs=[vmem] * 3,
        out_specs=(anywhere,) * 5,
        scratch_shapes=[
            pltpu.VMEM((rows, D), HALF),
            pltpu.VMEM((TP, own, NEAR), HALF),
            pltpu.VMEM((TP, own, 2 * UNITS), HALF),
            pltpu.VMEM((TP, own, UNITS), HALF),
            pltpu.SemaphoreType.DMA((count,)),
            pltpu.SemaphoreType.DMA((count,)),
            pltpu.SemaphoreType.DMA((4,)),
        ],
        compiler_params=params(1),
        name="start",
        cost_estimate=cost(60),
    )(source, gain, weights)


def three(value):
    high = value.astype(HALF).astype(FULL)
    rest = value - high
    middle = rest.astype(HALF).astype(FULL)
    return high, middle, (rest - middle).astype(HALF).astype(FULL)


def two(value):
    high = value.astype(HALF)
    return high, (value - high.astype(FULL)).astype(HALF)


def at_lanes(lanes, pairs, other):
    for lane, value in pairs:
        other = jnp.where(lanes == lane, value, other)
    return other


def side_by_side(values, lanes):
    packed = jnp.zeros_like(values[0])
    for at, value in enumerate(values):
        if at:
            value = pltpu.roll(value, HEADS * at, 1)
        packed = jnp.where((lanes >= HEADS * at) & (lanes < HEADS * (at + 1)), value, packed)
    return packed.astype(HALF)


def picker(targets):
    def build(width, find, sign=1.0):
        row = lax.broadcasted_iota(jnp.int32, (LANES, width), 0)
        col = lax.broadcasted_iota(jnp.int32, (LANES, width), 1)
        return jnp.where(row == find(col), sign, 0.0).astype(HALF)

    return build(*targets)


def spread_lanes(first, at):
    def find(col):
        head, lane = lax.div(col, LANES), lax.rem(col, LANES) - at
        return jnp.where((lane >= 0) & (lane < 3), HEADS * (first + lane) + head, -1)

    return find


def halves_matrix(scale):
    row = lax.broadcasted_iota(jnp.int32, (LANES, LANES), 0)
    col = lax.broadcasted_iota(jnp.int32, (LANES, LANES), 1)
    return jnp.where((row < DH) == (col < DH), scale, 0.0).astype(HALF)


def halves_mean(value, matrix):
    high, least = two(value)
    return dot(high, matrix) + dot(least, matrix)


def side_plan(lines, pair_ref, all_ref):
    member = place()[2]
    plan = {}
    for at, bits in ((0, 0), (1, 4)):
        there = flip(member, bits)
        plan[bits + 2] = lines.plan(pair_ref.at[at], all_ref.at[there], group_device(2))
        plan[bits + 1] = lines.plan(pair_ref.at[at], all_ref.at[there], group_device(1))
    for bits in (2, 6):
        slot = all_ref.at[flip(member, bits)]
        plan[bits + 1] = lines.plan(slot, slot, group_device(1))
    return plan


def first_leg(lines, block, all_ref):
    member = place()[2]
    return {bits: lines.plan(block, all_ref.at[member], group_device(bits)) for bits in (2, 4)}


def third_leg(lines, all_ref):
    member = place()[2]

    def copy(block, bits):
        slot = all_ref.at[flip(member, block)]
        return lines.plan(slot, slot, group_device(bits))

    return {6: copy(4, 2), 1: copy(0, 1), 3: copy(2, 1), 5: copy(4, 1), 7: copy(6, 1)}


def project_kernel(
    groups, a_ref, n_ref, w_ref, f_ref, b_ref, g_ref, c_ref,
    q_ref, k_ref, v_ref, p_ref, t_ref, z_ref, all_ref, others, decays, totals, send, receive, local,
):
    turn = pl.program_id(0)
    grp, group, member = place()
    own = a_ref.shape[0]
    rows = own // TP
    lanes = lax.broadcasted_iota(jnp.int32, (TALL, LANES), 1)

    def plans():
        lines = Lines(send, receive)
        sides = [side_plan(lines, n_ref.at[at], others.at[at]) for at in range(groups - 1)]
        copies = [
            pltpu.make_async_copy(n_ref.at[at, half], others.at[at, flip(member, 4 * half)], local.at[2 * at + half])
            for at in range(groups - 1)
            for half in range(2)
        ]
        copies.append(pltpu.make_async_copy(c_ref, all_ref.at[member], local.at[2 * groups - 2]))
        return lines, sides, copies, first_leg(lines, c_ref, all_ref)

    def low_rows(index, start, count):
        if index == 0:
            return a_ref[start : start + count]
        return others[index - 1, start // rows : (start + count) // rows].reshape(count, D)

    def scan(index):
        row = lax.broadcasted_iota(jnp.int32, (ROWS, ROWS), 0)
        col = lax.broadcasted_iota(jnp.int32, (ROWS, ROWS), 1)
        lower = jnp.where(col <= row, 1.0, 0.0)
        carry = jnp.zeros((1, LANES), FULL)
        for start in range(0, own, ROWS):
            logit = dot(low_rows(index, start, ROWS), f_ref[...]) + b_ref[...]
            if index == 0:
                z_ref[start : start + ROWS] = logit
            log_gate = jnp.minimum(logit, 0.0) - jnp.log1p(jnp.exp(-jnp.abs(logit)))
            part = carry + lax.dot_general(
                lower,
                log_gate,
                (((1,), (0,)), ((), ())),
                precision=lax.Precision.HIGHEST,
                preferred_element_type=FULL,
            )
            decays[index, start : start + ROWS] = part
            carry = part[ROWS - 1 : ROWS]
        totals[index : index + 1] = carry

    def rows_done(low, sums, start, first):
        here = slice(start, start + TALL)
        made = dot(low, w_ref[...])
        means = halves_matrix(1.0 / DH)
        packed = side_by_side(three(jnp.where(lanes < HEADS, sums, 0.0)), lanes)
        plus = dot(packed, picker((HEADS * LANES, spread_lanes(0, DH))))
        minus = dot(packed, picker((HEADS * LANES, spread_lanes(0, DH + 3), -1.0)))
        ones_of_query = jnp.where((lanes >= DH + 3) & (lanes < DH + 6), 1.0, 0.0)
        ones_of_value = jnp.where((lanes >= DH) & (lanes < DH + 3), 1.0, 0.0)
        ones_of_key = jnp.where((lanes >= DH + 6) & (lanes < DH + 9), 1.0, ones_of_value)
        for head in range(HEADS):
            register = slice(LANES * head, LANES * (head + 1))
            pair = made[:, 256 * head : 256 * head + LANES]
            value = made[:, 256 * head + LANES : 256 * head + 2 * LANES]
            normal = pair * lax.rsqrt(halves_mean(pair * pair, means) + EPS) * g_ref[head : head + 1]
            normal = normal.astype(HALF).astype(FULL)
            q_ref[head, here] = jnp.where(
                lanes < DH, normal * (DH**-0.5), plus[:, register] + ones_of_query
            ).astype(HALF)
            k_ref[head, here] = jnp.where(
                lanes < DH, pltpu.roll(normal, DH, 1), minus[:, register] + ones_of_key
            ).astype(HALF)
            v_ref[head, here] = jnp.where(lanes < DH, value, ones_of_value).astype(HALF)
            if first:
                p_ref[here, register] = pair
        if first:
            left, right = gates_of(made, lanes)
            t_ref[here, :LANES] = left
            t_ref[here, LANES:] = right

    @pl.when(turn == 0)
    def begin():
        greet([group_device(bits) for bits in (4, 2, 1)])
        lines, sides, copies, leg = plans()
        for copy in copies:
            copy.start()
        for side in sides:
            for bits in (2, 6, 1, 5):
                side[bits].start()
        leg[4].start()
        scan(0)
        for start in range(0, own, TALL):
            rows_done(low_rows(0, start, TALL), decays[0, start : start + TALL], start, True)
        leg[2].start()
        for side in sides:
            for bits in (2, 6):
                side[bits].wait_recv()
                side[bits + 1].start()

    @pl.when(turn == 1)
    def arrived():
        lines, sides, copies, leg = plans()
        for copy in copies[:-1]:
            copy.wait()
        for side in sides:
            for bits in (1, 3, 5, 7):
                side[bits].wait_recv()
        for index in range(1, groups):
            scan(index)

    @pl.when(turn > 0)
    def next_group():
        ahead = turn < groups - group
        base = jnp.zeros((1, LANES), FULL)
        for index in range(groups):
            weight = jnp.where(ahead, jnp.where(index < turn, 1.0, 0.0), jnp.where(index >= turn, -1.0, 0.0))
            base = base + weight * totals[index : index + 1]
        for start in range(0, own, TALL):
            low = others[turn - 1, start // rows : (start + TALL) // rows].reshape(TALL, D)
            rows_done(low, decays[turn, start : start + TALL] + base, start, False)

    @pl.when(turn == groups - 1)
    def end():
        lines, sides, copies, leg = plans()
        copies[-1].wait()
        for copy in leg.values():
            copy.wait_recv()
        for copy in lines.made:
            copy.wait_send()


def project(tokens, following, full, forget, bias, gains, returned):
    own, groups = tokens.shape[0], following.shape[0] + 1
    rows = returned.shape[0]
    count = 6 * (groups - 1) + 2
    tile = pl.BlockSpec((HEADS, own, LANES), lambda i: (0, i, 0))
    anywhere = pl.BlockSpec(memory_space=pl.ANY)
    return pl.pallas_call(
        functools.partial(project_kernel, groups),
        grid=(groups,),
        out_shape=(
            jax.ShapeDtypeStruct((HEADS, groups * own, LANES), HALF),
            jax.ShapeDtypeStruct((HEADS, groups * own, LANES), HALF),
            jax.ShapeDtypeStruct((HEADS, groups * own, LANES), HALF),
            jax.ShapeDtypeStruct((own, HEADS * LANES), FULL),
            jax.ShapeDtypeStruct((own, OUT), FULL),
            jax.ShapeDtypeStruct((own, LANES), FULL),
            jax.ShapeDtypeStruct((TP, rows, D), HALF),
        ),
        in_specs=[
            whole_spec((own, D)),
            anywhere,
            weight_spec(QKVG, 0),
            whole_spec((D, LANES)),
            whole_spec((1, LANES)),
            whole_spec((8, LANES)),
            whole_spec((rows, D)),
        ],
        out_specs=(
            tile,
            tile,
            tile,
            whole_spec((own, HEADS * LANES)),
            whole_spec((own, OUT)),
            whole_spec((own, LANES)),
            anywhere,
        ),
        scratch_shapes=[
            pltpu.VMEM((groups - 1, TP, rows, D), HALF),
            pltpu.VMEM((groups, own, LANES), FULL),
            pltpu.VMEM((max(groups, 8), LANES), FULL),
            pltpu.SemaphoreType.DMA((count,)),
            pltpu.SemaphoreType.DMA((count,)),
            pltpu.SemaphoreType.DMA((2 * groups - 1,)),
        ],
        compiler_params=params(8),
        name="project",
        cost_estimate=cost(25),
    )(tokens, following, full, forget, bias, gains, returned)


def sigmoid(value):
    return 1.0 / (1.0 + jnp.exp(-value))


def gates_of(made, lanes):
    second = [made[:, 256 * head + LANES : 256 * head + 2 * LANES] for head in range(HEADS)]
    left = jnp.where(lanes < DH, pltpu.roll(second[0], DH, 1), second[1])
    right = jnp.where(lanes < DH, pltpu.roll(second[2], DH, 1), 0.0)
    return left, right


def attend_kernel(
    groups, steps, q_ref, k_ref, v_ref, t_ref, c_ref, u_ref, o_ref, l_ref, all_ref, send, receive
):
    count = u_ref.shape[0]
    at_step = pl.program_id(0)

    @pl.when(at_step == 0)
    def begin():
        greet([group_device(bits) for bits in (2, 1)])
        plan = third_leg(Lines(send, receive), all_ref)
        for bits in (6, 1, 3, 5):
            plan[bits].start()

    @pl.when(at_step == steps - 1)
    def pass_on():
        plan = third_leg(Lines(send, receive), all_ref)
        plan[6].wait_recv()
        plan[7].start()

    queries = [q_ref[head] for head in range(HEADS)]

    def visit(state, at, masked):
        new = []
        for head in range(HEADS):
            top, accum = state[head]
            scores = dot(queries[head], k_ref[head, pl.ds(at * count, count)], (1, 1))
            if masked:
                row = lax.broadcasted_iota(jnp.int32, scores.shape, 0)
                col = lax.broadcasted_iota(jnp.int32, scores.shape, 1)
                scores = jnp.where(col <= row, scores, NEGATIVE)
            high = jnp.maximum(top, jnp.max(scores, axis=1, keepdims=True))
            weight = jnp.exp(scores - high)
            accum = accum * jnp.exp(top - high) + dot(weight.astype(HALF), v_ref[head, pl.ds(at * count, count)])
            new.append((high, accum))
        return tuple(new)

    state = tuple(
        (jnp.full((count, 1), NEGATIVE, FULL), jnp.zeros((count, LANES), FULL)) for head in range(HEADS)
    )
    earlier = (groups - place()[1]) * steps
    state = lax.fori_loop(earlier, groups * steps, lambda at, inner: visit(inner, at, False), state)
    state = lax.fori_loop(0, at_step, lambda at, inner: visit(inner, at, False), state)
    state = visit(state, at_step, True)
    lanes = lax.broadcasted_iota(jnp.int32, (count, LANES), 1)
    out, logs = [], []
    for top, accum in state:
        total = jnp.sum(jnp.where(lanes == DH, accum, 0.0), axis=1, keepdims=True)
        out.append(jnp.where(lanes < DH, accum / total, 0.0))
        logs.append(top + jnp.log(total))
    left, right = t_ref[:, :LANES], t_ref[:, LANES:]
    pair = out[0] + pltpu.roll(out[1], DH, 1)
    o_ref[:, :LANES] = pair
    o_ref[:, LANES:] = out[2]
    u_ref[:, :LANES] = (pair * sigmoid(left)).astype(HALF)
    u_ref[:, LANES:] = (out[2] * sigmoid(right)).astype(HALF)
    l_ref[...] = at_lanes(lanes, tuple(enumerate(logs)), 0.0)

    @pl.when(at_step == steps - 1)
    def end():
        plan = third_leg(Lines(send, receive), all_ref)
        for bits in (1, 3, 5, 7):
            plan[bits].wait_recv()
        for copy in plan.values():
            copy.wait_send()


def attend(queries, keys, values, gates, gathered, groups):
    tokens = keys.shape[1]
    own = tokens // groups
    count = min(BLOCK, own)
    steps = own // count
    whole = pl.BlockSpec((HEADS, tokens, LANES), lambda i: (0, 0, 0), pipeline_mode=pl.Buffered(1))
    anywhere = pl.BlockSpec(memory_space=pl.ANY)
    return pl.pallas_call(
        functools.partial(attend_kernel, groups, steps),
        grid=(steps,),
        in_specs=[
            pl.BlockSpec((HEADS, count, LANES), lambda i: (0, i, 0)),
            whole,
            whole,
            pl.BlockSpec((count, OUT), lambda i: (i, 0)),
            anywhere,
        ],
        out_specs=(
            pl.BlockSpec((count, OUT), lambda i: (i, 0)),
            pl.BlockSpec((count, OUT), lambda i: (i, 0)),
            pl.BlockSpec((count, LANES), lambda i: (i, 0)),
            anywhere,
        ),
        out_shape=(
            jax.ShapeDtypeStruct((own, OUT), HALF),
            jax.ShapeDtypeStruct((own, OUT), FULL),
            jax.ShapeDtypeStruct((own, LANES), FULL),
            jax.ShapeDtypeStruct(gathered.shape, HALF),
        ),
        scratch_shapes=[pltpu.SemaphoreType.DMA((5,)), pltpu.SemaphoreType.DMA((5,))],
        input_output_aliases={4: 3},
        compiler_params=params(9),
        name="attend",
        cost_estimate=cost(16),
    )(queries, keys, values, gates, gathered)


def group_device(bits):
    grp, group, member = place()
    return (grp, group * TP + flip(member, bits))


def blocks_of(ref, core):
    value = ref[:, pl.ds(core, 1)]
    return value.reshape(ref.shape[0] * ref.shape[2], ref.shape[3])


def sum_plan(lines, stage):
    give, take, out, came = stage
    sibling = [lines.plan(give.at[at], take.at[at], group_device(1)) for at in range(4)]
    others = [lines.plan(out.at[at], came.at[at], group_device(bits)) for at, bits in enumerate((2, 4, 6))]
    return sibling, others


def sum_give(pairs, stage, plan, mine):
    give = stage[0]
    grp, group, member = place()
    core = lax.rem(member, 2)
    count = give.shape[1]
    theirs = sum(dot(blocks_of(left, 1 - core), right[...], (1, 1)) for left, right in pairs)
    mine[...] = theirs.reshape(4, count, D)
    for at, bits in enumerate((2, 4, 6, 0)):
        give[at] = mine[lax.div(flip(member, bits), 2)].astype(HALF)
        plan[0][at].start()
    own = sum(dot(blocks_of(left, core), right[...], (1, 1)) for left, right in pairs)
    mine[...] = own.reshape(4, count, D)


def sum_pass(stage, plan, mine):
    give, take, out, came = stage
    member = place()[2]
    for at, bits in enumerate((2, 4, 6)):
        plan[0][at].wait_recv()
        out[at] = (mine[lax.div(flip(member, bits), 2)] + take[at].astype(FULL)).astype(HALF)
        plan[1][at].start()
    plan[0][3].wait_recv()
    return mine[lax.div(member, 2)] + take[3].astype(FULL)


def sum_send(pairs, stage, plan, mine):
    sum_give(pairs, stage, plan, mine)
    return sum_pass(stage, plan, mine)


def sum_take(total, stage, plan):
    give, take, out, came = stage
    for at in range(3):
        plan[1][at].wait_recv()
        total = total + came[at].astype(FULL)
    return total


def sum_scratch(rows):
    return [
        pltpu.VMEM((4, rows, D), HALF),
        pltpu.VMEM((4, rows, D), HALF),
        pltpu.VMEM((3, rows, D), HALF),
        pltpu.VMEM((3, rows, D), HALF),
    ]


def gather_plan(lines, block, all_ref, light=False):
    member = place()[2]

    def slot(bits):
        return halves(all_ref.at[flip(member, bits)])

    plan = {(bits, half): lines.plan(halves(block)[half], slot(0)[half], group_device(bits)) for bits in (4, 2) for half in range(2)}
    plan[1] = lines.plan(block, all_ref.at[member], group_device(1))
    plan[6, 0] = lines.plan(slot(4)[0], slot(4)[0], group_device(2))
    if light:
        plan[6, 1] = lines.plan(slot(4)[1], slot(4)[1], group_device(2))
    else:
        plan[6, 1] = lines.plan(slot(2)[1], slot(2)[1], group_device(4))
    for bits in (4, 2, 6):
        for half in range(2):
            plan[bits + 1, half] = lines.plan(slot(bits)[half], slot(bits)[half], group_device(1))
    return plan


GATHER = 13


def gather_start(plan, own):
    own.start()
    for key in ((4, 0), (2, 1), (4, 1), (2, 0), 1):
        plan[key].start()


def gather_turn(plan, light=False):
    for bits, half in ((4, 0), (4, 1) if light else (2, 1)):
        plan[bits, half].wait_recv()
        plan[6, half].start()
        plan[bits + 1, half].start()


def gather_pass(plan, light=False):
    for bits, half in ((2, 1) if light else (4, 1), (2, 0), (6, 0), (6, 1)):
        plan[bits, half].wait_recv()
        plan[bits + 1, half].start()


def gather_end(plan, own):
    plan[1].wait_recv()
    for bits in (5, 3, 7):
        for half in range(2):
            plan[bits, half].wait_recv()
    own.wait()


def gather_run(plan, own):
    gather_start(plan, own)
    gather_turn(plan)
    gather_pass(plan)
    gather_end(plan, own)


def mix_kernel(u_ref, w_ref, x_ref, g_ref, y_ref, all_ref, mine, block, give, take, out, came, send, receive, local):
    greet([group_device(bits) for bits in (1, 2, 4, 6)])
    member = place()[2]
    lines = Lines(send, receive)
    stage = (give, take, out, came)
    sums = sum_plan(lines, stage)
    gathered = gather_plan(lines, block, all_ref)
    total = sum_take(sum_send([(u_ref, w_ref)], stage, sums, mine), stage, sums)
    mixed = x_ref[...].astype(FULL) + total
    y_ref[...] = mixed
    block[...] = rms_rows(mixed, g_ref[...]).astype(HALF)
    gather_run(gathered, pltpu.make_async_copy(block, all_ref.at[member], local.at[0]))
    for copy in lines.made:
        copy.wait_send()


def whole_spec(shape):
    zeros = (0,) * len(shape)
    return pl.BlockSpec(shape, lambda i: zeros)


def weight_spec(columns, at):
    return pl.BlockSpec((D, columns), lambda i: (0, at))


def mix(gated, full, source, gain):
    rows = source.shape[0]
    count = 7 + GATHER
    return pl.pallas_call(
        mix_kernel,
        grid=(1,),
        out_shape=(
            jax.ShapeDtypeStruct((rows, D), FULL),
            jax.ShapeDtypeStruct((TP, rows, D), HALF),
        ),
        in_specs=[
            whole_spec((4, 2, rows, OUT)),
            weight_spec(OUT, QKVG // OUT),
            whole_spec((rows, D)),
            whole_spec((1, D)),
        ],
        out_specs=(whole_spec((rows, D)), pl.BlockSpec(memory_space=pl.ANY)),
        scratch_shapes=[pltpu.VMEM((4, rows, D), FULL), pltpu.VMEM((rows, D), HALF)]
        + sum_scratch(rows)
        + [
            pltpu.SemaphoreType.DMA((count,)),
            pltpu.SemaphoreType.DMA((count,)),
            pltpu.SemaphoreType.DMA((1,)),
        ],
        compiler_params=params(2),
        name="mix",
        cost_estimate=cost(40),
    )(gated.reshape(4, 2, rows, OUT), full, source, gain)


def slabs(grps, groups):
    grp, group, member = place()
    return [
        (turn, step, lax.rem(grp + turn, grps) * groups + lax.rem(group + step, groups))
        for turn in range(grps)
        for step in range(groups)
    ]


def load_rows(refs, whole, semaphores, grps, groups):
    rows = whole.shape[0] // (grps * groups)
    copies = []
    for at, (turn, step, index) in enumerate(slabs(grps, groups)):
        copies.append(pltpu.make_async_copy(refs[at], whole.at[pl.ds(index * rows, rows)], semaphores.at[at]))
    return copies


def unmix_kernel(grps, groups, d_ref, x_ref, g_ref, c_ref, m_ref, a_ref, r_ref, *rest):
    total_slabs = grps * groups
    both_refs, down_refs = rest[:total_slabs], rest[total_slabs : 2 * total_slabs]
    dx_ref, dg_ref, all_ref, out_ref, gate_ref, down_ref, give_ref, *rest = rest[2 * total_slabs :]
    up_refs, rest = rest[:groups], rest[groups:]
    wgu, wdn, mine, block, give, take, out, came, give2, take2, *rest = rest
    grads, over_got, across_out, across_got, send, receive, local = rest
    device, everyone = neighbours(grps, groups)
    everyone = [group_device(bits) for bits in (1, 2, 4, 6)] + everyone[TP - 1 :]
    call_out(everyone)
    grp, group, member = place()
    core = lax.rem(member, 2)
    load_both = load_rows(both_refs, wgu, local.at[pl.ds(0, total_slabs)], grps, groups)
    load_down = load_rows(down_refs, wdn, local.at[pl.ds(total_slabs, total_slabs)], grps, groups)
    for copy in load_both + load_down:
        copy.start()
    lines = Lines(send, receive)
    stage = (give, take, out, came)
    sums = sum_plan(lines, stage)
    gathered = gather_plan(lines, block, all_ref)
    output = lines.plan(give2, take2, group_device(1))
    rows = D // total_slabs
    places = slabs(grps, groups)
    down, gate, up = range(3)
    over = [
        {
            (turn, step): lines.plan(
                grads.at[kind, pl.ds(index * rows, rows)], over_got.at[kind, turn - 1, step], device(turn)
            )
            for turn, step, index in places
            if turn and (step or kind != up)
        }
        for kind in range(3)
    ]
    across = [
        [
            lines.plan(across_out.at[kind, step - 1], across_got.at[kind, step - 1], device(to_group=step))
            for step in range(1, groups)
        ]
        for kind in (down, gate)
    ]
    cut = D // 4

    def grad_of(kind, left, right):
        for at in range(4):
            here = slice(at * cut, (at + 1) * cut)
            grads[kind, here] = dot(left[:, here], right, (0, 0)).astype(HALF)

    def over_sum(kind, step):
        value = grads[kind, pl.ds(places[step][2] * rows, rows)].astype(FULL)
        for turn in range(1, grps):
            over[kind][turn, step].wait_recv()
            value = value + over_got[kind, turn - 1, step].astype(FULL)
        return value

    def begin_over(kind, steps):
        for step in steps:
            for turn in range(1, grps):
                over[kind][turn, step].start()

    def cross(kind):
        for step in range(1, groups):
            across_out[kind, step - 1] = over_sum(kind, step).astype(HALF)
            across[kind][step - 1].start()

    def crossed(kind):
        value = over_sum(kind, 0)
        for step in range(1, groups):
            across[kind][step - 1].wait_recv()
            value = value + across_got[kind, step - 1].astype(FULL)
        return value.astype(HALF)

    tokens, count = r_ref.shape[0], x_ref.shape[0]
    hidden, both = m_ref[...].reshape(tokens, UNITS), d_ref[...].reshape(tokens, 2 * UNITS)
    grad_of(down, r_ref, hidden)
    hear(everyone)
    begin_over(down, range(1, groups))
    for copy in load_both:
        copy.wait()
    sum_give([(d_ref, wgu)], stage, sums, mine)
    grad_of(gate, a_ref, both[:, :UNITS])
    begin_over(gate, range(1, groups))
    total = sum_pass(stage, sums, mine)
    cross(down)
    begin_over(down, [0])
    for copy in load_down:
        copy.wait()
    give2[...] = dot(blocks_of(m_ref, 1 - core), wdn[...], (1, 1)).astype(HALF).reshape(4, count, D)
    output.start()
    grad_of(up, a_ref, both[:, UNITS:])
    cross(gate)
    begin_over(up, range(1, groups))
    mine[...] = dot(blocks_of(m_ref, core), wdn[...], (1, 1)).reshape(4, count, D)
    total = sum_take(total, stage, sums)
    pulled, dgain = rms_back(x_ref[...], g_ref[...], total)
    grad = c_ref[...].astype(FULL) + pulled
    block[...] = grad.astype(HALF)
    own = pltpu.make_async_copy(block, all_ref.at[member], local.at[2 * total_slabs])
    gather_start(gathered, own)
    dx_ref[...] = grad
    dg_ref[...] = dgain
    output.wait_recv()
    for at, bits in enumerate((2, 4, 6, 0)):
        chip = lax.div(flip(member, bits), 2)
        out_ref[at] = (mine[chip] + take2[chip].astype(FULL)).astype(HALF)
    gather_turn(gathered)
    begin_over(gate, [0])
    gather_pass(gathered)
    for step in range(1, groups):
        up_refs[step][...] = over_sum(up, step).astype(HALF)
    for turn, step, index in places:
        if step == 0:
            target = give_ref.at[turn - 1] if turn else up_refs[0]
            target[...] = grads[up, pl.ds(index * rows, rows)]
    gather_end(gathered, own)
    down_ref[...] = crossed(down)
    gate_ref[...] = crossed(gate)
    for copy in lines.made:
        copy.wait_send()


def unmix(grads, both, down, mixed, gain, returned, hidden, second, returned_all, grps, groups):
    rows, tokens = mixed.shape[0], second.shape[0]
    slab = both[0].shape[0]
    total_slabs = grps * groups
    count = 8 + GATHER + (grps - 1) * (3 * groups - 1) + 2 * (groups - 1)
    piece = jax.ShapeDtypeStruct((slab, UNITS), HALF)
    return pl.pallas_call(
        functools.partial(unmix_kernel, grps, groups),
        grid=(1,),
        out_shape=(
            jax.ShapeDtypeStruct((rows, D), FULL),
            jax.ShapeDtypeStruct((1, D), FULL),
            jax.ShapeDtypeStruct((TP, rows, D), HALF),
            jax.ShapeDtypeStruct((4, rows, D), HALF),
        )
        + (piece,) * 2
        + (jax.ShapeDtypeStruct((grps - 1, slab, UNITS), HALF),)
        + (piece,) * groups,
        in_specs=[
            whole_spec((4, 2, rows, 2 * UNITS)),
            whole_spec((rows, D)),
            whole_spec((1, D)),
            whole_spec((rows, D)),
            whole_spec((4, 2, rows, UNITS)),
            whole_spec((tokens, D)),
            whole_spec((tokens, D)),
        ]
        + [pl.BlockSpec(memory_space=pl.ANY)] * (2 * total_slabs),
        out_specs=(
            whole_spec((rows, D)),
            whole_spec((1, D)),
            pl.BlockSpec(memory_space=pl.ANY),
            whole_spec((4, rows, D)),
        )
        + (whole_spec((slab, UNITS)),) * 2
        + (whole_spec((grps - 1, slab, UNITS)),)
        + (whole_spec((slab, UNITS)),) * groups,
        scratch_shapes=[
            pltpu.VMEM((D, 2 * UNITS), HALF),
            pltpu.VMEM((D, UNITS), HALF),
            pltpu.VMEM((4, rows, D), FULL),
            pltpu.VMEM((rows, D), HALF),
        ]
        + sum_scratch(rows)
        + [
            pltpu.VMEM((4, rows, D), HALF),
            pltpu.VMEM((4, rows, D), HALF),
            pltpu.VMEM((3, D, UNITS), HALF),
            pltpu.VMEM((3, grps - 1, groups, slab, UNITS), HALF),
            pltpu.VMEM((2, groups - 1, slab, UNITS), HALF),
            pltpu.VMEM((2, groups - 1, slab, UNITS), HALF),
            pltpu.SemaphoreType.DMA((count,)),
            pltpu.SemaphoreType.DMA((count,)),
            pltpu.SemaphoreType.DMA((2 * total_slabs + 1,)),
        ],
        compiler_params=params(3),
        name="unmix",
        cost_estimate=cost(55),
    )(
        grads.reshape(4, 2, rows, 2 * UNITS),
        mixed,
        gain,
        returned,
        hidden.reshape(4, 2, rows, UNITS),
        second,
        returned_all,
        *both,
        *down,
    )


def feed_kernel(grps, groups, a_ref, c_ref, *rest):
    total_slabs = grps * groups
    both_refs, down_refs = rest[:total_slabs], rest[total_slabs : 2 * total_slabs]
    m_ref, d_ref, wgu, wdn, local = rest[2 * total_slabs :]

    @pl.when(pl.program_id(0) == 0)
    def load():
        copies = load_rows(both_refs, wgu, local.at[pl.ds(0, total_slabs)], grps, groups)
        copies = copies + load_rows(down_refs, wdn, local.at[pl.ds(total_slabs, total_slabs)], grps, groups)
        for copy in copies:
            copy.start()
        for copy in copies:
            copy.wait()

    made = dot(a_ref[...], wgu[...])
    gate, up = made[:, :UNITS], made[:, UNITS:]
    sig = sigmoid(gate)
    swish = gate * sig
    m_ref[...] = (swish * up).astype(HALF)
    grad = dot(c_ref[...], wdn[...])
    d_ref[:, :UNITS] = (grad * up * sig * (1.0 + gate * (1.0 - sig))).astype(HALF)
    d_ref[:, UNITS:] = (grad * swish).astype(HALF)


def feed(second, returned, both, down, grps, groups):
    tokens = second.shape[0]
    count = TALL
    return pl.pallas_call(
        functools.partial(feed_kernel, grps, groups),
        grid=(tokens // count,),
        out_shape=(
            jax.ShapeDtypeStruct((tokens, UNITS), HALF),
            jax.ShapeDtypeStruct((tokens, 2 * UNITS), HALF),
        ),
        in_specs=[
            pl.BlockSpec((count, D), lambda i: (i, 0)),
            pl.BlockSpec((count, D), lambda i: (i, 0)),
        ]
        + [pl.BlockSpec(memory_space=pl.ANY)] * (2 * grps * groups),
        out_specs=(
            pl.BlockSpec((count, UNITS), lambda i: (i, 0)),
            pl.BlockSpec((count, 2 * UNITS), lambda i: (i, 0)),
        ),
        scratch_shapes=[
            pltpu.VMEM((D, 2 * UNITS), HALF),
            pltpu.VMEM((D, UNITS), HALF),
            pltpu.SemaphoreType.DMA((2 * grps * groups,)),
        ],
        compiler_params=params(),
        name="feed",
        cost_estimate=cost(10),
    )(second, returned, *both, *down)


def ungate_kernel(
    grps, groups, steps, d_ref, w_ref, o_ref, t_ref, l_ref, q_ref, u_ref,
    do_ref, qb_ref, dg_ref, pack_ref, keep_ref, give_ref, whole,
):
    cut = D // 4
    for at in range(4):
        here = slice(at * cut, (at + 1) * cut)
        part = dot(d_ref[:, here], u_ref[...], (0, 0))
        whole[here] = jnp.where(pl.program_id(0) == 0, part, whole[here] + part)

    @pl.when(pl.program_id(0) == steps - 1)
    def sort():
        rows = D // (grps * groups)
        for turn, step, index in slabs(grps, groups):
            target = give_ref.at[turn - 1, step] if turn else keep_ref.at[step]
            target[...] = whole[pl.ds(index * rows, rows)].astype(HALF)

    grad = dot(d_ref[...], w_ref[...])
    count = grad.shape[0]
    lanes = lax.broadcasted_iota(jnp.int32, (count, LANES), 1)
    gates = (t_ref[:, :LANES], t_ref[:, LANES:])
    sums, sent = [], []
    for at in range(2):
        part = grad[:, LANES * at : LANES * (at + 1)]
        attended = o_ref[:, LANES * at : LANES * (at + 1)]
        sig = sigmoid(gates[at])
        low = (part * sig).astype(HALF).astype(FULL)
        sent.append(low)
        dg_ref[:, LANES * at : LANES * (at + 1)] = part * attended * sig * (1.0 - sig)
        sums.append(two(low * attended))
    row = lax.broadcasted_iota(jnp.int32, (LANES, LANES), 0)
    col = lax.broadcasted_iota(jnp.int32, (LANES, LANES), 1)
    of_left = jnp.where(((row < DH) & (col == 0)) | ((row >= DH) & (col == 1)), -1.0, 0.0).astype(HALF)
    of_right = jnp.where((row < DH) & (col == 2), -1.0, 0.0).astype(HALF)
    minus = dot(sums[0][0], of_left) + dot(sums[0][1], of_left) + dot(sums[1][0], of_right) + dot(sums[1][1], of_right)
    logs = jnp.where(lanes < HEADS, -l_ref[...], 0.0)
    packed = side_by_side(three(minus) + three(logs), lanes)
    grads = dot(packed, picker((HEADS * LANES, spread_lanes(0, DH))))
    sinks = dot(packed, picker((HEADS * LANES, spread_lanes(3, DH + 6))))

    def sent_lanes(col):
        head, part = lax.div(col - DH, 6), lax.rem(col - DH, 6)
        return jnp.where((col >= DH) & (col < DH + 6 * HEADS), HEADS * part + head, -1)

    extra = dot(packed, picker((LANES, sent_lanes)))
    heads = [sent[0], pltpu.roll(sent[0], DH, 1), sent[1]]
    for head in range(HEADS):
        here = slice(LANES * head, LANES * (head + 1))
        do_ref[head] = jnp.where(lanes < DH, heads[head], grads[:, here]).astype(HALF)
        qb_ref[head] = (q_ref[head].astype(FULL) + sinks[:, here]).astype(HALF)
    pack_ref[:, :LANES] = sent[0].astype(HALF)
    pack_ref[:, LANES:] = jnp.where(lanes < DH, sent[1], extra).astype(HALF)


def ungate(grads, full, attended, gates, logs, queries, gated, grps, groups):
    own = grads.shape[0]
    steps = own // TALL
    slab = D // (grps * groups)
    head_tile = pl.BlockSpec((HEADS, TALL, LANES), lambda i: (0, i, 0))
    wide_tile = pl.BlockSpec((TALL, OUT), lambda i: (i, 0))
    return pl.pallas_call(
        functools.partial(ungate_kernel, grps, groups, steps),
        grid=(steps,),
        in_specs=[
            pl.BlockSpec((TALL, D), lambda i: (i, 0)),
            weight_spec(OUT, QKVG // OUT),
            wide_tile,
            wide_tile,
            pl.BlockSpec((TALL, LANES), lambda i: (i, 0)),
            head_tile,
            wide_tile,
        ],
        out_specs=(
            head_tile,
            head_tile,
            wide_tile,
            wide_tile,
            whole_spec((groups, slab, OUT)),
            whole_spec((grps - 1, groups, slab, OUT)),
        ),
        out_shape=(
            jax.ShapeDtypeStruct((HEADS, own, LANES), HALF),
            jax.ShapeDtypeStruct((HEADS, own, LANES), HALF),
            jax.ShapeDtypeStruct((own, OUT), FULL),
            jax.ShapeDtypeStruct((own, OUT), HALF),
            jax.ShapeDtypeStruct((groups, slab, OUT), HALF),
            jax.ShapeDtypeStruct((grps - 1, groups, slab, OUT), HALF),
        ),
        scratch_shapes=[pltpu.VMEM((D, OUT), FULL)],
        compiler_params=params(),
        name="ungate",
        cost_estimate=cost(9),
    )(grads, full, attended, gates, logs, queries, gated)


def pieces(scores, product, masked, transposed):
    prob = jnp.exp(scores)
    if masked:
        row = lax.broadcasted_iota(jnp.int32, scores.shape, 0)
        col = lax.broadcasted_iota(jnp.int32, scores.shape, 1)
        keep = row <= col if transposed else col <= row
        prob = jnp.where(keep, prob, 0.0)
    return prob.astype(HALF), (prob * product).astype(HALF)


def home_plan(lines, pairs):
    member = place()[2]
    return [
        lines.plan(source.at[flip(member, bits)], target.at[member], group_device(bits))
        for source, target in pairs
        for bits in range(1, TP)
    ]


def back_kernel(
    grps, groups, q_ref, do_ref, k_ref, v_ref, a_ref, pack_ref, out_ref, up_ref, out_give, up_give, gate_ref, down_ref,
    dq_ref, dk_ref, dv_ref, late_ref, done_ref, up_sum, hgate_ref, hdown_ref,
    others, out_got, up_got, across_out, across_got, send, receive, local,
):
    device, everyone = neighbours(grps, groups)
    call_out(everyone)
    group, member = place()[1:]
    own = q_ref.shape[1]
    count = min(BLOCK, own)
    steps = own // count
    lines = Lines(send, receive)
    halves_of = [pl.ds(at * count, count) for at in range(steps)]
    packs = [
        [lines.plan(pack_ref.at[half], others.at[step - 1, half], device(to_group=groups - step)) for step in range(1, groups)]
        for half in halves_of
    ]
    over = [lines.plan(out_give.at[turn - 1], out_got.at[turn - 1], device(to_grp=turn)) for turn in range(1, grps)]
    over_up = [lines.plan(up_give.at[turn - 1], up_got.at[turn - 1], device(to_grp=turn)) for turn in range(1, grps)]
    across = [
        lines.plan(across_out.at[step - 1], across_got.at[step - 1], device(to_group=step)) for step in range(1, groups)
    ]
    pairs = ((gate_ref, hgate_ref), (down_ref, hdown_ref))
    home = home_plan(lines, pairs)
    kept = [
        pltpu.make_async_copy(source.at[member], target.at[member], local.at[at])
        for at, (source, target) in enumerate(pairs)
    ]
    hear(everyone)
    for copy in packs[0] + over + home + kept + over_up:
        copy.start()
    dk_ref[...] = jnp.zeros_like(dk_ref)
    dv_ref[...] = jnp.zeros_like(dv_ref)
    earliest = (groups - group) * steps
    for head in range(HEADS):
        for at in range(steps):
            here = halves_of[at]
            query, grad = q_ref[head, here], do_ref[head, here]

            def earlier(step, inner):
                there = pl.ds(step * count, count)
                key = k_ref[head, there]
                prob, dscore = pieces(
                    dot(query, key, (1, 1)), dot(grad, v_ref[head, there], (1, 1)), False, False
                )
                return inner + dot(dscore, key)

            dquery = lax.fori_loop(earliest, groups * steps, earlier, jnp.zeros((count, LANES), FULL))
            for step in range(at + 1):
                there = halves_of[step]
                key = k_ref[head, there]
                prob, dscore = pieces(
                    dot(key, query, (1, 1)), dot(v_ref[head, there], grad, (1, 1)), step == at, True
                )
                dk_ref[head, there] += dot(dscore, query)
                dv_ref[head, there] += dot(prob, grad)
                dquery = dquery + dot(dscore, key, (0, 0))
            dq_ref[head, here] = dquery
        if head == 0:
            for copies in packs[1:]:
                for copy in copies:
                    copy.start()
        if head == 1:
            for copy in over:
                copy.wait_recv()
            for step in range(1, groups):
                value = out_ref[step].astype(FULL)
                for turn in range(1, grps):
                    value = value + out_got[turn - 1, step].astype(FULL)
                across_out[step - 1] = value.astype(HALF)
                across[step - 1].start()

    lanes = lax.broadcasted_iota(jnp.int32, (count, LANES), 1)
    late_ref[...] = jnp.zeros_like(late_ref)

    def visit(head, carry, step, at):
        def lanes_from(first, start):
            def find(col):
                part = col - start
                return jnp.where((part >= 0) & (part < 3), DH + 6 * head + first + part, -1)

            return picker((LANES, find))

        minus, logs = lanes_from(0, DH), lanes_from(3, DH + 6)
        sent = others[step - 1, halves_of[at]].astype(FULL)
        left, right = sent[:, :LANES], sent[:, LANES:]
        grad = jnp.where(head == 0, left, jnp.where(head == 1, pltpu.roll(left, DH, 1), right))
        packed = others[step - 1, halves_of[at], LANES:]
        grad = jnp.where(lanes < DH, grad, dot(packed, minus)).astype(HALF)
        query = a_ref[head, pl.ds(step * own + at * count, count)].astype(FULL)
        query = (query + dot(packed, logs)).astype(HALF)
        for there in halves_of:
            prob, dscore = pieces(
                dot(k_ref[head, there], query, (1, 1)), dot(v_ref[head, there], grad, (1, 1)), False, True
            )
            part = dot(dscore, query)
            dk_ref[head, there] += part
            dv_ref[head, there] += dot(prob, grad)
            late_ref[head] += jnp.broadcast_to(jnp.sum(part, axis=0, keepdims=True), (8, LANES))
        return carry

    for at in range(steps):
        for step in range(1, groups):
            packs[at][step - 1].wait_recv()

            @pl.when(step < groups - group)
            def later():
                lax.fori_loop(0, HEADS, functools.partial(visit, step=step, at=at), 0)

    value = out_ref[0].astype(FULL)
    for turn in range(1, grps):
        value = value + out_got[turn - 1, 0].astype(FULL)
    for step in range(1, groups):
        across[step - 1].wait_recv()
        value = value + across_got[step - 1].astype(FULL)
    done_ref[...] = value.astype(HALF)
    value = up_ref[...].astype(FULL)
    for turn in range(1, grps):
        over_up[turn - 1].wait_recv()
        value = value + up_got[turn - 1].astype(FULL)
    up_sum[...] = value.astype(HALF)
    for copy in home:
        copy.wait_recv()
    for copy in kept:
        copy.wait()
    for copy in lines.made:
        copy.wait_send()


def attend_back(queries, grads, keys, values, span_queries, pack, out, up, out_give, up_give, gate, down):
    own, tokens = queries.shape[1], keys.shape[1]
    grps, groups, slab = out_give.shape[0] + 1, out.shape[0], out.shape[1]
    steps = own // min(BLOCK, own)
    count = steps * (groups - 1) + 2 * (grps - 1) + groups - 1 + 2 * (TP - 1)
    vmem, anywhere = pl.BlockSpec(memory_space=pltpu.VMEM), pl.BlockSpec(memory_space=pl.ANY)
    return pl.pallas_call(
        functools.partial(back_kernel, grps, groups),
        in_specs=[vmem] * 5 + [anywhere, vmem, vmem] + [anywhere] * 4,
        out_specs=(vmem,) * 6 + (anywhere,) * 2,
        out_shape=(jax.ShapeDtypeStruct((HEADS, own, LANES), FULL),) * 3
        + (
            jax.ShapeDtypeStruct((HEADS, 8, LANES), FULL),
            jax.ShapeDtypeStruct((slab, OUT), HALF),
            jax.ShapeDtypeStruct(up.shape, HALF),
            jax.ShapeDtypeStruct(gate.shape, HALF),
            jax.ShapeDtypeStruct(down.shape, HALF),
        ),
        scratch_shapes=[
            pltpu.VMEM((groups - 1, own, OUT), HALF),
            pltpu.VMEM(out_give.shape, HALF),
            pltpu.VMEM(up_give.shape, HALF),
            pltpu.VMEM((groups - 1, slab, OUT), HALF),
            pltpu.VMEM((groups - 1, slab, OUT), HALF),
            pltpu.SemaphoreType.DMA((count,)),
            pltpu.SemaphoreType.DMA((count,)),
            pltpu.SemaphoreType.DMA((2,)),
        ],
        compiler_params=params(5),
        name="attend_back",
        cost_estimate=cost(35),
    )(queries, grads, keys, values, span_queries, pack, out, up, out_give, up_give, gate, down)


def unproject_kernel(
    dq_ref, dk_ref, dv_ref, dg_ref, p_ref, z_ref, g_ref, late_ref, dp_ref, dz_ref, gain_ref, bias_ref, carry
):
    @pl.when(pl.program_id(0) == 0)
    def clear():
        carry[0:1] = late_ref[...]
        gain_ref[...] = jnp.zeros_like(gain_ref)
        bias_ref[...] = jnp.zeros_like(bias_ref)

    count = p_ref.shape[0]
    lanes = lax.broadcasted_iota(jnp.int32, (count, LANES), 1)
    sums = jnp.zeros((count, LANES), FULL)
    means = halves_matrix(1.0 / DH)
    gates = [
        pltpu.roll(dg_ref[:, :LANES], DH, 1),
        dg_ref[:, :LANES],
        pltpu.roll(dg_ref[:, LANES:], DH, 1),
    ]
    for head in range(HEADS):
        dquery, dkey = dq_ref[head], dk_ref[head]
        found = pltpu.roll(dquery, DH + head, 1) - pltpu.roll(dkey, DH - 3 + head, 1)
        sums = jnp.where(lanes == head, found, sums)
        grad = jnp.where(lanes < DH, dquery * (DH**-0.5), pltpu.roll(dkey, DH, 1))
        pair = p_ref[:, LANES * head : LANES * (head + 1)]
        inverse = lax.rsqrt(halves_mean(pair * pair, means) + EPS)
        normal = pair * inverse
        scaled = grad * g_ref[head : head + 1]
        gain_ref[head : head + 1] += jnp.sum(grad * normal, axis=0, keepdims=True)
        pulled = inverse * (scaled - normal * halves_mean(scaled * normal, means))
        dp_ref[:, 256 * head : 256 * head + LANES] = pulled.astype(HALF)
        dp_ref[:, 256 * head + LANES : 256 * head + 2 * LANES] = jnp.where(
            lanes < DH, dv_ref[head], gates[head]
        ).astype(HALF)
    row = lax.broadcasted_iota(jnp.int32, (count, count), 0)
    col = lax.broadcasted_iota(jnp.int32, (count, count), 1)
    later = (
        lax.dot_general(
            jnp.where(col >= row, 1.0, 0.0),
            sums,
            (((1,), (0,)), ((), ())),
            precision=lax.Precision.HIGHEST,
            preferred_element_type=FULL,
        )
        + carry[0:1]
    )
    carry[0:1] = later[0:1]
    low = jnp.where(lanes < HEADS, later * sigmoid(-z_ref[...]), 0.0).astype(HALF)
    dz_ref[...] = low
    bias_ref[0:1] += jnp.sum(low.astype(FULL), axis=0, keepdims=True)


def unproject(dqueries, dkeys, dvalues, dgates, pairs, logits, gains, late):
    own = dqueries.shape[1]
    steps = own // TALL

    def back(width):
        return pl.BlockSpec((TALL, width), lambda i: (steps - 1 - i, 0))

    head_tile = pl.BlockSpec((HEADS, TALL, LANES), lambda i: (0, steps - 1 - i, 0))
    small = whole_spec((8, LANES))
    return pl.pallas_call(
        unproject_kernel,
        grid=(steps,),
        in_specs=[
            head_tile,
            head_tile,
            head_tile,
            back(OUT),
            back(HEADS * LANES),
            back(LANES),
            small,
            whole_spec((1, LANES)),
        ],
        out_specs=(back(QKVG), back(LANES), small, small),
        scratch_shapes=[pltpu.VMEM((8, LANES), FULL)],
        out_shape=(
            jax.ShapeDtypeStruct((own, QKVG), HALF),
            jax.ShapeDtypeStruct((own, LANES), HALF),
            jax.ShapeDtypeStruct((8, LANES), FULL),
            jax.ShapeDtypeStruct((8, LANES), FULL),
        ),
        compiler_params=params(),
        name="unproject",
        cost_estimate=cost(9),
    )(dqueries, dkeys, dvalues, dgates, pairs, logits, gains, late)


def across_groups(part, groups):
    size = groups * TP
    return [part] + [
        lax.ppermute(part, "fsdp", [((at + step * TP) % size, at) for at in range(size)])
        for step in range(1, groups)
    ]


def over_grps(parts, grps):
    return [
        [part] + [lax.ppermute(part, "grp", [((at + turn) % grps, at) for at in range(grps)]) for turn in range(1, grps)]
        for part in parts
    ]


def in_order(parts):
    return [turns[turn] for turn in range(len(parts[0])) for turns in parts]


def collected(kept):
    return sum(part.astype(FULL) for part in kept).astype(HALF)


def unpack(grad_ref, near, gate, up, down, out):
    lanes = lax.broadcasted_iota(jnp.int32, (near.shape[1], LANES), 1)

    def half(ref, part, upper):
        member, at, side = part
        value = ref[member, :, at : at + LANES].astype(FULL)
        return pltpu.roll(value, DH, 1) if side != upper else value

    def store(at, ref, lower, upper):
        value = jnp.where(lanes < DH, half(ref, lower, False), half(ref, upper, True))
        grad_ref[:, at : at + LANES] = value.astype(HALF)

    for at in range(0, H, 2):
        for kind in range(4):
            pair = [
                (head // HEADS, 256 * (head % HEADS) + LANES * (kind // 2), kind % 2 == 1) for head in (at, at + 1)
            ]
            store(kind * D + at * DH, near, *pair)
        pair = [
            (head // HEADS, LANES * (head % HEADS // 2), head % HEADS % 2 == 1) for head in (at, at + 1)
        ]
        store(4 * D + at * DH, out, *pair)
    for member in range(TP):
        at = 5 * D + member * UNITS
        grad_ref[:, at : at + UNITS] = gate[member]
        grad_ref[:, at + F : at + F + UNITS] = up[member]
        grad_ref[:, at + 2 * F : at + 2 * F + UNITS] = down[member]


PARTS = 2


def end_counts(grps, groups):
    replicas = grps * groups - 1
    return 7 + PARTS * ((grps - 1) * groups + groups - 1) + 4 * (TP - 1) + replicas


def sort_small(every, gains_ref, forget_ref, bias_ref):
    lanes = lax.broadcasted_iota(jnp.int32, (1, LANES), 1)
    rest = HEADS + 2
    gains_ref[0:2] = jnp.sum(every[:, HEADS : HEADS + 2], axis=0)

    def part(head, kind, upper):
        row = every[head // HEADS, rest : rest + 1]
        return half_lanes(row, (kind * HEADS + head % HEADS) * DH, upper)

    for kind in range(2):
        for head in range(0, H, 2):
            gains_ref[2 + kind : 3 + kind, head * DH : (head + 2) * DH] = jnp.where(
                lanes < DH, part(head, kind, False), part(head + 1, kind, True)
            )
    bias = jnp.zeros((1, LANES), FULL)
    edge = 2 * HEADS * DH
    for member in range(TP):
        forget_ref[member * HEADS : (member + 1) * HEADS] = every[member, :HEADS]
        moved = every[member, rest : rest + 1, edge : edge + LANES]
        if member:
            moved = pltpu.roll(moved, member * HEADS, 1)
        bias = jnp.where((lanes >= member * HEADS) & (lanes < (member + 1) * HEADS), moved, bias)
    bias_ref[...] = jnp.broadcast_to(bias, bias_ref.shape)


def end_kernel(
    grps, groups,
    p_ref, z_ref, f_ref, x_ref, g_ref, d_ref, s_ref, out_ref, up_ref, hgate_ref, hdown_ref, w_ref, t_ref, *rest
):
    y_ref, grad_ref, gains_ref, forget_ref, bias_ref, norm_ref, *rest = rest
    small_ref, hnear_ref, hup_ref, hout_ref, *rest = rest
    weights, tokens, near, mine, give, take, out, came, over_got, across_out, across_got, last, *rest = rest
    packet, packets, send, receive, local = rest
    grp, group, member = place()
    device, everyone = neighbours(grps, groups)
    replicas = [(turn, step) for turn in range(grps) for step in range(groups) if turn or step]
    everyone = everyone + [device(turn, step) for turn, step in replicas if turn and step]
    call_out(everyone)
    count = tokens.shape[0]
    load_tokens = pltpu.make_async_copy(t_ref, tokens, local.at[0])
    load_weights = pltpu.make_async_copy(w_ref.at[:, pl.ds(0, QKVG)], weights, local.at[1])
    load_tokens.start()
    load_weights.start()
    lines = Lines(send, receive)
    stage = (give, take, out, came)
    sums = sum_plan(lines, stage)
    slab = near.shape[0] // (grps * groups)
    part_rows = slab // PARTS
    own = last.shape[2]
    over, across, home = {}, {}, {}

    def rows_of(turn, step, part):
        side = lax.div(member, 4)
        side = side + part - 2 * part * side
        index = lax.rem(grp + turn, grps) * groups + lax.rem(group + step, groups)
        return pl.ds(index * slab + side * part_rows, part_rows)

    order = [(ahead, part) for ahead in list(range(1, groups)) + [0] for part in (1, 0)]
    for ahead, part in order:
        for turn in range(1, grps):
            over[turn, ahead, part] = lines.plan(
                near.at[rows_of(turn, ahead, part)], over_got.at[turn - 1, ahead, part], device(turn)
            )
        if ahead:
            across[ahead, part] = lines.plan(
                across_out.at[ahead - 1, part], across_got.at[ahead - 1, part], device(to_group=ahead)
            )
    for bits in range(1, TP):
        source = last.at[bits // 4, lax.rem(flip(member, bits), 4)]
        home[bits] = lines.plan(source, hnear_ref.at[member], device(bits=bits))
    far = home_plan(lines, ((out_ref, hout_ref), (up_ref, hup_ref)))
    shared = [lines.plan(packet, packets.at[at], device(turn, step)) for at, (turn, step) in enumerate(replicas)]
    told = [lines.plan(small_ref.at[member], small_ref.at[member], device(bits=bits)) for bits in range(1, TP)]

    projected = p_ref[...].reshape(count, QKVG)
    cut = D // 4
    load_tokens.wait()
    for at in range(4):
        here = slice(at * cut, (at + 1) * cut)
        near[here] = dot(tokens[:, here], projected, (0, 0)).astype(HALF)
    hear(everyone)
    for turn in range(1, grps):
        for ahead in range(1, groups):
            over[turn, ahead, 1].start()
    load_weights.wait()
    sum_give([(p_ref, weights), (z_ref, f_ref)], stage, sums, mine)
    summed = sum_pass(stage, sums, mine)
    for part in (1, 0):
        for ahead in range(1, groups):
            if part == 1:
                for turn in range(1, grps):
                    over[turn, ahead, 1].wait_recv()
                    over[turn, ahead, 0].start()
            elif ahead == 1:
                for turn in range(1, grps):
                    for last_part in (1, 0):
                        over[turn, 0, last_part].start()
            total = near[rows_of(0, ahead, part)].astype(FULL)
            for turn in range(1, grps):
                if part == 0:
                    over[turn, ahead, part].wait_recv()
                total = total + over_got[turn - 1, ahead, part].astype(FULL)
            across_out[ahead - 1, part] = total.astype(HALF)
            across[ahead, part].start()
    packet[...] = s_ref[...]
    forget = dot(z_ref[...].reshape(count, LANES), tokens[...], (0, 0))
    packet[0:HEADS] = forget[0:HEADS]

    def square(value):
        value = value.astype(FULL)
        return jnp.sum(value * value)

    squares = square(hgate_ref[...]) + square(hdown_ref[...]) + square(out_ref[...]) + square(up_ref[...])
    summed = sum_take(summed, stage, sums)
    for copy in far:
        copy.start()
    for source, target in ((out_ref, hout_ref), (up_ref, hup_ref)):
        target[member] = source[member]
    pulled, dgain = rms_back(x_ref[...].astype(FULL), g_ref[...], summed)
    y_ref[...] = (d_ref[...] + pulled).astype(HALF)
    packet[HEADS : HEADS + 1] = dgain
    for part in (1, 0):
        total = near[rows_of(0, 0, part)].astype(FULL)
        for turn in range(1, grps):
            over[turn, 0, part].wait_recv()
            total = total + over_got[turn - 1, 0, part].astype(FULL)
        for ahead in range(1, groups):
            across[ahead, part].wait_recv()
            total = total + across_got[ahead - 1, part].astype(FULL)
        squares = squares + square(total)
        for at in range(4):
            last[part, at] = total[at * own : (at + 1) * own].astype(HALF)
        for bits in range(max(4 * part, 1), 4 * part + 4):
            home[bits].start()
    packet[HEADS + 3 : HEADS + 4] = jnp.full((1, D), squares, FULL)
    for copy in shared:
        copy.start()
    hnear_ref[member] = last[0, lax.rem(member, 4)]
    total = packet[...]
    for at, copy in enumerate(shared):
        copy.wait_recv()
        total = total + packets[at]
    small_ref[member] = total
    for copy in told:
        copy.start()
    for copy in far + list(home.values()):
        copy.wait_recv()
    unpack(grad_ref, hnear_ref, hgate_ref, hup_ref, hdown_ref, hout_ref)
    for copy in told:
        copy.wait_recv()
    every = small_ref[...]
    sort_small(every, gains_ref, forget_ref, bias_ref)
    gains = gains_ref[...]
    heads = jnp.sum(every[:, :HEADS] * every[:, :HEADS]) + jnp.sum(gains * gains)
    edge = 2 * HEADS * DH
    heads = heads + jnp.sum(every[:, HEADS + 2, edge : edge + LANES] * every[:, HEADS + 2, edge : edge + LANES])
    matrices = jnp.sum(every[:, HEADS + 3, :LANES], axis=0, keepdims=True)
    norm_ref[...] = jnp.sqrt(jnp.broadcast_to(matrices + heads, (8, LANES)))
    for copy in lines.made:
        copy.wait_send()


def end(projected, logits, forget, source, gain, grad, small, out, up, gate, down, near, tokens, grps, groups):
    rows, own = source.shape[0], gate.shape[1]
    count = end_counts(grps, groups)
    replicas = grps * groups - 1
    slab = TP * own
    part = (slab // PARTS, QKVG)
    vmem, anywhere = pl.BlockSpec(memory_space=pltpu.VMEM), pl.BlockSpec(memory_space=pl.ANY)
    return pl.pallas_call(
        functools.partial(end_kernel, grps, groups),
        out_shape=(
            jax.ShapeDtypeStruct((rows, D), HALF),
            jax.ShapeDtypeStruct((own, 5 * D + 3 * F), HALF),
            jax.ShapeDtypeStruct((4, D), FULL),
            jax.ShapeDtypeStruct((H, D), FULL),
            jax.ShapeDtypeStruct((8, LANES), FULL),
            jax.ShapeDtypeStruct((8, LANES), FULL),
        ),
        in_specs=[vmem] * 11 + [anywhere] * 2,
        out_specs=(vmem,) * 6,
        scratch_shapes=[
            pltpu.VMEM((TP, 8, D), FULL),
            pltpu.VMEM((TP, own, QKVG), HALF),
            pltpu.VMEM((TP, own, UNITS), HALF),
            pltpu.VMEM((TP, own, OUT), HALF),
            pltpu.VMEM((D, QKVG), HALF),
            pltpu.VMEM((TP * rows, D), HALF),
            pltpu.VMEM((D, QKVG), HALF),
            pltpu.VMEM((4, rows, D), FULL),
        ]
        + sum_scratch(rows)
        + [
            pltpu.VMEM((grps - 1, groups, PARTS) + part, HALF),
            pltpu.VMEM((groups - 1, PARTS) + part, HALF),
            pltpu.VMEM((groups - 1, PARTS) + part, HALF),
            pltpu.VMEM((PARTS, 4, own, QKVG), HALF),
            pltpu.VMEM((8, D), FULL),
            pltpu.VMEM((replicas, 8, D), FULL),
            pltpu.SemaphoreType.DMA((count,)),
            pltpu.SemaphoreType.DMA((count,)),
            pltpu.SemaphoreType.DMA((2,)),
        ],
        compiler_params=params(4),
        name="end",
        cost_estimate=cost(60),
    )(
        projected.reshape(4, 2, rows, QKVG),
        logits.reshape(4, 2, rows, LANES),
        forget,
        source,
        gain,
        grad,
        small,
        out,
        up,
        gate,
        down,
        near,
        tokens,
    )


def adam(value, first, second, grad, rate, decay):
    first = BETA_ONE * first + (1.0 - BETA_ONE) * grad
    second = BETA_TWO * second + (1.0 - BETA_TWO) * grad * grad
    unbiased_first = first * (1.0 / (1.0 - BETA_ONE**STEP))
    unbiased_second = second * (1.0 / (1.0 - BETA_TWO**STEP))
    value = value - rate * (unbiased_first / (jnp.sqrt(unbiased_second) + ADAM_EPS) + decay * value)
    return (value, first, second)


def update_kernel(norm_ref, w_ref, m_ref, v_ref, g_ref, nw_ref, nm_ref, nv_ref):
    factor = CLIP / jnp.maximum(norm_ref[0:1, 0:1], CLIP)
    new = adam(w_ref[...], m_ref[...], v_ref[...], g_ref[...].astype(FULL) * factor, RATE_MATRIX, DECAY)
    nw_ref[...], nm_ref[...], nv_ref[...] = new


def update(norm, weights, first, second, grads):
    own, width = weights.shape
    rows = 8 if own % 8 == 0 else own
    tile = pl.BlockSpec((rows, width), lambda i: (i, 0))
    return pl.pallas_call(
        update_kernel,
        grid=(own // rows,),
        out_shape=(jax.ShapeDtypeStruct((own, width), FULL),) * 3,
        in_specs=[whole_spec((8, LANES)), tile, tile, tile, tile],
        out_specs=(tile,) * 3,
        compiler_params=params(),
        name="update",
        cost_estimate=cost(9),
    )(norm, weights, first, second, grads)


def pad_lanes(value, width=LANES):
    return jnp.pad(value, ((0, 0), (0, width - value.shape[1])))


def shards(
    inputs,
    cotangent,
    weights,
    weights_first,
    weights_second,
    gains,
    gains_first,
    gains_second,
    forget_weight,
    forget_first,
    forget_second,
    forget_bias,
    bias_first,
    bias_second,
):
    grps, groups = lax.axis_size("grp"), lax.axis_size("fsdp") // TP
    grp, group, member = place()
    rows, own_rows = inputs.shape[1], weights.shape[0]
    group_tokens = TP * rows
    source, returned = inputs[0], cotangent[0]

    tokens, following, near, both, down = start(source, gains[0:1], weights, grps, groups)
    slab = TP * own_rows
    both, down = both.reshape(slab, 2 * UNITS), down.reshape(slab, UNITS)
    tokens = tokens.reshape(group_tokens, D)
    near = near.reshape(D, NEAR)
    both_parts = across_groups(both, groups)
    both_own, down_own = over_grps(both_parts[:1], grps), over_grps([down], grps)

    forget_low = pad_lanes(lax.dynamic_slice_in_dim(forget_weight, member * HEADS, HEADS, 1).astype(HALF))
    bias = pad_lanes(lax.dynamic_slice_in_dim(forget_bias[None], member * HEADS, HEADS, 1))
    head_gains = lax.dynamic_slice_in_dim(gains[2:4], member * HEADS * DH, HEADS * DH, 1)
    head_gains = head_gains.reshape(2, HEADS, DH).transpose(1, 0, 2).reshape(HEADS, 2 * DH)
    head_gains = jnp.pad(head_gains, ((0, 8 - HEADS), (0, 0)))
    queries, keys, values, pairs, gates, logits, gathered = project(
        tokens, following, near, forget_low, bias, head_gains, returned
    )
    queries, down = lax.optimization_barrier((queries, down))
    down_parts = across_groups(down, groups)
    gated, attended, logs, gathered = attend(queries, keys, values, gates, gathered, groups)
    returned_all = gathered.reshape(group_tokens, D)
    gated, both_parts, down_parts = lax.optimization_barrier((gated, both_parts[1:], down_parts[1:]))
    both_pieces = in_order(both_own + over_grps(both_parts, grps))
    down_pieces = in_order(down_own + over_grps(down_parts, grps))
    mixed, second = mix(gated, near, source, gains[1:2])
    second = second.reshape(group_tokens, D)
    hidden, grad_both = feed(second, returned_all, both_pieces, down_pieces, grps, groups)
    grad_mixed, grad_gain_mid, branch, out_sums, far_gate, far_down, up_give, *far_up = unmix(
        grad_both, both_pieces, down_pieces, mixed, gains[1:2], returned, hidden, second, returned_all, grps, groups
    )
    branch = branch.reshape(group_tokens, D)
    size = lax.axis_size("fsdp")
    up_keep = far_up[0]
    far_up = [
        lax.ppermute(far_up[step], "fsdp", [(at, (at + step * TP) % size) for at in range(size)])
        for step in range(1, groups)
    ]

    grads_low, queries_back, grad_gates, pack, out_keep, out_give = ungate(
        branch, near, attended, gates, logs, queries, gated, grps, groups
    )
    dqueries, dkeys, dvalues, late, far_out, up_sum, home_gate, home_down = attend_back(
        queries_back,
        grads_low,
        keys,
        values,
        queries,
        pack,
        out_keep,
        up_keep,
        out_give,
        up_give,
        far_gate.reshape(TP, own_rows, UNITS),
        far_down.reshape(TP, own_rows, UNITS),
    )
    later = pad_lanes(late[:, 0, DH + 3][None])
    if groups > 2:
        everyone = lax.all_gather(dkeys[:, :, DH + 3].sum(axis=1) - dqueries[:, :, DH].sum(axis=1), "fsdp")
        ahead = (jnp.arange(size) // TP > group) & (jnp.arange(size) % TP == member)
        later = pad_lanes(-jnp.sum(jnp.where(ahead[:, None], everyone, 0.0), axis=0)[None])
    grad_projected, grad_logits, grad_heads, grad_bias = unproject(
        dqueries, dkeys, dvalues, grad_gates, pairs, logits, head_gains, later
    )

    grad_heads = grad_heads[:HEADS].reshape(HEADS, 2, DH).transpose(1, 0, 2).reshape(1, 2 * HEADS * DH)
    rest = jnp.concatenate([grad_heads, grad_bias[0:1, :HEADS]], axis=1)
    small = jnp.concatenate(
        [jnp.zeros((HEADS + 1, D), FULL), grad_gain_mid, pad_lanes(rest, D), jnp.zeros((2, D), FULL)], axis=0
    )
    input_grad, grads, grad_gains, grad_forget, grad_bias, norm = end(
        grad_projected,
        grad_logits,
        forget_low,
        source,
        gains[0:1],
        grad_mixed,
        small,
        far_out.reshape(TP, own_rows, OUT),
        collected([up_sum] + far_up).reshape(TP, own_rows, UNITS),
        home_gate,
        home_down,
        near,
        tokens,
        grps,
        groups,
    )
    norm, out_sums = lax.optimization_barrier((norm, out_sums))
    result = mixed + out_sums[3].astype(FULL)
    for at, bits in enumerate((2, 4, 6)):
        result = result + lax.ppermute(out_sums[at], "fsdp", [(to, to ^ bits) for to in range(size)]).astype(FULL)
    output = result.astype(HALF)
    grad_norm = norm[0, 0]
    grad_forget, grad_bias = grad_forget.T, grad_bias[0, :H]
    factor = CLIP / jnp.maximum(grad_norm, CLIP)
    new_w, new_wf, new_ws = update(norm, weights, weights_first, weights_second, grads)
    new_g, new_gf, new_gs = adam(gains, gains_first, gains_second, grad_gains * factor, RATE_GAIN, 0.0)
    new_fw, new_ff, new_fs = adam(
        forget_weight, forget_first, forget_second, grad_forget * factor, RATE_MATRIX, DECAY
    )
    new_fb, new_bf, new_bs = adam(
        forget_bias, bias_first, bias_second, grad_bias * factor, RATE_BIAS, 0.0
    )
    return (
        output[None],
        input_grad[None],
        grad_norm,
        new_w,
        new_wf,
        new_ws,
        new_g,
        new_gf,
        new_gs,
        new_fw,
        new_ff,
        new_fs,
        new_fb,
        new_bf,
        new_bs,
    )


def solution(mesh):
    tokens = P("grp", "fsdp", None)
    matrix = P(("grp", "fsdp"), None)
    return jax.shard_map(
        shards,
        mesh=mesh,
        in_specs=(tokens,) * 2 + (matrix,) * 3 + (P(),) * 9,
        out_specs=(tokens,) * 2 + (P(),) + (matrix,) * 3 + (P(),) * 9,
        check_vma=False,
    )
```

```python
import functools

import jax
import jax.numpy as jnp
from jax import lax
from jax.experimental import pallas as pl
from jax.experimental.pallas import tpu as pltpu
from jax.sharding import PartitionSpec as P

D = 1536
H = 24
DH = 64
F = 4096
STEP = 5

EPS = 1e-06
BETA_ONE = 0.9
BETA_TWO = 0.95
ADAM_EPS = 1e-08
RATE_MATRIX = 0.1
RATE_GAIN = 1.2
RATE_BIAS = 3.0
DECAY = 0.1
CLIP = 1.0
NEGATIVE = -1e30

TP = 8
HEADS = H // TP
UNITS = F // TP
QKVG = HEADS * 4 * DH
OUT = 256
NEAR = QKVG + OUT
LANES = 128
ROWS = 256
TALL = 512
BLOCK = 512
MESH = pl.DeviceIdType.MESH
HALF = jnp.bfloat16
FULL = jnp.float32
VMEM_BYTES = 56 * 1024 * 1024


def params(collective=None, **more):
    if collective is None:
        return pltpu.CompilerParams(vmem_limit_bytes=VMEM_BYTES, **more)
    return pltpu.CompilerParams(
        collective_id=collective, has_side_effects=True, vmem_limit_bytes=VMEM_BYTES, **more
    )


def flip(member, bits):
    for bit in (1, 2, 4):
        if bits & bit:
            member = member + bit - 2 * bit * lax.rem(lax.div(member, bit), 2)
    return member


def place():
    position = lax.axis_index("fsdp")
    return lax.axis_index("grp"), lax.div(position, TP), lax.rem(position, TP)


def cost(micros):
    return pl.CostEstimate(flops=0, bytes_accessed=3_000_000 * micros, transcendentals=0)


def call_out(targets):
    barrier = pltpu.get_barrier_semaphore()
    for target in targets:
        pl.semaphore_signal(barrier, inc=1, device_id=target, device_id_type=MESH)


def hear(targets):
    pl.semaphore_wait(pltpu.get_barrier_semaphore(), len(targets))


def greet(targets):
    call_out(targets)
    hear(targets)


def neighbours(grps, groups):
    grp, group, member = place()

    def device(to_grp=0, to_group=0, bits=0):
        return (
            lax.rem(grp + to_grp, grps),
            lax.rem(group + to_group, groups) * TP + flip(member, bits),
        )

    return device, (
        [device(bits=bits) for bits in range(1, TP)]
        + [device(to_group=step) for step in range(1, groups)]
        + [device(to_grp=step) for step in range(1, grps)]
    )


class Lines:
    def __init__(self, send, receive):
        self.send, self.receive, self.count, self.made = send, receive, 0, []

    def plan(self, source, target, device):
        copy = pltpu.make_async_remote_copy(
            src_ref=source,
            dst_ref=target,
            send_sem=self.send.at[self.count],
            recv_sem=self.receive.at[self.count],
            device_id=device,
            device_id_type=MESH,
        )
        self.count += 1
        self.made.append(copy)
        return copy


def dot(left, right, contract=(1, 0)):
    return lax.dot_general(
        left, right, (((contract[0],), (contract[1],)), ((), ())), preferred_element_type=FULL
    )


def rms_rows(value, gain):
    return value * lax.rsqrt(jnp.mean(value * value, axis=-1, keepdims=True) + EPS) * gain


def rms_back(value, gain, grad):
    inverse = lax.rsqrt(jnp.mean(value * value, axis=-1, keepdims=True) + EPS)
    normal = value * inverse
    scaled = grad * gain
    pulled = inverse * (scaled - normal * jnp.mean(scaled * normal, axis=-1, keepdims=True))
    return pulled, jnp.sum(grad * normal, axis=0, keepdims=True)


def half_lanes(value, column, upper):
    base = column // LANES * LANES
    part = value[:, base : base + LANES]
    if (column % LANES != 0) != upper:
        part = pltpu.roll(part, DH, 1)
    return part


def two_halves(value, lower, upper, lanes):
    low = half_lanes(value, lower, False)
    if upper is None:
        return jnp.where(lanes < DH, low, 0.0)
    return jnp.where(lanes < DH, low, half_lanes(value, upper, True))


def pack_near(w_ref, near):
    lanes = lax.broadcasted_iota(jnp.int32, (w_ref.shape[0], LANES), 1)
    for member in range(TP):
        for head in range(HEADS):
            at = (member * HEADS + head) * DH
            near[member, :, 256 * head : 256 * head + LANES] = two_halves(w_ref, at, D + at, lanes).astype(HALF)
            near[member, :, 256 * head + LANES : 256 * head + 256] = two_halves(
                w_ref, 2 * D + at, 3 * D + at, lanes
            ).astype(HALF)
        at = 4 * D + member * HEADS * DH
        near[member, :, QKVG : QKVG + LANES] = two_halves(w_ref, at, at + DH, lanes).astype(HALF)
        near[member, :, QKVG + LANES :] = two_halves(w_ref, at + 2 * DH, None, lanes).astype(HALF)


def pack_far(w_ref, both, down):
    edge = 5 * D
    for member in range(TP):
        at = edge + member * UNITS
        both[member, :, :UNITS] = w_ref[:, at : at + UNITS].astype(HALF)
        both[member, :, UNITS:] = w_ref[:, at + F : at + F + UNITS].astype(HALF)
        down[member] = w_ref[:, at + 2 * F : at + 2 * F + UNITS].astype(HALF)


def halves(ref):
    count = ref.shape[0] // 2
    return [ref.at[pl.ds(at * count, count)] for at in range(2)]


def halves(ref):
    count = ref.shape[0] // 2
    return [ref.at[pl.ds(at * count, count)] for at in range(2)]


def start_counts(grps, groups):
    weights = (TP - 1) + (groups - 1) * TP + (grps - 1) * groups * TP
    return GATHER + 2 * (groups - 1) + weights + 2 * (TP - 1)


def start_kernel(
    grps, groups, x_ref, g_ref, w_ref, all_ref, next_ref, full_ref, both_ref, down_ref,
    block, near, both, down, send, receive, local,
):
    grp, group, member = place()
    device, everyone = neighbours(grps, groups)
    call_out(everyone)
    block[...] = rms_rows(x_ref[...].astype(FULL), g_ref[...]).astype(HALF)
    lines = Lines(send, receive)
    first, across, over, far = {}, {}, {}, []
    tokens = gather_plan(lines, block, all_ref, True)
    ahead, aside = [], []
    for back in range(1, groups):
        ahead.append(lines.plan(block, next_ref.at[back - 1, 0], device(to_group=groups - back)))
        aside.append(lines.plan(next_ref.at[back - 1, 0], next_ref.at[back - 1, 1], device(bits=4)))
    for bits in range(1, TP):
        first[bits] = lines.plan(near.at[flip(member, bits)], full_ref.at[grp, group, member], device(bits=bits))
    for bits in range(TP):
        slot = full_ref.at[grp, group, flip(member, bits)]
        source = near.at[member] if bits == 0 else slot
        for back in range(1, groups):
            across[back, bits] = lines.plan(source, slot, device(to_group=groups - back))
        for step in range(1, grps):
            over[step, 0, bits] = lines.plan(source, slot, device(to_grp=step))
        for back in range(1, groups):
            passed = full_ref.at[grp, lax.rem(group + back, groups), flip(member, bits)]
            for step in range(1, grps):
                over[step, back, bits] = lines.plan(passed, passed, device(to_grp=step))
    for bits in range(1, TP):
        there = flip(member, bits)
        far.append(lines.plan(both.at[there], both_ref.at[member], device(bits=bits)))
        far.append(lines.plan(down.at[there], down_ref.at[member], device(bits=bits)))

    own_tokens = pltpu.make_async_copy(block, all_ref.at[member], local.at[0])
    own = [
        pltpu.make_async_copy(near.at[member], full_ref.at[grp, group, member], local.at[1]),
        pltpu.make_async_copy(both.at[member], both_ref.at[member], local.at[2]),
        pltpu.make_async_copy(down.at[member], down_ref.at[member], local.at[3]),
    ]
    hear(everyone)
    for copy in ahead:
        copy.start()
    pack_near(w_ref, near)
    for bits in (4, 2, 6, 1, 5, 3, 7):
        first[bits].start()
    for back in range(1, groups):
        across[back, 0].start()
    for step in range(1, grps):
        over[step, 0, 0].start()
    gather_start(tokens, own_tokens)
    own[0].start()
    pack_far(w_ref, both, down)
    for bits in (1, 5, 3, 7, 2, 4, 6):
        first[bits].wait_recv()
        for back in range(1, groups):
            across[back, bits].start()
        for step in range(1, grps):
            over[step, 0, bits].start()
    gather_turn(tokens, True)
    for copy in far:
        copy.start()
    for copy in own[1:]:
        copy.start()
    for come, gone in zip(ahead, aside):
        come.wait_recv()
        gone.start()
    gather_pass(tokens, True)
    for back in range(1, groups):
        for bits in (0, 1, 5, 3, 7, 2, 4, 6):
            across[back, bits].wait_recv()
            for step in range(1, grps):
                over[step, back, bits].start()
    gather_end(tokens, own_tokens)
    for copy in aside + far + list(over.values()):
        copy.wait_recv()
    for copy in lines.made:
        copy.wait_send()
    for copy in own:
        copy.wait()


def start(source, gain, weights, grps, groups):
    rows, own = source.shape[0], weights.shape[0]
    count = start_counts(grps, groups)
    vmem, anywhere = pl.BlockSpec(memory_space=pltpu.VMEM), pl.BlockSpec(memory_space=pl.ANY)
    return pl.pallas_call(
        functools.partial(start_kernel, grps, groups),
        out_shape=(
            jax.ShapeDtypeStruct((TP, rows, D), HALF),
            jax.ShapeDtypeStruct((groups - 1, 2, rows, D), HALF),
            jax.ShapeDtypeStruct((grps, groups, TP, own, NEAR), HALF),
            jax.ShapeDtypeStruct((TP, own, 2 * UNITS), HALF),
            jax.ShapeDtypeStruct((TP, own, UNITS), HALF),
        ),
        in_specs=[vmem] * 3,
        out_specs=(anywhere,) * 5,
        scratch_shapes=[
            pltpu.VMEM((rows, D), HALF),
            pltpu.VMEM((TP, own, NEAR), HALF),
            pltpu.VMEM((TP, own, 2 * UNITS), HALF),
            pltpu.VMEM((TP, own, UNITS), HALF),
            pltpu.SemaphoreType.DMA((count,)),
            pltpu.SemaphoreType.DMA((count,)),
            pltpu.SemaphoreType.DMA((4,)),
        ],
        compiler_params=params(1),
        name="start",
        cost_estimate=cost(60),
    )(source, gain, weights)


def three(value):
    high = value.astype(HALF).astype(FULL)
    rest = value - high
    middle = rest.astype(HALF).astype(FULL)
    return high, middle, (rest - middle).astype(HALF).astype(FULL)


def two(value):
    high = value.astype(HALF)
    return high, (value - high.astype(FULL)).astype(HALF)


def at_lanes(lanes, pairs, other):
    for lane, value in pairs:
        other = jnp.where(lanes == lane, value, other)
    return other


def side_by_side(values, lanes):
    packed = jnp.zeros_like(values[0])
    for at, value in enumerate(values):
        if at:
            value = pltpu.roll(value, HEADS * at, 1)
        packed = jnp.where((lanes >= HEADS * at) & (lanes < HEADS * (at + 1)), value, packed)
    return packed.astype(HALF)


def picker(targets):
    def build(width, find, sign=1.0):
        row = lax.broadcasted_iota(jnp.int32, (LANES, width), 0)
        col = lax.broadcasted_iota(jnp.int32, (LANES, width), 1)
        return jnp.where(row == find(col), sign, 0.0).astype(HALF)

    return build(*targets)


def spread_lanes(first, at):
    def find(col):
        head, lane = lax.div(col, LANES), lax.rem(col, LANES) - at
        return jnp.where((lane >= 0) & (lane < 3), HEADS * (first + lane) + head, -1)

    return find


def halves_matrix(scale):
    row = lax.broadcasted_iota(jnp.int32, (LANES, LANES), 0)
    col = lax.broadcasted_iota(jnp.int32, (LANES, LANES), 1)
    return jnp.where((row < DH) == (col < DH), scale, 0.0).astype(HALF)


def halves_mean(value, matrix):
    high, least = two(value)
    return dot(high, matrix) + dot(least, matrix)


def side_plan(lines, pair_ref, all_ref):
    member = place()[2]
    plan = {}
    for at, bits in ((0, 0), (1, 4)):
        there = flip(member, bits)
        plan[bits + 2] = lines.plan(pair_ref.at[at], all_ref.at[there], group_device(2))
        plan[bits + 1] = lines.plan(pair_ref.at[at], all_ref.at[there], group_device(1))
    for bits in (2, 6):
        slot = all_ref.at[flip(member, bits)]
        plan[bits + 1] = lines.plan(slot, slot, group_device(1))
    return plan


def first_leg(lines, block, all_ref):
    member = place()[2]
    return {bits: lines.plan(block, all_ref.at[member], group_device(bits)) for bits in (2, 4)}


def third_leg(lines, all_ref):
    member = place()[2]

    def copy(block, bits):
        slot = all_ref.at[flip(member, block)]
        return lines.plan(slot, slot, group_device(bits))

    return {6: copy(4, 2), 1: copy(0, 1), 3: copy(2, 1), 5: copy(4, 1), 7: copy(6, 1)}


def project_kernel(
    groups, a_ref, n_ref, w_ref, f_ref, b_ref, g_ref, c_ref,
    q_ref, k_ref, v_ref, p_ref, t_ref, z_ref, all_ref, others, decays, totals, send, receive, local,
):
    turn = pl.program_id(0)
    grp, group, member = place()
    own = a_ref.shape[0]
    rows = own // TP
    lanes = lax.broadcasted_iota(jnp.int32, (TALL, LANES), 1)

    def plans():
        lines = Lines(send, receive)
        sides = [side_plan(lines, n_ref.at[at], others.at[at]) for at in range(groups - 1)]
        copies = [
            pltpu.make_async_copy(n_ref.at[at, half], others.at[at, flip(member, 4 * half)], local.at[2 * at + half])
            for at in range(groups - 1)
            for half in range(2)
        ]
        copies.append(pltpu.make_async_copy(c_ref, all_ref.at[member], local.at[2 * groups - 2]))
        return lines, sides, copies, first_leg(lines, c_ref, all_ref)

    def low_rows(index, start, count):
        if index == 0:
            return a_ref[start : start + count]
        return others[index - 1, start // rows : (start + count) // rows].reshape(count, D)

    def scan(index):
        row = lax.broadcasted_iota(jnp.int32, (ROWS, ROWS), 0)
        col = lax.broadcasted_iota(jnp.int32, (ROWS, ROWS), 1)
        lower = jnp.where(col <= row, 1.0, 0.0)
        carry = jnp.zeros((1, LANES), FULL)
        for start in range(0, own, ROWS):
            logit = dot(low_rows(index, start, ROWS), f_ref[...]) + b_ref[...]
            if index == 0:
                z_ref[start : start + ROWS] = logit
            log_gate = jnp.minimum(logit, 0.0) - jnp.log1p(jnp.exp(-jnp.abs(logit)))
            part = carry + lax.dot_general(
                lower,
                log_gate,
                (((1,), (0,)), ((), ())),
                precision=lax.Precision.HIGHEST,
                preferred_element_type=FULL,
            )
            decays[index, start : start + ROWS] = part
            carry = part[ROWS - 1 : ROWS]
        totals[index : index + 1] = carry

    def rows_done(low, sums, start, first):
        here = slice(start, start + TALL)
        made = dot(low, w_ref[...])
        means = halves_matrix(1.0 / DH)
        packed = side_by_side(three(jnp.where(lanes < HEADS, sums, 0.0)), lanes)
        plus = dot(packed, picker((HEADS * LANES, spread_lanes(0, DH))))
        minus = dot(packed, picker((HEADS * LANES, spread_lanes(0, DH + 3), -1.0)))
        ones_of_query = jnp.where((lanes >= DH + 3) & (lanes < DH + 6), 1.0, 0.0)
        ones_of_value = jnp.where((lanes >= DH) & (lanes < DH + 3), 1.0, 0.0)
        ones_of_key = jnp.where((lanes >= DH + 6) & (lanes < DH + 9), 1.0, ones_of_value)
        for head in range(HEADS):
            register = slice(LANES * head, LANES * (head + 1))
            pair = made[:, 256 * head : 256 * head + LANES]
            value = made[:, 256 * head + LANES : 256 * head + 2 * LANES]
            normal = pair * lax.rsqrt(halves_mean(pair * pair, means) + EPS) * g_ref[head : head + 1]
            normal = normal.astype(HALF).astype(FULL)
            q_ref[head, here] = jnp.where(
                lanes < DH, normal * (DH**-0.5), plus[:, register] + ones_of_query
            ).astype(HALF)
            k_ref[head, here] = jnp.where(
                lanes < DH, pltpu.roll(normal, DH, 1), minus[:, register] + ones_of_key
            ).astype(HALF)
            v_ref[head, here] = jnp.where(lanes < DH, value, ones_of_value).astype(HALF)
            if first:
                p_ref[here, register] = pair
        if first:
            left, right = gates_of(made, lanes)
            t_ref[here, :LANES] = left
            t_ref[here, LANES:] = right

    @pl.when(turn == 0)
    def begin():
        greet([group_device(bits) for bits in (4, 2, 1)])
        lines, sides, copies, leg = plans()
        for copy in copies:
            copy.start()
        for side in sides:
            for bits in (2, 6, 1, 5):
                side[bits].start()
        leg[4].start()
        scan(0)
        for start in range(0, own, TALL):
            rows_done(low_rows(0, start, TALL), decays[0, start : start + TALL], start, True)
        leg[2].start()
        for side in sides:
            for bits in (2, 6):
                side[bits].wait_recv()
                side[bits + 1].start()

    @pl.when(turn == 1)
    def arrived():
        lines, sides, copies, leg = plans()
        for copy in copies[:-1]:
            copy.wait()
        for side in sides:
            for bits in (1, 3, 5, 7):
                side[bits].wait_recv()
        for index in range(1, groups):
            scan(index)

    @pl.when(turn > 0)
    def next_group():
        ahead = turn < groups - group
        base = jnp.zeros((1, LANES), FULL)
        for index in range(groups):
            weight = jnp.where(ahead, jnp.where(index < turn, 1.0, 0.0), jnp.where(index >= turn, -1.0, 0.0))
            base = base + weight * totals[index : index + 1]
        for start in range(0, own, TALL):
            low = others[turn - 1, start // rows : (start + TALL) // rows].reshape(TALL, D)
            rows_done(low, decays[turn, start : start + TALL] + base, start, False)

    @pl.when(turn == groups - 1)
    def end():
        lines, sides, copies, leg = plans()
        copies[-1].wait()
        for copy in leg.values():
            copy.wait_recv()
        for copy in lines.made:
            copy.wait_send()


def project(tokens, following, full, forget, bias, gains, returned):
    own, groups = tokens.shape[0], following.shape[0] + 1
    rows = returned.shape[0]
    count = 6 * (groups - 1) + 2
    tile = pl.BlockSpec((HEADS, own, LANES), lambda i: (0, i, 0))
    anywhere = pl.BlockSpec(memory_space=pl.ANY)
    return pl.pallas_call(
        functools.partial(project_kernel, groups),
        grid=(groups,),
        out_shape=(
            jax.ShapeDtypeStruct((HEADS, groups * own, LANES), HALF),
            jax.ShapeDtypeStruct((HEADS, groups * own, LANES), HALF),
            jax.ShapeDtypeStruct((HEADS, groups * own, LANES), HALF),
            jax.ShapeDtypeStruct((own, HEADS * LANES), FULL),
            jax.ShapeDtypeStruct((own, OUT), FULL),
            jax.ShapeDtypeStruct((own, LANES), FULL),
            jax.ShapeDtypeStruct((TP, rows, D), HALF),
        ),
        in_specs=[
            whole_spec((own, D)),
            anywhere,
            weight_spec(QKVG, 0),
            whole_spec((D, LANES)),
            whole_spec((1, LANES)),
            whole_spec((8, LANES)),
            whole_spec((rows, D)),
        ],
        out_specs=(
            tile,
            tile,
            tile,
            whole_spec((own, HEADS * LANES)),
            whole_spec((own, OUT)),
            whole_spec((own, LANES)),
            anywhere,
        ),
        scratch_shapes=[
            pltpu.VMEM((groups - 1, TP, rows, D), HALF),
            pltpu.VMEM((groups, own, LANES), FULL),
            pltpu.VMEM((max(groups, 8), LANES), FULL),
            pltpu.SemaphoreType.DMA((count,)),
            pltpu.SemaphoreType.DMA((count,)),
            pltpu.SemaphoreType.DMA((2 * groups - 1,)),
        ],
        compiler_params=params(8),
        name="project",
        cost_estimate=cost(25),
    )(tokens, following, full, forget, bias, gains, returned)


def sigmoid(value):
    return 1.0 / (1.0 + jnp.exp(-value))


def gates_of(made, lanes):
    second = [made[:, 256 * head + LANES : 256 * head + 2 * LANES] for head in range(HEADS)]
    left = jnp.where(lanes < DH, pltpu.roll(second[0], DH, 1), second[1])
    right = jnp.where(lanes < DH, pltpu.roll(second[2], DH, 1), 0.0)
    return left, right


def attend_kernel(
    groups, steps, q_ref, k_ref, v_ref, t_ref, c_ref, u_ref, o_ref, l_ref, all_ref, send, receive
):
    count = u_ref.shape[0]
    at_step = pl.program_id(0)

    @pl.when(at_step == 0)
    def begin():
        greet([group_device(bits) for bits in (2, 1)])
        plan = third_leg(Lines(send, receive), all_ref)
        for bits in (6, 1, 3, 5):
            plan[bits].start()

    @pl.when(at_step == steps - 1)
    def pass_on():
        plan = third_leg(Lines(send, receive), all_ref)
        plan[6].wait_recv()
        plan[7].start()

    queries = [q_ref[head] for head in range(HEADS)]

    def visit(state, at, masked):
        new = []
        for head in range(HEADS):
            top, accum = state[head]
            scores = dot(queries[head], k_ref[head, pl.ds(at * count, count)], (1, 1))
            if masked:
                row = lax.broadcasted_iota(jnp.int32, scores.shape, 0)
                col = lax.broadcasted_iota(jnp.int32, scores.shape, 1)
                scores = jnp.where(col <= row, scores, NEGATIVE)
            high = jnp.maximum(top, jnp.max(scores, axis=1, keepdims=True))
            weight = jnp.exp(scores - high)
            accum = accum * jnp.exp(top - high) + dot(weight.astype(HALF), v_ref[head, pl.ds(at * count, count)])
            new.append((high, accum))
        return tuple(new)

    state = tuple(
        (jnp.full((count, 1), NEGATIVE, FULL), jnp.zeros((count, LANES), FULL)) for head in range(HEADS)
    )
    earlier = (groups - place()[1]) * steps
    state = lax.fori_loop(earlier, groups * steps, lambda at, inner: visit(inner, at, False), state)
    state = lax.fori_loop(0, at_step, lambda at, inner: visit(inner, at, False), state)
    state = visit(state, at_step, True)
    lanes = lax.broadcasted_iota(jnp.int32, (count, LANES), 1)
    out, logs = [], []
    for top, accum in state:
        total = jnp.sum(jnp.where(lanes == DH, accum, 0.0), axis=1, keepdims=True)
        out.append(jnp.where(lanes < DH, accum / total, 0.0))
        logs.append(top + jnp.log(total))
    left, right = t_ref[:, :LANES], t_ref[:, LANES:]
    pair = out[0] + pltpu.roll(out[1], DH, 1)
    o_ref[:, :LANES] = pair
    o_ref[:, LANES:] = out[2]
    u_ref[:, :LANES] = (pair * sigmoid(left)).astype(HALF)
    u_ref[:, LANES:] = (out[2] * sigmoid(right)).astype(HALF)
    l_ref[...] = at_lanes(lanes, tuple(enumerate(logs)), 0.0)

    @pl.when(at_step == steps - 1)
    def end():
        plan = third_leg(Lines(send, receive), all_ref)
        for bits in (1, 3, 5, 7):
            plan[bits].wait_recv()
        for copy in plan.values():
            copy.wait_send()


def attend(queries, keys, values, gates, gathered, groups):
    tokens = keys.shape[1]
    own = tokens // groups
    count = min(BLOCK, own)
    steps = own // count
    whole = pl.BlockSpec((HEADS, tokens, LANES), lambda i: (0, 0, 0), pipeline_mode=pl.Buffered(1))
    anywhere = pl.BlockSpec(memory_space=pl.ANY)
    return pl.pallas_call(
        functools.partial(attend_kernel, groups, steps),
        grid=(steps,),
        in_specs=[
            pl.BlockSpec((HEADS, count, LANES), lambda i: (0, i, 0)),
            whole,
            whole,
            pl.BlockSpec((count, OUT), lambda i: (i, 0)),
            anywhere,
        ],
        out_specs=(
            pl.BlockSpec((count, OUT), lambda i: (i, 0)),
            pl.BlockSpec((count, OUT), lambda i: (i, 0)),
            pl.BlockSpec((count, LANES), lambda i: (i, 0)),
            anywhere,
        ),
        out_shape=(
            jax.ShapeDtypeStruct((own, OUT), HALF),
            jax.ShapeDtypeStruct((own, OUT), FULL),
            jax.ShapeDtypeStruct((own, LANES), FULL),
            jax.ShapeDtypeStruct(gathered.shape, HALF),
        ),
        scratch_shapes=[pltpu.SemaphoreType.DMA((5,)), pltpu.SemaphoreType.DMA((5,))],
        input_output_aliases={4: 3},
        compiler_params=params(9),
        name="attend",
        cost_estimate=cost(16),
    )(queries, keys, values, gates, gathered)


def group_device(bits):
    grp, group, member = place()
    return (grp, group * TP + flip(member, bits))


def blocks_of(ref, core):
    value = ref[:, pl.ds(core, 1)]
    return value.reshape(ref.shape[0] * ref.shape[2], ref.shape[3])


def sum_plan(lines, stage):
    give, take, out, came = stage
    sibling = [lines.plan(give.at[at], take.at[at], group_device(1)) for at in range(4)]
    others = [lines.plan(out.at[at], came.at[at], group_device(bits)) for at, bits in enumerate((2, 4, 6))]
    return sibling, others


def sum_give(pairs, stage, plan, mine):
    give = stage[0]
    grp, group, member = place()
    core = lax.rem(member, 2)
    count = give.shape[1]
    theirs = sum(dot(blocks_of(left, 1 - core), right[...], (1, 1)) for left, right in pairs)
    mine[...] = theirs.reshape(4, count, D)
    for at, bits in enumerate((2, 4, 6, 0)):
        give[at] = mine[lax.div(flip(member, bits), 2)].astype(HALF)
        plan[0][at].start()
    own = sum(dot(blocks_of(left, core), right[...], (1, 1)) for left, right in pairs)
    mine[...] = own.reshape(4, count, D)


def sum_pass(stage, plan, mine):
    give, take, out, came = stage
    member = place()[2]
    for at, bits in enumerate((2, 4, 6)):
        plan[0][at].wait_recv()
        out[at] = (mine[lax.div(flip(member, bits), 2)] + take[at].astype(FULL)).astype(HALF)
        plan[1][at].start()
    plan[0][3].wait_recv()
    return mine[lax.div(member, 2)] + take[3].astype(FULL)


def sum_send(pairs, stage, plan, mine):
    sum_give(pairs, stage, plan, mine)
    return sum_pass(stage, plan, mine)


def sum_take(total, stage, plan):
    give, take, out, came = stage
    for at in range(3):
        plan[1][at].wait_recv()
        total = total + came[at].astype(FULL)
    return total


def sum_scratch(rows):
    return [
        pltpu.VMEM((4, rows, D), HALF),
        pltpu.VMEM((4, rows, D), HALF),
        pltpu.VMEM((3, rows, D), HALF),
        pltpu.VMEM((3, rows, D), HALF),
    ]


def gather_plan(lines, block, all_ref, light=False):
    member = place()[2]

    def slot(bits):
        return halves(all_ref.at[flip(member, bits)])

    plan = {(bits, half): lines.plan(halves(block)[half], slot(0)[half], group_device(bits)) for bits in (4, 2) for half in range(2)}
    plan[1] = lines.plan(block, all_ref.at[member], group_device(1))
    plan[6, 0] = lines.plan(slot(4)[0], slot(4)[0], group_device(2))
    if light:
        plan[6, 1] = lines.plan(slot(4)[1], slot(4)[1], group_device(2))
    else:
        plan[6, 1] = lines.plan(slot(2)[1], slot(2)[1], group_device(4))
    for bits in (4, 2, 6):
        for half in range(2):
            plan[bits + 1, half] = lines.plan(slot(bits)[half], slot(bits)[half], group_device(1))
    return plan


GATHER = 13


def gather_start(plan, own):
    own.start()
    for key in ((4, 0), (2, 1), (4, 1), (2, 0), 1):
        plan[key].start()


def gather_turn(plan, light=False):
    for bits, half in ((4, 0), (4, 1) if light else (2, 1)):
        plan[bits, half].wait_recv()
        plan[6, half].start()
        plan[bits + 1, half].start()


def gather_pass(plan, light=False):
    for bits, half in ((2, 1) if light else (4, 1), (2, 0), (6, 0), (6, 1)):
        plan[bits, half].wait_recv()
        plan[bits + 1, half].start()


def gather_end(plan, own):
    plan[1].wait_recv()
    for bits in (5, 3, 7):
        for half in range(2):
            plan[bits, half].wait_recv()
    own.wait()


def gather_run(plan, own):
    gather_start(plan, own)
    gather_turn(plan)
    gather_pass(plan)
    gather_end(plan, own)


def mix_kernel(u_ref, w_ref, x_ref, g_ref, y_ref, all_ref, mine, block, give, take, out, came, send, receive, local):
    greet([group_device(bits) for bits in (1, 2, 4, 6)])
    member = place()[2]
    lines = Lines(send, receive)
    stage = (give, take, out, came)
    sums = sum_plan(lines, stage)
    gathered = gather_plan(lines, block, all_ref)
    total = sum_take(sum_send([(u_ref, w_ref)], stage, sums, mine), stage, sums)
    mixed = x_ref[...].astype(FULL) + total
    y_ref[...] = mixed
    block[...] = rms_rows(mixed, g_ref[...]).astype(HALF)
    gather_run(gathered, pltpu.make_async_copy(block, all_ref.at[member], local.at[0]))
    for copy in lines.made:
        copy.wait_send()


def whole_spec(shape):
    zeros = (0,) * len(shape)
    return pl.BlockSpec(shape, lambda i: zeros)


def weight_spec(columns, at):
    return pl.BlockSpec((D, columns), lambda i: (0, at))


def mix(gated, full, source, gain):
    rows = source.shape[0]
    count = 7 + GATHER
    return pl.pallas_call(
        mix_kernel,
        grid=(1,),
        out_shape=(
            jax.ShapeDtypeStruct((rows, D), FULL),
            jax.ShapeDtypeStruct((TP, rows, D), HALF),
        ),
        in_specs=[
            whole_spec((4, 2, rows, OUT)),
            weight_spec(OUT, QKVG // OUT),
            whole_spec((rows, D)),
            whole_spec((1, D)),
        ],
        out_specs=(whole_spec((rows, D)), pl.BlockSpec(memory_space=pl.ANY)),
        scratch_shapes=[pltpu.VMEM((4, rows, D), FULL), pltpu.VMEM((rows, D), HALF)]
        + sum_scratch(rows)
        + [
            pltpu.SemaphoreType.DMA((count,)),
            pltpu.SemaphoreType.DMA((count,)),
            pltpu.SemaphoreType.DMA((1,)),
        ],
        compiler_params=params(2),
        name="mix",
        cost_estimate=cost(40),
    )(gated.reshape(4, 2, rows, OUT), full, source, gain)


def slabs(grps, groups):
    grp, group, member = place()
    return [
        (turn, step, lax.rem(grp + turn, grps) * groups + lax.rem(group + step, groups))
        for turn in range(grps)
        for step in range(groups)
    ]


def load_rows(refs, whole, semaphores, grps, groups):
    rows = whole.shape[0] // (grps * groups)
    copies = []
    for at, (turn, step, index) in enumerate(slabs(grps, groups)):
        copies.append(pltpu.make_async_copy(refs[at], whole.at[pl.ds(index * rows, rows)], semaphores.at[at]))
    return copies


def unmix_kernel(grps, groups, d_ref, x_ref, g_ref, c_ref, m_ref, a_ref, r_ref, *rest):
    total_slabs = grps * groups
    both_refs, down_refs = rest[:total_slabs], rest[total_slabs : 2 * total_slabs]
    dx_ref, dg_ref, all_ref, beside_ref, along_ref, gate_ref, down_ref, give_ref, *rest = rest[2 * total_slabs :]
    up_refs, rest = rest[:groups], rest[groups:]
    wgu, wdn, mine, block, give, take, out, came, give2, take2, *rest = rest
    grads, over_got, across_out, across_got, send, receive, local = rest
    device, everyone = neighbours(grps, groups)
    everyone = [group_device(bits) for bits in (1, 2, 4, 6)] + everyone[TP - 1 :]
    call_out(everyone)
    grp, group, member = place()
    core = lax.rem(member, 2)
    load_both = load_rows(both_refs, wgu, local.at[pl.ds(0, total_slabs)], grps, groups)
    load_down = load_rows(down_refs, wdn, local.at[pl.ds(total_slabs, total_slabs)], grps, groups)
    for copy in load_both + load_down:
        copy.start()
    lines = Lines(send, receive)
    stage = (give, take, out, came)
    sums = sum_plan(lines, stage)
    gathered = gather_plan(lines, block, all_ref)
    output = lines.plan(give2, take2, group_device(1))
    rows = D // total_slabs
    places = slabs(grps, groups)
    down, gate, up = range(3)
    over = [
        {
            (turn, step): lines.plan(
                grads.at[kind, pl.ds(index * rows, rows)], over_got.at[kind, turn - 1, step], device(turn)
            )
            for turn, step, index in places
            if turn and (step or kind != up)
        }
        for kind in range(3)
    ]
    across = [
        [
            lines.plan(across_out.at[kind, step - 1], across_got.at[kind, step - 1], device(to_group=step))
            for step in range(1, groups)
        ]
        for kind in (down, gate)
    ]
    cut = D // 4

    def grad_of(kind, left, right):
        for at in range(4):
            here = slice(at * cut, (at + 1) * cut)
            grads[kind, here] = dot(left[:, here], right, (0, 0)).astype(HALF)

    def over_sum(kind, step):
        value = grads[kind, pl.ds(places[step][2] * rows, rows)].astype(FULL)
        for turn in range(1, grps):
            over[kind][turn, step].wait_recv()
            value = value + over_got[kind, turn - 1, step].astype(FULL)
        return value

    def begin_over(kind, steps):
        for step in steps:
            for turn in range(1, grps):
                over[kind][turn, step].start()

    def cross(kind):
        for step in range(1, groups):
            across_out[kind, step - 1] = over_sum(kind, step).astype(HALF)
            across[kind][step - 1].start()

    def crossed(kind):
        value = over_sum(kind, 0)
        for step in range(1, groups):
            across[kind][step - 1].wait_recv()
            value = value + across_got[kind, step - 1].astype(FULL)
        return value.astype(HALF)

    tokens, count = r_ref.shape[0], x_ref.shape[0]
    hidden, both = m_ref[...].reshape(tokens, UNITS), d_ref[...].reshape(tokens, 2 * UNITS)
    grad_of(down, r_ref, hidden)
    hear(everyone)
    begin_over(down, range(1, groups))
    for copy in load_both:
        copy.wait()
    sum_give([(d_ref, wgu)], stage, sums, mine)
    grad_of(gate, a_ref, both[:, :UNITS])
    begin_over(gate, range(1, groups))
    total = sum_pass(stage, sums, mine)
    cross(down)
    begin_over(down, [0])
    for copy in load_down:
        copy.wait()
    give2[...] = dot(blocks_of(m_ref, 1 - core), wdn[...], (1, 1)).astype(HALF).reshape(4, count, D)
    output.start()
    grad_of(up, a_ref, both[:, UNITS:])
    cross(gate)
    begin_over(up, range(1, groups))
    mine[...] = dot(blocks_of(m_ref, core), wdn[...], (1, 1)).reshape(4, count, D)
    total = sum_take(total, stage, sums)
    pulled, dgain = rms_back(x_ref[...], g_ref[...], total)
    grad = c_ref[...].astype(FULL) + pulled
    block[...] = grad.astype(HALF)
    own = pltpu.make_async_copy(block, all_ref.at[member], local.at[2 * total_slabs])
    gather_start(gathered, own)
    dx_ref[...] = grad
    dg_ref[...] = dgain
    output.wait_recv()
    for at, bits in enumerate((2, 6, 4, 0)):
        chip = lax.div(flip(member, bits), 2)
        target = (beside_ref if at < 2 else along_ref).at[at % 2]
        target[...] = (mine[chip] + take2[chip].astype(FULL)).astype(HALF)
    gather_turn(gathered)
    begin_over(gate, [0])
    gather_pass(gathered)
    for step in range(1, groups):
        up_refs[step][...] = over_sum(up, step).astype(HALF)
    for turn, step, index in places:
        if step == 0:
            target = give_ref.at[turn - 1] if turn else up_refs[0]
            target[...] = grads[up, pl.ds(index * rows, rows)]
    gather_end(gathered, own)
    down_ref[...] = crossed(down)
    gate_ref[...] = crossed(gate)
    for copy in lines.made:
        copy.wait_send()


def unmix(grads, both, down, mixed, gain, returned, hidden, second, returned_all, grps, groups):
    rows, tokens = mixed.shape[0], second.shape[0]
    slab = both[0].shape[0]
    total_slabs = grps * groups
    count = 8 + GATHER + (grps - 1) * (3 * groups - 1) + 2 * (groups - 1)
    piece = jax.ShapeDtypeStruct((slab, UNITS), HALF)
    return pl.pallas_call(
        functools.partial(unmix_kernel, grps, groups),
        grid=(1,),
        out_shape=(
            jax.ShapeDtypeStruct((rows, D), FULL),
            jax.ShapeDtypeStruct((1, D), FULL),
            jax.ShapeDtypeStruct((TP, rows, D), HALF),
            jax.ShapeDtypeStruct((2, rows, D), HALF),
            jax.ShapeDtypeStruct((2, rows, D), HALF),
        )
        + (piece,) * 2
        + (jax.ShapeDtypeStruct((grps - 1, slab, UNITS), HALF),)
        + (piece,) * groups,
        in_specs=[
            whole_spec((4, 2, rows, 2 * UNITS)),
            whole_spec((rows, D)),
            whole_spec((1, D)),
            whole_spec((rows, D)),
            whole_spec((4, 2, rows, UNITS)),
            whole_spec((tokens, D)),
            whole_spec((tokens, D)),
        ]
        + [pl.BlockSpec(memory_space=pl.ANY)] * (2 * total_slabs),
        out_specs=(
            whole_spec((rows, D)),
            whole_spec((1, D)),
            pl.BlockSpec(memory_space=pl.ANY),
            whole_spec((2, rows, D)),
            whole_spec((2, rows, D)),
        )
        + (whole_spec((slab, UNITS)),) * 2
        + (whole_spec((grps - 1, slab, UNITS)),)
        + (whole_spec((slab, UNITS)),) * groups,
        scratch_shapes=[
            pltpu.VMEM((D, 2 * UNITS), HALF),
            pltpu.VMEM((D, UNITS), HALF),
            pltpu.VMEM((4, rows, D), FULL),
            pltpu.VMEM((rows, D), HALF),
        ]
        + sum_scratch(rows)
        + [
            pltpu.VMEM((4, rows, D), HALF),
            pltpu.VMEM((4, rows, D), HALF),
            pltpu.VMEM((3, D, UNITS), HALF),
            pltpu.VMEM((3, grps - 1, groups, slab, UNITS), HALF),
            pltpu.VMEM((2, groups - 1, slab, UNITS), HALF),
            pltpu.VMEM((2, groups - 1, slab, UNITS), HALF),
            pltpu.SemaphoreType.DMA((count,)),
            pltpu.SemaphoreType.DMA((count,)),
            pltpu.SemaphoreType.DMA((2 * total_slabs + 1,)),
        ],
        compiler_params=params(3),
        name="unmix",
        cost_estimate=cost(55),
    )(
        grads.reshape(4, 2, rows, 2 * UNITS),
        mixed,
        gain,
        returned,
        hidden.reshape(4, 2, rows, UNITS),
        second,
        returned_all,
        *both,
        *down,
    )


def feed_kernel(grps, groups, a_ref, c_ref, *rest):
    total_slabs = grps * groups
    both_refs, down_refs = rest[:total_slabs], rest[total_slabs : 2 * total_slabs]
    m_ref, d_ref, wgu, wdn, local = rest[2 * total_slabs :]

    @pl.when(pl.program_id(0) == 0)
    def load():
        copies = load_rows(both_refs, wgu, local.at[pl.ds(0, total_slabs)], grps, groups)
        copies = copies + load_rows(down_refs, wdn, local.at[pl.ds(total_slabs, total_slabs)], grps, groups)
        for copy in copies:
            copy.start()
        for copy in copies:
            copy.wait()

    made = dot(a_ref[...], wgu[...])
    gate, up = made[:, :UNITS], made[:, UNITS:]
    sig = sigmoid(gate)
    swish = gate * sig
    m_ref[...] = (swish * up).astype(HALF)
    grad = dot(c_ref[...], wdn[...])
    d_ref[:, :UNITS] = (grad * up * sig * (1.0 + gate * (1.0 - sig))).astype(HALF)
    d_ref[:, UNITS:] = (grad * swish).astype(HALF)


def feed(second, returned, both, down, grps, groups):
    tokens = second.shape[0]
    count = TALL
    return pl.pallas_call(
        functools.partial(feed_kernel, grps, groups),
        grid=(tokens // count,),
        out_shape=(
            jax.ShapeDtypeStruct((tokens, UNITS), HALF),
            jax.ShapeDtypeStruct((tokens, 2 * UNITS), HALF),
        ),
        in_specs=[
            pl.BlockSpec((count, D), lambda i: (i, 0)),
            pl.BlockSpec((count, D), lambda i: (i, 0)),
        ]
        + [pl.BlockSpec(memory_space=pl.ANY)] * (2 * grps * groups),
        out_specs=(
            pl.BlockSpec((count, UNITS), lambda i: (i, 0)),
            pl.BlockSpec((count, 2 * UNITS), lambda i: (i, 0)),
        ),
        scratch_shapes=[
            pltpu.VMEM((D, 2 * UNITS), HALF),
            pltpu.VMEM((D, UNITS), HALF),
            pltpu.SemaphoreType.DMA((2 * grps * groups,)),
        ],
        compiler_params=params(),
        name="feed",
        cost_estimate=cost(10),
    )(second, returned, *both, *down)


def ungate_kernel(
    grps, groups, steps, d_ref, w_ref, o_ref, t_ref, l_ref, q_ref, u_ref,
    do_ref, qb_ref, dg_ref, pack_ref, keep_ref, give_ref, whole,
):
    cut = D // 4
    for at in range(4):
        here = slice(at * cut, (at + 1) * cut)
        part = dot(d_ref[:, here], u_ref[...], (0, 0))
        whole[here] = jnp.where(pl.program_id(0) == 0, part, whole[here] + part)

    @pl.when(pl.program_id(0) == steps - 1)
    def sort():
        rows = D // (grps * groups)
        for turn, step, index in slabs(grps, groups):
            target = give_ref.at[turn - 1, step] if turn else keep_ref.at[step]
            target[...] = whole[pl.ds(index * rows, rows)].astype(HALF)

    grad = dot(d_ref[...], w_ref[...])
    count = grad.shape[0]
    lanes = lax.broadcasted_iota(jnp.int32, (count, LANES), 1)
    gates = (t_ref[:, :LANES], t_ref[:, LANES:])
    sums, sent = [], []
    for at in range(2):
        part = grad[:, LANES * at : LANES * (at + 1)]
        attended = o_ref[:, LANES * at : LANES * (at + 1)]
        sig = sigmoid(gates[at])
        low = (part * sig).astype(HALF).astype(FULL)
        sent.append(low)
        dg_ref[:, LANES * at : LANES * (at + 1)] = part * attended * sig * (1.0 - sig)
        sums.append(two(low * attended))
    row = lax.broadcasted_iota(jnp.int32, (LANES, LANES), 0)
    col = lax.broadcasted_iota(jnp.int32, (LANES, LANES), 1)
    of_left = jnp.where(((row < DH) & (col == 0)) | ((row >= DH) & (col == 1)), -1.0, 0.0).astype(HALF)
    of_right = jnp.where((row < DH) & (col == 2), -1.0, 0.0).astype(HALF)
    minus = dot(sums[0][0], of_left) + dot(sums[0][1], of_left) + dot(sums[1][0], of_right) + dot(sums[1][1], of_right)
    logs = jnp.where(lanes < HEADS, -l_ref[...], 0.0)
    packed = side_by_side(three(minus) + three(logs), lanes)
    grads = dot(packed, picker((HEADS * LANES, spread_lanes(0, DH))))
    sinks = dot(packed, picker((HEADS * LANES, spread_lanes(3, DH + 6))))

    def sent_lanes(col):
        head, part = lax.div(col - DH, 6), lax.rem(col - DH, 6)
        return jnp.where((col >= DH) & (col < DH + 6 * HEADS), HEADS * part + head, -1)

    extra = dot(packed, picker((LANES, sent_lanes)))
    heads = [sent[0], pltpu.roll(sent[0], DH, 1), sent[1]]
    for head in range(HEADS):
        here = slice(LANES * head, LANES * (head + 1))
        do_ref[head] = jnp.where(lanes < DH, heads[head], grads[:, here]).astype(HALF)
        qb_ref[head] = (q_ref[head].astype(FULL) + sinks[:, here]).astype(HALF)
    pack_ref[:, :LANES] = sent[0].astype(HALF)
    pack_ref[:, LANES:] = jnp.where(lanes < DH, sent[1], extra).astype(HALF)


def ungate(grads, full, attended, gates, logs, queries, gated, grps, groups):
    own = grads.shape[0]
    steps = own // TALL
    slab = D // (grps * groups)
    head_tile = pl.BlockSpec((HEADS, TALL, LANES), lambda i: (0, i, 0))
    wide_tile = pl.BlockSpec((TALL, OUT), lambda i: (i, 0))
    return pl.pallas_call(
        functools.partial(ungate_kernel, grps, groups, steps),
        grid=(steps,),
        in_specs=[
            pl.BlockSpec((TALL, D), lambda i: (i, 0)),
            weight_spec(OUT, QKVG // OUT),
            wide_tile,
            wide_tile,
            pl.BlockSpec((TALL, LANES), lambda i: (i, 0)),
            head_tile,
            wide_tile,
        ],
        out_specs=(
            head_tile,
            head_tile,
            wide_tile,
            wide_tile,
            whole_spec((groups, slab, OUT)),
            whole_spec((grps - 1, groups, slab, OUT)),
        ),
        out_shape=(
            jax.ShapeDtypeStruct((HEADS, own, LANES), HALF),
            jax.ShapeDtypeStruct((HEADS, own, LANES), HALF),
            jax.ShapeDtypeStruct((own, OUT), FULL),
            jax.ShapeDtypeStruct((own, OUT), HALF),
            jax.ShapeDtypeStruct((groups, slab, OUT), HALF),
            jax.ShapeDtypeStruct((grps - 1, groups, slab, OUT), HALF),
        ),
        scratch_shapes=[pltpu.VMEM((D, OUT), FULL)],
        compiler_params=params(),
        name="ungate",
        cost_estimate=cost(9),
    )(grads, full, attended, gates, logs, queries, gated)


def pieces(scores, product, masked, transposed):
    prob = jnp.exp(scores)
    if masked:
        row = lax.broadcasted_iota(jnp.int32, scores.shape, 0)
        col = lax.broadcasted_iota(jnp.int32, scores.shape, 1)
        keep = row <= col if transposed else col <= row
        prob = jnp.where(keep, prob, 0.0)
    return prob.astype(HALF), (prob * product).astype(HALF)


def home_plan(lines, pairs):
    member = place()[2]
    return [
        lines.plan(source.at[flip(member, bits)], target.at[member], group_device(bits))
        for source, target in pairs
        for bits in range(1, TP)
    ]


def back_kernel(
    grps, groups, q_ref, do_ref, k_ref, v_ref, a_ref, pack_ref, out_ref, up_ref, out_give, up_give, gate_ref, down_ref,
    dq_ref, dk_ref, dv_ref, late_ref, done_ref, up_sum, hgate_ref, hdown_ref,
    others, out_got, up_got, across_out, across_got, send, receive, local,
):
    device, everyone = neighbours(grps, groups)
    call_out(everyone)
    group, member = place()[1:]
    own = q_ref.shape[1]
    count = min(BLOCK, own)
    steps = own // count
    lines = Lines(send, receive)
    halves_of = [pl.ds(at * count, count) for at in range(steps)]
    packs = [
        [lines.plan(pack_ref.at[half], others.at[step - 1, half], device(to_group=groups - step)) for step in range(1, groups)]
        for half in halves_of
    ]
    over = [lines.plan(out_give.at[turn - 1], out_got.at[turn - 1], device(to_grp=turn)) for turn in range(1, grps)]
    over_up = [lines.plan(up_give.at[turn - 1], up_got.at[turn - 1], device(to_grp=turn)) for turn in range(1, grps)]
    across = [
        lines.plan(across_out.at[step - 1], across_got.at[step - 1], device(to_group=step)) for step in range(1, groups)
    ]
    pairs = ((gate_ref, hgate_ref), (down_ref, hdown_ref))
    home = home_plan(lines, pairs)
    kept = [
        pltpu.make_async_copy(source.at[member], target.at[member], local.at[at])
        for at, (source, target) in enumerate(pairs)
    ]
    hear(everyone)
    for copy in packs[0] + over + home + kept + over_up:
        copy.start()
    dk_ref[...] = jnp.zeros_like(dk_ref)
    dv_ref[...] = jnp.zeros_like(dv_ref)
    earliest = (groups - group) * steps
    for head in range(HEADS):
        for at in range(steps):
            here = halves_of[at]
            query, grad = q_ref[head, here], do_ref[head, here]

            def earlier(step, inner):
                there = pl.ds(step * count, count)
                key = k_ref[head, there]
                prob, dscore = pieces(
                    dot(query, key, (1, 1)), dot(grad, v_ref[head, there], (1, 1)), False, False
                )
                return inner + dot(dscore, key)

            dquery = lax.fori_loop(earliest, groups * steps, earlier, jnp.zeros((count, LANES), FULL))
            for step in range(at + 1):
                there = halves_of[step]
                key = k_ref[head, there]
                prob, dscore = pieces(
                    dot(key, query, (1, 1)), dot(v_ref[head, there], grad, (1, 1)), step == at, True
                )
                dk_ref[head, there] += dot(dscore, query)
                dv_ref[head, there] += dot(prob, grad)
                dquery = dquery + dot(dscore, key, (0, 0))
            dq_ref[head, here] = dquery
        if head == 0:
            for copies in packs[1:]:
                for copy in copies:
                    copy.start()
        if head == 1:
            for copy in over:
                copy.wait_recv()
            for step in range(1, groups):
                value = out_ref[step].astype(FULL)
                for turn in range(1, grps):
                    value = value + out_got[turn - 1, step].astype(FULL)
                across_out[step - 1] = value.astype(HALF)
                across[step - 1].start()

    lanes = lax.broadcasted_iota(jnp.int32, (count, LANES), 1)
    late_ref[...] = jnp.zeros_like(late_ref)

    def visit(head, carry, step, at):
        def lanes_from(first, start):
            def find(col):
                part = col - start
                return jnp.where((part >= 0) & (part < 3), DH + 6 * head + first + part, -1)

            return picker((LANES, find))

        minus, logs = lanes_from(0, DH), lanes_from(3, DH + 6)
        sent = others[step - 1, halves_of[at]].astype(FULL)
        left, right = sent[:, :LANES], sent[:, LANES:]
        grad = jnp.where(head == 0, left, jnp.where(head == 1, pltpu.roll(left, DH, 1), right))
        packed = others[step - 1, halves_of[at], LANES:]
        grad = jnp.where(lanes < DH, grad, dot(packed, minus)).astype(HALF)
        query = a_ref[head, pl.ds(step * own + at * count, count)].astype(FULL)
        query = (query + dot(packed, logs)).astype(HALF)
        for there in halves_of:
            prob, dscore = pieces(
                dot(k_ref[head, there], query, (1, 1)), dot(v_ref[head, there], grad, (1, 1)), False, True
            )
            part = dot(dscore, query)
            dk_ref[head, there] += part
            dv_ref[head, there] += dot(prob, grad)
            late_ref[head] += jnp.broadcast_to(jnp.sum(part, axis=0, keepdims=True), (8, LANES))
        return carry

    for at in range(steps):
        for step in range(1, groups):
            packs[at][step - 1].wait_recv()

            @pl.when(step < groups - group)
            def later():
                lax.fori_loop(0, HEADS, functools.partial(visit, step=step, at=at), 0)

    value = out_ref[0].astype(FULL)
    for turn in range(1, grps):
        value = value + out_got[turn - 1, 0].astype(FULL)
    for step in range(1, groups):
        across[step - 1].wait_recv()
        value = value + across_got[step - 1].astype(FULL)
    done_ref[...] = value.astype(HALF)
    value = up_ref[...].astype(FULL)
    for turn in range(1, grps):
        over_up[turn - 1].wait_recv()
        value = value + up_got[turn - 1].astype(FULL)
    up_sum[...] = value.astype(HALF)
    for copy in home:
        copy.wait_recv()
    for copy in kept:
        copy.wait()
    for copy in lines.made:
        copy.wait_send()


def attend_back(queries, grads, keys, values, span_queries, pack, out, up, out_give, up_give, gate, down):
    own, tokens = queries.shape[1], keys.shape[1]
    grps, groups, slab = out_give.shape[0] + 1, out.shape[0], out.shape[1]
    steps = own // min(BLOCK, own)
    count = steps * (groups - 1) + 2 * (grps - 1) + groups - 1 + 2 * (TP - 1)
    vmem, anywhere = pl.BlockSpec(memory_space=pltpu.VMEM), pl.BlockSpec(memory_space=pl.ANY)
    return pl.pallas_call(
        functools.partial(back_kernel, grps, groups),
        in_specs=[vmem] * 5 + [anywhere, vmem, vmem] + [anywhere] * 4,
        out_specs=(vmem,) * 6 + (anywhere,) * 2,
        out_shape=(jax.ShapeDtypeStruct((HEADS, own, LANES), FULL),) * 3
        + (
            jax.ShapeDtypeStruct((HEADS, 8, LANES), FULL),
            jax.ShapeDtypeStruct((slab, OUT), HALF),
            jax.ShapeDtypeStruct(up.shape, HALF),
            jax.ShapeDtypeStruct(gate.shape, HALF),
            jax.ShapeDtypeStruct(down.shape, HALF),
        ),
        scratch_shapes=[
            pltpu.VMEM((groups - 1, own, OUT), HALF),
            pltpu.VMEM(out_give.shape, HALF),
            pltpu.VMEM(up_give.shape, HALF),
            pltpu.VMEM((groups - 1, slab, OUT), HALF),
            pltpu.VMEM((groups - 1, slab, OUT), HALF),
            pltpu.SemaphoreType.DMA((count,)),
            pltpu.SemaphoreType.DMA((count,)),
            pltpu.SemaphoreType.DMA((2,)),
        ],
        compiler_params=params(5),
        name="attend_back",
        cost_estimate=cost(35),
    )(queries, grads, keys, values, span_queries, pack, out, up, out_give, up_give, gate, down)


def unproject_kernel(
    dq_ref, dk_ref, dv_ref, dg_ref, p_ref, z_ref, g_ref, late_ref, dp_ref, dz_ref, gain_ref, bias_ref, carry
):
    @pl.when(pl.program_id(0) == 0)
    def clear():
        first_lanes = lax.broadcasted_iota(jnp.int32, (1, LANES), 1)
        start = jnp.zeros((1, LANES), FULL)
        for head in range(HEADS):
            start = jnp.where(first_lanes == head, pltpu.roll(late_ref[head, 0:1], DH - 3 + head, 1), start)
        carry[0:1] = start
        gain_ref[...] = jnp.zeros_like(gain_ref)
        bias_ref[...] = jnp.zeros_like(bias_ref)

    count = p_ref.shape[0]
    lanes = lax.broadcasted_iota(jnp.int32, (count, LANES), 1)
    sums = jnp.zeros((count, LANES), FULL)
    means = halves_matrix(1.0 / DH)
    gates = [
        pltpu.roll(dg_ref[:, :LANES], DH, 1),
        dg_ref[:, :LANES],
        pltpu.roll(dg_ref[:, LANES:], DH, 1),
    ]
    for head in range(HEADS):
        dquery, dkey = dq_ref[head], dk_ref[head]
        found = pltpu.roll(dquery, DH + head, 1) - pltpu.roll(dkey, DH - 3 + head, 1)
        sums = jnp.where(lanes == head, found, sums)
        grad = jnp.where(lanes < DH, dquery * (DH**-0.5), pltpu.roll(dkey, DH, 1))
        pair = p_ref[:, LANES * head : LANES * (head + 1)]
        inverse = lax.rsqrt(halves_mean(pair * pair, means) + EPS)
        normal = pair * inverse
        scaled = grad * g_ref[head : head + 1]
        gain_ref[head : head + 1] += jnp.sum(grad * normal, axis=0, keepdims=True)
        pulled = inverse * (scaled - normal * halves_mean(scaled * normal, means))
        dp_ref[:, 256 * head : 256 * head + LANES] = pulled.astype(HALF)
        dp_ref[:, 256 * head + LANES : 256 * head + 2 * LANES] = jnp.where(
            lanes < DH, dv_ref[head], gates[head]
        ).astype(HALF)
    row = lax.broadcasted_iota(jnp.int32, (count, count), 0)
    col = lax.broadcasted_iota(jnp.int32, (count, count), 1)
    later = (
        lax.dot_general(
            jnp.where(col >= row, 1.0, 0.0),
            sums,
            (((1,), (0,)), ((), ())),
            precision=lax.Precision.HIGHEST,
            preferred_element_type=FULL,
        )
        + carry[0:1]
    )
    carry[0:1] = later[0:1]
    low = jnp.where(lanes < HEADS, later * sigmoid(-z_ref[...]), 0.0).astype(HALF)
    dz_ref[...] = low
    bias_ref[0:1] += jnp.sum(low.astype(FULL), axis=0, keepdims=True)


def unproject(dqueries, dkeys, dvalues, dgates, pairs, logits, gains, late):
    own = dqueries.shape[1]
    steps = own // TALL

    def back(width):
        return pl.BlockSpec((TALL, width), lambda i: (steps - 1 - i, 0))

    head_tile = pl.BlockSpec((HEADS, TALL, LANES), lambda i: (0, steps - 1 - i, 0))
    small = whole_spec((8, LANES))
    return pl.pallas_call(
        unproject_kernel,
        grid=(steps,),
        in_specs=[
            head_tile,
            head_tile,
            head_tile,
            back(OUT),
            back(HEADS * LANES),
            back(LANES),
            small,
            whole_spec((HEADS, 8, LANES)),
        ],
        out_specs=(back(QKVG), back(LANES), small, small),
        scratch_shapes=[pltpu.VMEM((8, LANES), FULL)],
        out_shape=(
            jax.ShapeDtypeStruct((own, QKVG), HALF),
            jax.ShapeDtypeStruct((own, LANES), HALF),
            jax.ShapeDtypeStruct((8, LANES), FULL),
            jax.ShapeDtypeStruct((8, LANES), FULL),
        ),
        compiler_params=params(),
        name="unproject",
        cost_estimate=cost(9),
    )(dqueries, dkeys, dvalues, dgates, pairs, logits, gains, late)


def across_groups(part, groups):
    size = groups * TP
    return [part] + [
        lax.ppermute(part, "fsdp", [((at + step * TP) % size, at) for at in range(size)])
        for step in range(1, groups)
    ]


def over_grps(parts, grps):
    return [
        [part] + [lax.ppermute(part, "grp", [((at + turn) % grps, at) for at in range(grps)]) for turn in range(1, grps)]
        for part in parts
    ]


def in_order(parts):
    return [turns[turn] for turn in range(len(parts[0])) for turns in parts]


def collected(kept):
    return sum(part.astype(FULL) for part in kept).astype(HALF)


def unpack(grad_ref, near, gate, up, down, out):
    lanes = lax.broadcasted_iota(jnp.int32, (near.shape[1], LANES), 1)

    def half(ref, part, upper):
        member, at, side = part
        value = ref[member, :, at : at + LANES].astype(FULL)
        return pltpu.roll(value, DH, 1) if side != upper else value

    def store(at, ref, lower, upper):
        value = jnp.where(lanes < DH, half(ref, lower, False), half(ref, upper, True))
        grad_ref[:, at : at + LANES] = value.astype(HALF)

    for at in range(0, H, 2):
        for kind in range(4):
            pair = [
                (head // HEADS, 256 * (head % HEADS) + LANES * (kind // 2), kind % 2 == 1) for head in (at, at + 1)
            ]
            store(kind * D + at * DH, near, *pair)
        pair = [
            (head // HEADS, LANES * (head % HEADS // 2), head % HEADS % 2 == 1) for head in (at, at + 1)
        ]
        store(4 * D + at * DH, out, *pair)
    for member in range(TP):
        at = 5 * D + member * UNITS
        grad_ref[:, at : at + UNITS] = gate[member]
        grad_ref[:, at + F : at + F + UNITS] = up[member]
        grad_ref[:, at + 2 * F : at + 2 * F + UNITS] = down[member]


PARTS = 2


def end_counts(grps, groups):
    replicas = grps * groups - 1
    return 7 + PARTS * ((grps - 1) * groups + groups - 1) + 4 * (TP - 1) + replicas


def sort_small(every, gains_ref, forget_ref, bias_ref):
    lanes = lax.broadcasted_iota(jnp.int32, (1, LANES), 1)
    rest = HEADS + 2
    gains_ref[0:2] = jnp.sum(every[:, HEADS : HEADS + 2], axis=0)

    def part(head, kind, upper):
        row = every[head // HEADS, rest : rest + 1]
        return half_lanes(row, (kind * HEADS + head % HEADS) * DH, upper)

    for kind in range(2):
        for head in range(0, H, 2):
            gains_ref[2 + kind : 3 + kind, head * DH : (head + 2) * DH] = jnp.where(
                lanes < DH, part(head, kind, False), part(head + 1, kind, True)
            )
    bias = jnp.zeros((1, LANES), FULL)
    edge = 2 * HEADS * DH
    for member in range(TP):
        forget_ref[member * HEADS : (member + 1) * HEADS] = every[member, :HEADS]
        moved = every[member, rest : rest + 1, edge : edge + LANES]
        if member:
            moved = pltpu.roll(moved, member * HEADS, 1)
        bias = jnp.where((lanes >= member * HEADS) & (lanes < (member + 1) * HEADS), moved, bias)
    bias_ref[...] = jnp.broadcast_to(bias, bias_ref.shape)


def end_kernel(
    grps, groups,
    p_ref, z_ref, f_ref, x_ref, g_ref, d_ref, mid_ref, heads_ref, bias_ref_in, out_ref, up_ref, hgate_ref, hdown_ref, w_ref, t_ref, *rest
):
    y_ref, grad_ref, gains_ref, forget_ref, bias_ref, norm_ref, *rest = rest
    small_ref, hnear_ref, hup_ref, hout_ref, *rest = rest
    weights, tokens, near, mine, give, take, out, came, over_got, across_out, across_got, last, *rest = rest
    packet, packets, send, receive, local = rest
    grp, group, member = place()
    device, everyone = neighbours(grps, groups)
    replicas = [(turn, step) for turn in range(grps) for step in range(groups) if turn or step]
    everyone = everyone + [device(turn, step) for turn, step in replicas if turn and step]
    call_out(everyone)
    count = tokens.shape[0]
    load_tokens = pltpu.make_async_copy(t_ref, tokens, local.at[0])
    load_weights = pltpu.make_async_copy(w_ref.at[:, pl.ds(0, QKVG)], weights, local.at[1])
    load_tokens.start()
    load_weights.start()
    lines = Lines(send, receive)
    stage = (give, take, out, came)
    sums = sum_plan(lines, stage)
    slab = near.shape[0] // (grps * groups)
    part_rows = slab // PARTS
    own = last.shape[2]
    over, across, home = {}, {}, {}

    def rows_of(turn, step, part):
        side = lax.div(member, 4)
        side = side + part - 2 * part * side
        index = lax.rem(grp + turn, grps) * groups + lax.rem(group + step, groups)
        return pl.ds(index * slab + side * part_rows, part_rows)

    order = [(ahead, part) for ahead in list(range(1, groups)) + [0] for part in (1, 0)]
    for ahead, part in order:
        for turn in range(1, grps):
            over[turn, ahead, part] = lines.plan(
                near.at[rows_of(turn, ahead, part)], over_got.at[turn - 1, ahead, part], device(turn)
            )
        if ahead:
            across[ahead, part] = lines.plan(
                across_out.at[ahead - 1, part], across_got.at[ahead - 1, part], device(to_group=ahead)
            )
    for bits in range(1, TP):
        source = last.at[bits // 4, lax.rem(flip(member, bits), 4)]
        home[bits] = lines.plan(source, hnear_ref.at[member], device(bits=bits))
    far = home_plan(lines, ((out_ref, hout_ref), (up_ref, hup_ref)))
    shared = [lines.plan(packet, packets.at[at], device(turn, step)) for at, (turn, step) in enumerate(replicas)]
    told = [lines.plan(small_ref.at[member], small_ref.at[member], device(bits=bits)) for bits in range(1, TP)]

    projected = p_ref[...].reshape(count, QKVG)
    cut = D // 4
    load_tokens.wait()
    for at in range(4):
        here = slice(at * cut, (at + 1) * cut)
        near[here] = dot(tokens[:, here], projected, (0, 0)).astype(HALF)
    hear(everyone)
    for turn in range(1, grps):
        for ahead in range(1, groups):
            over[turn, ahead, 1].start()
    load_weights.wait()
    sum_give([(p_ref, weights), (z_ref, f_ref)], stage, sums, mine)
    summed = sum_pass(stage, sums, mine)
    for part in (1, 0):
        for ahead in range(1, groups):
            if part == 1:
                for turn in range(1, grps):
                    over[turn, ahead, 1].wait_recv()
                    over[turn, ahead, 0].start()
            elif ahead == 1:
                for turn in range(1, grps):
                    for last_part in (1, 0):
                        over[turn, 0, last_part].start()
            total = near[rows_of(0, ahead, part)].astype(FULL)
            for turn in range(1, grps):
                if part == 0:
                    over[turn, ahead, part].wait_recv()
                total = total + over_got[turn - 1, ahead, part].astype(FULL)
            across_out[ahead - 1, part] = total.astype(HALF)
            across[ahead, part].start()
    packet[...] = jnp.zeros_like(packet)
    packet[HEADS + 1 : HEADS + 2] = mid_ref[...]
    lanes = lax.broadcasted_iota(jnp.int32, (1, LANES), 1)
    pairs_of = [heads_ref[head : head + 1] for head in range(HEADS)]
    swapped = [pltpu.roll(pair, DH, 1) for pair in pairs_of]
    rest_row = slice(HEADS + 2, HEADS + 3)
    packet[rest_row, :LANES] = jnp.where(lanes < DH, pairs_of[0], swapped[1])
    packet[rest_row, LANES : 2 * LANES] = jnp.where(lanes < DH, pairs_of[2], pairs_of[0])
    packet[rest_row, 2 * LANES : 3 * LANES] = jnp.where(lanes < DH, swapped[1], pairs_of[2])
    packet[rest_row, 3 * LANES : 4 * LANES] = jnp.where(lanes < HEADS, bias_ref_in[0:1], 0.0)
    forget = dot(z_ref[...].reshape(count, LANES), tokens[...], (0, 0))
    packet[0:HEADS] = forget[0:HEADS]

    def square(value):
        value = value.astype(FULL)
        return jnp.sum(value * value)

    squares = square(hgate_ref[...]) + square(hdown_ref[...]) + square(out_ref[...]) + square(up_ref[...])
    summed = sum_take(summed, stage, sums)
    for copy in far:
        copy.start()
    for source, target in ((out_ref, hout_ref), (up_ref, hup_ref)):
        target[member] = source[member]
    pulled, dgain = rms_back(x_ref[...].astype(FULL), g_ref[...], summed)
    y_ref[...] = (d_ref[...] + pulled).astype(HALF)
    packet[HEADS : HEADS + 1] = dgain
    for part in (1, 0):
        total = near[rows_of(0, 0, part)].astype(FULL)
        for turn in range(1, grps):
            over[turn, 0, part].wait_recv()
            total = total + over_got[turn - 1, 0, part].astype(FULL)
        for ahead in range(1, groups):
            across[ahead, part].wait_recv()
            total = total + across_got[ahead - 1, part].astype(FULL)
        squares = squares + square(total)
        for at in range(4):
            last[part, at] = total[at * own : (at + 1) * own].astype(HALF)
        for bits in range(max(4 * part, 1), 4 * part + 4):
            home[bits].start()
    packet[HEADS + 3 : HEADS + 4] = jnp.full((1, D), squares, FULL)
    for copy in shared:
        copy.start()
    hnear_ref[member] = last[0, lax.rem(member, 4)]
    total = packet[...]
    for at, copy in enumerate(shared):
        copy.wait_recv()
        total = total + packets[at]
    small_ref[member] = total
    for copy in told:
        copy.start()
    for copy in far + list(home.values()):
        copy.wait_recv()
    unpack(grad_ref, hnear_ref, hgate_ref, hup_ref, hdown_ref, hout_ref)
    for copy in told:
        copy.wait_recv()
    every = small_ref[...]
    sort_small(every, gains_ref, forget_ref, bias_ref)
    gains = gains_ref[...]
    heads = jnp.sum(every[:, :HEADS] * every[:, :HEADS]) + jnp.sum(gains * gains)
    edge = 2 * HEADS * DH
    heads = heads + jnp.sum(every[:, HEADS + 2, edge : edge + LANES] * every[:, HEADS + 2, edge : edge + LANES])
    matrices = jnp.sum(every[:, HEADS + 3, :LANES], axis=0, keepdims=True)
    norm_ref[...] = jnp.sqrt(jnp.broadcast_to(matrices + heads, (8, LANES)))
    for copy in lines.made:
        copy.wait_send()


def end(projected, logits, forget, source, gain, grad, mid, heads, bias, out, up, gate, down, near, tokens, grps, groups):
    rows, own = source.shape[0], gate.shape[1]
    count = end_counts(grps, groups)
    replicas = grps * groups - 1
    slab = TP * own
    part = (slab // PARTS, QKVG)
    vmem, anywhere = pl.BlockSpec(memory_space=pltpu.VMEM), pl.BlockSpec(memory_space=pl.ANY)
    return pl.pallas_call(
        functools.partial(end_kernel, grps, groups),
        out_shape=(
            jax.ShapeDtypeStruct((rows, D), HALF),
            jax.ShapeDtypeStruct((own, 5 * D + 3 * F), HALF),
            jax.ShapeDtypeStruct((4, D), FULL),
            jax.ShapeDtypeStruct((H, D), FULL),
            jax.ShapeDtypeStruct((8, LANES), FULL),
            jax.ShapeDtypeStruct((8, LANES), FULL),
        ),
        in_specs=[vmem] * 13 + [anywhere] * 2,
        out_specs=(vmem,) * 6,
        scratch_shapes=[
            pltpu.VMEM((TP, 8, D), FULL),
            pltpu.VMEM((TP, own, QKVG), HALF),
            pltpu.VMEM((TP, own, UNITS), HALF),
            pltpu.VMEM((TP, own, OUT), HALF),
            pltpu.VMEM((D, QKVG), HALF),
            pltpu.VMEM((TP * rows, D), HALF),
            pltpu.VMEM((D, QKVG), HALF),
            pltpu.VMEM((4, rows, D), FULL),
        ]
        + sum_scratch(rows)
        + [
            pltpu.VMEM((grps - 1, groups, PARTS) + part, HALF),
            pltpu.VMEM((groups - 1, PARTS) + part, HALF),
            pltpu.VMEM((groups - 1, PARTS) + part, HALF),
            pltpu.VMEM((PARTS, 4, own, QKVG), HALF),
            pltpu.VMEM((8, D), FULL),
            pltpu.VMEM((replicas, 8, D), FULL),
            pltpu.SemaphoreType.DMA((count,)),
            pltpu.SemaphoreType.DMA((count,)),
            pltpu.SemaphoreType.DMA((2,)),
        ],
        compiler_params=params(4),
        name="end",
        cost_estimate=cost(60),
    )(
        projected.reshape(4, 2, rows, QKVG),
        logits.reshape(4, 2, rows, LANES),
        forget,
        source,
        gain,
        grad,
        mid,
        heads,
        bias,
        out,
        up,
        gate,
        down,
        near,
        tokens,
    )


def adam(value, first, second, grad, rate, decay):
    first = BETA_ONE * first + (1.0 - BETA_ONE) * grad
    second = BETA_TWO * second + (1.0 - BETA_TWO) * grad * grad
    unbiased_first = first * (1.0 / (1.0 - BETA_ONE**STEP))
    unbiased_second = second * (1.0 / (1.0 - BETA_TWO**STEP))
    value = value - rate * (unbiased_first / (jnp.sqrt(unbiased_second) + ADAM_EPS) + decay * value)
    return (value, first, second)


def pad_lanes(value, width=LANES):
    return jnp.pad(value, ((0, 0), (0, width - value.shape[1])))


def shards(
    inputs,
    cotangent,
    weights,
    weights_first,
    weights_second,
    gains,
    gains_first,
    gains_second,
    forget_weight,
    forget_first,
    forget_second,
    forget_bias,
    bias_first,
    bias_second,
):
    grps, groups = lax.axis_size("grp"), lax.axis_size("fsdp") // TP
    grp, group, member = place()
    rows, own_rows = inputs.shape[1], weights.shape[0]
    group_tokens = TP * rows
    source, returned = inputs[0], cotangent[0]

    tokens, following, near, both, down = start(source, gains[0:1], weights, grps, groups)
    slab = TP * own_rows
    both, down = both.reshape(slab, 2 * UNITS), down.reshape(slab, UNITS)
    tokens = tokens.reshape(group_tokens, D)
    near = near.reshape(D, NEAR)
    both_parts = across_groups(both, groups)
    both_own, down_own = over_grps(both_parts[:1], grps), over_grps([down], grps)

    forget_low = pad_lanes(lax.dynamic_slice_in_dim(forget_weight, member * HEADS, HEADS, 1).astype(HALF))
    bias = pad_lanes(lax.dynamic_slice_in_dim(forget_bias[None], member * HEADS, HEADS, 1))
    head_gains = lax.dynamic_slice_in_dim(gains[2:4], member * HEADS * DH, HEADS * DH, 1)
    head_gains = head_gains.reshape(2, HEADS, DH).transpose(1, 0, 2).reshape(HEADS, 2 * DH)
    head_gains = jnp.pad(head_gains, ((0, 8 - HEADS), (0, 0)))
    queries, keys, values, pairs, gates, logits, gathered = project(
        tokens, following, near, forget_low, bias, head_gains, returned
    )
    queries, down = lax.optimization_barrier((queries, down))
    down_parts = across_groups(down, groups)
    gated, attended, logs, gathered = attend(queries, keys, values, gates, gathered, groups)
    returned_all = gathered.reshape(group_tokens, D)
    gated, both_parts, down_parts = lax.optimization_barrier((gated, both_parts[1:], down_parts[1:]))
    both_pieces = in_order(both_own + over_grps(both_parts, grps))
    down_pieces = in_order(down_own + over_grps(down_parts, grps))
    mixed, second = mix(gated, near, source, gains[1:2])
    second = second.reshape(group_tokens, D)
    hidden, grad_both = feed(second, returned_all, both_pieces, down_pieces, grps, groups)
    grad_mixed, grad_gain_mid, branch, beside, along, far_gate, far_down, up_give, *far_up = unmix(
        grad_both, both_pieces, down_pieces, mixed, gains[1:2], returned, hidden, second, returned_all, grps, groups
    )
    branch = branch.reshape(group_tokens, D)
    size = lax.axis_size("fsdp")
    beside = lax.ppermute(beside, "fsdp", [(to, to ^ 2) for to in range(size)])
    up_keep = far_up[0]
    far_up = [
        lax.ppermute(far_up[step], "fsdp", [(at, (at + step * TP) % size) for at in range(size)])
        for step in range(1, groups)
    ]

    grads_low, queries_back, grad_gates, pack, out_keep, out_give = ungate(
        branch, near, attended, gates, logs, queries, gated, grps, groups
    )
    dqueries, dkeys, dvalues, late, far_out, up_sum, home_gate, home_down = attend_back(
        queries_back,
        grads_low,
        keys,
        values,
        queries,
        pack,
        out_keep,
        up_keep,
        out_give,
        up_give,
        far_gate.reshape(TP, own_rows, UNITS),
        far_down.reshape(TP, own_rows, UNITS),
    )
    if groups > 2:
        everyone = lax.all_gather(dkeys[:, :, DH + 3].sum(axis=1) - dqueries[:, :, DH].sum(axis=1), "fsdp")
        ahead = (jnp.arange(size) // TP > group) & (jnp.arange(size) % TP == member)
        later = -jnp.sum(jnp.where(ahead[:, None], everyone, 0.0), axis=0)
        late = jnp.broadcast_to(later[:, None, None], late.shape)
    grad_projected, grad_logits, grad_heads, grad_bias = unproject(
        dqueries, dkeys, dvalues, grad_gates, pairs, logits, head_gains, late
    )

    input_grad, grads, grad_gains, grad_forget, grad_bias, norm = end(
        grad_projected,
        grad_logits,
        forget_low,
        source,
        gains[0:1],
        grad_mixed,
        grad_gain_mid,
        grad_heads,
        grad_bias,
        far_out.reshape(TP, own_rows, OUT),
        collected([up_sum] + far_up).reshape(TP, own_rows, UNITS),
        home_gate,
        home_down,
        near,
        tokens,
        grps,
        groups,
    )
    norm, beside = lax.optimization_barrier((norm, beside))
    across_chip = (along[0].astype(FULL) + beside[1].astype(FULL)).astype(HALF)
    result = mixed + along[1].astype(FULL) + beside[0].astype(FULL)
    result = result + lax.ppermute(across_chip, "fsdp", [(to, to ^ 4) for to in range(size)]).astype(FULL)
    output = result.astype(HALF)
    grad_norm = norm[0, 0]
    grad_forget, grad_bias = grad_forget.T, grad_bias[0, :H]
    factor = CLIP / jnp.maximum(grad_norm, CLIP)
    new_w, new_wf, new_ws = adam(
        weights, weights_first, weights_second, grads.astype(FULL) * factor, RATE_MATRIX, DECAY
    )
    new_g, new_gf, new_gs = adam(gains, gains_first, gains_second, grad_gains * factor, RATE_GAIN, 0.0)
    new_fw, new_ff, new_fs = adam(
        forget_weight, forget_first, forget_second, grad_forget * factor, RATE_MATRIX, DECAY
    )
    new_fb, new_bf, new_bs = adam(
        forget_bias, bias_first, bias_second, grad_bias * factor, RATE_BIAS, 0.0
    )
    return (
        output[None],
        input_grad[None],
        grad_norm,
        new_w,
        new_wf,
        new_ws,
        new_g,
        new_gf,
        new_gs,
        new_fw,
        new_ff,
        new_fs,
        new_fb,
        new_bf,
        new_bs,
    )


def solution(mesh):
    tokens = P("grp", "fsdp", None)
    matrix = P(("grp", "fsdp"), None)
    return jax.shard_map(
        shards,
        mesh=mesh,
        in_specs=(tokens,) * 2 + (matrix,) * 3 + (P(),) * 9,
        out_specs=(tokens,) * 2 + (P(),) + (matrix,) * 3 + (P(),) * 9,
        check_vma=False,
    )
```

```python
import functools

import jax
import jax.numpy as jnp
from jax import lax
from jax.experimental import pallas as pl
from jax.experimental.pallas import tpu as pltpu
from jax.sharding import PartitionSpec as P

D = 1536
H = 24
DH = 64
F = 4096
STEP = 5

EPS = 1e-06
BETA_ONE = 0.9
BETA_TWO = 0.95
ADAM_EPS = 1e-08
RATE_MATRIX = 0.1
RATE_GAIN = 1.2
RATE_BIAS = 3.0
DECAY = 0.1
CLIP = 1.0
NEGATIVE = -1e30

TP = 8
HEADS = H // TP
UNITS = F // TP
QKVG = HEADS * 4 * DH
OUT = 256
NEAR = QKVG + OUT
LANES = 128
ROWS = 256
TALL = 512
BLOCK = 512
MESH = pl.DeviceIdType.MESH
HALF = jnp.bfloat16
FULL = jnp.float32
VMEM_BYTES = 56 * 1024 * 1024


def params(collective=None, **more):
    if collective is None:
        return pltpu.CompilerParams(vmem_limit_bytes=VMEM_BYTES, **more)
    return pltpu.CompilerParams(
        collective_id=collective, has_side_effects=True, vmem_limit_bytes=VMEM_BYTES, **more
    )


def flip(member, bits):
    for bit in (1, 2, 4):
        if bits & bit:
            member = member + bit - 2 * bit * lax.rem(lax.div(member, bit), 2)
    return member


def place():
    position = lax.axis_index("fsdp")
    return lax.axis_index("grp"), lax.div(position, TP), lax.rem(position, TP)


def cost(micros):
    return pl.CostEstimate(flops=0, bytes_accessed=3_000_000 * micros, transcendentals=0)


def call_out(targets):
    barrier = pltpu.get_barrier_semaphore()
    for target in targets:
        pl.semaphore_signal(barrier, inc=1, device_id=target, device_id_type=MESH)


def hear(targets):
    pl.semaphore_wait(pltpu.get_barrier_semaphore(), len(targets))


def greet(targets):
    call_out(targets)
    hear(targets)


def neighbours(grps, groups):
    grp, group, member = place()

    def device(to_grp=0, to_group=0, bits=0):
        return (
            lax.rem(grp + to_grp, grps),
            lax.rem(group + to_group, groups) * TP + flip(member, bits),
        )

    return device, (
        [device(bits=bits) for bits in range(1, TP)]
        + [device(to_group=step) for step in range(1, groups)]
        + [device(to_grp=step) for step in range(1, grps)]
    )


class Lines:
    def __init__(self, send, receive):
        self.send, self.receive, self.count, self.made = send, receive, 0, []

    def plan(self, source, target, device):
        copy = pltpu.make_async_remote_copy(
            src_ref=source,
            dst_ref=target,
            send_sem=self.send.at[self.count],
            recv_sem=self.receive.at[self.count],
            device_id=device,
            device_id_type=MESH,
        )
        self.count += 1
        self.made.append(copy)
        return copy


def dot(left, right, contract=(1, 0)):
    return lax.dot_general(
        left, right, (((contract[0],), (contract[1],)), ((), ())), preferred_element_type=FULL
    )


def rms_rows(value, gain):
    return value * lax.rsqrt(jnp.mean(value * value, axis=-1, keepdims=True) + EPS) * gain


def rms_back(value, gain, grad):
    inverse = lax.rsqrt(jnp.mean(value * value, axis=-1, keepdims=True) + EPS)
    normal = value * inverse
    scaled = grad * gain
    pulled = inverse * (scaled - normal * jnp.mean(scaled * normal, axis=-1, keepdims=True))
    return pulled, jnp.sum(grad * normal, axis=0, keepdims=True)


def half_lanes(value, column, upper):
    base = column // LANES * LANES
    part = value[:, base : base + LANES]
    if (column % LANES != 0) != upper:
        part = pltpu.roll(part, DH, 1)
    return part


def two_halves(value, lower, upper, lanes):
    low = half_lanes(value, lower, False)
    if upper is None:
        return jnp.where(lanes < DH, low, 0.0)
    return jnp.where(lanes < DH, low, half_lanes(value, upper, True))


def pack_near(w_ref, near):
    lanes = lax.broadcasted_iota(jnp.int32, (w_ref.shape[0], LANES), 1)
    for member in range(TP):
        for head in range(HEADS):
            at = (member * HEADS + head) * DH
            near[member, :, 256 * head : 256 * head + LANES] = two_halves(w_ref, at, D + at, lanes).astype(HALF)
            near[member, :, 256 * head + LANES : 256 * head + 256] = two_halves(
                w_ref, 2 * D + at, 3 * D + at, lanes
            ).astype(HALF)
        at = 4 * D + member * HEADS * DH
        near[member, :, QKVG : QKVG + LANES] = two_halves(w_ref, at, at + DH, lanes).astype(HALF)
        near[member, :, QKVG + LANES :] = two_halves(w_ref, at + 2 * DH, None, lanes).astype(HALF)


def pack_far(w_ref, both, down):
    edge = 5 * D
    for member in range(TP):
        at = edge + member * UNITS
        both[member, :, :UNITS] = w_ref[:, at : at + UNITS].astype(HALF)
        both[member, :, UNITS:] = w_ref[:, at + F : at + F + UNITS].astype(HALF)
        down[member] = w_ref[:, at + 2 * F : at + 2 * F + UNITS].astype(HALF)


def halves(ref):
    count = ref.shape[0] // 2
    return [ref.at[pl.ds(at * count, count)] for at in range(2)]


def halves(ref):
    count = ref.shape[0] // 2
    return [ref.at[pl.ds(at * count, count)] for at in range(2)]


def start_counts(grps, groups):
    weights = (TP - 1) + (groups - 1) * TP + (grps - 1) * groups * TP
    return GATHER + 2 * (groups - 1) + weights + 2 * (TP - 1)


def start_kernel(
    grps, groups, x_ref, g_ref, w_ref, all_ref, next_ref, full_ref, both_ref, down_ref,
    block, near, both, down, send, receive, local,
):
    grp, group, member = place()
    device, everyone = neighbours(grps, groups)
    call_out(everyone)
    block[...] = rms_rows(x_ref[...].astype(FULL), g_ref[...]).astype(HALF)
    lines = Lines(send, receive)
    first, across, over, far = {}, {}, {}, []
    tokens = gather_plan(lines, block, all_ref, True)
    ahead, aside = [], []
    for back in range(1, groups):
        ahead.append(lines.plan(block, next_ref.at[back - 1, 0], device(to_group=groups - back)))
        aside.append(lines.plan(next_ref.at[back - 1, 0], next_ref.at[back - 1, 1], device(bits=4)))
    for bits in range(1, TP):
        first[bits] = lines.plan(near.at[flip(member, bits)], full_ref.at[grp, group, member], device(bits=bits))
    for bits in range(TP):
        slot = full_ref.at[grp, group, flip(member, bits)]
        source = near.at[member] if bits == 0 else slot
        for back in range(1, groups):
            across[back, bits] = lines.plan(source, slot, device(to_group=groups - back))
        for step in range(1, grps):
            over[step, 0, bits] = lines.plan(source, slot, device(to_grp=step))
        for back in range(1, groups):
            passed = full_ref.at[grp, lax.rem(group + back, groups), flip(member, bits)]
            for step in range(1, grps):
                over[step, back, bits] = lines.plan(passed, passed, device(to_grp=step))
    for bits in range(1, TP):
        there = flip(member, bits)
        far.append(lines.plan(both.at[there], both_ref.at[member], device(bits=bits)))
        far.append(lines.plan(down.at[there], down_ref.at[member], device(bits=bits)))

    own_tokens = pltpu.make_async_copy(block, all_ref.at[member], local.at[0])
    own = [
        pltpu.make_async_copy(near.at[member], full_ref.at[grp, group, member], local.at[1]),
        pltpu.make_async_copy(both.at[member], both_ref.at[member], local.at[2]),
        pltpu.make_async_copy(down.at[member], down_ref.at[member], local.at[3]),
    ]
    hear(everyone)
    for copy in ahead:
        copy.start()
    pack_near(w_ref, near)
    for bits in (4, 2, 6, 1, 5, 3, 7):
        first[bits].start()
    for back in range(1, groups):
        across[back, 0].start()
    for step in range(1, grps):
        over[step, 0, 0].start()
    gather_start(tokens, own_tokens)
    own[0].start()
    pack_far(w_ref, both, down)
    for bits in (1, 5, 3, 7, 2, 4, 6):
        first[bits].wait_recv()
        for back in range(1, groups):
            across[back, bits].start()
        for step in range(1, grps):
            over[step, 0, bits].start()
    gather_turn(tokens, True)
    for copy in far:
        copy.start()
    for copy in own[1:]:
        copy.start()
    for come, gone in zip(ahead, aside):
        come.wait_recv()
        gone.start()
    gather_pass(tokens, True)
    for back in range(1, groups):
        for bits in (0, 1, 5, 3, 7, 2, 4, 6):
            across[back, bits].wait_recv()
            for step in range(1, grps):
                over[step, back, bits].start()
    gather_end(tokens, own_tokens)
    for copy in aside + far + list(over.values()):
        copy.wait_recv()
    for copy in lines.made:
        copy.wait_send()
    for copy in own:
        copy.wait()


def start(source, gain, weights, grps, groups):
    rows, own = source.shape[0], weights.shape[0]
    count = start_counts(grps, groups)
    vmem, anywhere = pl.BlockSpec(memory_space=pltpu.VMEM), pl.BlockSpec(memory_space=pl.ANY)
    return pl.pallas_call(
        functools.partial(start_kernel, grps, groups),
        out_shape=(
            jax.ShapeDtypeStruct((TP, rows, D), HALF),
            jax.ShapeDtypeStruct((groups - 1, 2, rows, D), HALF),
            jax.ShapeDtypeStruct((grps, groups, TP, own, NEAR), HALF),
            jax.ShapeDtypeStruct((TP, own, 2 * UNITS), HALF),
            jax.ShapeDtypeStruct((TP, own, UNITS), HALF),
        ),
        in_specs=[vmem] * 3,
        out_specs=(anywhere,) * 5,
        scratch_shapes=[
            pltpu.VMEM((rows, D), HALF),
            pltpu.VMEM((TP, own, NEAR), HALF),
            pltpu.VMEM((TP, own, 2 * UNITS), HALF),
            pltpu.VMEM((TP, own, UNITS), HALF),
            pltpu.SemaphoreType.DMA((count,)),
            pltpu.SemaphoreType.DMA((count,)),
            pltpu.SemaphoreType.DMA((4,)),
        ],
        compiler_params=params(1),
        name="start",
        cost_estimate=cost(60),
    )(source, gain, weights)


def three(value):
    high = value.astype(HALF).astype(FULL)
    rest = value - high
    middle = rest.astype(HALF).astype(FULL)
    return high, middle, (rest - middle).astype(HALF).astype(FULL)


def two(value):
    high = value.astype(HALF)
    return high, (value - high.astype(FULL)).astype(HALF)


def at_lanes(lanes, pairs, other):
    for lane, value in pairs:
        other = jnp.where(lanes == lane, value, other)
    return other


def side_by_side(values, lanes):
    packed = jnp.zeros_like(values[0])
    for at, value in enumerate(values):
        if at:
            value = pltpu.roll(value, HEADS * at, 1)
        packed = jnp.where((lanes >= HEADS * at) & (lanes < HEADS * (at + 1)), value, packed)
    return packed.astype(HALF)


def picker(targets):
    def build(width, find, sign=1.0):
        row = lax.broadcasted_iota(jnp.int32, (LANES, width), 0)
        col = lax.broadcasted_iota(jnp.int32, (LANES, width), 1)
        return jnp.where(row == find(col), sign, 0.0).astype(HALF)

    return build(*targets)


def spread_lanes(first, at):
    def find(col):
        head, lane = lax.div(col, LANES), lax.rem(col, LANES) - at
        return jnp.where((lane >= 0) & (lane < 3), HEADS * (first + lane) + head, -1)

    return find


def halves_matrix(scale):
    row = lax.broadcasted_iota(jnp.int32, (LANES, LANES), 0)
    col = lax.broadcasted_iota(jnp.int32, (LANES, LANES), 1)
    return jnp.where((row < DH) == (col < DH), scale, 0.0).astype(HALF)


def halves_mean(value, matrix):
    high, least = two(value)
    return dot(high, matrix) + dot(least, matrix)


def side_plan(lines, pair_ref, all_ref):
    member = place()[2]
    plan = {}
    for at, bits in ((0, 0), (1, 4)):
        there = flip(member, bits)
        plan[bits + 2] = lines.plan(pair_ref.at[at], all_ref.at[there], group_device(2))
        plan[bits + 1] = lines.plan(pair_ref.at[at], all_ref.at[there], group_device(1))
    for bits in (2, 6):
        slot = all_ref.at[flip(member, bits)]
        plan[bits + 1] = lines.plan(slot, slot, group_device(1))
    return plan


def first_leg(lines, block, all_ref):
    member = place()[2]
    return {bits: lines.plan(block, all_ref.at[member], group_device(bits)) for bits in (2, 4)}


def third_leg(lines, all_ref):
    member = place()[2]

    def copy(block, bits):
        slot = all_ref.at[flip(member, block)]
        return lines.plan(slot, slot, group_device(bits))

    return {6: copy(4, 2), 1: copy(0, 1), 3: copy(2, 1), 5: copy(4, 1), 7: copy(6, 1)}


def project_kernel(
    groups, a_ref, n_ref, w_ref, f_ref, b_ref, g_ref, c_ref,
    q_ref, k_ref, v_ref, p_ref, t_ref, z_ref, all_ref, others, decays, totals, send, receive, local,
):
    turn = pl.program_id(0)
    grp, group, member = place()
    own = a_ref.shape[0]
    rows = own // TP
    lanes = lax.broadcasted_iota(jnp.int32, (TALL, LANES), 1)

    def plans():
        lines = Lines(send, receive)
        sides = [side_plan(lines, n_ref.at[at], others.at[at]) for at in range(groups - 1)]
        copies = [
            pltpu.make_async_copy(n_ref.at[at, half], others.at[at, flip(member, 4 * half)], local.at[2 * at + half])
            for at in range(groups - 1)
            for half in range(2)
        ]
        copies.append(pltpu.make_async_copy(c_ref, all_ref.at[member], local.at[2 * groups - 2]))
        return lines, sides, copies, first_leg(lines, c_ref, all_ref)

    def low_rows(index, start, count):
        if index == 0:
            return a_ref[start : start + count]
        return others[index - 1, start // rows : (start + count) // rows].reshape(count, D)

    def scan(index):
        row = lax.broadcasted_iota(jnp.int32, (ROWS, ROWS), 0)
        col = lax.broadcasted_iota(jnp.int32, (ROWS, ROWS), 1)
        lower = jnp.where(col <= row, 1.0, 0.0)
        carry = jnp.zeros((1, LANES), FULL)
        for start in range(0, own, ROWS):
            logit = dot(low_rows(index, start, ROWS), f_ref[...]) + b_ref[...]
            if index == 0:
                z_ref[start : start + ROWS] = logit
            log_gate = jnp.minimum(logit, 0.0) - jnp.log1p(jnp.exp(-jnp.abs(logit)))
            part = carry + lax.dot_general(
                lower,
                log_gate,
                (((1,), (0,)), ((), ())),
                precision=lax.Precision.HIGHEST,
                preferred_element_type=FULL,
            )
            decays[index, start : start + ROWS] = part
            carry = part[ROWS - 1 : ROWS]
        totals[index : index + 1] = carry

    def rows_done(low, sums, start, first):
        here = slice(start, start + TALL)
        made = dot(low, w_ref[...])
        means = halves_matrix(1.0 / DH)
        packed = side_by_side(three(jnp.where(lanes < HEADS, sums, 0.0)), lanes)
        plus = dot(packed, picker((HEADS * LANES, spread_lanes(0, DH))))
        minus = dot(packed, picker((HEADS * LANES, spread_lanes(0, DH + 3), -1.0)))
        ones_of_query = jnp.where((lanes >= DH + 3) & (lanes < DH + 6), 1.0, 0.0)
        ones_of_value = jnp.where((lanes >= DH) & (lanes < DH + 3), 1.0, 0.0)
        ones_of_key = jnp.where((lanes >= DH + 6) & (lanes < DH + 9), 1.0, ones_of_value)
        for head in range(HEADS):
            register = slice(LANES * head, LANES * (head + 1))
            pair = made[:, 256 * head : 256 * head + LANES]
            value = made[:, 256 * head + LANES : 256 * head + 2 * LANES]
            normal = pair * lax.rsqrt(halves_mean(pair * pair, means) + EPS) * g_ref[head : head + 1]
            normal = normal.astype(HALF).astype(FULL)
            q_ref[head, here] = jnp.where(
                lanes < DH, normal * (DH**-0.5), plus[:, register] + ones_of_query
            ).astype(HALF)
            k_ref[head, here] = jnp.where(
                lanes < DH, pltpu.roll(normal, DH, 1), minus[:, register] + ones_of_key
            ).astype(HALF)
            v_ref[head, here] = jnp.where(lanes < DH, value, ones_of_value).astype(HALF)
            if first:
                p_ref[here, register] = pair
        if first:
            left, right = gates_of(made, lanes)
            t_ref[here, :LANES] = left
            t_ref[here, LANES:] = right

    @pl.when(turn == 0)
    def begin():
        greet([group_device(bits) for bits in (4, 2, 1)])
        lines, sides, copies, leg = plans()
        for copy in copies:
            copy.start()
        for side in sides:
            for bits in (2, 6, 1, 5):
                side[bits].start()
        leg[4].start()
        scan(0)
        for start in range(0, own, TALL):
            rows_done(low_rows(0, start, TALL), decays[0, start : start + TALL], start, True)
        leg[2].start()
        for side in sides:
            for bits in (2, 6):
                side[bits].wait_recv()
                side[bits + 1].start()

    @pl.when(turn == 1)
    def arrived():
        lines, sides, copies, leg = plans()
        for copy in copies[:-1]:
            copy.wait()
        for side in sides:
            for bits in (1, 3, 5, 7):
                side[bits].wait_recv()
        for index in range(1, groups):
            scan(index)

    @pl.when(turn > 0)
    def next_group():
        ahead = turn < groups - group
        base = jnp.zeros((1, LANES), FULL)
        for index in range(groups):
            weight = jnp.where(ahead, jnp.where(index < turn, 1.0, 0.0), jnp.where(index >= turn, -1.0, 0.0))
            base = base + weight * totals[index : index + 1]
        for start in range(0, own, TALL):
            low = others[turn - 1, start // rows : (start + TALL) // rows].reshape(TALL, D)
            rows_done(low, decays[turn, start : start + TALL] + base, start, False)

    @pl.when(turn == groups - 1)
    def end():
        lines, sides, copies, leg = plans()
        copies[-1].wait()
        for copy in leg.values():
            copy.wait_recv()
        for copy in lines.made:
            copy.wait_send()


def project(tokens, following, full, forget, bias, gains, returned):
    own, groups = tokens.shape[0], following.shape[0] + 1
    rows = returned.shape[0]
    count = 6 * (groups - 1) + 2
    tile = pl.BlockSpec((HEADS, own, LANES), lambda i: (0, i, 0))
    anywhere = pl.BlockSpec(memory_space=pl.ANY)
    return pl.pallas_call(
        functools.partial(project_kernel, groups),
        grid=(groups,),
        out_shape=(
            jax.ShapeDtypeStruct((HEADS, groups * own, LANES), HALF),
            jax.ShapeDtypeStruct((HEADS, groups * own, LANES), HALF),
            jax.ShapeDtypeStruct((HEADS, groups * own, LANES), HALF),
            jax.ShapeDtypeStruct((own, HEADS * LANES), FULL),
            jax.ShapeDtypeStruct((own, OUT), FULL),
            jax.ShapeDtypeStruct((own, LANES), FULL),
            jax.ShapeDtypeStruct((TP, rows, D), HALF),
        ),
        in_specs=[
            whole_spec((own, D)),
            anywhere,
            weight_spec(QKVG, 0),
            whole_spec((D, LANES)),
            whole_spec((1, LANES)),
            whole_spec((8, LANES)),
            whole_spec((rows, D)),
        ],
        out_specs=(
            tile,
            tile,
            tile,
            whole_spec((own, HEADS * LANES)),
            whole_spec((own, OUT)),
            whole_spec((own, LANES)),
            anywhere,
        ),
        scratch_shapes=[
            pltpu.VMEM((groups - 1, TP, rows, D), HALF),
            pltpu.VMEM((groups, own, LANES), FULL),
            pltpu.VMEM((max(groups, 8), LANES), FULL),
            pltpu.SemaphoreType.DMA((count,)),
            pltpu.SemaphoreType.DMA((count,)),
            pltpu.SemaphoreType.DMA((2 * groups - 1,)),
        ],
        compiler_params=params(8),
        name="project",
        cost_estimate=cost(25),
    )(tokens, following, full, forget, bias, gains, returned)


def sigmoid(value):
    return 1.0 / (1.0 + jnp.exp(-value))


def gates_of(made, lanes):
    second = [made[:, 256 * head + LANES : 256 * head + 2 * LANES] for head in range(HEADS)]
    left = jnp.where(lanes < DH, pltpu.roll(second[0], DH, 1), second[1])
    right = jnp.where(lanes < DH, pltpu.roll(second[2], DH, 1), 0.0)
    return left, right


def attend_kernel(
    groups, steps, q_ref, k_ref, v_ref, t_ref, c_ref, u_ref, o_ref, l_ref, all_ref, send, receive
):
    count = u_ref.shape[0]
    at_step = pl.program_id(0)

    @pl.when(at_step == 0)
    def begin():
        greet([group_device(bits) for bits in (2, 1)])
        plan = third_leg(Lines(send, receive), all_ref)
        for bits in (6, 1, 3, 5):
            plan[bits].start()

    @pl.when(at_step == steps - 1)
    def pass_on():
        plan = third_leg(Lines(send, receive), all_ref)
        plan[6].wait_recv()
        plan[7].start()

    queries = [q_ref[head] for head in range(HEADS)]

    def visit(state, at, masked):
        new = []
        for head in range(HEADS):
            top, accum = state[head]
            scores = dot(queries[head], k_ref[head, pl.ds(at * count, count)], (1, 1))
            if masked:
                row = lax.broadcasted_iota(jnp.int32, scores.shape, 0)
                col = lax.broadcasted_iota(jnp.int32, scores.shape, 1)
                scores = jnp.where(col <= row, scores, NEGATIVE)
            high = jnp.maximum(top, jnp.max(scores, axis=1, keepdims=True))
            weight = jnp.exp(scores - high)
            accum = accum * jnp.exp(top - high) + dot(weight.astype(HALF), v_ref[head, pl.ds(at * count, count)])
            new.append((high, accum))
        return tuple(new)

    state = tuple(
        (jnp.full((count, 1), NEGATIVE, FULL), jnp.zeros((count, LANES), FULL)) for head in range(HEADS)
    )
    earlier = (groups - place()[1]) * steps
    state = lax.fori_loop(earlier, groups * steps, lambda at, inner: visit(inner, at, False), state)
    state = lax.fori_loop(0, at_step, lambda at, inner: visit(inner, at, False), state)
    state = visit(state, at_step, True)
    lanes = lax.broadcasted_iota(jnp.int32, (count, LANES), 1)
    out, logs = [], []
    for top, accum in state:
        total = jnp.sum(jnp.where(lanes == DH, accum, 0.0), axis=1, keepdims=True)
        out.append(jnp.where(lanes < DH, accum / total, 0.0))
        logs.append(top + jnp.log(total))
    left, right = t_ref[:, :LANES], t_ref[:, LANES:]
    pair = out[0] + pltpu.roll(out[1], DH, 1)
    o_ref[:, :LANES] = pair
    o_ref[:, LANES:] = out[2]
    u_ref[:, :LANES] = (pair * sigmoid(left)).astype(HALF)
    u_ref[:, LANES:] = (out[2] * sigmoid(right)).astype(HALF)
    l_ref[...] = at_lanes(lanes, tuple(enumerate(logs)), 0.0)

    @pl.when(at_step == steps - 1)
    def end():
        plan = third_leg(Lines(send, receive), all_ref)
        for bits in (1, 3, 5, 7):
            plan[bits].wait_recv()
        for copy in plan.values():
            copy.wait_send()


def attend(queries, keys, values, gates, gathered, groups):
    tokens = keys.shape[1]
    own = tokens // groups
    count = min(BLOCK, own)
    steps = own // count
    whole = pl.BlockSpec((HEADS, tokens, LANES), lambda i: (0, 0, 0), pipeline_mode=pl.Buffered(1))
    anywhere = pl.BlockSpec(memory_space=pl.ANY)
    return pl.pallas_call(
        functools.partial(attend_kernel, groups, steps),
        grid=(steps,),
        in_specs=[
            pl.BlockSpec((HEADS, count, LANES), lambda i: (0, i, 0)),
            whole,
            whole,
            pl.BlockSpec((count, OUT), lambda i: (i, 0)),
            anywhere,
        ],
        out_specs=(
            pl.BlockSpec((count, OUT), lambda i: (i, 0)),
            pl.BlockSpec((count, OUT), lambda i: (i, 0)),
            pl.BlockSpec((count, LANES), lambda i: (i, 0)),
            anywhere,
        ),
        out_shape=(
            jax.ShapeDtypeStruct((own, OUT), HALF),
            jax.ShapeDtypeStruct((own, OUT), FULL),
            jax.ShapeDtypeStruct((own, LANES), FULL),
            jax.ShapeDtypeStruct(gathered.shape, HALF),
        ),
        scratch_shapes=[pltpu.SemaphoreType.DMA((5,)), pltpu.SemaphoreType.DMA((5,))],
        input_output_aliases={4: 3},
        compiler_params=params(9),
        name="attend",
        cost_estimate=cost(16),
    )(queries, keys, values, gates, gathered)


def group_device(bits):
    grp, group, member = place()
    return (grp, group * TP + flip(member, bits))


def blocks_of(ref, core):
    value = ref[:, pl.ds(core, 1)]
    return value.reshape(ref.shape[0] * ref.shape[2], ref.shape[3])


def sum_plan(lines, stage):
    give, take, out, came = stage
    sibling = [lines.plan(give.at[at], take.at[at], group_device(1)) for at in range(4)]
    others = [lines.plan(out.at[at], came.at[at], group_device(bits)) for at, bits in enumerate((2, 4, 6))]
    return sibling, others


def sum_give(pairs, stage, plan, mine):
    give = stage[0]
    grp, group, member = place()
    core = lax.rem(member, 2)
    count = give.shape[1]
    theirs = sum(dot(blocks_of(left, 1 - core), right[...], (1, 1)) for left, right in pairs)
    mine[...] = theirs.reshape(4, count, D)
    for at, bits in enumerate((2, 4, 6, 0)):
        give[at] = mine[lax.div(flip(member, bits), 2)].astype(HALF)
        plan[0][at].start()
    own = sum(dot(blocks_of(left, core), right[...], (1, 1)) for left, right in pairs)
    mine[...] = own.reshape(4, count, D)


def sum_pass(stage, plan, mine):
    give, take, out, came = stage
    member = place()[2]
    for at, bits in enumerate((2, 4, 6)):
        plan[0][at].wait_recv()
        out[at] = (mine[lax.div(flip(member, bits), 2)] + take[at].astype(FULL)).astype(HALF)
        plan[1][at].start()
    plan[0][3].wait_recv()
    return mine[lax.div(member, 2)] + take[3].astype(FULL)


def sum_send(pairs, stage, plan, mine):
    sum_give(pairs, stage, plan, mine)
    return sum_pass(stage, plan, mine)


def sum_take(total, stage, plan):
    give, take, out, came = stage
    for at in range(3):
        plan[1][at].wait_recv()
        total = total + came[at].astype(FULL)
    return total


def sum_scratch(rows):
    return [
        pltpu.VMEM((4, rows, D), HALF),
        pltpu.VMEM((4, rows, D), HALF),
        pltpu.VMEM((3, rows, D), HALF),
        pltpu.VMEM((3, rows, D), HALF),
    ]


def gather_plan(lines, block, all_ref, light=False):
    member = place()[2]

    def slot(bits):
        return halves(all_ref.at[flip(member, bits)])

    plan = {(bits, half): lines.plan(halves(block)[half], slot(0)[half], group_device(bits)) for bits in (4, 2) for half in range(2)}
    plan[1] = lines.plan(block, all_ref.at[member], group_device(1))
    plan[6, 0] = lines.plan(slot(4)[0], slot(4)[0], group_device(2))
    if light:
        plan[6, 1] = lines.plan(slot(4)[1], slot(4)[1], group_device(2))
    else:
        plan[6, 1] = lines.plan(slot(2)[1], slot(2)[1], group_device(4))
    for bits in (4, 2, 6):
        for half in range(2):
            plan[bits + 1, half] = lines.plan(slot(bits)[half], slot(bits)[half], group_device(1))
    return plan


GATHER = 13


def gather_start(plan, own):
    own.start()
    for key in ((4, 0), (2, 1), (4, 1), (2, 0), 1):
        plan[key].start()


def gather_turn(plan, light=False):
    for bits, half in ((4, 0), (4, 1) if light else (2, 1)):
        plan[bits, half].wait_recv()
        plan[6, half].start()
        plan[bits + 1, half].start()


def gather_pass(plan, light=False):
    for bits, half in ((2, 1) if light else (4, 1), (2, 0), (6, 0), (6, 1)):
        plan[bits, half].wait_recv()
        plan[bits + 1, half].start()


def gather_end(plan, own):
    plan[1].wait_recv()
    for bits in (5, 3, 7):
        for half in range(2):
            plan[bits, half].wait_recv()
    own.wait()


def gather_run(plan, own):
    gather_start(plan, own)
    gather_turn(plan)
    gather_pass(plan)
    gather_end(plan, own)


def mix_kernel(u_ref, w_ref, x_ref, g_ref, y_ref, all_ref, mine, block, give, take, out, came, send, receive, local):
    greet([group_device(bits) for bits in (1, 2, 4, 6)])
    member = place()[2]
    lines = Lines(send, receive)
    stage = (give, take, out, came)
    sums = sum_plan(lines, stage)
    gathered = gather_plan(lines, block, all_ref)
    total = sum_take(sum_send([(u_ref, w_ref)], stage, sums, mine), stage, sums)
    mixed = x_ref[...].astype(FULL) + total
    y_ref[...] = mixed
    block[...] = rms_rows(mixed, g_ref[...]).astype(HALF)
    gather_run(gathered, pltpu.make_async_copy(block, all_ref.at[member], local.at[0]))
    for copy in lines.made:
        copy.wait_send()


def whole_spec(shape):
    zeros = (0,) * len(shape)
    return pl.BlockSpec(shape, lambda i: zeros)


def weight_spec(columns, at):
    return pl.BlockSpec((D, columns), lambda i: (0, at))


def mix(gated, full, source, gain):
    rows = source.shape[0]
    count = 7 + GATHER
    return pl.pallas_call(
        mix_kernel,
        grid=(1,),
        out_shape=(
            jax.ShapeDtypeStruct((rows, D), FULL),
            jax.ShapeDtypeStruct((TP, rows, D), HALF),
        ),
        in_specs=[
            whole_spec((4, 2, rows, OUT)),
            weight_spec(OUT, QKVG // OUT),
            whole_spec((rows, D)),
            whole_spec((1, D)),
        ],
        out_specs=(whole_spec((rows, D)), pl.BlockSpec(memory_space=pl.ANY)),
        scratch_shapes=[pltpu.VMEM((4, rows, D), FULL), pltpu.VMEM((rows, D), HALF)]
        + sum_scratch(rows)
        + [
            pltpu.SemaphoreType.DMA((count,)),
            pltpu.SemaphoreType.DMA((count,)),
            pltpu.SemaphoreType.DMA((1,)),
        ],
        compiler_params=params(2),
        name="mix",
        cost_estimate=cost(40),
    )(gated.reshape(4, 2, rows, OUT), full, source, gain)


def slabs(grps, groups):
    grp, group, member = place()
    return [
        (turn, step, lax.rem(grp + turn, grps) * groups + lax.rem(group + step, groups))
        for turn in range(grps)
        for step in range(groups)
    ]


def load_rows(refs, whole, semaphores, grps, groups):
    rows = whole.shape[0] // (grps * groups)
    copies = []
    for at, (turn, step, index) in enumerate(slabs(grps, groups)):
        copies.append(pltpu.make_async_copy(refs[at], whole.at[pl.ds(index * rows, rows)], semaphores.at[at]))
    return copies


def unmix_kernel(grps, groups, d_ref, x_ref, g_ref, c_ref, m_ref, a_ref, r_ref, *rest):
    total_slabs = grps * groups
    both_refs, down_refs = rest[:total_slabs], rest[total_slabs : 2 * total_slabs]
    dx_ref, dg_ref, all_ref, beside_ref, along_ref, gate_ref, down_ref, give_ref, *rest = rest[2 * total_slabs :]
    up_refs, rest = rest[:groups], rest[groups:]
    wgu, wdn, mine, block, give, take, out, came, give2, take2, *rest = rest
    grads, over_got, across_out, across_got, send, receive, local = rest
    device, everyone = neighbours(grps, groups)
    everyone = [group_device(bits) for bits in (1, 2, 4, 6)] + everyone[TP - 1 :]
    call_out(everyone)
    grp, group, member = place()
    core = lax.rem(member, 2)
    load_both = load_rows(both_refs, wgu, local.at[pl.ds(0, total_slabs)], grps, groups)
    load_down = load_rows(down_refs, wdn, local.at[pl.ds(total_slabs, total_slabs)], grps, groups)
    for copy in load_both + load_down:
        copy.start()
    lines = Lines(send, receive)
    stage = (give, take, out, came)
    sums = sum_plan(lines, stage)
    gathered = gather_plan(lines, block, all_ref)
    output = lines.plan(give2, take2, group_device(1))
    rows = D // total_slabs
    places = slabs(grps, groups)
    down, gate, up = range(3)
    over = [
        {
            (turn, step): lines.plan(
                grads.at[kind, pl.ds(index * rows, rows)], over_got.at[kind, turn - 1, step], device(turn)
            )
            for turn, step, index in places
            if turn and (step or kind != up)
        }
        for kind in range(3)
    ]
    across = [
        [
            lines.plan(across_out.at[kind, step - 1], across_got.at[kind, step - 1], device(to_group=step))
            for step in range(1, groups)
        ]
        for kind in (down, gate)
    ]
    cut = D // 4

    def grad_of(kind, left, right):
        for at in range(4):
            here = slice(at * cut, (at + 1) * cut)
            grads[kind, here] = dot(left[:, here], right, (0, 0)).astype(HALF)

    def over_sum(kind, step):
        value = grads[kind, pl.ds(places[step][2] * rows, rows)].astype(FULL)
        for turn in range(1, grps):
            over[kind][turn, step].wait_recv()
            value = value + over_got[kind, turn - 1, step].astype(FULL)
        return value

    def begin_over(kind, steps):
        for step in steps:
            for turn in range(1, grps):
                over[kind][turn, step].start()

    def cross(kind):
        for step in range(1, groups):
            across_out[kind, step - 1] = over_sum(kind, step).astype(HALF)
            across[kind][step - 1].start()

    def crossed(kind):
        value = over_sum(kind, 0)
        for step in range(1, groups):
            across[kind][step - 1].wait_recv()
            value = value + across_got[kind, step - 1].astype(FULL)
        return value.astype(HALF)

    tokens, count = r_ref.shape[0], x_ref.shape[0]
    hidden, both = m_ref[...].reshape(tokens, UNITS), d_ref[...].reshape(tokens, 2 * UNITS)
    grad_of(down, r_ref, hidden)
    hear(everyone)
    begin_over(down, range(1, groups))
    for copy in load_both:
        copy.wait()
    sum_give([(d_ref, wgu)], stage, sums, mine)
    grad_of(gate, a_ref, both[:, :UNITS])
    begin_over(gate, range(1, groups))
    total = sum_pass(stage, sums, mine)
    cross(down)
    begin_over(down, [0])
    for copy in load_down:
        copy.wait()
    give2[...] = dot(blocks_of(m_ref, 1 - core), wdn[...], (1, 1)).astype(HALF).reshape(4, count, D)
    output.start()
    grad_of(up, a_ref, both[:, UNITS:])
    cross(gate)
    begin_over(up, range(1, groups))
    mine[...] = dot(blocks_of(m_ref, core), wdn[...], (1, 1)).reshape(4, count, D)
    total = sum_take(total, stage, sums)
    pulled, dgain = rms_back(x_ref[...], g_ref[...], total)
    grad = c_ref[...].astype(FULL) + pulled
    block[...] = grad.astype(HALF)
    own = pltpu.make_async_copy(block, all_ref.at[member], local.at[2 * total_slabs])
    gather_start(gathered, own)
    dx_ref[...] = grad
    dg_ref[...] = dgain
    output.wait_recv()
    for at, bits in enumerate((2, 6, 4, 0)):
        chip = lax.div(flip(member, bits), 2)
        target = (beside_ref if at < 2 else along_ref).at[at % 2]
        target[...] = (mine[chip] + take2[chip].astype(FULL)).astype(HALF)
    gather_turn(gathered)
    begin_over(gate, [0])
    gather_pass(gathered)
    for step in range(1, groups):
        up_refs[step][...] = over_sum(up, step).astype(HALF)
    for turn, step, index in places:
        if step == 0:
            target = give_ref.at[turn - 1] if turn else up_refs[0]
            target[...] = grads[up, pl.ds(index * rows, rows)]
    gather_end(gathered, own)
    down_ref[...] = crossed(down)
    gate_ref[...] = crossed(gate)
    for copy in lines.made:
        copy.wait_send()


def unmix(grads, both, down, mixed, gain, returned, hidden, second, returned_all, grps, groups):
    rows, tokens = mixed.shape[0], second.shape[0]
    slab = both[0].shape[0]
    total_slabs = grps * groups
    count = 8 + GATHER + (grps - 1) * (3 * groups - 1) + 2 * (groups - 1)
    piece = jax.ShapeDtypeStruct((slab, UNITS), HALF)
    return pl.pallas_call(
        functools.partial(unmix_kernel, grps, groups),
        grid=(1,),
        out_shape=(
            jax.ShapeDtypeStruct((rows, D), FULL),
            jax.ShapeDtypeStruct((1, D), FULL),
            jax.ShapeDtypeStruct((TP, rows, D), HALF),
            jax.ShapeDtypeStruct((2, rows, D), HALF),
            jax.ShapeDtypeStruct((2, rows, D), HALF),
        )
        + (piece,) * 2
        + (jax.ShapeDtypeStruct((grps - 1, slab, UNITS), HALF),)
        + (piece,) * groups,
        in_specs=[
            whole_spec((4, 2, rows, 2 * UNITS)),
            whole_spec((rows, D)),
            whole_spec((1, D)),
            whole_spec((rows, D)),
            whole_spec((4, 2, rows, UNITS)),
            whole_spec((tokens, D)),
            whole_spec((tokens, D)),
        ]
        + [pl.BlockSpec(memory_space=pl.ANY)] * (2 * total_slabs),
        out_specs=(
            whole_spec((rows, D)),
            whole_spec((1, D)),
            pl.BlockSpec(memory_space=pl.ANY),
            whole_spec((2, rows, D)),
            whole_spec((2, rows, D)),
        )
        + (whole_spec((slab, UNITS)),) * 2
        + (whole_spec((grps - 1, slab, UNITS)),)
        + (whole_spec((slab, UNITS)),) * groups,
        scratch_shapes=[
            pltpu.VMEM((D, 2 * UNITS), HALF),
            pltpu.VMEM((D, UNITS), HALF),
            pltpu.VMEM((4, rows, D), FULL),
            pltpu.VMEM((rows, D), HALF),
        ]
        + sum_scratch(rows)
        + [
            pltpu.VMEM((4, rows, D), HALF),
            pltpu.VMEM((4, rows, D), HALF),
            pltpu.VMEM((3, D, UNITS), HALF),
            pltpu.VMEM((3, grps - 1, groups, slab, UNITS), HALF),
            pltpu.VMEM((2, groups - 1, slab, UNITS), HALF),
            pltpu.VMEM((2, groups - 1, slab, UNITS), HALF),
            pltpu.SemaphoreType.DMA((count,)),
            pltpu.SemaphoreType.DMA((count,)),
            pltpu.SemaphoreType.DMA((2 * total_slabs + 1,)),
        ],
        compiler_params=params(3),
        name="unmix",
        cost_estimate=cost(55),
    )(
        grads.reshape(4, 2, rows, 2 * UNITS),
        mixed,
        gain,
        returned,
        hidden.reshape(4, 2, rows, UNITS),
        second,
        returned_all,
        *both,
        *down,
    )


def feed_kernel(grps, groups, a_ref, c_ref, *rest):
    total_slabs = grps * groups
    both_refs, down_refs = rest[:total_slabs], rest[total_slabs : 2 * total_slabs]
    m_ref, d_ref, wgu, wdn, local = rest[2 * total_slabs :]

    @pl.when(pl.program_id(0) == 0)
    def load():
        copies = load_rows(both_refs, wgu, local.at[pl.ds(0, total_slabs)], grps, groups)
        copies = copies + load_rows(down_refs, wdn, local.at[pl.ds(total_slabs, total_slabs)], grps, groups)
        for copy in copies:
            copy.start()
        for copy in copies:
            copy.wait()

    made = dot(a_ref[...], wgu[...])
    gate, up = made[:, :UNITS], made[:, UNITS:]
    sig = sigmoid(gate)
    swish = gate * sig
    m_ref[...] = (swish * up).astype(HALF)
    grad = dot(c_ref[...], wdn[...])
    d_ref[:, :UNITS] = (grad * up * sig * (1.0 + gate * (1.0 - sig))).astype(HALF)
    d_ref[:, UNITS:] = (grad * swish).astype(HALF)


def feed(second, returned, both, down, grps, groups):
    tokens = second.shape[0]
    count = TALL
    return pl.pallas_call(
        functools.partial(feed_kernel, grps, groups),
        grid=(tokens // count,),
        out_shape=(
            jax.ShapeDtypeStruct((tokens, UNITS), HALF),
            jax.ShapeDtypeStruct((tokens, 2 * UNITS), HALF),
        ),
        in_specs=[
            pl.BlockSpec((count, D), lambda i: (i, 0)),
            pl.BlockSpec((count, D), lambda i: (i, 0)),
        ]
        + [pl.BlockSpec(memory_space=pl.ANY)] * (2 * grps * groups),
        out_specs=(
            pl.BlockSpec((count, UNITS), lambda i: (i, 0)),
            pl.BlockSpec((count, 2 * UNITS), lambda i: (i, 0)),
        ),
        scratch_shapes=[
            pltpu.VMEM((D, 2 * UNITS), HALF),
            pltpu.VMEM((D, UNITS), HALF),
            pltpu.SemaphoreType.DMA((2 * grps * groups,)),
        ],
        compiler_params=params(),
        name="feed",
        cost_estimate=cost(10),
    )(second, returned, *both, *down)


def ungate_kernel(
    grps, groups, steps, d_ref, w_ref, o_ref, t_ref, l_ref, q_ref, u_ref,
    do_ref, qb_ref, dg_ref, pack_ref, keep_ref, give_ref, whole,
):
    cut = D // 4
    for at in range(4):
        here = slice(at * cut, (at + 1) * cut)
        part = dot(d_ref[:, here], u_ref[...], (0, 0))
        whole[here] = jnp.where(pl.program_id(0) == 0, part, whole[here] + part)

    @pl.when(pl.program_id(0) == steps - 1)
    def sort():
        rows = D // (grps * groups)
        for turn, step, index in slabs(grps, groups):
            target = give_ref.at[turn - 1, step] if turn else keep_ref.at[step]
            target[...] = whole[pl.ds(index * rows, rows)].astype(HALF)

    grad = dot(d_ref[...], w_ref[...])
    count = grad.shape[0]
    lanes = lax.broadcasted_iota(jnp.int32, (count, LANES), 1)
    gates = (t_ref[:, :LANES], t_ref[:, LANES:])
    sums, sent = [], []
    for at in range(2):
        part = grad[:, LANES * at : LANES * (at + 1)]
        attended = o_ref[:, LANES * at : LANES * (at + 1)]
        sig = sigmoid(gates[at])
        low = (part * sig).astype(HALF).astype(FULL)
        sent.append(low)
        dg_ref[:, LANES * at : LANES * (at + 1)] = part * attended * sig * (1.0 - sig)
        sums.append(two(low * attended))
    row = lax.broadcasted_iota(jnp.int32, (LANES, LANES), 0)
    col = lax.broadcasted_iota(jnp.int32, (LANES, LANES), 1)
    of_left = jnp.where(((row < DH) & (col == 0)) | ((row >= DH) & (col == 1)), -1.0, 0.0).astype(HALF)
    of_right = jnp.where((row < DH) & (col == 2), -1.0, 0.0).astype(HALF)
    minus = dot(sums[0][0], of_left) + dot(sums[0][1], of_left) + dot(sums[1][0], of_right) + dot(sums[1][1], of_right)
    logs = jnp.where(lanes < HEADS, -l_ref[...], 0.0)
    packed = side_by_side(three(minus) + three(logs), lanes)
    grads = dot(packed, picker((HEADS * LANES, spread_lanes(0, DH))))
    sinks = dot(packed, picker((HEADS * LANES, spread_lanes(3, DH + 6))))

    def sent_lanes(col):
        head, part = lax.div(col - DH, 6), lax.rem(col - DH, 6)
        return jnp.where((col >= DH) & (col < DH + 6 * HEADS), HEADS * part + head, -1)

    extra = dot(packed, picker((LANES, sent_lanes)))
    heads = [sent[0], pltpu.roll(sent[0], DH, 1), sent[1]]
    for head in range(HEADS):
        here = slice(LANES * head, LANES * (head + 1))
        do_ref[head] = jnp.where(lanes < DH, heads[head], grads[:, here]).astype(HALF)
        qb_ref[head] = (q_ref[head].astype(FULL) + sinks[:, here]).astype(HALF)
    pack_ref[:, :LANES] = sent[0].astype(HALF)
    pack_ref[:, LANES:] = jnp.where(lanes < DH, sent[1], extra).astype(HALF)


def ungate(grads, full, attended, gates, logs, queries, gated, grps, groups):
    own = grads.shape[0]
    steps = own // TALL
    slab = D // (grps * groups)
    head_tile = pl.BlockSpec((HEADS, TALL, LANES), lambda i: (0, i, 0))
    wide_tile = pl.BlockSpec((TALL, OUT), lambda i: (i, 0))
    return pl.pallas_call(
        functools.partial(ungate_kernel, grps, groups, steps),
        grid=(steps,),
        in_specs=[
            pl.BlockSpec((TALL, D), lambda i: (i, 0)),
            weight_spec(OUT, QKVG // OUT),
            wide_tile,
            wide_tile,
            pl.BlockSpec((TALL, LANES), lambda i: (i, 0)),
            head_tile,
            wide_tile,
        ],
        out_specs=(
            head_tile,
            head_tile,
            wide_tile,
            wide_tile,
            whole_spec((groups, slab, OUT)),
            whole_spec((grps - 1, groups, slab, OUT)),
        ),
        out_shape=(
            jax.ShapeDtypeStruct((HEADS, own, LANES), HALF),
            jax.ShapeDtypeStruct((HEADS, own, LANES), HALF),
            jax.ShapeDtypeStruct((own, OUT), FULL),
            jax.ShapeDtypeStruct((own, OUT), HALF),
            jax.ShapeDtypeStruct((groups, slab, OUT), HALF),
            jax.ShapeDtypeStruct((grps - 1, groups, slab, OUT), HALF),
        ),
        scratch_shapes=[pltpu.VMEM((D, OUT), FULL)],
        compiler_params=params(),
        name="ungate",
        cost_estimate=cost(9),
    )(grads, full, attended, gates, logs, queries, gated)


def pieces(scores, product, masked, transposed):
    prob = jnp.exp(scores)
    if masked:
        row = lax.broadcasted_iota(jnp.int32, scores.shape, 0)
        col = lax.broadcasted_iota(jnp.int32, scores.shape, 1)
        keep = row <= col if transposed else col <= row
        prob = jnp.where(keep, prob, 0.0)
    return prob.astype(HALF), (prob * product).astype(HALF)


def home_plan(lines, pairs):
    member = place()[2]
    return [
        lines.plan(source.at[flip(member, bits)], target.at[member], group_device(bits))
        for source, target in pairs
        for bits in range(1, TP)
    ]


def back_kernel(
    grps, groups, q_ref, do_ref, k_ref, v_ref, a_ref, pack_ref, out_ref, up_ref, out_give, up_give, gate_ref, down_ref,
    dq_ref, dk_ref, dv_ref, late_ref, done_ref, up_sum, hgate_ref, hdown_ref,
    others, out_got, up_got, across_out, across_got, send, receive, local,
):
    device, everyone = neighbours(grps, groups)
    call_out(everyone)
    group, member = place()[1:]
    own = q_ref.shape[1]
    count = min(BLOCK, own)
    steps = own // count
    lines = Lines(send, receive)
    halves_of = [pl.ds(at * count, count) for at in range(steps)]
    packs = [
        [lines.plan(pack_ref.at[half], others.at[step - 1, half], device(to_group=groups - step)) for step in range(1, groups)]
        for half in halves_of
    ]
    over = [lines.plan(out_give.at[turn - 1], out_got.at[turn - 1], device(to_grp=turn)) for turn in range(1, grps)]
    over_up = [lines.plan(up_give.at[turn - 1], up_got.at[turn - 1], device(to_grp=turn)) for turn in range(1, grps)]
    across = [
        lines.plan(across_out.at[step - 1], across_got.at[step - 1], device(to_group=step)) for step in range(1, groups)
    ]
    pairs = ((gate_ref, hgate_ref), (down_ref, hdown_ref))
    home = home_plan(lines, pairs)
    kept = [
        pltpu.make_async_copy(source.at[member], target.at[member], local.at[at])
        for at, (source, target) in enumerate(pairs)
    ]
    hear(everyone)
    for copy in packs[0] + over + home + kept + over_up:
        copy.start()
    dk_ref[...] = jnp.zeros_like(dk_ref)
    dv_ref[...] = jnp.zeros_like(dv_ref)
    earliest = (groups - group) * steps
    for head in range(HEADS):
        for at in range(steps):
            here = halves_of[at]
            query, grad = q_ref[head, here], do_ref[head, here]

            def earlier(step, inner):
                there = pl.ds(step * count, count)
                key = k_ref[head, there]
                prob, dscore = pieces(
                    dot(query, key, (1, 1)), dot(grad, v_ref[head, there], (1, 1)), False, False
                )
                return inner + dot(dscore, key)

            dquery = lax.fori_loop(earliest, groups * steps, earlier, jnp.zeros((count, LANES), FULL))
            for step in range(at + 1):
                there = halves_of[step]
                key = k_ref[head, there]
                prob, dscore = pieces(
                    dot(key, query, (1, 1)), dot(v_ref[head, there], grad, (1, 1)), step == at, True
                )
                dk_ref[head, there] += dot(dscore, query)
                dv_ref[head, there] += dot(prob, grad)
                dquery = dquery + dot(dscore, key, (0, 0))
            dq_ref[head, here] = dquery
        if head == 0:
            for copies in packs[1:]:
                for copy in copies:
                    copy.start()
        if head == 1:
            for copy in over:
                copy.wait_recv()
            for step in range(1, groups):
                value = out_ref[step].astype(FULL)
                for turn in range(1, grps):
                    value = value + out_got[turn - 1, step].astype(FULL)
                across_out[step - 1] = value.astype(HALF)
                across[step - 1].start()

    lanes = lax.broadcasted_iota(jnp.int32, (count, LANES), 1)
    late_ref[...] = jnp.zeros_like(late_ref)

    def visit(head, carry, step, at):
        def lanes_from(first, start):
            def find(col):
                part = col - start
                return jnp.where((part >= 0) & (part < 3), DH + 6 * head + first + part, -1)

            return picker((LANES, find))

        minus, logs = lanes_from(0, DH), lanes_from(3, DH + 6)
        sent = others[step - 1, halves_of[at]].astype(FULL)
        left, right = sent[:, :LANES], sent[:, LANES:]
        grad = jnp.where(head == 0, left, jnp.where(head == 1, pltpu.roll(left, DH, 1), right))
        packed = others[step - 1, halves_of[at], LANES:]
        grad = jnp.where(lanes < DH, grad, dot(packed, minus)).astype(HALF)
        query = a_ref[head, pl.ds(step * own + at * count, count)].astype(FULL)
        query = (query + dot(packed, logs)).astype(HALF)
        for there in halves_of:
            prob, dscore = pieces(
                dot(k_ref[head, there], query, (1, 1)), dot(v_ref[head, there], grad, (1, 1)), False, True
            )
            part = dot(dscore, query)
            dk_ref[head, there] += part
            dv_ref[head, there] += dot(prob, grad)
            late_ref[head] += jnp.broadcast_to(jnp.sum(part, axis=0, keepdims=True), (8, LANES))
        return carry

    for at in range(steps):
        for step in range(1, groups):
            packs[at][step - 1].wait_recv()

            @pl.when(step < groups - group)
            def later():
                lax.fori_loop(0, HEADS, functools.partial(visit, step=step, at=at), 0)

    value = out_ref[0].astype(FULL)
    for turn in range(1, grps):
        value = value + out_got[turn - 1, 0].astype(FULL)
    for step in range(1, groups):
        across[step - 1].wait_recv()
        value = value + across_got[step - 1].astype(FULL)
    done_ref[...] = value.astype(HALF)
    value = up_ref[...].astype(FULL)
    for turn in range(1, grps):
        over_up[turn - 1].wait_recv()
        value = value + up_got[turn - 1].astype(FULL)
    up_sum[...] = value.astype(HALF)
    for copy in home:
        copy.wait_recv()
    for copy in kept:
        copy.wait()
    for copy in lines.made:
        copy.wait_send()


def attend_back(queries, grads, keys, values, span_queries, pack, out, up, out_give, up_give, gate, down):
    own, tokens = queries.shape[1], keys.shape[1]
    grps, groups, slab = out_give.shape[0] + 1, out.shape[0], out.shape[1]
    steps = own // min(BLOCK, own)
    count = steps * (groups - 1) + 2 * (grps - 1) + groups - 1 + 2 * (TP - 1)
    vmem, anywhere = pl.BlockSpec(memory_space=pltpu.VMEM), pl.BlockSpec(memory_space=pl.ANY)
    return pl.pallas_call(
        functools.partial(back_kernel, grps, groups),
        in_specs=[vmem] * 5 + [anywhere, vmem, vmem] + [anywhere] * 4,
        out_specs=(vmem,) * 6 + (anywhere,) * 2,
        out_shape=(jax.ShapeDtypeStruct((HEADS, own, LANES), FULL),) * 3
        + (
            jax.ShapeDtypeStruct((HEADS, 8, LANES), FULL),
            jax.ShapeDtypeStruct((slab, OUT), HALF),
            jax.ShapeDtypeStruct(up.shape, HALF),
            jax.ShapeDtypeStruct(gate.shape, HALF),
            jax.ShapeDtypeStruct(down.shape, HALF),
        ),
        scratch_shapes=[
            pltpu.VMEM((groups - 1, own, OUT), HALF),
            pltpu.VMEM(out_give.shape, HALF),
            pltpu.VMEM(up_give.shape, HALF),
            pltpu.VMEM((groups - 1, slab, OUT), HALF),
            pltpu.VMEM((groups - 1, slab, OUT), HALF),
            pltpu.SemaphoreType.DMA((count,)),
            pltpu.SemaphoreType.DMA((count,)),
            pltpu.SemaphoreType.DMA((2,)),
        ],
        compiler_params=params(5),
        name="attend_back",
        cost_estimate=cost(35),
    )(queries, grads, keys, values, span_queries, pack, out, up, out_give, up_give, gate, down)


def unproject_kernel(
    dq_ref, dk_ref, dv_ref, dg_ref, p_ref, z_ref, g_ref, late_ref, dp_ref, dz_ref, gain_ref, bias_ref, carry
):
    @pl.when(pl.program_id(0) == 0)
    def clear():
        first_lanes = lax.broadcasted_iota(jnp.int32, (1, LANES), 1)
        start = jnp.zeros((1, LANES), FULL)
        for head in range(HEADS):
            start = jnp.where(first_lanes == head, pltpu.roll(late_ref[head, 0:1], DH - 3 + head, 1), start)
        carry[0:1] = start
        gain_ref[...] = jnp.zeros_like(gain_ref)
        bias_ref[...] = jnp.zeros_like(bias_ref)

    count = p_ref.shape[0]
    lanes = lax.broadcasted_iota(jnp.int32, (count, LANES), 1)
    sums = jnp.zeros((count, LANES), FULL)
    means = halves_matrix(1.0 / DH)
    gates = [
        pltpu.roll(dg_ref[:, :LANES], DH, 1),
        dg_ref[:, :LANES],
        pltpu.roll(dg_ref[:, LANES:], DH, 1),
    ]
    for head in range(HEADS):
        dquery, dkey = dq_ref[head], dk_ref[head]
        found = pltpu.roll(dquery, DH + head, 1) - pltpu.roll(dkey, DH - 3 + head, 1)
        sums = jnp.where(lanes == head, found, sums)
        grad = jnp.where(lanes < DH, dquery * (DH**-0.5), pltpu.roll(dkey, DH, 1))
        pair = p_ref[:, LANES * head : LANES * (head + 1)]
        inverse = lax.rsqrt(halves_mean(pair * pair, means) + EPS)
        normal = pair * inverse
        scaled = grad * g_ref[head : head + 1]
        gain_ref[head : head + 1] += jnp.sum(grad * normal, axis=0, keepdims=True)
        pulled = inverse * (scaled - normal * halves_mean(scaled * normal, means))
        dp_ref[:, 256 * head : 256 * head + LANES] = pulled.astype(HALF)
        dp_ref[:, 256 * head + LANES : 256 * head + 2 * LANES] = jnp.where(
            lanes < DH, dv_ref[head], gates[head]
        ).astype(HALF)
    row = lax.broadcasted_iota(jnp.int32, (count, count), 0)
    col = lax.broadcasted_iota(jnp.int32, (count, count), 1)
    later = (
        lax.dot_general(
            jnp.where(col >= row, 1.0, 0.0),
            sums,
            (((1,), (0,)), ((), ())),
            precision=lax.Precision.HIGHEST,
            preferred_element_type=FULL,
        )
        + carry[0:1]
    )
    carry[0:1] = later[0:1]
    low = jnp.where(lanes < HEADS, later * sigmoid(-z_ref[...]), 0.0).astype(HALF)
    dz_ref[...] = low
    bias_ref[0:1] += jnp.sum(low.astype(FULL), axis=0, keepdims=True)


def unproject(dqueries, dkeys, dvalues, dgates, pairs, logits, gains, late):
    own = dqueries.shape[1]
    steps = own // TALL

    def back(width):
        return pl.BlockSpec((TALL, width), lambda i: (steps - 1 - i, 0))

    head_tile = pl.BlockSpec((HEADS, TALL, LANES), lambda i: (0, steps - 1 - i, 0))
    small = whole_spec((8, LANES))
    return pl.pallas_call(
        unproject_kernel,
        grid=(steps,),
        in_specs=[
            head_tile,
            head_tile,
            head_tile,
            back(OUT),
            back(HEADS * LANES),
            back(LANES),
            small,
            whole_spec((HEADS, 8, LANES)),
        ],
        out_specs=(back(QKVG), back(LANES), small, small),
        scratch_shapes=[pltpu.VMEM((8, LANES), FULL)],
        out_shape=(
            jax.ShapeDtypeStruct((own, QKVG), HALF),
            jax.ShapeDtypeStruct((own, LANES), HALF),
            jax.ShapeDtypeStruct((8, LANES), FULL),
            jax.ShapeDtypeStruct((8, LANES), FULL),
        ),
        compiler_params=params(),
        name="unproject",
        cost_estimate=cost(9),
    )(dqueries, dkeys, dvalues, dgates, pairs, logits, gains, late)


def across_groups(part, groups):
    size = groups * TP
    return [part] + [
        lax.ppermute(part, "fsdp", [((at + step * TP) % size, at) for at in range(size)])
        for step in range(1, groups)
    ]


def over_grps(parts, grps):
    return [
        [part] + [lax.ppermute(part, "grp", [((at + turn) % grps, at) for at in range(grps)]) for turn in range(1, grps)]
        for part in parts
    ]


def in_order(parts):
    return [turns[turn] for turn in range(len(parts[0])) for turns in parts]


def collected(kept):
    return sum(part.astype(FULL) for part in kept).astype(HALF)


def unpack(grad_ref, near, gate, up, down, out):
    lanes = lax.broadcasted_iota(jnp.int32, (near.shape[1], LANES), 1)

    def half(ref, part, upper):
        member, at, side = part
        value = ref[member, :, at : at + LANES].astype(FULL)
        return pltpu.roll(value, DH, 1) if side != upper else value

    def store(at, ref, lower, upper):
        value = jnp.where(lanes < DH, half(ref, lower, False), half(ref, upper, True))
        grad_ref[:, at : at + LANES] = value.astype(HALF)

    for at in range(0, H, 2):
        for kind in range(4):
            pair = [
                (head // HEADS, 256 * (head % HEADS) + LANES * (kind // 2), kind % 2 == 1) for head in (at, at + 1)
            ]
            store(kind * D + at * DH, near, *pair)
        pair = [
            (head // HEADS, LANES * (head % HEADS // 2), head % HEADS % 2 == 1) for head in (at, at + 1)
        ]
        store(4 * D + at * DH, out, *pair)
    for member in range(TP):
        at = 5 * D + member * UNITS
        grad_ref[:, at : at + UNITS] = gate[member]
        grad_ref[:, at + F : at + F + UNITS] = up[member]
        grad_ref[:, at + 2 * F : at + 2 * F + UNITS] = down[member]


PARTS = 2


def end_counts(grps, groups):
    replicas = grps * groups - 1
    return 7 + PARTS * ((grps - 1) * groups + groups - 1) + 4 * (TP - 1) + replicas


def sort_small(every, gains_ref, forget_ref, bias_ref):
    lanes = lax.broadcasted_iota(jnp.int32, (1, LANES), 1)
    rest = HEADS + 2
    gains_ref[0:2] = jnp.sum(every[:, HEADS : HEADS + 2], axis=0)

    def part(head, kind, upper):
        row = every[head // HEADS, rest : rest + 1]
        return half_lanes(row, (kind * HEADS + head % HEADS) * DH, upper)

    for kind in range(2):
        for head in range(0, H, 2):
            gains_ref[2 + kind : 3 + kind, head * DH : (head + 2) * DH] = jnp.where(
                lanes < DH, part(head, kind, False), part(head + 1, kind, True)
            )
    bias = jnp.zeros((1, LANES), FULL)
    edge = 2 * HEADS * DH
    for member in range(TP):
        forget_ref[member * HEADS : (member + 1) * HEADS] = every[member, :HEADS]
        moved = every[member, rest : rest + 1, edge : edge + LANES]
        if member:
            moved = pltpu.roll(moved, member * HEADS, 1)
        bias = jnp.where((lanes >= member * HEADS) & (lanes < (member + 1) * HEADS), moved, bias)
    bias_ref[...] = jnp.broadcast_to(bias, bias_ref.shape)


def end_kernel(
    grps, groups,
    p_ref, z_ref, f_ref, x_ref, g_ref, d_ref, mid_ref, heads_ref, bias_ref_in, out_ref, up_ref, hgate_ref, hdown_ref, w_ref, t_ref, *rest
):
    y_ref, grad_ref, gains_ref, forget_ref, bias_ref, norm_ref, *rest = rest
    small_ref, hnear_ref, hup_ref, hout_ref, *rest = rest
    weights, tokens, near, mine, give, take, out, came, over_got, across_out, across_got, last, *rest = rest
    packet, packets, send, receive, local = rest
    grp, group, member = place()
    device, everyone = neighbours(grps, groups)
    replicas = [(turn, step) for turn in range(grps) for step in range(groups) if turn or step]
    everyone = everyone + [device(turn, step) for turn, step in replicas if turn and step]
    call_out(everyone)
    count = tokens.shape[0]
    load_tokens = pltpu.make_async_copy(t_ref, tokens, local.at[0])
    load_weights = pltpu.make_async_copy(w_ref.at[:, pl.ds(0, QKVG)], weights, local.at[1])
    load_tokens.start()
    load_weights.start()
    lines = Lines(send, receive)
    stage = (give, take, out, came)
    sums = sum_plan(lines, stage)
    slab = near.shape[0] // (grps * groups)
    part_rows = slab // PARTS
    own = last.shape[2]
    over, across, home = {}, {}, {}

    def rows_of(turn, step, part):
        side = lax.div(member, 4)
        side = side + part - 2 * part * side
        index = lax.rem(grp + turn, grps) * groups + lax.rem(group + step, groups)
        return pl.ds(index * slab + side * part_rows, part_rows)

    order = [(ahead, part) for ahead in list(range(1, groups)) + [0] for part in (1, 0)]
    for ahead, part in order:
        for turn in range(1, grps):
            over[turn, ahead, part] = lines.plan(
                near.at[rows_of(turn, ahead, part)], over_got.at[turn - 1, ahead, part], device(turn)
            )
        if ahead:
            across[ahead, part] = lines.plan(
                across_out.at[ahead - 1, part], across_got.at[ahead - 1, part], device(to_group=ahead)
            )
    for bits in range(1, TP):
        source = last.at[bits // 4, lax.rem(flip(member, bits), 4)]
        home[bits] = lines.plan(source, hnear_ref.at[member], device(bits=bits))
    far = home_plan(lines, ((out_ref, hout_ref), (up_ref, hup_ref)))
    shared = [lines.plan(packet, packets.at[at], device(turn, step)) for at, (turn, step) in enumerate(replicas)]
    told = [lines.plan(small_ref.at[member], small_ref.at[member], device(bits=bits)) for bits in range(1, TP)]

    projected = p_ref[...].reshape(count, QKVG)
    cut = D // 4
    load_tokens.wait()
    for at in range(4):
        here = slice(at * cut, (at + 1) * cut)
        near[here] = dot(tokens[:, here], projected, (0, 0)).astype(HALF)
    hear(everyone)
    for turn in range(1, grps):
        for ahead in range(1, groups):
            over[turn, ahead, 1].start()
    for copy in far:
        copy.start()
    load_weights.wait()
    sum_give([(p_ref, weights), (z_ref, f_ref)], stage, sums, mine)
    summed = sum_pass(stage, sums, mine)
    for part in (1, 0):
        for ahead in range(1, groups):
            if part == 1:
                for turn in range(1, grps):
                    over[turn, ahead, 1].wait_recv()
                    over[turn, ahead, 0].start()
            elif ahead == 1:
                for turn in range(1, grps):
                    for last_part in (1, 0):
                        over[turn, 0, last_part].start()
            total = near[rows_of(0, ahead, part)].astype(FULL)
            for turn in range(1, grps):
                if part == 0:
                    over[turn, ahead, part].wait_recv()
                total = total + over_got[turn - 1, ahead, part].astype(FULL)
            across_out[ahead - 1, part] = total.astype(HALF)
            across[ahead, part].start()
    packet[...] = jnp.zeros_like(packet)
    packet[HEADS + 1 : HEADS + 2] = mid_ref[...]
    lanes = lax.broadcasted_iota(jnp.int32, (1, LANES), 1)
    pairs_of = [heads_ref[head : head + 1] for head in range(HEADS)]
    swapped = [pltpu.roll(pair, DH, 1) for pair in pairs_of]
    rest_row = slice(HEADS + 2, HEADS + 3)
    packet[rest_row, :LANES] = jnp.where(lanes < DH, pairs_of[0], swapped[1])
    packet[rest_row, LANES : 2 * LANES] = jnp.where(lanes < DH, pairs_of[2], pairs_of[0])
    packet[rest_row, 2 * LANES : 3 * LANES] = jnp.where(lanes < DH, swapped[1], pairs_of[2])
    packet[rest_row, 3 * LANES : 4 * LANES] = jnp.where(lanes < HEADS, bias_ref_in[0:1], 0.0)
    forget = dot(z_ref[...].reshape(count, LANES), tokens[...], (0, 0))
    packet[0:HEADS] = forget[0:HEADS]

    def square(value):
        value = value.astype(FULL)
        return jnp.sum(value * value)

    squares = square(hgate_ref[...]) + square(hdown_ref[...]) + square(out_ref[...]) + square(up_ref[...])
    summed = sum_take(summed, stage, sums)
    for source, target in ((out_ref, hout_ref), (up_ref, hup_ref)):
        target[member] = source[member]
    pulled, dgain = rms_back(x_ref[...].astype(FULL), g_ref[...], summed)
    y_ref[...] = (d_ref[...] + pulled).astype(HALF)
    packet[HEADS : HEADS + 1] = dgain
    for part in (1, 0):
        total = near[rows_of(0, 0, part)].astype(FULL)
        for turn in range(1, grps):
            over[turn, 0, part].wait_recv()
            total = total + over_got[turn - 1, 0, part].astype(FULL)
        for ahead in range(1, groups):
            across[ahead, part].wait_recv()
            total = total + across_got[ahead - 1, part].astype(FULL)
        squares = squares + square(total)
        for at in range(4):
            last[part, at] = total[at * own : (at + 1) * own].astype(HALF)
        for bits in range(max(4 * part, 1), 4 * part + 4):
            home[bits].start()
    packet[HEADS + 3 : HEADS + 4] = jnp.full((1, D), squares, FULL)
    for copy in shared:
        copy.start()
    hnear_ref[member] = last[0, lax.rem(member, 4)]
    total = packet[...]
    for at, copy in enumerate(shared):
        copy.wait_recv()
        total = total + packets[at]
    small_ref[member] = total
    for copy in told:
        copy.start()
    for copy in far + list(home.values()):
        copy.wait_recv()
    unpack(grad_ref, hnear_ref, hgate_ref, hup_ref, hdown_ref, hout_ref)
    for copy in told:
        copy.wait_recv()
    every = small_ref[...]
    sort_small(every, gains_ref, forget_ref, bias_ref)
    gains = gains_ref[...]
    heads = jnp.sum(every[:, :HEADS] * every[:, :HEADS]) + jnp.sum(gains * gains)
    edge = 2 * HEADS * DH
    heads = heads + jnp.sum(every[:, HEADS + 2, edge : edge + LANES] * every[:, HEADS + 2, edge : edge + LANES])
    matrices = jnp.sum(every[:, HEADS + 3, :LANES], axis=0, keepdims=True)
    norm_ref[...] = jnp.sqrt(jnp.broadcast_to(matrices + heads, (8, LANES)))
    for copy in lines.made:
        copy.wait_send()


def end(projected, logits, forget, source, gain, grad, mid, heads, bias, out, up, gate, down, near, tokens, grps, groups):
    rows, own = source.shape[0], gate.shape[1]
    count = end_counts(grps, groups)
    replicas = grps * groups - 1
    slab = TP * own
    part = (slab // PARTS, QKVG)
    vmem, anywhere = pl.BlockSpec(memory_space=pltpu.VMEM), pl.BlockSpec(memory_space=pl.ANY)
    return pl.pallas_call(
        functools.partial(end_kernel, grps, groups),
        out_shape=(
            jax.ShapeDtypeStruct((rows, D), HALF),
            jax.ShapeDtypeStruct((own, 5 * D + 3 * F), HALF),
            jax.ShapeDtypeStruct((4, D), FULL),
            jax.ShapeDtypeStruct((H, D), FULL),
            jax.ShapeDtypeStruct((8, LANES), FULL),
            jax.ShapeDtypeStruct((8, LANES), FULL),
        ),
        in_specs=[vmem] * 13 + [anywhere] * 2,
        out_specs=(vmem,) * 6,
        scratch_shapes=[
            pltpu.VMEM((TP, 8, D), FULL),
            pltpu.VMEM((TP, own, QKVG), HALF),
            pltpu.VMEM((TP, own, UNITS), HALF),
            pltpu.VMEM((TP, own, OUT), HALF),
            pltpu.VMEM((D, QKVG), HALF),
            pltpu.VMEM((TP * rows, D), HALF),
            pltpu.VMEM((D, QKVG), HALF),
            pltpu.VMEM((4, rows, D), FULL),
        ]
        + sum_scratch(rows)
        + [
            pltpu.VMEM((grps - 1, groups, PARTS) + part, HALF),
            pltpu.VMEM((groups - 1, PARTS) + part, HALF),
            pltpu.VMEM((groups - 1, PARTS) + part, HALF),
            pltpu.VMEM((PARTS, 4, own, QKVG), HALF),
            pltpu.VMEM((8, D), FULL),
            pltpu.VMEM((replicas, 8, D), FULL),
            pltpu.SemaphoreType.DMA((count,)),
            pltpu.SemaphoreType.DMA((count,)),
            pltpu.SemaphoreType.DMA((2,)),
        ],
        compiler_params=params(4),
        name="end",
        cost_estimate=cost(60),
    )(
        projected.reshape(4, 2, rows, QKVG),
        logits.reshape(4, 2, rows, LANES),
        forget,
        source,
        gain,
        grad,
        mid,
        heads,
        bias,
        out,
        up,
        gate,
        down,
        near,
        tokens,
    )


def adam(value, first, second, grad, rate, decay):
    first = BETA_ONE * first + (1.0 - BETA_ONE) * grad
    second = BETA_TWO * second + (1.0 - BETA_TWO) * grad * grad
    unbiased_first = first * (1.0 / (1.0 - BETA_ONE**STEP))
    unbiased_second = second * (1.0 / (1.0 - BETA_TWO**STEP))
    value = value - rate * (unbiased_first / (jnp.sqrt(unbiased_second) + ADAM_EPS) + decay * value)
    return (value, first, second)


def pad_lanes(value, width=LANES):
    return jnp.pad(value, ((0, 0), (0, width - value.shape[1])))


def shards(
    inputs,
    cotangent,
    weights,
    weights_first,
    weights_second,
    gains,
    gains_first,
    gains_second,
    forget_weight,
    forget_first,
    forget_second,
    forget_bias,
    bias_first,
    bias_second,
):
    grps, groups = lax.axis_size("grp"), lax.axis_size("fsdp") // TP
    grp, group, member = place()
    rows, own_rows = inputs.shape[1], weights.shape[0]
    group_tokens = TP * rows
    source, returned = inputs[0], cotangent[0]

    tokens, following, near, both, down = start(source, gains[0:1], weights, grps, groups)
    slab = TP * own_rows
    both, down = both.reshape(slab, 2 * UNITS), down.reshape(slab, UNITS)
    tokens = tokens.reshape(group_tokens, D)
    near = near.reshape(D, NEAR)
    both_parts = across_groups(both, groups)
    both_own, down_own = over_grps(both_parts[:1], grps), over_grps([down], grps)

    forget_low = pad_lanes(lax.dynamic_slice_in_dim(forget_weight, member * HEADS, HEADS, 1).astype(HALF))
    bias = pad_lanes(lax.dynamic_slice_in_dim(forget_bias[None], member * HEADS, HEADS, 1))
    head_gains = lax.dynamic_slice_in_dim(gains[2:4], member * HEADS * DH, HEADS * DH, 1)
    head_gains = head_gains.reshape(2, HEADS, DH).transpose(1, 0, 2).reshape(HEADS, 2 * DH)
    head_gains = jnp.pad(head_gains, ((0, 8 - HEADS), (0, 0)))
    queries, keys, values, pairs, gates, logits, gathered = project(
        tokens, following, near, forget_low, bias, head_gains, returned
    )
    queries, down = lax.optimization_barrier((queries, down))
    down_parts = across_groups(down, groups)
    gated, attended, logs, gathered = attend(queries, keys, values, gates, gathered, groups)
    returned_all = gathered.reshape(group_tokens, D)
    gated, both_parts, down_parts = lax.optimization_barrier((gated, both_parts[1:], down_parts[1:]))
    both_pieces = in_order(both_own + over_grps(both_parts, grps))
    down_pieces = in_order(down_own + over_grps(down_parts, grps))
    mixed, second = mix(gated, near, source, gains[1:2])
    second = second.reshape(group_tokens, D)
    hidden, grad_both = feed(second, returned_all, both_pieces, down_pieces, grps, groups)
    grad_mixed, grad_gain_mid, branch, beside, along, far_gate, far_down, up_give, *far_up = unmix(
        grad_both, both_pieces, down_pieces, mixed, gains[1:2], returned, hidden, second, returned_all, grps, groups
    )
    branch = branch.reshape(group_tokens, D)
    size = lax.axis_size("fsdp")
    beside = lax.ppermute(beside, "fsdp", [(to, to ^ 2) for to in range(size)])
    up_keep = far_up[0]
    far_up = [
        lax.ppermute(far_up[step], "fsdp", [(at, (at + step * TP) % size) for at in range(size)])
        for step in range(1, groups)
    ]

    grads_low, queries_back, grad_gates, pack, out_keep, out_give = ungate(
        branch, near, attended, gates, logs, queries, gated, grps, groups
    )
    dqueries, dkeys, dvalues, late, far_out, up_sum, home_gate, home_down = attend_back(
        queries_back,
        grads_low,
        keys,
        values,
        queries,
        pack,
        out_keep,
        up_keep,
        out_give,
        up_give,
        far_gate.reshape(TP, own_rows, UNITS),
        far_down.reshape(TP, own_rows, UNITS),
    )
    if groups > 2:
        everyone = lax.all_gather(dkeys[:, :, DH + 3].sum(axis=1) - dqueries[:, :, DH].sum(axis=1), "fsdp")
        ahead = (jnp.arange(size) // TP > group) & (jnp.arange(size) % TP == member)
        later = -jnp.sum(jnp.where(ahead[:, None], everyone, 0.0), axis=0)
        late = jnp.broadcast_to(later[:, None, None], late.shape)
    grad_projected, grad_logits, grad_heads, grad_bias = unproject(
        dqueries, dkeys, dvalues, grad_gates, pairs, logits, head_gains, late
    )

    input_grad, grads, grad_gains, grad_forget, grad_bias, norm = end(
        grad_projected,
        grad_logits,
        forget_low,
        source,
        gains[0:1],
        grad_mixed,
        grad_gain_mid,
        grad_heads,
        grad_bias,
        far_out.reshape(TP, own_rows, OUT),
        collected([up_sum] + far_up).reshape(TP, own_rows, UNITS),
        home_gate,
        home_down,
        near,
        tokens,
        grps,
        groups,
    )
    norm, beside = lax.optimization_barrier((norm, beside))
    across_chip = (along[0].astype(FULL) + beside[1].astype(FULL)).astype(HALF)
    result = mixed + along[1].astype(FULL) + beside[0].astype(FULL)
    result = result + lax.ppermute(across_chip, "fsdp", [(to, to ^ 4) for to in range(size)]).astype(FULL)
    output = result.astype(HALF)
    grad_norm = norm[0, 0]
    grad_forget, grad_bias = grad_forget.T, grad_bias[0, :H]
    factor = CLIP / jnp.maximum(grad_norm, CLIP)
    new_w, new_wf, new_ws = adam(
        weights, weights_first, weights_second, grads.astype(FULL) * factor, RATE_MATRIX, DECAY
    )
    new_g, new_gf, new_gs = adam(gains, gains_first, gains_second, grad_gains * factor, RATE_GAIN, 0.0)
    new_fw, new_ff, new_fs = adam(
        forget_weight, forget_first, forget_second, grad_forget * factor, RATE_MATRIX, DECAY
    )
    new_fb, new_bf, new_bs = adam(
        forget_bias, bias_first, bias_second, grad_bias * factor, RATE_BIAS, 0.0
    )
    return (
        output[None],
        input_grad[None],
        grad_norm,
        new_w,
        new_wf,
        new_ws,
        new_g,
        new_gf,
        new_gs,
        new_fw,
        new_ff,
        new_fs,
        new_fb,
        new_bf,
        new_bs,
    )


def solution(mesh):
    tokens = P("grp", "fsdp", None)
    matrix = P(("grp", "fsdp"), None)
    return jax.shard_map(
        shards,
        mesh=mesh,
        in_specs=(tokens,) * 2 + (matrix,) * 3 + (P(),) * 9,
        out_specs=(tokens,) * 2 + (P(),) + (matrix,) * 3 + (P(),) * 9,
        check_vma=False,
    )
```
